32 devices in a mesh: ctx: 8 (over z, core), fsdp: 4 (over y, x).
Axes of the slice: x: 2, y: 2, z: 4, core: 2. Of those that a mesh axis runs over, the one named last changes fastest.
Arguments:
- hidden: bfloat16 [4, 1024, 2048], P('fsdp', 'ctx'), may hold values from -8 to 8
- ln1_gain: float32 [2048], P('fsdp'), may hold values from 0.5 to 1.5
- ln1_bias: float32 [2048], P('fsdp'), may hold values from -1.75 to 1.75
- qkv_weight: bfloat16 [2048, 6144], P('fsdp'), may hold values from -0.125 to 0.125
- qkv_bias: float32 [6144], P('fsdp'), may hold values from -1.75 to 1.75
- dense_weight: bfloat16 [2048, 2048], P('fsdp'), may hold values from -0.75 to 0.75
- dense_bias: float32 [2048], P('fsdp'), may hold values from -1.75 to 1.75
- ln2_gain: float32 [2048], P('fsdp'), may hold values from 0.5 to 1.5
- ln2_bias: float32 [2048], P('fsdp'), may hold values from -1.75 to 1.75
- fc1_weight: bfloat16 [2048, 8192], P('fsdp'), may hold values from -0.125 to 0.125
- fc1_bias: float32 [8192], P('fsdp'), may hold values from -1.75 to 1.75
- fc2_weight: bfloat16 [8192, 2048], P('fsdp'), may hold values from -0.0625 to 0.0625
- fc2_bias: float32 [2048], P('fsdp'), may hold values from -1.75 to 1.75
- segments: int32 [4, 1024], P('fsdp', 'ctx'), may hold values from 0 to 6, as said below
- out_grad: bfloat16 [4, 1024, 2048], P('fsdp', 'ctx'), may hold values from -6 to 6
Outputs:
- layer_output: bfloat16 [4, 1024, 2048], P('fsdp', 'ctx')
- input_grad: bfloat16 [4, 1024, 2048], P('fsdp', 'ctx')
- ln1_gain_grad: float32 [2048], P('fsdp')
- ln1_bias_grad: float32 [2048], P('fsdp')
- qkv_weight_grad: float32 [2048, 6144], P('fsdp')
- qkv_bias_grad: float32 [6144], P('fsdp')
- dense_weight_grad: float32 [2048, 2048], P('fsdp')
- dense_bias_grad: float32 [2048], P('fsdp')
- ln2_gain_grad: float32 [2048], P('fsdp')
- ln2_bias_grad: float32 [2048], P('fsdp')
- fc1_weight_grad: float32 [2048, 8192], P('fsdp')
- fc1_bias_grad: float32 [8192], P('fsdp')
- fc2_weight_grad: float32 [8192, 2048], P('fsdp')
- fc2_bias_grad: float32 [2048], P('fsdp')
The draws below stay inside these ranges and needn't reach their ends.
Inputs may be any that keep to these rules, and one draw needn't show every extreme that they name: `segments`: never decreases along a sequence.
All inputs are finite; a program needn't handle non-finite values.
Results may differ from the reference program's by a relative error of at most 0.01.
Values may be sent and summed in bfloat16 or wider, within the bound.
A program may use at most 576 MiB of HBM per device.

```python
import math
import jax
import jax.numpy as jnp
from jax import lax

D = 2048
HEADS = 8
FF = 8192
ROT = 64
TOK_DEV = 128
HEAD_DIM = 256
LEN = 1024
SEQS = 4


def draw_segments(key, part):
    key = jax.random.fold_in(key, 7)
    key_first, key_last = jax.random.split(key)
    first_cuts = jax.random.randint(key_first, (SEQS, 3), 1, TOK_DEV)
    last_cuts = jax.random.randint(key_last, (SEQS, 3), LEN - TOK_DEV + 1, LEN)
    cuts = jnp.concatenate([first_cuts, last_cuts], axis=1).astype(jnp.int32)
    places = jnp.arange(LEN, dtype=jnp.int32)
    return jnp.sum((cuts[:, None, :] <= places[None, :, None]).astype(jnp.int32), axis=2).astype(jnp.int32)


def with_spikes(entries, own_key, source, target, blocks, factor):
    owner, partner = [(jnp.arange(entries.shape[axis_at]) // (entries.shape[axis_at] // blocks)).reshape([-1 if axis == axis_at else 1 for axis in range(entries.ndim)]) for axis_at in (source, target)]
    chosen = jax.random.permutation(own_key, blocks)[partner]
    strong = (owner == chosen) | (owner == (partner + blocks // 2) % blocks)
    return jnp.where(strong, factor * entries, entries)


def levels(rng, dims, shards, least, largest):
    def one(axis_at, parts):
        steps = jax.random.uniform(jax.random.fold_in(jax.random.fold_in(rng, 6), axis_at), (parts,), jnp.float32, least / len(shards), largest / len(shards))
        return jnp.repeat(jnp.exp(steps), dims[axis_at] // parts).reshape((-1,) + (1,) * (len(dims) - axis_at - 1))

    level = one(*shards[0])
    for cut in shards[1:]:
        level = level * one(*cut)
    return level


def noise(stream_key, shape, scale, most, cuts=(), held_as=jnp.bfloat16):
    values = scale * jax.random.normal(stream_key, shape, jnp.float32)
    if cuts:
        values = values * levels(stream_key, shape, cuts, -0.22, 0.18)
    return jnp.clip(values, -most, most).astype(held_as)


def noise_with(stream_key, extent, scale, limit, cuts, heavy, kind=jnp.bfloat16):
    values = scale * jax.random.normal(stream_key, extent, jnp.float32)
    if cuts:
        values = values * levels(stream_key, extent, cuts, -0.22, 0.18)
    return jnp.clip(with_spikes(values, jax.random.fold_in(stream_key, 3), *heavy), -limit, limit).astype(kind)


def setup_inputs(seed: int = 0) -> dict:
    arg_keys = jax.random.split(jax.random.key(seed), 16)
    return {
        "hidden": noise_with(arg_keys[0], (SEQS, LEN, D), 1.0, 8.0, ((0, 4), (1, 8)), (1, 2, 8, 2.0)),
        "ln1_gain": jnp.clip(1.0 + 0.1 * jax.random.normal(arg_keys[1], (D,), jnp.float32), 0.5, 1.5),
        "ln1_bias": noise(arg_keys[2], (D,), 0.3, 1.75, ((0, 4),), jnp.float32),
        "qkv_weight": noise(arg_keys[3], (D, 3 * D), D ** -0.5, 0.125, ((0, 4),)),
        "qkv_bias": noise(arg_keys[4], (3 * D,), 0.3, 1.75, ((0, 4),), jnp.float32),
        "dense_weight": noise(arg_keys[5], (D, D), (D // 32) ** -0.5, 0.75, ((0, 4),)),
        "dense_bias": noise(arg_keys[6], (D,), 0.3, 1.75, ((0, 4),), jnp.float32),
        "ln2_gain": jnp.clip(1.0 + 0.1 * jax.random.normal(arg_keys[7], (D,), jnp.float32), 0.5, 1.5),
        "ln2_bias": noise(arg_keys[8], (D,), 0.3, 1.75, ((0, 4),), jnp.float32),
        "fc1_weight": noise(arg_keys[9], (D, FF), D ** -0.5, 0.125, ((0, 4),)),
        "fc1_bias": noise(arg_keys[10], (FF,), 0.3, 1.75, ((0, 4),), jnp.float32),
        "fc2_weight": noise(arg_keys[11], (FF, D), FF ** -0.5, 0.0625, ((0, 4),)),
        "fc2_bias": noise(arg_keys[12], (D,), 0.3, 1.75, ((0, 4),), jnp.float32),
        "segments": draw_segments(jax.random.fold_in(arg_keys[15], 71), 0),
        "out_grad": noise(arg_keys[14], (SEQS, LEN, D), 1.0, 6.0, ((0, 4), (1, 8))),
    }


@jax.custom_vjp
def low(v):
    return lax.optimization_barrier(v.astype(jnp.bfloat16)).astype(jnp.float32)

@jax.custom_vjp
def low_back(v):
    return v

def low_keep(v):
    return (low(v), None)

def low_pass(kept, grad):
    return (grad,)

def back_keep(v):
    return (v, None)

def back_low(kept, grad):
    return (low(grad),)
low.defvjp(low_keep, low_pass)
low_back.defvjp(back_keep, back_low)

def matmul_high(left, right):
    return jnp.matmul(left, right, precision=lax.Precision.HIGHEST, preferred_element_type=jnp.float32)

def layer_norm(values, gain, shift):
    center = values - lax.optimization_barrier(jnp.mean(values, axis=-1, keepdims=True))
    spread = lax.optimization_barrier(jnp.mean(center * center, axis=-1, keepdims=True))
    return center * lax.rsqrt(spread + 1e-05) * gain + shift

def rotary_tables(places, width):
    half_rot = width // 2
    freqs = 10000.0 ** (-2.0 * jnp.arange(half_rot, dtype=jnp.float32) / width)
    angles = places.astype(jnp.float32)[:, None] * freqs[None, :]
    return (jnp.cos(angles), jnp.sin(angles))

def rotate(values, cosine, sine):
    half_rot = cosine.shape[-1]
    first = values[..., :half_rot]
    second = values[..., half_rot:2 * half_rot]
    remain = values[..., 2 * half_rot:]
    cos_b = cosine[:, None, :]
    sin_b = sine[:, None, :]
    return jnp.concatenate([first * cos_b - second * sin_b, second * cos_b + first * sin_b, remain], axis=-1)

def reference(hidden, ln1_gain, ln1_bias, qkv_weight, qkv_bias, dense_weight, dense_bias, ln2_gain, ln2_bias, fc1_weight, fc1_bias, fc2_weight, fc2_bias, segments, out_grad):
    places = jnp.arange(LEN, dtype=jnp.int32)
    cosine, sine = rotary_tables(places, ROT)
    query_rows = math.gcd(LEN, 512)
    blocks_per = LEN // query_rows
    factor = HEAD_DIM ** (-0.5)

    def forward(residual, gain_one, shift_one, joined_w, joined_b, dense_w, dense_b, gain_two, shift_two, up_w, up_b, down_w, down_b):
        normed_one = low(layer_norm(residual, gain_one, shift_one))
        joined = low_back(matmul_high(normed_one, joined_w) + joined_b)
        query_all = low(rotate(joined[..., :D].reshape(SEQS, LEN, HEADS, HEAD_DIM), cosine, sine))
        key_all = low(rotate(joined[..., D:2 * D].reshape(SEQS, LEN, HEADS, HEAD_DIM), cosine, sine))
        value_all = low(joined[..., 2 * D:].reshape(SEQS, LEN, HEADS, HEAD_DIM))

        def attend(item):
            queries, index = item
            sequence = index // blocks_per
            offset = index % blocks_per * query_rows
            key_rows = lax.dynamic_index_in_dim(key_all, sequence, 0, keepdims=False)
            value_rows = lax.dynamic_index_in_dim(value_all, sequence, 0, keepdims=False)
            seg_row = lax.dynamic_index_in_dim(segments, sequence, 0, keepdims=False)
            query_seg = lax.dynamic_slice_in_dim(seg_row, offset, query_rows)
            query_place = offset + jnp.arange(query_rows, dtype=jnp.int32)
            allowed = (places[None, :] <= query_place[:, None]) & (seg_row[None, :] == query_seg[:, None])
            scores = jnp.einsum('qhd,khd->hqk', queries, key_rows, precision=lax.Precision.HIGHEST) * factor
            scores = low_back(jnp.where(allowed[None], scores, -1e+30))
            probs = jax.nn.softmax(scores, axis=-1)
            return jnp.einsum('hqk,khd->qhd', low(probs), value_rows, precision=lax.Precision.HIGHEST)
        pieces = query_all.reshape(SEQS * blocks_per, query_rows, HEADS, HEAD_DIM)
        indexes = jnp.arange(SEQS * blocks_per, dtype=jnp.int32)
        attended = lax.map(jax.checkpoint(attend), (pieces, indexes))
        attended = low(low_back(attended.reshape(SEQS, LEN, D)))
        branch_one = matmul_high(attended, dense_w) + dense_b
        normed_two = low(layer_norm(residual, gain_two, shift_two))
        up_value = low_back(matmul_high(normed_two, up_w) + up_b)
        activated = low(jax.nn.gelu(up_value, approximate=False))
        branch_two = matmul_high(activated, down_w) + down_b
        return residual + branch_one + branch_two
    primals = (hidden.astype(jnp.float32), ln1_gain.astype(jnp.float32), ln1_bias.astype(jnp.float32), qkv_weight.astype(jnp.float32), qkv_bias.astype(jnp.float32), dense_weight.astype(jnp.float32), dense_bias.astype(jnp.float32), ln2_gain.astype(jnp.float32), ln2_bias.astype(jnp.float32), fc1_weight.astype(jnp.float32), fc1_bias.astype(jnp.float32), fc2_weight.astype(jnp.float32), fc2_bias.astype(jnp.float32))
    result, pullback = jax.vjp(forward, *primals)
    grads = pullback(out_grad.astype(jnp.float32))
    return (result.astype(jnp.bfloat16), grads[0].astype(jnp.bfloat16), grads[1], grads[2], grads[3], grads[4], grads[5], grads[6], grads[7], grads[8], grads[9], grads[10], grads[11], grads[12])
```

```python
import jax
import jax.numpy as jnp
from jax import lax
from jax.sharding import PartitionSpec as P

HEADS = 8
ROT = 64
CORES = 2


def dot(left, right):
    return jnp.dot(left, right, preferred_element_type=jnp.float32)


def dot_rows(left, right):
    return lax.dot_general(
        left, right, (((0,), (0,)), ((), ())), preferred_element_type=jnp.float32
    )


def dot_cols(left, right):
    return lax.dot_general(
        left, right, (((1,), (1,)), ((), ())), preferred_element_type=jnp.float32
    )


def gelu_and_slope(values):
    cdf = 0.5 * (1.0 + lax.erf(values * (0.5**0.5)))
    density = jnp.exp(-0.5 * values * values) * ((2.0 * jnp.pi) ** -0.5)
    return values * cdf, cdf + values * density


def rotary_tables(places, width):
    half_rot = width // 2
    freqs = 10000.0 ** (-2.0 * jnp.arange(half_rot, dtype=jnp.float32) / width)
    angles = places.astype(jnp.float32)[:, None] * freqs[None, :]
    return (jnp.cos(angles), jnp.sin(angles))


def rotate(values, cosine, sine):
    half = cosine.shape[-1]
    first, second, remain = values[:, :half], values[:, half : 2 * half], values[:, 2 * half :]
    return jnp.concatenate(
        [first * cosine - second * sine, second * cosine + first * sine, remain], axis=1
    )


def line_gather(block):
    count = lax.axis_size("ctx")
    chips = count // CORES
    ctx = lax.axis_index("ctx")
    place, core = ctx // CORES, ctx % CORES
    up = down = block
    ups, downs = [], []
    for hop in range(1, chips):
        up = lax.ppermute(
            up,
            "ctx",
            [
                (i * CORES + k, (i + 1) * CORES + k)
                for i in range(hop - 1, chips - 1)
                for k in range(CORES)
            ],
        )
        down = lax.ppermute(
            down,
            "ctx",
            [
                (i * CORES + k, (i - 1) * CORES + k)
                for i in range(1, chips - hop + 1)
                for k in range(CORES)
            ],
        )
        ups.append(up)
        downs.append(down)
    around = jnp.stack(ups[::-1] + [block] + downs)
    mine = lax.dynamic_slice_in_dim(around, chips - 1 - place, chips, 0)
    other = lax.ppermute(mine, "ctx", [(i, i ^ 1) for i in range(count)])
    is_mine = (jnp.arange(CORES) == core).reshape((1, CORES) + (1,) * block.ndim)
    return jnp.where(is_mine, mine[:, None], other[:, None]).reshape((count,) + block.shape)


def gather_fsdp(values, axis=0):
    return lax.all_gather(values, "fsdp", axis=axis, tiled=True)


def scatter_fsdp(values):
    return lax.psum_scatter(values, "fsdp", scatter_dimension=0, tiled=True)


def per_device(
    hidden,
    ln1_gain,
    ln1_bias,
    qkv_weight,
    qkv_bias,
    dense_weight,
    dense_bias,
    ln2_gain,
    ln2_bias,
    fc1_weight,
    fc1_bias,
    fc2_weight,
    fc2_bias,
    segments,
    out_grad,
):
    ctx_count = lax.axis_size("ctx")
    shards = lax.axis_size("fsdp")
    ctx = lax.axis_index("ctx")
    tokens, width = hidden.shape[1], hidden.shape[2]
    length = tokens * ctx_count
    head_dim = width // HEADS
    repeat = ctx_count // HEADS
    head = ctx // repeat
    factor = head_dim ** (-0.5)
    rows = width // shards
    ff = fc1_weight.shape[1]
    units = ff // shards // ctx_count
    bf16, f32 = jnp.bfloat16, jnp.float32

    vectors = [
        ln1_gain, ln1_bias, dense_bias, ln2_gain, ln2_bias, fc2_bias, qkv_bias, fc1_bias
    ]
    packed = lax.all_gather(jnp.concatenate(vectors), "fsdp", axis=0)
    split, at = [], 0
    for vector in vectors:
        split.append(packed[:, at : at + vector.shape[0]].reshape(-1))
        at += vector.shape[0]
    gain_one, shift_one, dense_shift, gain_two, shift_two, down_shift, qkv_shift, up_shift = split
    query_seg = lax.all_gather(segments[0], "ctx", axis=0, tiled=True)

    up_part = lax.dynamic_index_in_dim(
        fc1_weight.reshape(rows, shards, ctx_count, units), ctx, 2, keepdims=False
    ).reshape(rows, shards * units)
    down_part = lax.dynamic_slice_in_dim(fc2_weight, ctx * units, units, 0)
    qkv_part = lax.dynamic_index_in_dim(
        qkv_weight.reshape(rows, 3, HEADS, head_dim), head, 2, keepdims=False
    ).reshape(rows, 3 * head_dim)
    dense_cols = lax.all_to_all(
        dense_weight, "fsdp", split_axis=1, concat_axis=0, tiled=True
    )
    dense_part = lax.dynamic_slice_in_dim(dense_cols, head * head_dim, head_dim, 0)
    up_w = gather_fsdp(up_part)
    down_w = gather_fsdp(down_part)
    qkv_w = gather_fsdp(qkv_part)
    dense_w = gather_fsdp(dense_part, axis=1)

    hidden_all = line_gather(hidden[0]).reshape(length, width)
    grad_all = line_gather(out_grad[0]).reshape(length, width)

    residual = hidden_all.astype(f32)
    center = residual - jnp.mean(residual, axis=-1, keepdims=True)
    spread = lax.rsqrt(jnp.mean(center * center, axis=-1, keepdims=True) + 1e-05)
    scaled = center * spread
    normed_one = (scaled * gain_one + shift_one).astype(bf16)
    normed_two = (scaled * gain_two + shift_two).astype(bf16)

    up_shift_part = lax.dynamic_index_in_dim(
        up_shift.reshape(shards, ctx_count, units), ctx, 1, keepdims=False
    ).reshape(-1)
    up_value = dot(normed_two, up_w) + up_shift_part
    act_f, slope = gelu_and_slope(up_value)
    act = act_f.astype(bf16)
    down_grad = scatter_fsdp(dot_rows(act, grad_all).astype(bf16))
    d_up_f = dot_cols(grad_all, down_w) * slope
    d_up = d_up_f.astype(bf16)
    up_grad = scatter_fsdp(dot_rows(normed_two, d_up).astype(bf16))

    qkv_shift_part = lax.dynamic_index_in_dim(
        qkv_shift.reshape(3, HEADS, head_dim), head, 1, keepdims=False
    ).reshape(-1)
    joined = dot(normed_one, qkv_w) + qkv_shift_part
    places = jnp.arange(length, dtype=jnp.int32)
    cosine, sine = rotary_tables(places, ROT)
    queries = rotate(joined[:, :head_dim], cosine, sine).astype(bf16)
    keys = rotate(joined[:, head_dim : 2 * head_dim], cosine, sine).astype(bf16)
    values = joined[:, 2 * head_dim :].astype(bf16)
    allowed = (places[None, :] <= places[:, None]) & (query_seg[None, :] == query_seg[:, None])
    if repeat > 1:
        allowed = allowed & (places // (length // repeat) == ctx % repeat)[:, None]
    scores = jnp.where(allowed, dot_cols(queries, keys) * factor, -1e30)
    top = jnp.max(scores, axis=-1, keepdims=True)
    terms = jnp.where(allowed, jnp.exp(scores - top), 0.0)
    total = jnp.sum(terms, axis=-1, keepdims=True)
    probs = terms * jnp.where(total > 0.0, 1.0 / total, 0.0)
    probs_low = probs.astype(bf16)
    att_f = dot(probs_low, values)
    att = att_f.astype(bf16)
    partial = dot(att, dense_w) + dot(act, down_w)
    branch = lax.psum_scatter(partial.astype(bf16), "ctx", scatter_dimension=0, tiled=True)
    own = hidden[0].astype(f32)
    layer_output = (own + branch.astype(f32) + dense_shift + down_shift).astype(bf16)

    d_att = dot_cols(grad_all, dense_w).astype(bf16)
    delta = jnp.sum(d_att.astype(f32) * att_f, axis=-1, keepdims=True)
    dense_grad = dot_rows(att, grad_all).astype(bf16)
    d_scores = (probs * (dot_cols(d_att, values) - delta)).astype(bf16)
    d_queries = rotate(dot(d_scores, keys) * factor, cosine, -sine)
    d_keys = rotate(dot_rows(d_scores, queries) * factor, cosine, -sine)
    d_values = dot_rows(probs_low, d_att)
    d_joined = jnp.concatenate([d_queries, d_keys, d_values], axis=1).astype(bf16)
    qkv_grad = dot_rows(normed_one, d_joined).astype(bf16)

    d_one = dot_cols(d_joined, qkv_w)
    d_two = dot_cols(d_up, up_w)
    both = (d_one * gain_one + d_two * gain_two).astype(bf16)
    back = lax.psum_scatter(both, "ctx", scatter_dimension=0, tiled=True).astype(f32)
    own_center = own - jnp.mean(own, axis=-1, keepdims=True)
    own_spread = lax.rsqrt(jnp.mean(own_center * own_center, axis=-1, keepdims=True) + 1e-05)
    own_scaled = own_center * own_spread
    input_part = own_spread * (
        back
        - jnp.mean(back, axis=-1, keepdims=True)
        - own_scaled * jnp.mean(back * own_scaled, axis=-1, keepdims=True)
    )
    input_grad = (out_grad[0].astype(f32) + input_part).astype(bf16)

    first = (ctx == 0).astype(f32)
    columns = jnp.sum(grad_all.astype(f32), axis=0) * first
    joined_sum = jnp.sum(d_joined.astype(f32), axis=0).reshape(3, 1, head_dim)
    joined_full = jnp.where((jnp.arange(HEADS) == head)[None, :, None], joined_sum, 0.0)
    up_sum = jnp.sum(d_up.astype(f32), axis=0).reshape(shards, 1, units)
    up_full = jnp.where((jnp.arange(ctx_count) == ctx)[None, :, None], up_sum, 0.0)
    small = [
        jnp.sum(d_one * scaled, axis=0),
        jnp.sum(d_one, axis=0),
        columns,
        jnp.sum(d_two * scaled, axis=0),
        jnp.sum(d_two, axis=0),
        joined_full,
        up_full,
    ]
    small = jnp.concatenate([piece.reshape(shards, -1) for piece in small], axis=1).astype(bf16)
    small_size = small.shape[1]
    small_rows = -(-small_size // (3 * head_dim * 16)) * 16
    small = jnp.pad(small, ((0, 0), (0, small_rows * 3 * head_dim - small_size)))
    last_grad = scatter_fsdp(
        jnp.concatenate(
            [
                qkv_grad.reshape(shards, rows, 3 * head_dim),
                small.reshape(shards, small_rows, 3 * head_dim),
            ],
            axis=1,
        ).reshape(-1, 3 * head_dim)
    )
    dense_share = scatter_fsdp(
        dense_grad.reshape(head_dim, shards, rows).transpose(1, 0, 2).reshape(-1, rows)
    )

    down_all = line_gather(down_grad).astype(f32).reshape(ctx_count * units, width)
    up_all = (
        line_gather(up_grad)
        .astype(f32)
        .reshape(ctx_count, rows, shards, units)
        .transpose(1, 2, 0, 3)
        .reshape(rows, ff)
    )
    dense_cols_all = line_gather(dense_share)
    if repeat > 1:
        dense_cols_all = jnp.sum(
            dense_cols_all.astype(f32).reshape(HEADS, repeat, head_dim, rows), axis=1
        ).astype(bf16)
    dense_all = lax.all_to_all(
        dense_cols_all.reshape(width, rows), "fsdp", split_axis=0, concat_axis=1, tiled=True
    ).astype(f32)
    last_all = line_gather(last_grad)
    qkv_all = last_all[:, :rows].astype(f32)
    if repeat > 1:
        qkv_all = jnp.sum(qkv_all.reshape(HEADS, repeat, rows, 3 * head_dim), axis=1)
    qkv_all = (
        qkv_all.reshape(HEADS, rows, 3, head_dim).transpose(1, 2, 0, 3).reshape(rows, 3 * width)
    )
    small_all = jnp.sum(last_all[:, rows:].astype(f32), axis=0).reshape(-1)
    sizes = [rows] * 5 + [3 * rows, ff // shards]
    parts, at = [], 0
    for size in sizes:
        parts.append(small_all[at : at + size])
        at += size
    gain_one_grad, shift_one_grad, columns_grad, gain_two_grad, shift_two_grad, joined_grad, up_b_grad = parts
    return (
        layer_output[None],
        input_grad[None],
        gain_one_grad,
        shift_one_grad,
        qkv_all,
        joined_grad,
        dense_all,
        columns_grad,
        gain_two_grad,
        shift_two_grad,
        up_all,
        up_b_grad,
        down_all,
        columns_grad,
    )


def solution(mesh):
    vec, mat, act = P("fsdp"), P("fsdp", None), P("fsdp", "ctx", None)
    return jax.shard_map(
        per_device,
        mesh=mesh,
        in_specs=(
            act, vec, vec, mat, vec, mat, vec, vec, vec, mat, vec, mat, vec, P("fsdp", "ctx"), act
        ),
        out_specs=(act, act, vec, vec, mat, vec, mat, vec, vec, vec, mat, vec, mat, vec),
        check_vma=False,
    )
```

```python
import functools
import math

import jax
import jax.numpy as jnp
from jax import lax
from jax.experimental import pallas as pl
from jax.experimental.pallas import tpu as pltpu
from jax.sharding import PartitionSpec as P

HEADS = 8
ROT = 64
CORES = 2


def dot(left, right):
    return jnp.dot(left, right, preferred_element_type=jnp.float32)


def dot_rows(left, right):
    return lax.dot_general(
        left, right, (((0,), (0,)), ((), ())), preferred_element_type=jnp.float32
    )


def dot_cols(left, right):
    return lax.dot_general(
        left, right, (((1,), (1,)), ((), ())), preferred_element_type=jnp.float32
    )


def gelu_and_slope(values):
    cdf = 0.5 * (1.0 + lax.erf(values * (0.5**0.5)))
    density = jnp.exp(-0.5 * values * values) * ((2.0 * jnp.pi) ** -0.5)
    return values * cdf, cdf + values * density


def centred(values):
    values = values.astype(jnp.float32)
    center = values - jnp.mean(values, axis=-1, keepdims=True)
    spread = lax.rsqrt(jnp.mean(center * center, axis=-1, keepdims=True) + 1e-05)
    return center * spread, spread


def rotary_tables(places, width):
    half_rot = width // 2
    freqs = 10000.0 ** (-2.0 * jnp.arange(half_rot, dtype=jnp.float32) / width)
    angles = places.astype(jnp.float32)[:, None] * freqs[None, :]
    return (jnp.cos(angles), jnp.sin(angles))


def rotate(values, cosine, sine):
    half = cosine.shape[-1]
    first, second, remain = values[:, :half], values[:, half : 2 * half], values[:, 2 * half :]
    return jnp.concatenate(
        [first * cosine - second * sine, second * cosine + first * sine, remain], axis=1
    )


def line_gather(block):
    count = lax.axis_size("ctx")
    chips = count // CORES
    ctx = lax.axis_index("ctx")
    place, core = ctx // CORES, ctx % CORES
    up = down = block
    ups, downs = [], []
    for hop in range(1, chips):
        up = lax.ppermute(
            up,
            "ctx",
            [
                (i * CORES + k, (i + 1) * CORES + k)
                for i in range(hop - 1, chips - 1)
                for k in range(CORES)
            ],
        )
        down = lax.ppermute(
            down,
            "ctx",
            [
                (i * CORES + k, (i - 1) * CORES + k)
                for i in range(1, chips - hop + 1)
                for k in range(CORES)
            ],
        )
        ups.append(up)
        downs.append(down)
    around = jnp.stack(ups[::-1] + [block] + downs)
    mine = lax.dynamic_slice_in_dim(around, chips - 1 - place, chips, 0)
    other = lax.ppermute(mine, "ctx", [(i, i ^ 1) for i in range(count)])
    is_mine = (jnp.arange(CORES) == core).reshape((1, CORES) + (1,) * block.ndim)
    return jnp.where(is_mine, mine[:, None], other[:, None]).reshape((count,) + block.shape)


def gather_fsdp(values, axis=0):
    return lax.all_gather(values, "fsdp", axis=axis, tiled=True)


def scatter_fsdp(values):
    return lax.psum_scatter(values, "fsdp", scatter_dimension=0, tiled=True)


def remote(src, dst, sems, slot, device):
    return pltpu.make_async_remote_copy(
        src_ref=src,
        dst_ref=dst,
        send_sem=sems[0].at[slot],
        recv_sem=sems[1].at[slot],
        device_id=device,
        device_id_type=pl.DeviceIdType.MESH,
    )


class Line:
    def __init__(self, source, blocks, sems, base, place, chips):
        self.source, self.sems, self.base, self.chips = source, sems, base, chips
        self.ctx, self.shard = place
        self.chip = self.ctx // CORES
        rows = source.shape[0]
        self.block = lambda index: blocks.at[pl.ds(pl.multiple_of(index * rows, rows), rows)]
        self.swap_base = base + 2 * (chips - 1)
        self.own_slot = base + 4 * (chips - 1)

    @staticmethod
    def slots(chips):
        return 4 * (chips - 1) + 2

    def hop(self, up, number):
        step = 1 if up else -1
        slot = (0 if up else self.chips - 1) + number - 1
        origin = self.ctx - step * (number - 1) * CORES
        if up:
            sends = (self.chip >= number - 1) & (self.chip < self.chips - 1)
            gets = self.chip >= number
        else:
            sends = (self.chip <= self.chips - number) & (self.chip > 0)
            gets = self.chip <= self.chips - 1 - number
        return slot, step, origin, sends, gets

    def send(self, up, number):
        slot, step, origin, sends, _ = self.hop(up, number)

        @pl.when(sends)
        def _():
            remote(
                self.source if number == 1 else self.block(origin),
                self.block(origin),
                self.sems,
                self.base + slot,
                (self.ctx + step * CORES, self.shard),
            ).start()

    def start(self):
        self.send(True, 1)
        self.send(False, 1)
        remote(
            self.source, self.block(self.ctx), self.sems, self.own_slot, (self.ctx ^ 1, self.shard)
        ).start()
        self.local = pltpu.make_async_copy(
            self.source, self.block(self.ctx), self.sems[0].at[self.own_slot + 1]
        )
        self.local.start()

    def land(self, number):
        for up in (True, False):
            slot, step, origin, _, gets = self.hop(up, number)
            block = self.block(origin - step * CORES)

            @pl.when(gets)
            def _(block=block, slot=slot):
                remote(
                    block, block, self.sems, self.base + slot, (self.ctx ^ 1, self.shard)
                ).wait_recv()

            if number < self.chips - 1:
                self.send(up, number + 1)

            @pl.when(gets)
            def _(block=block, slot=slot):
                remote(
                    block, block, self.sems, self.swap_base + slot, (self.ctx ^ 1, self.shard)
                ).start()

    def arrived(self):
        other = self.block(self.ctx ^ 1)
        remote(other, other, self.sems, self.own_slot, (self.ctx ^ 1, self.shard)).wait_recv()
        self.local.wait()
        for up in (True, False):
            for number in range(1, self.chips):
                slot, step, origin, _, gets = self.hop(up, number)
                block = self.block((origin - step * CORES) ^ 1)

                @pl.when(gets)
                def _(block=block, slot=slot):
                    remote(
                        block, block, self.sems, self.swap_base + slot, (self.ctx ^ 1, self.shard)
                    ).wait_recv()

    def sent(self):
        source = self.source
        peer = (self.ctx ^ 1, self.shard)
        remote(source, source, self.sems, self.own_slot, peer).wait_send()
        for up in (True, False):
            for number in range(1, self.chips):
                slot, _, _, sends, gets = self.hop(up, number)

                @pl.when(sends)
                def _(slot=slot):
                    remote(source, source, self.sems, self.base + slot, peer).wait_send()

                @pl.when(gets)
                def _(slot=slot):
                    remote(source, source, self.sems, self.swap_base + slot, peer).wait_send()


class Square:
    SLOTS = 8

    def __init__(self, pieces, blocks, sems, base, place):
        self.pieces, self.sems, self.base = pieces, sems, base
        self.ctx, self.shard = place
        half = blocks.shape[0] // 8

        def part(owner, which, columns=slice(None)):
            start = pl.multiple_of((2 * owner + which) * half, half)
            return blocks.at[pl.ds(start, half), columns]

        self.part = part

    def to(self, bit):
        return (self.ctx, self.shard ^ bit)

    def own(self, bit, which):
        for source, columns in self.pieces(which):
            remote(
                source,
                self.part(self.shard, which, columns),
                self.sems,
                self.base + 2 * (bit - 1) + which,
                self.to(bit),
            ).start()

    def start(self):
        self.own(1, 0)
        self.own(2, 1)
        self.own(1, 1)
        self.own(2, 0)
        for which in (0, 1):
            for source, columns in self.pieces(which):
                pltpu.make_async_copy(
                    source,
                    self.part(self.shard, which, columns),
                    self.sems[0].at[self.base + 6 + which],
                ).start()

    def wait(self, owner, which, slot, bit):
        part = self.part(owner, which)
        remote(part, part, self.sems, self.base + slot, self.to(bit)).wait_recv()

    def forward(self):
        for bit in (1, 2):
            which = bit - 1
            owner = self.shard ^ bit
            self.wait(owner, which, 2 * (bit - 1) + which, bit)
            part = self.part(owner, which)
            remote(part, part, self.sems, self.base + 4 + which, self.to(3 - bit)).start()

    def arrived(self):
        self.wait(self.shard ^ 1, 1, 1, 1)
        self.wait(self.shard ^ 2, 0, 2, 2)
        self.wait(self.shard ^ 3, 0, 4, 2)
        self.wait(self.shard ^ 3, 1, 5, 1)
        for which in (0, 1):
            part = self.part(self.shard, which)
            pltpu.make_async_copy(part, part, self.sems[0].at[self.base + 6 + which]).wait()

    def sent(self):
        for slot in range(6):
            part = self.part(self.shard, 0)
            remote(part, part, self.sems, self.base + slot, self.to(1)).wait_send()


class Tree:
    SLOTS = 8

    def __init__(self, source, block, sems, base, place, owner):
        self.source, self.block, self.sems, self.base = source, block, sems, base
        self.ctx, self.shard = place
        self.turn = self.shard ^ owner
        self.half = block.shape[0] // 2

    def rows(self, ref, which):
        return ref.at[pl.ds(which * self.half, self.half)]

    def copy(self, ref, which, slot, bit):
        return remote(
            self.rows(ref, which),
            self.rows(self.block, which),
            self.sems,
            self.base + slot,
            (self.ctx, self.shard ^ bit),
        )

    def start(self):
        @pl.when(self.turn == 0)
        def _():
            self.copy(self.source, 0, 0, 1).start()
            self.copy(self.source, 1, 3, 2).start()
            self.copy(self.source, 1, 1, 1).start()
            self.copy(self.source, 0, 2, 2).start()
            pltpu.make_async_copy(self.source, self.block, self.sems[0].at[self.base + 6]).start()

    def forward(self):
        for bit in (1, 2):
            which = bit - 1

            @pl.when(self.turn == bit)
            def _(bit=bit, which=which):
                self.copy(self.block, which, 2 * (bit - 1) + which, bit).wait_recv()
                self.copy(self.block, which, 4 + which, 3 - bit).start()

    def arrived(self):
        @pl.when(self.turn == 0)
        def _():
            pltpu.make_async_copy(self.source, self.block, self.sems[0].at[self.base + 6]).wait()

        for bit in (1, 2):

            @pl.when(self.turn == bit)
            def _(bit=bit):
                which = 2 - bit
                self.copy(self.block, which, 2 * (bit - 1) + which, bit).wait_recv()

        @pl.when(self.turn == 3)
        def _():
            self.copy(self.block, 0, 4, 2).wait_recv()
            self.copy(self.block, 1, 5, 1).wait_recv()

    def sent(self):
        @pl.when(self.turn == 0)
        def _():
            for slot in range(4):
                self.copy(self.block, 0, slot, 1).wait_send()

        for bit in (1, 2):

            @pl.when(self.turn == bit)
            def _(bit=bit):
                self.copy(self.block, bit - 1, 3 + bit, 3 - bit).wait_send()


TILE = 256


def gather_kernel(
    sizes,
    hidden, grad, fc1, fc2, qkv, dense, vectors, segs,
    hidden_out, n1_out, grad_out, qkv_out, dense_out, vec_out, seg_out,
    down_grad_out, up_grad_out, ff_out, e_out, sums_out,
    hid, gra, n1, n2, w_up, w_down, vec, act, slope, d_up, down_grad, up_grad, ff, e_two, sums,
    send_sems, recv_sems, out_sems,
):
    chips, shards, units = sizes
    place = ctx, shard = lax.axis_index("ctx"), lax.axis_index("fsdp")
    chip, core = ctx // CORES, ctx % CORES
    sems = (send_sems, recv_sems)
    width = hidden.shape[1]
    length = hid.shape[0]
    ff_units = w_down.shape[0]
    tiles = length // TILE
    f32, bf16 = jnp.float32, jnp.bfloat16

    barrier = pltpu.get_barrier_semaphore()
    peers = [(ctx, shard ^ bit) for bit in (1, 2, 3)]
    peers += [(lax.rem(ctx + step, CORES * chips), shard) for step in range(1, CORES * chips)]
    for peer in peers:
        pl.semaphore_signal(barrier, inc=1, device_id=peer, device_id_type=pl.DeviceIdType.MESH)
    pl.semaphore_wait(barrier, len(peers))

    base = 0
    lines = []
    for source, blocks in ((hidden, hid), (grad, gra)):
        lines.append(Line(source, blocks, sems, base, place, chips))
        base += Line.slots(chips)
    hid_line, gra_line = lines
    columns = units // shards

    def halves(ref, which, start, size):
        half = ref.shape[0] // 2
        return ref.at[pl.ds(which * half, half), pl.ds(pl.multiple_of(start, size), size)]

    def up_pieces(which):
        stride = fc1.shape[1] // shards
        return [
            (
                halves(fc1, which, index * stride + ctx * columns, columns),
                pl.ds(index * columns, columns),
            )
            for index in range(shards)
        ]

    def down_pieces(which):
        half = columns // 2
        start = pl.multiple_of(ctx * columns + which * half, half)
        return [(fc2.at[pl.ds(start, half)], slice(None))]

    head_dim = qkv_out.shape[1] // 3

    def qkv_pieces(which):
        return [
            (
                halves(qkv, which, index * width + ctx * head_dim, head_dim),
                pl.ds(index * head_dim, head_dim),
            )
            for index in range(3)
        ]

    squares = []
    for pieces, blocks in ((up_pieces, w_up), (down_pieces, w_down), (qkv_pieces, qkv_out)):
        squares.append(Square(pieces, blocks, sems, base, place))
        base += Square.SLOTS
    up_square, down_square, qkv_square = squares
    heads_here = dense.shape[0] // head_dim
    dense_rows = dense.at[
        pl.ds(pl.multiple_of(lax.rem(ctx, heads_here) * head_dim, head_dim), head_dim)
    ]
    tree = Tree(dense_rows, dense_out, sems, base, place, ctx // heads_here)
    base += Tree.SLOTS

    small = []
    for bit in (1, 2, 3):
        small.append((remote(vectors, vec.at[shard], sems, base, (ctx, shard ^ bit)), vec.at[shard ^ bit]))
        base += 1
    seg_rows = segs.shape[0]

    def seg_block(index):
        return seg_out.at[pl.ds(pl.multiple_of(index * seg_rows, seg_rows), seg_rows)]

    for step in range(1, CORES * chips):
        peer = lax.rem(ctx + step, CORES * chips)
        origin = lax.rem(ctx + CORES * chips - step, CORES * chips)
        small.append((remote(segs, seg_block(ctx), sems, base, (peer, shard)), seg_block(origin)))
        base += 1
    for copy, _ in small:
        copy.start()
    own_vec = pltpu.make_async_copy(vectors, vec.at[shard], out_sems.at[0])
    own_seg = pltpu.make_async_copy(segs, seg_block(ctx), out_sems.at[1])
    own_vec.start()
    own_seg.start()

    hid_line.start()
    up_square.start()
    hid_line.land(1)
    up_square.forward()
    down_square.start()
    hid_line.land(2)
    gra_line.start()
    hid_line.land(3)
    for slot, (copy, landing) in enumerate(small):
        remote(landing, landing, sems, base - len(small) + slot, (ctx ^ 1, shard)).wait_recv()
    own_vec.wait()
    own_seg.wait()
    hid_line.arrived()

    def vector(row):
        return jnp.concatenate([vec[index, row : row + 1] for index in range(shards)], axis=1)

    def rows_of(index):
        return pl.ds(pl.multiple_of(index * TILE, TILE), TILE)

    def centred(rows):
        values = hid[rows].astype(f32)
        center = values - jnp.mean(values, axis=-1, keepdims=True)
        return center * lax.rsqrt(jnp.mean(center * center, axis=-1, keepdims=True) + 1e-05)

    def loop(body):
        lax.fori_loop(0, tiles, lambda index, carry: (body(rows_of(index)), carry)[1], 0)

    def norms(rows):
        scaled = centred(rows)
        n1[rows] = (scaled * vector(0) + vector(1)).astype(bf16)
        n2[rows] = (scaled * vector(2) + vector(3)).astype(bf16)

    loop(norms)
    up_square.arrived()
    down_square.forward()
    qkv_square.start()
    gra_line.land(1)

    row_size = vec.shape[2]
    bias_start = ctx * columns
    bias_row = 9 + bias_start // row_size
    bias_column = pl.multiple_of(lax.rem(bias_start, row_size), columns)
    bias = jnp.concatenate(
        [vec[index, pl.ds(bias_row, 1), pl.ds(bias_column, columns)] for index in range(shards)],
        axis=1,
    )

    def forward(rows):
        value = dot(n2[rows], w_up[...]) + bias
        cdf = 0.5 * (1.0 + lax.erf(value * (0.5**0.5)))
        density = jnp.exp(-0.5 * value * value) * ((2.0 * math.pi) ** -0.5)
        act[rows] = (value * cdf).astype(bf16)
        slope[rows] = cdf + value * density

    loop(forward)
    gra_line.land(2)
    down_square.arrived()
    qkv_square.forward()
    tree.start()

    def output(rows):
        ff[rows] = dot(act[rows], w_down[...]).astype(bf16)

    loop(output)
    gra_line.land(3)
    gra_line.arrived()

    def backward(rows):
        d_up[rows] = (dot_cols(gra[rows], w_down[...]) * slope[rows]).astype(bf16)

    loop(backward)
    tree.forward()

    def fc2_grad(rows):
        down_grad[rows] = dot_rows(act[:, rows], gra[...]).astype(bf16)

    lax.fori_loop(
        0, ff_units // TILE, lambda index, carry: (fc2_grad(rows_of(index)), carry)[1], 0
    )

    def fc1_grad(rows):
        up_grad[rows] = dot_rows(n2[:, rows], d_up[...]).astype(bf16)

    lax.fori_loop(0, width // TILE, lambda index, carry: (fc1_grad(rows_of(index)), carry)[1], 0)
    sums[...] = jnp.zeros_like(sums)

    def inputs(rows):
        d_two = dot_cols(d_up[rows], w_up[...])
        sums[0:1] += jnp.sum(d_two * centred(rows), axis=0, keepdims=True)
        sums[1:2] += jnp.sum(d_two, axis=0, keepdims=True)
        sums[2:3] += jnp.sum(gra[rows].astype(f32), axis=0, keepdims=True)
        sums[3:4, :ff_units] += jnp.sum(d_up[rows].astype(f32), axis=0, keepdims=True)
        e_two[rows] = (d_two * vector(2)).astype(bf16)

    loop(inputs)

    pairs = (
        (hid, hidden_out), (n1, n1_out), (gra, grad_out), (vec, vec_out), (down_grad, down_grad_out),
        (up_grad, up_grad_out), (ff, ff_out), (e_two, e_out), (sums, sums_out),
    )
    writes = [
        pltpu.make_async_copy(src, dst, out_sems.at[index]) for index, (src, dst) in enumerate(pairs)
    ]
    for write in writes:
        write.start()
    qkv_square.arrived()
    tree.arrived()
    for item in lines + squares + [tree]:
        item.sent()
    for copy, _ in small:
        copy.wait_send()
    for write in writes:
        write.wait()


def gather_and_feed_forward(hidden, grad, fc1, fc2, qkv, dense, vectors, segs):
    chips, shards = lax.axis_size("ctx") // CORES, lax.axis_size("fsdp")
    tokens, width = hidden.shape
    length = tokens * chips * CORES
    units = fc1.shape[1] // (chips * CORES)
    head_dim = width // HEADS
    bf16, f32 = jnp.bfloat16, jnp.float32
    wide = (length, width)
    shapes = [
        (wide, bf16), (wide, bf16), (wide, bf16), ((width, 3 * head_dim), bf16), ((head_dim, width), bf16),
        ((shards,) + vectors.shape, f32), ((segs.shape[0] * chips * CORES, segs.shape[1]), segs.dtype),
        ((units, width), bf16), ((width, units), bf16), (wide, bf16), (wide, bf16), ((8, width), f32),
    ]
    scratch = [
        (wide, bf16), (wide, bf16), (wide, bf16), (wide, bf16), ((width, units), bf16), ((units, width), bf16),
        ((shards,) + vectors.shape, f32), ((length, units), bf16), ((length, units), f32), ((length, units), bf16),
        ((units, width), bf16), ((width, units), bf16), (wide, bf16), (wide, bf16), ((8, width), f32),
    ]
    count = 2 * Line.slots(chips) + 3 * Square.SLOTS + Tree.SLOTS + 3 + CORES * chips - 1
    return pl.pallas_call(
        functools.partial(gather_kernel, (chips, shards, units)),
        out_shape=[jax.ShapeDtypeStruct(shape, kind) for shape, kind in shapes],
        in_specs=[pl.BlockSpec(memory_space=pl.ANY)] * 8,
        out_specs=[pl.BlockSpec(memory_space=pl.ANY)] * len(shapes),
        scratch_shapes=[pltpu.VMEM(shape, kind) for shape, kind in scratch]
        + [
            pltpu.SemaphoreType.DMA((count,)),
            pltpu.SemaphoreType.DMA((count,)),
            pltpu.SemaphoreType.DMA((9,)),
        ],
        compiler_params=pltpu.CompilerParams(
            collective_id=0, has_side_effects=True, vmem_limit_bytes=60 * 2**20
        ),
        name="gather_and_feed_forward",
    )(hidden, grad, fc1, fc2, qkv, dense, vectors, segs)


def per_device(
    hidden,
    ln1_gain,
    ln1_bias,
    qkv_weight,
    qkv_bias,
    dense_weight,
    dense_bias,
    ln2_gain,
    ln2_bias,
    fc1_weight,
    fc1_bias,
    fc2_weight,
    fc2_bias,
    segments,
    out_grad,
):
    ctx_count = lax.axis_size("ctx")
    shards = lax.axis_size("fsdp")
    ctx = lax.axis_index("ctx")
    tokens, width = hidden.shape[1], hidden.shape[2]
    length = tokens * ctx_count
    head_dim = width // HEADS
    repeat = ctx_count // HEADS
    head = ctx // repeat
    factor = head_dim ** (-0.5)
    rows = width // shards
    ff = fc1_weight.shape[1]
    units = ff // shards // ctx_count
    bf16, f32 = jnp.bfloat16, jnp.float32

    vectors = jnp.concatenate(
        [ln1_gain, ln1_bias, ln2_gain, ln2_bias, dense_bias, fc2_bias, qkv_bias, fc1_bias]
    ).reshape(-1, rows)
    vectors = jnp.pad(vectors, ((0, -vectors.shape[0] % 8), (0, 0)))
    if ctx_count == HEADS and shards == 4:
        (
            hidden_all, normed_one, grad_all, qkv_w, dense_w, vec, seg_all,
            down_part_grad, up_part_grad, ff_part, e_two, sums,
        ) = gather_and_feed_forward(
            hidden[0], out_grad[0], fc1_weight, fc2_weight, qkv_weight, dense_weight, vectors,
            jnp.broadcast_to(segments, (8, tokens)),
        )
        query_seg = seg_all.reshape(ctx_count, 8, tokens)[:, 0].reshape(-1)
        gain_two_sum, shift_two_sum, columns = sums[0], sums[1], sums[2]
        up_sum = sums[3, : shards * units]
    else:
        vec = lax.all_gather(vectors, "fsdp", axis=0)
        query_seg = lax.all_gather(segments[0], "ctx", axis=0, tiled=True)
        up_part = lax.dynamic_index_in_dim(
            fc1_weight.reshape(rows, shards, ctx_count, units), ctx, 2, keepdims=False
        ).reshape(rows, shards * units)
        down_part = lax.dynamic_slice_in_dim(fc2_weight, ctx * units, units, 0)
        qkv_part = lax.dynamic_index_in_dim(
            qkv_weight.reshape(rows, 3, HEADS, head_dim), head, 2, keepdims=False
        ).reshape(rows, 3 * head_dim)
        dense_cols = lax.all_to_all(
            dense_weight, "fsdp", split_axis=1, concat_axis=0, tiled=True
        )
        dense_part = lax.dynamic_slice_in_dim(dense_cols, head * head_dim, head_dim, 0)
        up_w = gather_fsdp(up_part)
        down_w = gather_fsdp(down_part)
        qkv_w = gather_fsdp(qkv_part)
        dense_w = gather_fsdp(dense_part, axis=1)
        hidden_all = line_gather(hidden[0]).reshape(length, width)
        grad_all = line_gather(out_grad[0]).reshape(length, width)
        normed_one = (centred(hidden_all)[0] * vec[:, 0].reshape(-1) + vec[:, 1].reshape(-1)).astype(bf16)
        scaled = centred(hidden_all)[0]
        gain_two = vec[:, 2].reshape(-1)
        normed_two = (scaled * gain_two + vec[:, 3].reshape(-1)).astype(bf16)
        up_shift = lax.dynamic_index_in_dim(
            vec[:, 9 : 9 + ff // width].reshape(shards, ctx_count, units), ctx, 1, keepdims=False
        ).reshape(-1)
        act_f, slope = gelu_and_slope(dot(normed_two, up_w) + up_shift)
        act = act_f.astype(bf16)
        d_up = (dot_cols(grad_all, down_w) * slope).astype(bf16)
        down_part_grad = dot_rows(act, grad_all).astype(bf16)
        up_part_grad = dot_rows(normed_two, d_up).astype(bf16)
        ff_part = dot(act, down_w).astype(bf16)
        d_two = dot_cols(d_up, up_w)
        e_two = (d_two * gain_two).astype(bf16)
        gain_two_sum, shift_two_sum = jnp.sum(d_two * scaled, axis=0), jnp.sum(d_two, axis=0)
        columns = jnp.sum(grad_all.astype(f32), axis=0)
        up_sum = jnp.sum(d_up.astype(f32), axis=0)
    gain_one = vec[:, 0].reshape(-1)
    dense_shift, down_shift = vec[:, 4].reshape(-1), vec[:, 5].reshape(-1)
    qkv_shift = vec[:, 6:9].reshape(-1)
    down_grad = scatter_fsdp(down_part_grad)
    up_grad = scatter_fsdp(up_part_grad)

    qkv_shift_part = lax.dynamic_index_in_dim(
        qkv_shift.reshape(3, HEADS, head_dim), head, 1, keepdims=False
    ).reshape(-1)
    joined = dot(normed_one, qkv_w) + qkv_shift_part
    places = jnp.arange(length, dtype=jnp.int32)
    cosine, sine = rotary_tables(places, ROT)
    queries = rotate(joined[:, :head_dim], cosine, sine).astype(bf16)
    keys = rotate(joined[:, head_dim : 2 * head_dim], cosine, sine).astype(bf16)
    values = joined[:, 2 * head_dim :].astype(bf16)
    allowed = (places[None, :] <= places[:, None]) & (query_seg[None, :] == query_seg[:, None])
    if repeat > 1:
        allowed = allowed & (places // (length // repeat) == ctx % repeat)[:, None]
    scores = jnp.where(allowed, dot_cols(queries, keys) * factor, -1e30)
    top = jnp.max(scores, axis=-1, keepdims=True)
    terms = jnp.where(allowed, jnp.exp(scores - top), 0.0)
    total = jnp.sum(terms, axis=-1, keepdims=True)
    probs = terms * jnp.where(total > 0.0, 1.0 / total, 0.0)
    probs_low = probs.astype(bf16)
    att_f = dot(probs_low, values)
    att = att_f.astype(bf16)
    partial = dot(att, dense_w) + ff_part.astype(f32)
    branch = lax.psum_scatter(partial.astype(bf16), "ctx", scatter_dimension=0, tiled=True)
    own = hidden[0].astype(f32)
    layer_output = (own + branch.astype(f32) + dense_shift + down_shift).astype(bf16)

    d_att = dot_cols(grad_all, dense_w).astype(bf16)
    delta = jnp.sum(d_att.astype(f32) * att_f, axis=-1, keepdims=True)
    dense_grad = dot_rows(att, grad_all).astype(bf16)
    d_scores = (probs * (dot_cols(d_att, values) - delta)).astype(bf16)
    d_queries = rotate(dot(d_scores, keys) * factor, cosine, -sine)
    d_keys = rotate(dot_rows(d_scores, queries) * factor, cosine, -sine)
    d_values = dot_rows(probs_low, d_att)
    d_joined = jnp.concatenate([d_queries, d_keys, d_values], axis=1).astype(bf16)
    qkv_grad = dot_rows(normed_one, d_joined).astype(bf16)

    d_one = dot_cols(d_joined, qkv_w)
    both = (d_one * gain_one + e_two.astype(f32)).astype(bf16)
    back = lax.psum_scatter(both, "ctx", scatter_dimension=0, tiled=True).astype(f32)
    own_scaled, own_spread = centred(own)
    input_part = own_spread * (
        back
        - jnp.mean(back, axis=-1, keepdims=True)
        - own_scaled * jnp.mean(back * own_scaled, axis=-1, keepdims=True)
    )
    input_grad = (out_grad[0].astype(f32) + input_part).astype(bf16)

    first = (ctx == 0).astype(f32)
    joined_sum = jnp.sum(d_joined.astype(f32), axis=0).reshape(3, 1, head_dim)
    joined_full = jnp.where((jnp.arange(HEADS) == head)[None, :, None], joined_sum, 0.0)
    up_sum = up_sum.reshape(shards, 1, units)
    up_full = jnp.where((jnp.arange(ctx_count) == ctx)[None, :, None], up_sum, 0.0)
    small = [
        jnp.sum(d_one * centred(hidden_all)[0], axis=0),
        jnp.sum(d_one, axis=0),
        columns * first,
        gain_two_sum,
        shift_two_sum,
        joined_full,
        up_full,
    ]
    small = jnp.concatenate([piece.reshape(shards, -1) for piece in small], axis=1).astype(bf16)
    small_size = small.shape[1]
    small_rows = -(-small_size // (3 * head_dim * 16)) * 16
    small = jnp.pad(small, ((0, 0), (0, small_rows * 3 * head_dim - small_size)))
    last_grad = scatter_fsdp(
        jnp.concatenate(
            [
                qkv_grad.reshape(shards, rows, 3 * head_dim),
                small.reshape(shards, small_rows, 3 * head_dim),
            ],
            axis=1,
        ).reshape(-1, 3 * head_dim)
    )
    dense_share = scatter_fsdp(
        dense_grad.reshape(head_dim, shards, rows).transpose(1, 0, 2).reshape(-1, rows)
    )

    down_all = line_gather(down_grad).astype(f32).reshape(ctx_count * units, width)
    up_all = (
        line_gather(up_grad)
        .astype(f32)
        .reshape(ctx_count, rows, shards, units)
        .transpose(1, 2, 0, 3)
        .reshape(rows, ff)
    )
    dense_cols_all = line_gather(dense_share)
    if repeat > 1:
        dense_cols_all = jnp.sum(
            dense_cols_all.astype(f32).reshape(HEADS, repeat, head_dim, rows), axis=1
        ).astype(bf16)
    dense_all = lax.all_to_all(
        dense_cols_all.reshape(width, rows), "fsdp", split_axis=0, concat_axis=1, tiled=True
    ).astype(f32)
    last_all = line_gather(last_grad)
    qkv_all = last_all[:, :rows].astype(f32)
    if repeat > 1:
        qkv_all = jnp.sum(qkv_all.reshape(HEADS, repeat, rows, 3 * head_dim), axis=1)
    qkv_all = (
        qkv_all.reshape(HEADS, rows, 3, head_dim).transpose(1, 2, 0, 3).reshape(rows, 3 * width)
    )
    small_all = jnp.sum(last_all[:, rows:].astype(f32), axis=0).reshape(-1)
    sizes = [rows] * 5 + [3 * rows, ff // shards]
    parts, at = [], 0
    for size in sizes:
        parts.append(small_all[at : at + size])
        at += size
    gain_one_grad, shift_one_grad, columns_grad, gain_two_grad, shift_two_grad, joined_grad, up_b_grad = parts
    return (
        layer_output[None],
        input_grad[None],
        gain_one_grad,
        shift_one_grad,
        qkv_all,
        joined_grad,
        dense_all,
        columns_grad,
        gain_two_grad,
        shift_two_grad,
        up_all,
        up_b_grad,
        down_all,
        columns_grad,
    )


def solution(mesh):
    vec, mat, act = P("fsdp"), P("fsdp", None), P("fsdp", "ctx", None)
    return jax.shard_map(
        per_device,
        mesh=mesh,
        in_specs=(
            act, vec, vec, mat, vec, mat, vec, vec, vec, mat, vec, mat, vec, P("fsdp", "ctx"), act
        ),
        out_specs=(act, act, vec, vec, mat, vec, mat, vec, vec, vec, mat, vec, mat, vec),
        check_vma=False,
    )
```

```python
import functools
import math

import jax
import jax.numpy as jnp
import numpy as np
from jax import lax
from jax.experimental import pallas as pl
from jax.experimental.pallas import tpu as pltpu
from jax.sharding import PartitionSpec as P

HEADS = 8
ROT = 64
CORES = 2


def dot(left, right):
    return jnp.dot(left, right, preferred_element_type=jnp.float32)


def dot_rows(left, right):
    return lax.dot_general(
        left, right, (((0,), (0,)), ((), ())), preferred_element_type=jnp.float32
    )


def dot_cols(left, right):
    return lax.dot_general(
        left, right, (((1,), (1,)), ((), ())), preferred_element_type=jnp.float32
    )


def gelu_and_slope(values):
    cdf = 0.5 * (1.0 + lax.erf(values * (0.5**0.5)))
    density = jnp.exp(-0.5 * values * values) * ((2.0 * jnp.pi) ** -0.5)
    return values * cdf, cdf + values * density


def centred(values):
    values = values.astype(jnp.float32)
    center = values - jnp.mean(values, axis=-1, keepdims=True)
    spread = lax.rsqrt(jnp.mean(center * center, axis=-1, keepdims=True) + 1e-05)
    return center * spread, spread


def rotary_tables(places, width):
    half_rot = width // 2
    freqs = 10000.0 ** (-2.0 * jnp.arange(half_rot, dtype=jnp.float32) / width)
    angles = places.astype(jnp.float32)[:, None] * freqs[None, :]
    return (jnp.cos(angles), jnp.sin(angles))


def rotate(values, cosine, sine):
    half = cosine.shape[-1]
    first, second, remain = values[:, :half], values[:, half : 2 * half], values[:, 2 * half :]
    return jnp.concatenate(
        [first * cosine - second * sine, second * cosine + first * sine, remain], axis=1
    )


def line_gather(block):
    count = lax.axis_size("ctx")
    chips = count // CORES
    ctx = lax.axis_index("ctx")
    place, core = ctx // CORES, ctx % CORES
    up = down = block
    ups, downs = [], []
    for hop in range(1, chips):
        up = lax.ppermute(
            up,
            "ctx",
            [
                (i * CORES + k, (i + 1) * CORES + k)
                for i in range(hop - 1, chips - 1)
                for k in range(CORES)
            ],
        )
        down = lax.ppermute(
            down,
            "ctx",
            [
                (i * CORES + k, (i - 1) * CORES + k)
                for i in range(1, chips - hop + 1)
                for k in range(CORES)
            ],
        )
        ups.append(up)
        downs.append(down)
    around = jnp.stack(ups[::-1] + [block] + downs)
    mine = lax.dynamic_slice_in_dim(around, chips - 1 - place, chips, 0)
    other = lax.ppermute(mine, "ctx", [(i, i ^ 1) for i in range(count)])
    is_mine = (jnp.arange(CORES) == core).reshape((1, CORES) + (1,) * block.ndim)
    return jnp.where(is_mine, mine[:, None], other[:, None]).reshape((count,) + block.shape)


def gather_fsdp(values, axis=0):
    return lax.all_gather(values, "fsdp", axis=axis, tiled=True)


def scatter_fsdp(values):
    return lax.psum_scatter(values, "fsdp", scatter_dimension=0, tiled=True)


def remote(src, dst, sems, slot, device):
    return pltpu.make_async_remote_copy(
        src_ref=src,
        dst_ref=dst,
        send_sem=sems[0].at[slot],
        recv_sem=sems[1].at[slot],
        device_id=device,
        device_id_type=pl.DeviceIdType.MESH,
    )


class Line:
    def __init__(self, source, blocks, sems, base, place, chips, stride=None, offset=0):
        self.source, self.sems, self.base, self.chips = source, sems, base, chips
        self.ctx, self.shard = place
        self.chip = self.ctx // CORES
        rows = source.shape[0]
        stride = stride or rows
        self.block = lambda index: blocks.at[pl.ds(pl.multiple_of(index * stride + offset, rows), rows)]
        self.swap_base = base + 2 * (chips - 1)
        self.own_slot = base + 4 * (chips - 1)

    @staticmethod
    def slots(chips):
        return 4 * (chips - 1) + 2

    def hop(self, up, number):
        step = 1 if up else -1
        slot = (0 if up else self.chips - 1) + number - 1
        origin = self.ctx - step * (number - 1) * CORES
        if up:
            sends = (self.chip >= number - 1) & (self.chip < self.chips - 1)
            gets = self.chip >= number
        else:
            sends = (self.chip <= self.chips - number) & (self.chip > 0)
            gets = self.chip <= self.chips - 1 - number
        return slot, step, origin, sends, gets

    def send(self, up, number):
        slot, step, origin, sends, _ = self.hop(up, number)

        @pl.when(sends)
        def _():
            remote(
                self.source if number == 1 else self.block(origin),
                self.block(origin),
                self.sems,
                self.base + slot,
                (self.ctx + step * CORES, self.shard),
            ).start()

    def start(self):
        self.send(True, 1)
        self.send(False, 1)
        remote(
            self.source, self.block(self.ctx), self.sems, self.own_slot, (self.ctx ^ 1, self.shard)
        ).start()
        self.local = pltpu.make_async_copy(
            self.source, self.block(self.ctx), self.sems[0].at[self.own_slot + 1]
        )
        self.local.start()

    def land(self, number):
        for up in (True, False):
            slot, step, origin, _, gets = self.hop(up, number)
            block = self.block(origin - step * CORES)

            @pl.when(gets)
            def _(block=block, slot=slot):
                remote(
                    block, block, self.sems, self.base + slot, (self.ctx ^ 1, self.shard)
                ).wait_recv()

            if number < self.chips - 1:
                self.send(up, number + 1)

            @pl.when(gets)
            def _(block=block, slot=slot):
                remote(
                    block, block, self.sems, self.swap_base + slot, (self.ctx ^ 1, self.shard)
                ).start()

    def arrived(self):
        other = self.block(self.ctx ^ 1)
        remote(other, other, self.sems, self.own_slot, (self.ctx ^ 1, self.shard)).wait_recv()
        self.local.wait()
        for up in (True, False):
            for number in range(1, self.chips):
                slot, step, origin, _, gets = self.hop(up, number)
                block = self.block((origin - step * CORES) ^ 1)

                @pl.when(gets)
                def _(block=block, slot=slot):
                    remote(
                        block, block, self.sems, self.swap_base + slot, (self.ctx ^ 1, self.shard)
                    ).wait_recv()

    def sent(self):
        source = self.source
        peer = (self.ctx ^ 1, self.shard)
        remote(source, source, self.sems, self.own_slot, peer).wait_send()
        for up in (True, False):
            for number in range(1, self.chips):
                slot, _, _, sends, gets = self.hop(up, number)

                @pl.when(sends)
                def _(slot=slot):
                    remote(source, source, self.sems, self.base + slot, peer).wait_send()

                @pl.when(gets)
                def _(slot=slot):
                    remote(source, source, self.sems, self.swap_base + slot, peer).wait_send()


class Square:
    SLOTS = 8

    def __init__(self, pieces, blocks, sems, base, place):
        self.pieces, self.sems, self.base = pieces, sems, base
        self.ctx, self.shard = place
        half = blocks.shape[0] // 8

        def part(owner, which, columns=slice(None)):
            start = pl.multiple_of((2 * owner + which) * half, half)
            return blocks.at[pl.ds(start, half), columns]

        self.part = part

    def to(self, bit):
        return (self.ctx, self.shard ^ bit)

    def own(self, bit, which):
        for source, columns in self.pieces(which):
            remote(
                source,
                self.part(self.shard, which, columns),
                self.sems,
                self.base + 2 * (bit - 1) + which,
                self.to(bit),
            ).start()

    def start(self):
        self.own(1, 0)
        self.own(2, 1)
        self.own(1, 1)
        self.own(2, 0)
        for which in (0, 1):
            for source, columns in self.pieces(which):
                pltpu.make_async_copy(
                    source,
                    self.part(self.shard, which, columns),
                    self.sems[0].at[self.base + 6 + which],
                ).start()

    def wait(self, owner, which, slot, bit):
        part = self.part(owner, which)
        remote(part, part, self.sems, self.base + slot, self.to(bit)).wait_recv()

    def forward(self):
        for bit in (1, 2):
            which = bit - 1
            owner = self.shard ^ bit
            self.wait(owner, which, 2 * (bit - 1) + which, bit)
            part = self.part(owner, which)
            remote(part, part, self.sems, self.base + 4 + which, self.to(3 - bit)).start()

    def arrived(self):
        self.wait(self.shard ^ 1, 1, 1, 1)
        self.wait(self.shard ^ 2, 0, 2, 2)
        self.wait(self.shard ^ 3, 0, 4, 2)
        self.wait(self.shard ^ 3, 1, 5, 1)
        for which in (0, 1):
            part = self.part(self.shard, which)
            pltpu.make_async_copy(part, part, self.sems[0].at[self.base + 6 + which]).wait()

    def sent(self):
        for slot in range(6):
            part = self.part(self.shard, 0)
            remote(part, part, self.sems, self.base + slot, self.to(1)).wait_send()


class Tree:
    SLOTS = 8

    def __init__(self, source, block, sems, base, place, owner):
        self.source, self.block, self.sems, self.base = source, block, sems, base
        self.ctx, self.shard = place
        self.turn = self.shard ^ owner
        self.half = block.shape[0] // 2

    def rows(self, ref, which):
        return ref.at[pl.ds(which * self.half, self.half)]

    def copy(self, ref, which, slot, bit):
        return remote(
            self.rows(ref, which),
            self.rows(self.block, which),
            self.sems,
            self.base + slot,
            (self.ctx, self.shard ^ bit),
        )

    def start(self):
        @pl.when(self.turn == 0)
        def _():
            self.copy(self.source, 0, 0, 1).start()
            self.copy(self.source, 1, 3, 2).start()
            self.copy(self.source, 1, 1, 1).start()
            self.copy(self.source, 0, 2, 2).start()
            pltpu.make_async_copy(self.source, self.block, self.sems[0].at[self.base + 6]).start()

    def forward(self):
        for bit in (1, 2):
            which = bit - 1

            @pl.when(self.turn == bit)
            def _(bit=bit, which=which):
                self.copy(self.block, which, 2 * (bit - 1) + which, bit).wait_recv()
                self.copy(self.block, which, 4 + which, 3 - bit).start()

    def arrived(self):
        @pl.when(self.turn == 0)
        def _():
            pltpu.make_async_copy(self.source, self.block, self.sems[0].at[self.base + 6]).wait()

        for bit in (1, 2):

            @pl.when(self.turn == bit)
            def _(bit=bit):
                which = 2 - bit
                self.copy(self.block, which, 2 * (bit - 1) + which, bit).wait_recv()

        @pl.when(self.turn == 3)
        def _():
            self.copy(self.block, 0, 4, 2).wait_recv()
            self.copy(self.block, 1, 5, 1).wait_recv()

    def sent(self):
        @pl.when(self.turn == 0)
        def _():
            for slot in range(4):
                self.copy(self.block, 0, slot, 1).wait_send()

        for bit in (1, 2):

            @pl.when(self.turn == bit)
            def _(bit=bit):
                self.copy(self.block, bit - 1, 3 + bit, 3 - bit).wait_send()


def add_rows(dst, sources):
    step = 32

    def body(index, carry):
        rows = pl.ds(pl.multiple_of(index * step, step), step)
        total = sources[0][rows].astype(jnp.float32)
        for source in sources[1:]:
            total += source[rows].astype(jnp.float32)
        dst[rows] = total.astype(dst.dtype)
        return carry

    lax.fori_loop(0, dst.shape[0] // step, body, 0)


class Fold:
    SLOTS = 6

    def __init__(self, parts, landing, stage, carry, final, sems, local, base, place):
        self.parts, self.landing, self.stage, self.carry, self.final = parts, landing, stage, carry, final
        self.sems, self.local, self.base = sems, local, base
        self.ctx, self.shard = place
        self.half = final.shape[0] // 2

    def part(self, owner, which):
        start = pl.multiple_of((2 * owner + which) * self.half, self.half)
        return self.parts.at[pl.ds(start, self.half)]

    def landed(self, slot):
        return self.landing.at[pl.ds(slot * self.half, self.half)]

    def copy(self, src, slot, bit):
        return remote(
            src, self.landed(slot), self.sems, self.base + slot, (self.ctx, self.shard ^ bit)
        )

    def send(self, slot):
        bit, which = (1, 0) if slot < 2 else (2, 1)
        owner = self.shard ^ (3 if slot % 2 else bit)
        self.copy(self.part(owner, which), slot, bit).start()

    def add(self, dst, sources):
        copies = []
        for index, source in enumerate(sources):
            copies.append(
                pltpu.make_async_copy(source, self.stage.at[index], self.local.at[index])
            )
            copies[-1].start()
        for copy in copies:
            copy.wait()
        add_rows(dst, [self.stage.at[index] for index in range(len(sources))])

    def wait(self, slot, bit):
        self.copy(self.landed(slot), slot, bit).wait_recv()

    def middle(self, which):
        first, second = (1, 2) if which == 0 else (2, 1)
        slot = 1 + 2 * which
        self.wait(slot, first)
        carry = self.carry.at[which]
        self.add(carry, [self.part(self.shard ^ second, which), self.landed(slot)])
        self.copy(carry, 4 + which, second).start()

    def finish(self, which):
        first, second = (1, 2) if which == 0 else (2, 1)
        self.wait(2 * which, first)
        self.wait(4 + which, second)
        self.add(
            self.final.at[pl.ds(which * self.half, self.half)],
            [self.part(self.shard, which), self.landed(2 * which), self.landed(4 + which)],
        )

    def sent(self):
        for slot in range(6):
            self.copy(self.part(self.shard, 0), slot, 1).wait_send()


class Sink:
    def __init__(self, parts, swapped, landing, stage, carry, final, sems, local, base, place, chips):
        self.parts, self.swapped, self.landing, self.stage = parts, swapped, landing, stage
        self.carry, self.final, self.sems, self.local, self.base = carry, final, sems, local, base
        self.ctx, self.shard = place
        self.chip, self.core, self.chips = self.ctx // CORES, self.ctx % CORES, chips
        self.rows = final.shape[0]

    @staticmethod
    def slots(chips):
        return 2 * (chips - 1) + 1

    def block(self, ref, index):
        return ref.at[pl.ds(pl.multiple_of(index * self.rows, self.rows), self.rows)]

    def start(self):
        for chip in range(self.chips):
            remote(
                self.block(self.parts, CORES * chip + (self.core ^ 1)),
                self.block(self.swapped, chip),
                self.sems,
                self.base,
                (self.ctx ^ 1, self.shard),
            ).start()

    def swap(self):
        swapped = self.swapped
        remote(swapped, swapped, self.sems, self.base, (self.ctx ^ 1, self.shard)).wait_recv()

    def hop(self, up, step):
        place = self.chip if up else self.chips - 1 - self.chip
        target = place + self.chips - step
        target = target if up else self.chips - 1 - target
        slot = (0 if up else self.chips - 1) + step - 1
        sends = (place + 1 <= step) & (place < self.chips - 1)
        gets = (place <= step) & (place > 0)
        return slot, target, sends, gets, place > 0

    def landed(self, slot):
        return self.landing.at[pl.ds(slot * self.rows, self.rows)]

    def copy(self, up, slot):
        way = CORES if up else -CORES
        return remote(
            self.carry.at[0 if up else 1],
            self.landed(slot),
            self.sems,
            self.base + 1 + slot,
            (self.ctx + way, self.shard),
        )

    def load(self, index, source):
        return pltpu.make_async_copy(source, self.stage.at[index], self.local.at[index])

    def own(self, target):
        return [
            self.load(0, self.block(self.parts, CORES * target + self.core)),
            self.load(1, self.block(self.swapped, target)),
        ]

    def step(self, number):
        for up in (True, False):
            slot, target, sends, _, passes = self.hop(up, number)
            if number > 1:
                before, _, sent, gets, _ = self.hop(up, number - 1)

                @pl.when(gets)
                def _(before=before, up=up):
                    remote(
                        self.landed(before), self.landed(before), self.sems, self.base + 1 + before,
                        (self.ctx ^ 1, self.shard),
                    ).wait_recv()

                @pl.when(sent)
                def _(before=before, up=up):
                    self.copy(up, before).wait_send()

            @pl.when(sends)
            def _(up=up, slot=slot, target=target, passes=passes):
                loads = self.own(target)
                for load in loads:
                    load.start()
                carry = self.carry.at[0 if up else 1]
                stage = self.stage
                if number > 1:

                    @pl.when(passes)
                    def _():
                        more = self.load(2, self.landed(slot - 1))
                        more.start()
                        for load in loads + [more]:
                            load.wait()
                        add_rows(carry, [stage.at[0], stage.at[1], stage.at[2]])

                    @pl.when(jnp.logical_not(passes))
                    def _():
                        for load in loads:
                            load.wait()
                        add_rows(carry, [stage.at[0], stage.at[1]])
                else:
                    for load in loads:
                        load.wait()
                    add_rows(carry, [stage.at[0], stage.at[1]])
                self.copy(up, slot).start()

    def finish(self, dst, sem):
        loads = self.own(self.chip)
        for load in loads:
            load.start()
        for load in loads:
            load.wait()
        add_rows(self.final, [self.stage.at[0], self.stage.at[1]])
        for up in (True, False):
            slot, _, sends, gets, _ = self.hop(up, self.chips - 1)

            @pl.when(gets)
            def _(slot=slot):
                landed = self.landed(slot)
                remote(
                    landed, landed, self.sems, self.base + 1 + slot, (self.ctx ^ 1, self.shard)
                ).wait_recv()
                load = self.load(2, landed)
                load.start()
                load.wait()
                add_rows(self.final, [self.final, self.stage.at[2]])

            @pl.when(sends)
            def _(up=up, slot=slot):
                self.copy(up, slot).wait_send()

        swapped = self.swapped
        remote(swapped, swapped, self.sems, self.base, (self.ctx ^ 1, self.shard)).wait_send()
        copy = pltpu.make_async_copy(self.final, dst, sem)
        copy.start()
        copy.wait()


TILE = 256


def block_kernel(
    sizes,
    hidden, grad, fc1, fc2, qkv, dense, vectors, segs, tables,
    vec_out, output_out, input_out, down_all, up_all, qkv_all, dense_all, sums_all,
    down_parts, up_parts, qkv_parts, dense_parts, down_land, up_land, qkv_land, dense_land,
    out_parts, out_swap, out_land, in_parts, in_swap, in_land, dense_lines,
    hid, gra, norm, w_up, w_down, w_qkv, w_dense, vec, seg, seg_col, table,
    act, wide_f, d_up, queries, keys, values, att_f, att, d_keys, d_values, d_joined, sums, sums_got, sums_tot,
    stage, down_stage, up_stage,
    down_carry, up_carry, qkv_carry, dense_carry, down_final, up_final, qkv_final, dense_final,
    out_carry, in_carry, sink_final,
    send_sems, recv_sems, local_sems,
):
    chips, shards, columns = sizes
    place = ctx, shard = lax.axis_index("ctx"), lax.axis_index("fsdp")
    chip, core = ctx // CORES, ctx % CORES
    count = CORES * chips
    sems = (send_sems, recv_sems)
    width, length = hidden.shape[1], hid.shape[0]
    ff_units = w_down.shape[0]
    head_dim = w_dense.shape[0]
    row_size = vec.shape[2]
    tiles = length // TILE
    f32, bf16 = jnp.float32, jnp.bfloat16
    factor = head_dim ** (-0.5)

    barrier = pltpu.get_barrier_semaphore()
    peers = [(ctx, shard ^ bit) for bit in (1, 2, 3)]
    peers += [(lax.rem(ctx + step, count), shard) for step in range(1, count)]
    for peer in peers:
        pl.semaphore_signal(barrier, inc=1, device_id=peer, device_id_type=pl.DeviceIdType.MESH)
    pl.semaphore_wait(barrier, len(peers))

    base = 0

    def take(slots):
        nonlocal base
        base += slots
        return base - slots

    def line(source, blocks, stride=None, offset=0):
        return Line(source, blocks, sems, take(Line.slots(chips)), place, chips, stride, offset)

    def line_pair(final, blocks):
        half = final.shape[0] // 2
        return [
            line(final.at[pl.ds(which * half, half)], blocks, final.shape[0], which * half)
            for which in (0, 1)
        ]

    def fold(parts, landing, stage, carry, final):
        return Fold(
            parts, landing, stage, carry, final, sems, local_sems.at[pl.ds(4, 4)], take(Fold.SLOTS), place
        )

    def sink(parts, swapped, landing, carry):
        return Sink(
            parts, swapped, landing, down_stage, carry, sink_final, sems, local_sems.at[pl.ds(4, 4)],
            take(Sink.slots(chips)), place, chips,
        )

    def halves(ref, which, start, size):
        half = ref.shape[0] // 2
        return ref.at[pl.ds(which * half, half), pl.ds(pl.multiple_of(start, size), size)]

    def up_pieces(which):
        stride = fc1.shape[1] // shards
        return [
            (
                halves(fc1, which, index * stride + ctx * columns, columns),
                pl.ds(index * columns, columns),
            )
            for index in range(shards)
        ]

    def down_pieces(which):
        half = columns // 2
        start = pl.multiple_of(ctx * columns + which * half, half)
        return [(fc2.at[pl.ds(start, half)], slice(None))]

    def qkv_pieces(which):
        return [
            (
                halves(qkv, which, index * width + ctx * head_dim, head_dim),
                pl.ds(index * head_dim, head_dim),
            )
            for index in range(3)
        ]

    hid_line, gra_line = line(hidden, hid), line(grad, gra)
    squares = [
        Square(pieces, blocks, sems, take(Square.SLOTS), place)
        for pieces, blocks in ((up_pieces, w_up), (down_pieces, w_down), (qkv_pieces, w_qkv))
    ]
    up_square, down_square, qkv_square = squares
    heads_here = dense.shape[0] // head_dim
    dense_rows = dense.at[
        pl.ds(pl.multiple_of(lax.rem(ctx, heads_here) * head_dim, head_dim), head_dim)
    ]
    tree = Tree(dense_rows, w_dense, sems, take(Tree.SLOTS), place, ctx // heads_here)
    down_fold = fold(down_parts, down_land, down_stage, down_carry, down_final)
    up_fold = fold(up_parts, up_land, up_stage, up_carry, up_final)
    qkv_fold = fold(
        qkv_parts, qkv_land, up_stage.at[:, :, : 3 * head_dim], qkv_carry, qkv_final
    )
    dense_fold = fold(
        dense_parts, dense_land, down_stage.at[:, :, : width // shards], dense_carry, dense_final
    )
    down_lines = line_pair(down_final, down_all)
    up_lines = line_pair(up_final, up_all)
    qkv_lines = line_pair(qkv_final, qkv_all)
    dense_line = line(dense_final, dense_lines)
    sums_line = line(sums_tot, sums_all)
    out_sink = sink(out_parts, out_swap, out_land, out_carry)
    in_sink = sink(in_parts, in_swap, in_land, in_carry)

    small = []

    def send_small(src, dst, landing, device):
        slot = take(1)
        small.append((remote(src, dst, sems, slot, device), landing, slot))

    seg_rows = segs.shape[0]

    def seg_block(index):
        return seg.at[pl.ds(pl.multiple_of(index * seg_rows, seg_rows), seg_rows)]

    for bit in (1, 2, 3):
        send_small(vectors, vec.at[shard], vec.at[shard ^ bit], (ctx, shard ^ bit))
    for step in range(1, count):
        send_small(
            segs, seg_block(ctx), seg_block(lax.rem(ctx + count - step, count)),
            (lax.rem(ctx + step, count), shard),
        )
    for copy, _, _ in small:
        copy.start()
    locals_in = [
        pltpu.make_async_copy(src, dst, local_sems.at[8 + index])
        for index, (src, dst) in enumerate(
            ((vectors, vec.at[shard]), (segs, seg_block(ctx)), (tables, table))
        )
    ]
    for copy in locals_in:
        copy.start()

    hid_line.start()
    up_square.start()
    hid_line.land(1)
    up_square.forward()
    down_square.start()
    hid_line.land(2)
    gra_line.start()
    hid_line.land(3)
    for _, landing, slot in small:
        remote(landing, landing, sems, slot, (ctx ^ 1, shard)).wait_recv()
    for copy in locals_in:
        copy.wait()
    hid_line.arrived()

    def vector(row):
        return jnp.concatenate([vec[index, row : row + 1] for index in range(shards)], axis=1)

    def rows_of(index):
        return pl.ds(pl.multiple_of(index * TILE, TILE), TILE)

    def loop(body, steps=tiles):
        lax.fori_loop(0, steps, lambda index, carry: (body(rows_of(index)), carry)[1], 0)

    def scaled_rows(rows):
        return centred(hid[rows])[0]

    def norm_two(rows):
        norm[rows] = (scaled_rows(rows) * vector(2) + vector(3)).astype(bf16)

    def norm_one(rows):
        norm[rows] = (scaled_rows(rows) * vector(0) + vector(1)).astype(bf16)

    def emit(steps, compute, dst, size):
        def write(index):
            slot = lax.rem(index, 2)
            return pltpu.make_async_copy(
                stage.at[slot, :, :size], dst.at[rows_of(index)], local_sems.at[slot]
            )

        def body(index, carry):
            @pl.when(index >= 2)
            def _():
                write(index - 2).wait()

            stage[lax.rem(index, 2), :, :size] = compute(index).astype(bf16)
            write(index).start()
            return carry

        lax.fori_loop(0, steps, body, 0)
        write(steps - 2).wait()
        write(steps - 1).wait()

    loop(norm_two)
    up_square.arrived()
    down_square.forward()
    gra_line.land(1)

    bias_start = ctx * columns
    bias_row = 9 + bias_start // row_size
    bias_column = pl.multiple_of(lax.rem(bias_start, row_size), columns)
    up_bias = jnp.concatenate(
        [vec[index, pl.ds(bias_row, 1), pl.ds(bias_column, columns)] for index in range(shards)],
        axis=1,
    )

    def feed_forward(rows):
        value = dot(norm[rows], w_up[...]) + up_bias
        cdf = 0.5 * (1.0 + lax.erf(value * (0.5**0.5)))
        density = jnp.exp(-0.5 * value * value) * ((2.0 * math.pi) ** -0.5)
        act[rows] = (value * cdf).astype(bf16)
        wide_f[rows] = cdf + value * density

    loop(feed_forward)
    gra_line.land(2)
    down_square.arrived()
    gra_line.land(3)
    gra_line.arrived()

    def fc2_grad(index, carry):
        owner = shard ^ (3 - index)
        rows = rows_of(owner)
        stage[0] = dot_rows(act[:, rows], gra[...]).astype(bf16)
        write = pltpu.make_async_copy(stage.at[0], down_parts.at[rows], local_sems.at[0])
        write.start()
        write.wait()
        for step, slot in ((0, 1), (1, 2), (2, 0)):

            @pl.when(index == step)
            def _(slot=slot):
                down_fold.send(slot)

        return carry

    lax.fori_loop(0, shards, fc2_grad, 0)

    def feed_back(rows):
        d_up[rows] = (dot_cols(gra[rows], w_down[...]) * wide_f[rows]).astype(bf16)

    loop(feed_back)
    down_fold.middle(0)
    down_fold.send(3)
    emit(
        width // TILE,
        lambda index: dot_rows(norm[:, rows_of(index)], d_up[...]),
        up_parts,
        ff_units,
    )
    down_fold.finish(0)
    down_lines[0].start()
    qkv_square.start()
    loop(norm_one)
    down_fold.middle(1)
    down_lines[0].land(1)
    qkv_square.forward()
    for slot in (1, 2, 0):
        up_fold.send(slot)
    tree.start()
    down_lines[0].land(2)
    down_fold.finish(1)
    down_lines[1].start()

    per = 3 * HEADS // shards
    bias_parts = []
    for index in range(3):
        at = index * HEADS + ctx
        rest = lax.rem(at, per) * head_dim
        bias_parts.append(
            vec[
                at // per,
                pl.ds(6 + rest // row_size, 1),
                pl.ds(pl.multiple_of(lax.rem(rest, row_size), head_dim), head_dim),
            ]
        )
    rotary = table.shape[2]

    def turn(entries, rows, way):
        first = entries[:, :rotary]
        first = (
            first * table[0, rows]
            + way * (pltpu.roll(first, ROT // 2, 1) * table[1, rows])
            + way * (pltpu.roll(first, rotary - ROT // 2, 1) * table[2, rows])
        )
        return jnp.concatenate([first, entries[:, rotary:]], axis=1)

    def project(rows):
        joined = dot(norm[rows], w_qkv[...])
        parts = [
            joined[:, index * head_dim : (index + 1) * head_dim] + bias_parts[index]
            for index in range(3)
        ]
        queries[rows] = turn(parts[0], rows, 1.0).astype(bf16)
        keys[rows] = turn(parts[1], rows, 1.0).astype(bf16)
        values[rows] = parts[2].astype(bf16)

    seg_row = jnp.concatenate(
        [seg[index * seg_rows : index * seg_rows + 1] for index in range(count)], axis=1
    )
    side = segs.shape[1]
    for index in range(count):
        block = seg[index * seg_rows : index * seg_rows + 1].astype(f32)
        seg_col[index * side : (index + 1) * side] = jnp.broadcast_to(block, (side, side)).T

    qkv_square.arrived()
    loop(project)
    down_lines[0].land(3)
    down_lines[1].land(1)
    up_fold.middle(0)
    up_fold.send(3)
    tree.forward()

    def attend(index):
        rows = pl.ds(index * TILE, TILE)
        size = (index + 1) * TILE
        scores = dot_cols(queries[rows], keys[:size]) * factor
        query_place = index * TILE + lax.broadcasted_iota(jnp.int32, (TILE, size), 0)
        key_place = lax.broadcasted_iota(jnp.int32, (TILE, size), 1)
        same = seg_col[rows][:, :1] == seg_row[:, :size].astype(f32)
        allowed = (key_place <= query_place) & same
        scores = jnp.where(allowed, scores, -1e30)
        terms = jnp.where(
            allowed, jnp.exp(scores - jnp.max(scores, axis=-1, keepdims=True)), 0.0
        )
        probs = terms / jnp.sum(terms, axis=-1, keepdims=True)
        wide_f[rows, :size] = probs
        result = dot(probs.astype(bf16), values[:size])
        att_f[rows] = result
        att[rows] = result.astype(bf16)

    attend(0)
    attend(1)
    down_lines[1].land(2)
    up_fold.finish(0)
    up_lines[0].start()
    attend(2)
    attend(3)
    up_fold.middle(1)
    tree.arrived()

    def output(index):
        rows = rows_of(index)
        return dot(att[rows], w_dense[...]) + dot(act[rows], w_down[...])

    emit(tiles, output, out_parts, width)
    out_sink.start()
    down_lines[1].land(3)
    up_lines[0].land(1)
    up_fold.finish(1)
    up_lines[1].start()

    dense_size = width // shards

    def dense_grad(index):
        start = pl.multiple_of(index * dense_size, dense_size)
        return dot_rows(att[...], gra[:, pl.ds(start, dense_size)])

    emit(shards, dense_grad, dense_parts, dense_size)
    for slot in (1, 2, 0, 3):
        dense_fold.send(slot)
    out_sink.swap()
    out_sink.step(1)

    d_keys[...] = jnp.zeros_like(d_keys)
    d_values[...] = jnp.zeros_like(d_values)

    def attend_back(index):
        rows = pl.ds(index * TILE, TILE)
        size = (index + 1) * TILE
        d_att = dot_cols(gra[rows], w_dense[...]).astype(bf16)
        delta = jnp.sum(d_att.astype(f32) * att_f[rows], axis=-1, keepdims=True)
        probs = wide_f[rows, :size]
        d_scores = (probs * (dot_cols(d_att, values[:size]) - delta)).astype(bf16)
        d_queries = dot(d_scores, keys[:size]) * factor
        d_joined[rows, :head_dim] = turn(d_queries, rows, -1.0).astype(bf16)
        d_keys[:size] += dot_rows(d_scores, queries[rows])
        d_values[:size] += dot_rows(probs.astype(bf16), d_att)

    attend_back(0)
    attend_back(1)
    up_lines[0].land(2)
    dense_fold.middle(0)
    dense_fold.middle(1)
    attend_back(2)
    attend_back(3)
    up_lines[1].land(1)

    def join(rows):
        d_joined[rows, head_dim : 2 * head_dim] = turn(d_keys[rows] * factor, rows, -1.0).astype(bf16)
        d_joined[rows, 2 * head_dim :] = d_values[rows].astype(bf16)

    loop(join)
    emit(
        width // TILE,
        lambda index: dot_rows(norm[:, rows_of(index)], d_joined[...]),
        qkv_parts,
        3 * head_dim,
    )
    for slot in (1, 2, 0, 3):
        qkv_fold.send(slot)
    out_sink.step(2)
    dense_fold.finish(0)
    dense_fold.finish(1)
    dense_line.start()
    up_lines[0].land(3)
    up_lines[1].land(2)
    qkv_fold.middle(0)
    qkv_fold.middle(1)

    sums[...] = jnp.zeros_like(sums)

    def inputs(index):
        rows = rows_of(index)
        d_one = dot_cols(d_joined[rows], w_qkv[...])
        d_two = dot_cols(d_up[rows], w_up[...])
        scaled = scaled_rows(rows)

        def gather(row, entries):
            sums[row : row + 1, : entries.shape[1]] += jnp.sum(
                entries.astype(f32), axis=0, keepdims=True
            )

        gather(0, d_two * scaled)
        gather(1, d_two)
        gather(2, gra[rows])
        gather(3, d_up[rows])
        gather(4, d_one * scaled)
        gather(5, d_one)
        gather(6, d_joined[rows])
        return d_one * vector(0) + d_two * vector(2)

    emit(tiles, inputs, in_parts, width)
    in_sink.start()
    sums_sent = []
    for bit in (1, 2, 3):
        slot = take(1)
        copy = remote(sums, sums_got.at[shard], sems, slot, (ctx, shard ^ bit))
        copy.start()
        sums_sent.append((copy, sums_got.at[shard ^ bit], slot))
    sums_got[shard] = sums[...]
    dense_line.land(1)
    out_sink.step(3)
    up_lines[1].land(3)
    qkv_fold.finish(0)
    qkv_lines[0].start()
    qkv_fold.finish(1)
    qkv_lines[1].start()
    in_sink.swap()
    in_sink.step(1)
    dense_line.land(2)
    for copy, landing, slot in sums_sent:
        remote(landing, landing, sems, slot, (ctx ^ 1, shard)).wait_recv()
    total = sums_got[0]
    for index in range(1, shards):
        total = total + sums_got[index]
    sums_tot[...] = total
    sums_line.start()
    dense_line.land(3)
    qkv_lines[0].land(1)
    in_sink.step(2)
    sums_line.land(1)
    qkv_lines[1].land(1)
    dense_line.arrived()
    dense_block = dense_size
    exchanged = []
    for bit in (1, 2, 3):
        slot = take(1)
        peer = shard ^ bit
        rows = pl.ds(pl.multiple_of(peer * dense_block, dense_block), dense_block)
        own_rows = pl.ds(pl.multiple_of(shard * dense_block, dense_block), dense_block)
        copy = remote(dense_lines.at[rows], dense_all.at[own_rows], sems, slot, (ctx, peer))
        copy.start()
        exchanged.append((copy, dense_all.at[rows], slot))
    own_dense = pltpu.make_async_copy(
        dense_lines.at[own_rows], dense_all.at[own_rows], local_sems.at[2]
    )
    own_dense.start()
    out_sink.finish(output_out, local_sems.at[3])
    qkv_lines[0].land(2)
    in_sink.step(3)
    sums_line.land(2)
    qkv_lines[1].land(2)
    qkv_lines[0].land(3)
    sums_line.land(3)
    qkv_lines[1].land(3)
    in_sink.finish(input_out, local_sems.at[3])

    write_vec = pltpu.make_async_copy(vec, vec_out, local_sems.at[8])
    write_vec.start()
    lines = down_lines + up_lines + qkv_lines + [sums_line]
    for item in lines:
        item.arrived()
    for copy, landing, slot in exchanged:
        remote(landing, landing, sems, slot, (ctx ^ 1, shard)).wait_recv()
    own_dense.wait()
    for item in [hid_line, gra_line, dense_line] + lines + squares + [tree]:
        item.sent()
    for item in (down_fold, up_fold, qkv_fold, dense_fold):
        item.sent()
    for copy, _, _ in small + sums_sent + exchanged:
        copy.wait_send()
    write_vec.wait()


def rotary_table(length, lanes):
    half = ROT // 2
    freqs = (10000.0 ** (-2.0 * np.arange(half, dtype=np.float32) / ROT)).astype(np.float32)
    angles = np.arange(length, dtype=np.float32)[:, None] * freqs[None]
    cosine, sine = np.cos(angles), np.sin(angles)
    table = np.zeros((3, length, lanes), np.float32)
    table[0] = 1.0
    table[0, :, :half], table[0, :, half:ROT] = cosine, cosine
    table[1, :, half:ROT] = sine
    table[2, :, :half] = -sine
    return table


def whole_block(hidden, grad, fc1, fc2, qkv, dense, vectors, segs):
    chips, shards = lax.axis_size("ctx") // CORES, lax.axis_size("fsdp")
    count = chips * CORES
    tokens, width = hidden.shape
    length = tokens * count
    units = fc1.shape[1] // count
    head_dim = width // HEADS
    part = units // shards
    rows = width // shards
    bf16, f32 = jnp.bfloat16, jnp.float32
    wide, joint = (length, width), 3 * head_dim
    vec_shape = (shards,) + vectors.shape
    seg_shape = (segs.shape[0] * count, segs.shape[1])
    line = (tokens, width)
    hops = (2 * (chips - 1) * tokens, width)
    outs = [
        (vec_shape, f32), (line, f32), (line, f32), ((count * part, width), bf16), ((count * rows, units), bf16),
        ((count * rows, joint), bf16), ((width, rows), bf16), ((count * 8, width), f32),
        ((units, width), bf16), ((width, units), bf16), ((width, joint), bf16), ((shards * head_dim, rows), bf16),
        ((3 * part, width), bf16), ((3 * rows, units), bf16), ((3 * rows, joint), bf16), ((3 * head_dim, rows), bf16),
        (wide, bf16), ((chips * tokens, width), bf16), (hops, bf16),
        (wide, bf16), ((chips * tokens, width), bf16), (hops, bf16), ((count * head_dim, rows), bf16),
    ]
    table = rotary_table(length, 128)
    halves = [(part // 2, width), (rows // 2, units), (rows // 2, joint), (head_dim // 2, rows)]
    scratch = [
        (wide, bf16), (wide, bf16), (wide, bf16), ((width, units), bf16), ((units, width), bf16),
        ((width, joint), bf16), ((head_dim, width), bf16), (vec_shape, f32), (seg_shape, segs.dtype),
        ((length, segs.shape[1]), f32), (table.shape, f32),
        ((length, units), bf16), ((length, max(units, length)), f32), ((length, units), bf16),
        ((length, head_dim), bf16), ((length, head_dim), bf16), ((length, head_dim), bf16),
        ((length, head_dim), f32), ((length, head_dim), bf16), ((length, head_dim), f32), ((length, head_dim), f32),
        ((length, joint), bf16), ((8, width), f32), ((shards, 8, width), f32), ((8, width), f32),
        ((2, TILE, width), bf16),
    ]
    scratch += [((3,) + half, bf16) for half in halves[:2]]
    scratch += [((2,) + half, bf16) for half in halves]
    scratch += [((2 * half[0], half[1]), bf16) for half in halves]
    scratch += [((2, tokens, width), bf16), ((2, tokens, width), bf16), (line, f32)]
    slots = (
        10 * Line.slots(chips) + 3 * Square.SLOTS + Tree.SLOTS + 4 * Fold.SLOTS + 2 * Sink.slots(chips)
        + 9 + count - 1
    )
    outputs = pl.pallas_call(
        functools.partial(block_kernel, (chips, shards, part)),
        out_shape=[jax.ShapeDtypeStruct(shape, kind) for shape, kind in outs],
        in_specs=[pl.BlockSpec(memory_space=pl.ANY)] * 9,
        out_specs=[pl.BlockSpec(memory_space=pl.ANY)] * len(outs),
        scratch_shapes=[pltpu.VMEM(shape, kind) for shape, kind in scratch]
        + [
            pltpu.SemaphoreType.DMA((slots,)),
            pltpu.SemaphoreType.DMA((slots,)),
            pltpu.SemaphoreType.DMA((11,)),
        ],
        compiler_params=pltpu.CompilerParams(
            collective_id=0, has_side_effects=True, vmem_limit_bytes=62 * 2**20
        ),
        name="whole_block",
    )(hidden, grad, fc1, fc2, qkv, dense, vectors, segs, jnp.asarray(table))
    return outputs[:8]


def widen(blocks, groups, pieces):
    rows, size = blocks.shape[0] // groups, blocks.shape[1] // pieces

    def body(src, dst):
        dst[...] = src[...].astype(jnp.float32)

    return pl.pallas_call(
        body,
        grid=(groups, pieces),
        in_specs=[pl.BlockSpec((rows, size), lambda group, piece: (group, piece))],
        out_specs=pl.BlockSpec((rows, size), lambda group, piece: (0, piece * groups + group)),
        out_shape=jax.ShapeDtypeStruct((rows, pieces * groups * size), jnp.float32),
        name="widen",
    )(blocks)


def one_kernel(
    hidden, qkv_weight, dense_weight, fc1_weight, fc2_weight, segments, out_grad, vectors
):
    shards, count = lax.axis_size("fsdp"), lax.axis_size("ctx")
    shard = lax.axis_index("fsdp")
    tokens, width = hidden.shape[1], hidden.shape[2]
    rows = width // shards
    head_dim = width // HEADS
    f32, bf16 = jnp.float32, jnp.bfloat16
    vec, branch, back, down_all, up_all, qkv_all, dense_all, sums_all = whole_block(
        hidden[0], out_grad[0], fc1_weight, fc2_weight, qkv_weight, dense_weight, vectors,
        jnp.broadcast_to(segments, (8, tokens)),
    )
    own = hidden[0].astype(f32)
    shift = vec[:, 4].reshape(-1) + vec[:, 5].reshape(-1)
    layer_output = (own + branch + shift).astype(bf16)
    scaled, spread = centred(own)
    input_part = spread * (
        back
        - jnp.mean(back, axis=-1, keepdims=True)
        - scaled * jnp.mean(back * scaled, axis=-1, keepdims=True)
    )
    input_grad = (out_grad[0].astype(f32) + input_part).astype(bf16)
    sums = sums_all.reshape(count, 8, width)
    mine = lax.dynamic_slice_in_dim(sums, shard * rows, rows, 2)
    totals = jnp.sum(mine, axis=0)
    part = fc1_weight.shape[1] // count // shards
    up_sum = lax.dynamic_slice_in_dim(sums[:, 3], shard * part, part, 1).reshape(-1)
    joined = sums[:, 6, : 3 * head_dim].reshape(count, 3, head_dim).transpose(1, 0, 2).reshape(-1)
    joined = lax.dynamic_slice_in_dim(joined, shard * 3 * rows, 3 * rows, 0)
    columns = mine[0, 2]
    return (
        layer_output[None],
        input_grad[None],
        totals[4],
        totals[5],
        widen(qkv_all, count, 3),
        joined,
        widen(dense_all, shards, 1),
        columns,
        totals[0],
        totals[1],
        widen(up_all, count, shards),
        up_sum,
        widen(down_all, 1, 8),
        columns,
    )


def per_device(
    hidden,
    ln1_gain,
    ln1_bias,
    qkv_weight,
    qkv_bias,
    dense_weight,
    dense_bias,
    ln2_gain,
    ln2_bias,
    fc1_weight,
    fc1_bias,
    fc2_weight,
    fc2_bias,
    segments,
    out_grad,
):
    ctx_count = lax.axis_size("ctx")
    shards = lax.axis_size("fsdp")
    ctx = lax.axis_index("ctx")
    tokens, width = hidden.shape[1], hidden.shape[2]
    length = tokens * ctx_count
    head_dim = width // HEADS
    repeat = ctx_count // HEADS
    head = ctx // repeat
    factor = head_dim ** (-0.5)
    rows = width // shards
    ff = fc1_weight.shape[1]
    units = ff // shards // ctx_count
    bf16, f32 = jnp.bfloat16, jnp.float32

    vectors = jnp.concatenate(
        [ln1_gain, ln1_bias, ln2_gain, ln2_bias, dense_bias, fc2_bias, qkv_bias, fc1_bias]
    ).reshape(-1, rows)
    vectors = jnp.pad(vectors, ((0, -vectors.shape[0] % 8), (0, 0)))
    if ctx_count == HEADS and shards == 4:
        return one_kernel(
            hidden, qkv_weight, dense_weight, fc1_weight, fc2_weight, segments, out_grad, vectors
        )
    vec = lax.all_gather(vectors, "fsdp", axis=0)
    query_seg = lax.all_gather(segments[0], "ctx", axis=0, tiled=True)
    up_part = lax.dynamic_index_in_dim(
        fc1_weight.reshape(rows, shards, ctx_count, units), ctx, 2, keepdims=False
    ).reshape(rows, shards * units)
    down_part = lax.dynamic_slice_in_dim(fc2_weight, ctx * units, units, 0)
    qkv_part = lax.dynamic_index_in_dim(
        qkv_weight.reshape(rows, 3, HEADS, head_dim), head, 2, keepdims=False
    ).reshape(rows, 3 * head_dim)
    dense_cols = lax.all_to_all(
        dense_weight, "fsdp", split_axis=1, concat_axis=0, tiled=True
    )
    dense_part = lax.dynamic_slice_in_dim(dense_cols, head * head_dim, head_dim, 0)
    up_w = gather_fsdp(up_part)
    down_w = gather_fsdp(down_part)
    qkv_w = gather_fsdp(qkv_part)
    dense_w = gather_fsdp(dense_part, axis=1)
    hidden_all = line_gather(hidden[0]).reshape(length, width)
    grad_all = line_gather(out_grad[0]).reshape(length, width)
    normed_one = (centred(hidden_all)[0] * vec[:, 0].reshape(-1) + vec[:, 1].reshape(-1)).astype(bf16)
    scaled = centred(hidden_all)[0]
    gain_two = vec[:, 2].reshape(-1)
    normed_two = (scaled * gain_two + vec[:, 3].reshape(-1)).astype(bf16)
    up_shift = lax.dynamic_index_in_dim(
        vec[:, 9 : 9 + ff // width].reshape(shards, ctx_count, units), ctx, 1, keepdims=False
    ).reshape(-1)
    act_f, slope = gelu_and_slope(dot(normed_two, up_w) + up_shift)
    act = act_f.astype(bf16)
    d_up = (dot_cols(grad_all, down_w) * slope).astype(bf16)
    down_part_grad = dot_rows(act, grad_all).astype(bf16)
    up_part_grad = dot_rows(normed_two, d_up).astype(bf16)
    ff_part = dot(act, down_w).astype(bf16)
    d_two = dot_cols(d_up, up_w)
    e_two = (d_two * gain_two).astype(bf16)
    gain_two_sum, shift_two_sum = jnp.sum(d_two * scaled, axis=0), jnp.sum(d_two, axis=0)
    columns = jnp.sum(grad_all.astype(f32), axis=0)
    up_sum = jnp.sum(d_up.astype(f32), axis=0)
    gain_one = vec[:, 0].reshape(-1)
    dense_shift, down_shift = vec[:, 4].reshape(-1), vec[:, 5].reshape(-1)
    qkv_shift = vec[:, 6:9].reshape(-1)
    down_grad = scatter_fsdp(down_part_grad)
    up_grad = scatter_fsdp(up_part_grad)

    qkv_shift_part = lax.dynamic_index_in_dim(
        qkv_shift.reshape(3, HEADS, head_dim), head, 1, keepdims=False
    ).reshape(-1)
    joined = dot(normed_one, qkv_w) + qkv_shift_part
    places = jnp.arange(length, dtype=jnp.int32)
    cosine, sine = rotary_tables(places, ROT)
    queries = rotate(joined[:, :head_dim], cosine, sine).astype(bf16)
    keys = rotate(joined[:, head_dim : 2 * head_dim], cosine, sine).astype(bf16)
    values = joined[:, 2 * head_dim :].astype(bf16)
    allowed = (places[None, :] <= places[:, None]) & (query_seg[None, :] == query_seg[:, None])
    if repeat > 1:
        allowed = allowed & (places // (length // repeat) == ctx % repeat)[:, None]
    scores = jnp.where(allowed, dot_cols(queries, keys) * factor, -1e30)
    top = jnp.max(scores, axis=-1, keepdims=True)
    terms = jnp.where(allowed, jnp.exp(scores - top), 0.0)
    total = jnp.sum(terms, axis=-1, keepdims=True)
    probs = terms * jnp.where(total > 0.0, 1.0 / total, 0.0)
    probs_low = probs.astype(bf16)
    att_f = dot(probs_low, values)
    att = att_f.astype(bf16)
    partial = dot(att, dense_w) + ff_part.astype(f32)
    branch = lax.psum_scatter(partial.astype(bf16), "ctx", scatter_dimension=0, tiled=True)
    own = hidden[0].astype(f32)
    layer_output = (own + branch.astype(f32) + dense_shift + down_shift).astype(bf16)

    d_att = dot_cols(grad_all, dense_w).astype(bf16)
    delta = jnp.sum(d_att.astype(f32) * att_f, axis=-1, keepdims=True)
    dense_grad = dot_rows(att, grad_all).astype(bf16)
    d_scores = (probs * (dot_cols(d_att, values) - delta)).astype(bf16)
    d_queries = rotate(dot(d_scores, keys) * factor, cosine, -sine)
    d_keys = rotate(dot_rows(d_scores, queries) * factor, cosine, -sine)
    d_values = dot_rows(probs_low, d_att)
    d_joined = jnp.concatenate([d_queries, d_keys, d_values], axis=1).astype(bf16)
    qkv_grad = dot_rows(normed_one, d_joined).astype(bf16)

    d_one = dot_cols(d_joined, qkv_w)
    both = (d_one * gain_one + e_two.astype(f32)).astype(bf16)
    back = lax.psum_scatter(both, "ctx", scatter_dimension=0, tiled=True).astype(f32)
    own_scaled, own_spread = centred(own)
    input_part = own_spread * (
        back
        - jnp.mean(back, axis=-1, keepdims=True)
        - own_scaled * jnp.mean(back * own_scaled, axis=-1, keepdims=True)
    )
    input_grad = (out_grad[0].astype(f32) + input_part).astype(bf16)

    first = (ctx == 0).astype(f32)
    joined_sum = jnp.sum(d_joined.astype(f32), axis=0).reshape(3, 1, head_dim)
    joined_full = jnp.where((jnp.arange(HEADS) == head)[None, :, None], joined_sum, 0.0)
    up_sum = up_sum.reshape(shards, 1, units)
    up_full = jnp.where((jnp.arange(ctx_count) == ctx)[None, :, None], up_sum, 0.0)
    small = [
        jnp.sum(d_one * centred(hidden_all)[0], axis=0),
        jnp.sum(d_one, axis=0),
        columns * first,
        gain_two_sum,
        shift_two_sum,
        joined_full,
        up_full,
    ]
    small = jnp.concatenate([piece.reshape(shards, -1) for piece in small], axis=1).astype(bf16)
    small_size = small.shape[1]
    small_rows = -(-small_size // (3 * head_dim * 16)) * 16
    small = jnp.pad(small, ((0, 0), (0, small_rows * 3 * head_dim - small_size)))
    last_grad = scatter_fsdp(
        jnp.concatenate(
            [
                qkv_grad.reshape(shards, rows, 3 * head_dim),
                small.reshape(shards, small_rows, 3 * head_dim),
            ],
            axis=1,
        ).reshape(-1, 3 * head_dim)
    )
    dense_share = scatter_fsdp(
        dense_grad.reshape(head_dim, shards, rows).transpose(1, 0, 2).reshape(-1, rows)
    )

    down_all = line_gather(down_grad).astype(f32).reshape(ctx_count * units, width)
    up_all = (
        line_gather(up_grad)
        .astype(f32)
        .reshape(ctx_count, rows, shards, units)
        .transpose(1, 2, 0, 3)
        .reshape(rows, ff)
    )
    dense_cols_all = line_gather(dense_share)
    if repeat > 1:
        dense_cols_all = jnp.sum(
            dense_cols_all.astype(f32).reshape(HEADS, repeat, head_dim, rows), axis=1
        ).astype(bf16)
    dense_all = lax.all_to_all(
        dense_cols_all.reshape(width, rows), "fsdp", split_axis=0, concat_axis=1, tiled=True
    ).astype(f32)
    last_all = line_gather(last_grad)
    qkv_all = last_all[:, :rows].astype(f32)
    if repeat > 1:
        qkv_all = jnp.sum(qkv_all.reshape(HEADS, repeat, rows, 3 * head_dim), axis=1)
    qkv_all = (
        qkv_all.reshape(HEADS, rows, 3, head_dim).transpose(1, 2, 0, 3).reshape(rows, 3 * width)
    )
    small_all = jnp.sum(last_all[:, rows:].astype(f32), axis=0).reshape(-1)
    sizes = [rows] * 5 + [3 * rows, ff // shards]
    parts, at = [], 0
    for size in sizes:
        parts.append(small_all[at : at + size])
        at += size
    gain_one_grad, shift_one_grad, columns_grad, gain_two_grad, shift_two_grad, joined_grad, up_b_grad = parts
    return (
        layer_output[None],
        input_grad[None],
        gain_one_grad,
        shift_one_grad,
        qkv_all,
        joined_grad,
        dense_all,
        columns_grad,
        gain_two_grad,
        shift_two_grad,
        up_all,
        up_b_grad,
        down_all,
        columns_grad,
    )


def solution(mesh):
    vec, mat, act = P("fsdp"), P("fsdp", None), P("fsdp", "ctx", None)
    return jax.shard_map(
        per_device,
        mesh=mesh,
        in_specs=(
            act, vec, vec, mat, vec, mat, vec, vec, vec, mat, vec, mat, vec, P("fsdp", "ctx"), act
        ),
        out_specs=(act, act, vec, vec, mat, vec, mat, vec, vec, vec, mat, vec, mat, vec),
        check_vma=False,
    )
```

```python
import functools
import math

import jax
import jax.numpy as jnp
import numpy as np
from jax import lax
from jax.experimental import pallas as pl
from jax.experimental.pallas import tpu as pltpu
from jax.sharding import PartitionSpec as P

HEADS = 8
ROT = 64
CORES = 2


def dot(left, right):
    return jnp.dot(left, right, preferred_element_type=jnp.float32)


def dot_rows(left, right):
    return lax.dot_general(
        left, right, (((0,), (0,)), ((), ())), preferred_element_type=jnp.float32
    )


def dot_cols(left, right):
    return lax.dot_general(
        left, right, (((1,), (1,)), ((), ())), preferred_element_type=jnp.float32
    )


def gelu_and_slope(values):
    cdf = 0.5 * (1.0 + lax.erf(values * (0.5**0.5)))
    density = jnp.exp(-0.5 * values * values) * ((2.0 * jnp.pi) ** -0.5)
    return values * cdf, cdf + values * density


def centred(values):
    values = values.astype(jnp.float32)
    center = values - jnp.mean(values, axis=-1, keepdims=True)
    spread = lax.rsqrt(jnp.mean(center * center, axis=-1, keepdims=True) + 1e-05)
    return center * spread, spread


def rotary_tables(places, width):
    half_rot = width // 2
    freqs = 10000.0 ** (-2.0 * jnp.arange(half_rot, dtype=jnp.float32) / width)
    angles = places.astype(jnp.float32)[:, None] * freqs[None, :]
    return (jnp.cos(angles), jnp.sin(angles))


def rotate(values, cosine, sine):
    half = cosine.shape[-1]
    first, second, remain = values[:, :half], values[:, half : 2 * half], values[:, 2 * half :]
    return jnp.concatenate(
        [first * cosine - second * sine, second * cosine + first * sine, remain], axis=1
    )


def line_gather(block):
    count = lax.axis_size("ctx")
    chips = count // CORES
    ctx = lax.axis_index("ctx")
    place, core = ctx // CORES, ctx % CORES
    up = down = block
    ups, downs = [], []
    for hop in range(1, chips):
        up = lax.ppermute(
            up,
            "ctx",
            [
                (i * CORES + k, (i + 1) * CORES + k)
                for i in range(hop - 1, chips - 1)
                for k in range(CORES)
            ],
        )
        down = lax.ppermute(
            down,
            "ctx",
            [
                (i * CORES + k, (i - 1) * CORES + k)
                for i in range(1, chips - hop + 1)
                for k in range(CORES)
            ],
        )
        ups.append(up)
        downs.append(down)
    around = jnp.stack(ups[::-1] + [block] + downs)
    mine = lax.dynamic_slice_in_dim(around, chips - 1 - place, chips, 0)
    other = lax.ppermute(mine, "ctx", [(i, i ^ 1) for i in range(count)])
    is_mine = (jnp.arange(CORES) == core).reshape((1, CORES) + (1,) * block.ndim)
    return jnp.where(is_mine, mine[:, None], other[:, None]).reshape((count,) + block.shape)


def gather_fsdp(values, axis=0):
    return lax.all_gather(values, "fsdp", axis=axis, tiled=True)


def scatter_fsdp(values):
    return lax.psum_scatter(values, "fsdp", scatter_dimension=0, tiled=True)


def remote(src, dst, sems, slot, device):
    return pltpu.make_async_remote_copy(
        src_ref=src,
        dst_ref=dst,
        send_sem=sems[0].at[slot],
        recv_sem=sems[1].at[slot],
        device_id=device,
        device_id_type=pl.DeviceIdType.MESH,
    )


class Line:
    def __init__(self, source, blocks, sems, base, place, chips, stride=None, offset=0, columns=slice(None)):
        self.source, self.sems, self.base, self.chips = source, sems, base, chips
        self.ctx, self.shard = place
        self.chip = self.ctx // CORES
        rows = source.shape[0]
        stride = stride or rows
        self.block = lambda index: blocks.at[
            pl.ds(pl.multiple_of(index * stride + offset, rows), rows), columns
        ]
        self.swap_base = base + 2 * (chips - 1)
        self.own_slot = base + 4 * (chips - 1)

    @staticmethod
    def slots(chips):
        return 4 * (chips - 1) + 2

    def hop(self, up, number):
        step = 1 if up else -1
        slot = (0 if up else self.chips - 1) + number - 1
        origin = self.ctx - step * (number - 1) * CORES
        if up:
            sends = (self.chip >= number - 1) & (self.chip < self.chips - 1)
            gets = self.chip >= number
        else:
            sends = (self.chip <= self.chips - number) & (self.chip > 0)
            gets = self.chip <= self.chips - 1 - number
        return slot, step, origin, sends, gets

    def send(self, up, number):
        slot, step, origin, sends, _ = self.hop(up, number)

        @pl.when(sends)
        def _():
            remote(
                self.source if number == 1 else self.block(origin),
                self.block(origin),
                self.sems,
                self.base + slot,
                (self.ctx + step * CORES, self.shard),
            ).start()

    def start(self):
        self.send(True, 1)
        self.send(False, 1)
        remote(
            self.source, self.block(self.ctx), self.sems, self.own_slot, (self.ctx ^ 1, self.shard)
        ).start()
        self.local = pltpu.make_async_copy(
            self.source, self.block(self.ctx), self.sems[0].at[self.own_slot + 1]
        )
        self.local.start()

    def land(self, number):
        for up in (True, False):
            slot, step, origin, _, gets = self.hop(up, number)
            block = self.block(origin - step * CORES)

            @pl.when(gets)
            def _(block=block, slot=slot):
                remote(
                    block, block, self.sems, self.base + slot, (self.ctx ^ 1, self.shard)
                ).wait_recv()

            if number < self.chips - 1:
                self.send(up, number + 1)

            @pl.when(gets)
            def _(block=block, slot=slot):
                remote(
                    block, block, self.sems, self.swap_base + slot, (self.ctx ^ 1, self.shard)
                ).start()

    def arrived(self):
        other = self.block(self.ctx ^ 1)
        remote(other, other, self.sems, self.own_slot, (self.ctx ^ 1, self.shard)).wait_recv()
        self.local.wait()
        for up in (True, False):
            for number in range(1, self.chips):
                slot, step, origin, _, gets = self.hop(up, number)
                block = self.block((origin - step * CORES) ^ 1)

                @pl.when(gets)
                def _(block=block, slot=slot):
                    remote(
                        block, block, self.sems, self.swap_base + slot, (self.ctx ^ 1, self.shard)
                    ).wait_recv()

    def sent(self):
        source = self.source
        peer = (self.ctx ^ 1, self.shard)
        remote(source, source, self.sems, self.own_slot, peer).wait_send()
        for up in (True, False):
            for number in range(1, self.chips):
                slot, _, _, sends, gets = self.hop(up, number)

                @pl.when(sends)
                def _(slot=slot):
                    remote(source, source, self.sems, self.base + slot, peer).wait_send()

                @pl.when(gets)
                def _(slot=slot):
                    remote(source, source, self.sems, self.swap_base + slot, peer).wait_send()


class Square:
    SLOTS = 8

    def __init__(self, pieces, blocks, sems, base, place):
        self.pieces, self.sems, self.base = pieces, sems, base
        self.ctx, self.shard = place
        half = blocks.shape[0] // 8

        def part(owner, which, columns=slice(None)):
            start = pl.multiple_of((2 * owner + which) * half, half)
            return blocks.at[pl.ds(start, half), columns]

        self.part = part

    def to(self, bit):
        return (self.ctx, self.shard ^ bit)

    def own(self, bit, which):
        for source, columns in self.pieces(which):
            remote(
                source,
                self.part(self.shard, which, columns),
                self.sems,
                self.base + 2 * (bit - 1) + which,
                self.to(bit),
            ).start()

    def start(self):
        self.own(1, 0)
        self.own(2, 1)
        self.own(1, 1)
        self.own(2, 0)
        for which in (0, 1):
            for source, columns in self.pieces(which):
                pltpu.make_async_copy(
                    source,
                    self.part(self.shard, which, columns),
                    self.sems[0].at[self.base + 6 + which],
                ).start()

    def wait(self, owner, which, slot, bit):
        part = self.part(owner, which)
        remote(part, part, self.sems, self.base + slot, self.to(bit)).wait_recv()

    def forward(self):
        for bit in (1, 2):
            which = bit - 1
            owner = self.shard ^ bit
            self.wait(owner, which, 2 * (bit - 1) + which, bit)
            part = self.part(owner, which)
            remote(part, part, self.sems, self.base + 4 + which, self.to(3 - bit)).start()

    def arrived(self):
        self.wait(self.shard ^ 1, 1, 1, 1)
        self.wait(self.shard ^ 2, 0, 2, 2)
        self.wait(self.shard ^ 3, 0, 4, 2)
        self.wait(self.shard ^ 3, 1, 5, 1)
        for which in (0, 1):
            part = self.part(self.shard, which)
            pltpu.make_async_copy(part, part, self.sems[0].at[self.base + 6 + which]).wait()

    def sent(self):
        for slot in range(6):
            part = self.part(self.shard, 0)
            remote(part, part, self.sems, self.base + slot, self.to(1)).wait_send()


class Tree:
    SLOTS = 8

    def __init__(self, source, block, sems, base, place, owner):
        self.source, self.block, self.sems, self.base = source, block, sems, base
        self.ctx, self.shard = place
        self.turn = self.shard ^ owner
        self.half = block.shape[0] // 2

    def rows(self, ref, which):
        return ref.at[pl.ds(which * self.half, self.half)]

    def copy(self, ref, which, slot, bit):
        return remote(
            self.rows(ref, which),
            self.rows(self.block, which),
            self.sems,
            self.base + slot,
            (self.ctx, self.shard ^ bit),
        )

    def start(self):
        @pl.when(self.turn == 0)
        def _():
            self.copy(self.source, 0, 0, 1).start()
            self.copy(self.source, 1, 3, 2).start()
            self.copy(self.source, 1, 1, 1).start()
            self.copy(self.source, 0, 2, 2).start()
            pltpu.make_async_copy(self.source, self.block, self.sems[0].at[self.base + 6]).start()

    def forward(self):
        for bit in (1, 2):
            which = bit - 1

            @pl.when(self.turn == bit)
            def _(bit=bit, which=which):
                self.copy(self.block, which, 2 * (bit - 1) + which, bit).wait_recv()
                self.copy(self.block, which, 4 + which, 3 - bit).start()

    def arrived(self):
        @pl.when(self.turn == 0)
        def _():
            pltpu.make_async_copy(self.source, self.block, self.sems[0].at[self.base + 6]).wait()

        for bit in (1, 2):

            @pl.when(self.turn == bit)
            def _(bit=bit):
                which = 2 - bit
                self.copy(self.block, which, 2 * (bit - 1) + which, bit).wait_recv()

        @pl.when(self.turn == 3)
        def _():
            self.copy(self.block, 0, 4, 2).wait_recv()
            self.copy(self.block, 1, 5, 1).wait_recv()

    def sent(self):
        @pl.when(self.turn == 0)
        def _():
            for slot in range(4):
                self.copy(self.block, 0, slot, 1).wait_send()

        for bit in (1, 2):

            @pl.when(self.turn == bit)
            def _(bit=bit):
                self.copy(self.block, bit - 1, 3 + bit, 3 - bit).wait_send()


def add_rows(dst, sources):
    step = 32

    def body(index, carry):
        rows = pl.ds(pl.multiple_of(index * step, step), step)
        total = sources[0][rows].astype(jnp.float32)
        for source in sources[1:]:
            total += source[rows].astype(jnp.float32)
        dst[rows] = total.astype(dst.dtype)
        return carry

    lax.fori_loop(0, dst.shape[0] // step, body, 0)


class Fold:
    SLOTS = 6

    def __init__(self, parts, landing, stage, carry, final, sems, local, base, place):
        self.parts, self.landing, self.stage, self.carry, self.final = parts, landing, stage, carry, final
        self.sems, self.local, self.base = sems, local, base
        self.ctx, self.shard = place
        self.half = final.shape[0] // 2

    def part(self, owner, which):
        start = pl.multiple_of((2 * owner + which) * self.half, self.half)
        return self.parts.at[pl.ds(start, self.half)]

    def landed(self, slot):
        return self.landing.at[pl.ds(slot * self.half, self.half)]

    def copy(self, src, slot, bit):
        return remote(
            src, self.landed(slot), self.sems, self.base + slot, (self.ctx, self.shard ^ bit)
        )

    def send(self, slot):
        bit, which = (1, 0) if slot < 2 else (2, 1)
        owner = self.shard ^ (3 if slot % 2 else bit)
        self.copy(self.part(owner, which), slot, bit).start()

    def add(self, dst, sources):
        copies = []
        for index, source in enumerate(sources):
            copies.append(
                pltpu.make_async_copy(source, self.stage.at[index], self.local.at[index])
            )
            copies[-1].start()
        for copy in copies:
            copy.wait()
        add_rows(dst, [self.stage.at[index] for index in range(len(sources))])

    def wait(self, slot, bit):
        self.copy(self.landed(slot), slot, bit).wait_recv()

    def middle(self, which):
        first, second = (1, 2) if which == 0 else (2, 1)
        slot = 1 + 2 * which
        self.wait(slot, first)
        carry = self.carry.at[which]
        self.add(carry, [self.part(self.shard ^ second, which), self.landed(slot)])
        self.copy(carry, 4 + which, second).start()

    def finish(self, which):
        first, second = (1, 2) if which == 0 else (2, 1)
        self.wait(2 * which, first)
        self.wait(4 + which, second)
        self.add(
            self.final.at[pl.ds(which * self.half, self.half)],
            [self.part(self.shard, which), self.landed(2 * which), self.landed(4 + which)],
        )

    def sent(self):
        for slot in range(6):
            self.copy(self.part(self.shard, 0), slot, 1).wait_send()


class Sink:
    def __init__(self, parts, swapped, landing, stage, carry, final, sems, local, base, place, chips):
        self.parts, self.swapped, self.landing, self.stage = parts, swapped, landing, stage
        self.carry, self.final, self.sems, self.local, self.base = carry, final, sems, local, base
        self.ctx, self.shard = place
        self.chip, self.core, self.chips = self.ctx // CORES, self.ctx % CORES, chips
        self.rows = final.shape[0]

    @staticmethod
    def slots(chips):
        return 2 * (chips - 1) + 1

    def block(self, ref, index):
        return ref.at[pl.ds(pl.multiple_of(index * self.rows, self.rows), self.rows)]

    def start(self):
        for chip in range(self.chips):
            remote(
                self.block(self.parts, CORES * chip + (self.core ^ 1)),
                self.block(self.swapped, chip),
                self.sems,
                self.base,
                (self.ctx ^ 1, self.shard),
            ).start()

    def swap(self):
        swapped = self.swapped
        remote(swapped, swapped, self.sems, self.base, (self.ctx ^ 1, self.shard)).wait_recv()

    def hop(self, up, step):
        place = self.chip if up else self.chips - 1 - self.chip
        target = place + self.chips - step
        target = target if up else self.chips - 1 - target
        slot = (0 if up else self.chips - 1) + step - 1
        sends = (place + 1 <= step) & (place < self.chips - 1)
        gets = (place <= step) & (place > 0)
        return slot, target, sends, gets, place > 0

    def landed(self, slot):
        return self.landing.at[pl.ds(slot * self.rows, self.rows)]

    def copy(self, up, slot):
        way = CORES if up else -CORES
        return remote(
            self.carry.at[0 if up else 1],
            self.landed(slot),
            self.sems,
            self.base + 1 + slot,
            (self.ctx + way, self.shard),
        )

    def load(self, index, source):
        return pltpu.make_async_copy(source, self.stage.at[index], self.local.at[index])

    def own(self, target):
        return [
            self.load(0, self.block(self.parts, CORES * target + self.core)),
            self.load(1, self.block(self.swapped, target)),
        ]

    def step(self, number):
        for up in (True, False):
            slot, target, sends, _, passes = self.hop(up, number)
            if number > 1:
                before, _, sent, gets, _ = self.hop(up, number - 1)

                @pl.when(gets)
                def _(before=before, up=up):
                    remote(
                        self.landed(before), self.landed(before), self.sems, self.base + 1 + before,
                        (self.ctx ^ 1, self.shard),
                    ).wait_recv()

                @pl.when(sent)
                def _(before=before, up=up):
                    self.copy(up, before).wait_send()

            @pl.when(sends)
            def _(up=up, slot=slot, target=target, passes=passes):
                loads = self.own(target)
                for load in loads:
                    load.start()
                carry = self.carry.at[0 if up else 1]
                stage = self.stage
                if number > 1:

                    @pl.when(passes)
                    def _():
                        more = self.load(2, self.landed(slot - 1))
                        more.start()
                        for load in loads + [more]:
                            load.wait()
                        add_rows(carry, [stage.at[0], stage.at[1], stage.at[2]])

                    @pl.when(jnp.logical_not(passes))
                    def _():
                        for load in loads:
                            load.wait()
                        add_rows(carry, [stage.at[0], stage.at[1]])
                else:
                    for load in loads:
                        load.wait()
                    add_rows(carry, [stage.at[0], stage.at[1]])
                self.copy(up, slot).start()

    def finish(self, dst, sem):
        loads = self.own(self.chip)
        for load in loads:
            load.start()
        for load in loads:
            load.wait()
        add_rows(self.final, [self.stage.at[0], self.stage.at[1]])
        for up in (True, False):
            slot, _, sends, gets, _ = self.hop(up, self.chips - 1)

            @pl.when(gets)
            def _(slot=slot):
                landed = self.landed(slot)
                remote(
                    landed, landed, self.sems, self.base + 1 + slot, (self.ctx ^ 1, self.shard)
                ).wait_recv()
                load = self.load(2, landed)
                load.start()
                load.wait()
                add_rows(self.final, [self.final, self.stage.at[2]])

            @pl.when(sends)
            def _(up=up, slot=slot):
                self.copy(up, slot).wait_send()

        swapped = self.swapped
        remote(swapped, swapped, self.sems, self.base, (self.ctx ^ 1, self.shard)).wait_send()
        copy = pltpu.make_async_copy(self.final, dst, sem)
        copy.start()
        copy.wait()


TILE = 256


def block_kernel(
    sizes,
    hidden, grad, fc1, fc2, qkv, dense, segs, tables,
    ln1_gain, ln1_bias, ln2_gain, ln2_bias, dense_bias, fc2_bias, qkv_bias, fc1_bias,
    vec_out, output_out, input_out, down_all, up_all, qkv_all, dense_all, sums_all,
    down_parts, up_parts, qkv_parts, dense_parts, down_land, up_land, qkv_land, dense_land,
    out_parts, out_swap, out_land, in_parts, in_swap, in_land, dense_lines,
    hid, gra, norm, w_up, w_down, w_qkv, w_dense, vec, seg, seg_col, table,
    act, wide_f, d_up, queries, keys, values, att_f, att, d_keys, d_values, d_joined, sums, sums_got, sums_tot,
    stage, down_stage, up_stage,
    down_carry, up_carry, qkv_carry, dense_carry, down_final, up_final, qkv_final, dense_final,
    out_carry, in_carry, sink_final,
    send_sems, recv_sems, local_sems,
):
    chips, shards, columns = sizes
    place = ctx, shard = lax.axis_index("ctx"), lax.axis_index("fsdp")
    chip, core = ctx // CORES, ctx % CORES
    count = CORES * chips
    sems = (send_sems, recv_sems)
    width, length = hidden.shape[1], hid.shape[0]
    ff_units = w_down.shape[0]
    head_dim = w_dense.shape[0]
    row_size = vec.shape[3]
    tiles = length // TILE
    f32, bf16 = jnp.float32, jnp.bfloat16
    factor = head_dim ** (-0.5)

    barrier = pltpu.get_barrier_semaphore()
    peers = [(ctx, shard ^ bit) for bit in (1, 2, 3)]
    peers += [(lax.rem(ctx + step, count), shard) for step in range(1, count)]
    for peer in peers:
        pl.semaphore_signal(barrier, inc=1, device_id=peer, device_id_type=pl.DeviceIdType.MESH)
    pl.semaphore_wait(barrier, len(peers))

    base = 0

    def take(slots):
        nonlocal base
        base += slots
        return base - slots

    def line(source, blocks, stride=None, offset=0, cut=slice(None)):
        return Line(source, blocks, sems, take(Line.slots(chips)), place, chips, stride, offset, cut)

    def fold(parts, landing, stage, carry, final):
        return Fold(
            parts, landing, stage, carry, final, sems, local_sems.at[pl.ds(4, 4)], take(Fold.SLOTS), place
        )

    def sink(parts, swapped, landing, carry):
        return Sink(
            parts, swapped, landing, down_stage, carry, sink_final, sems, local_sems.at[pl.ds(4, 4)],
            take(Sink.slots(chips)), place, chips,
        )

    def halves(ref, which, start, size):
        half = ref.shape[0] // 2
        return ref.at[pl.ds(which * half, half), pl.ds(pl.multiple_of(start, size), size)]

    def up_pieces(which):
        stride = fc1.shape[1] // shards
        return [
            (
                halves(fc1, which, index * stride + ctx * columns, columns),
                pl.ds(index * columns, columns),
            )
            for index in range(shards)
        ]

    def down_pieces(which):
        half = columns // 2
        start = pl.multiple_of(ctx * columns + which * half, half)
        return [(fc2.at[pl.ds(start, half)], slice(None))]

    def qkv_pieces(which):
        return [
            (
                halves(qkv, which, index * width + ctx * head_dim, head_dim),
                pl.ds(index * head_dim, head_dim),
            )
            for index in range(3)
        ]

    hid_line, gra_line = line(hidden, hid), line(grad, gra)
    squares = [
        Square(pieces, blocks, sems, take(Square.SLOTS), place)
        for pieces, blocks in ((up_pieces, w_up), (down_pieces, w_down), (qkv_pieces, w_qkv))
    ]
    up_square, down_square, qkv_square = squares
    heads_here = dense.shape[0] // head_dim
    dense_rows = dense.at[
        pl.ds(pl.multiple_of(lax.rem(ctx, heads_here) * head_dim, head_dim), head_dim)
    ]
    tree = Tree(dense_rows, w_dense, sems, take(Tree.SLOTS), place, ctx // heads_here)
    named = {"hid": hid_line, "gra": gra_line, "wu": up_square, "wd": down_square, "wq": qkv_square, "wt": tree}
    folds, lines = [], []

    def gradient(letter, cuts, parts, landing, stage, carry, final, gathered):
        start, half = 0, final.shape[0] // 2
        for index, (size, split) in enumerate(cuts):
            cut = pl.ds(start, size)
            item = fold(
                parts.at[:, cut], landing.at[:, cut], stage.at[:, :, :size], carry.at[:, :, cut], final.at[:, cut]
            )
            folds.append(item)
            named[f"f{letter}{index}"] = item
            for which in range(2 if split else 1):
                rows = half if split else 2 * half
                item = line(
                    final.at[pl.ds(which * rows, rows), cut], gathered, final.shape[0], which * rows, cut
                )
                lines.append(item)
                named[f"l{letter}{index}{which}"] = item
            start += size

    gradient("d", DOWN_CUTS, down_parts, down_land, down_stage, down_carry, down_final, down_all)
    gradient("u", UP_CUTS, up_parts, up_land, up_stage, up_carry, up_final, up_all)
    gradient("q", QKV_CUTS, qkv_parts, qkv_land, up_stage, qkv_carry, qkv_final, qkv_all)
    gradient("e", DENSE_CUTS, dense_parts, dense_land, down_stage, dense_carry, dense_final, dense_lines)
    named["ls"] = line(sums_tot, sums_all)
    lines.append(named["ls"])
    out_sink = sink(out_parts, out_swap, out_land, out_carry)
    in_sink = sink(in_parts, in_swap, in_land, in_carry)
    named["so"], named["si"] = out_sink, in_sink

    small = []

    def send_small(src, dst, landing, device):
        slot = take(1)
        small.append((remote(src, dst, sems, slot, device), landing, slot))
        small[-1][0].start()

    def wait_small(items):
        for _, landing, slot in items:
            remote(landing, landing, sems, slot, (ctx ^ 1, shard)).wait_recv()

    vectors = (
        ln1_gain, ln1_bias, ln2_gain, ln2_bias, dense_bias, fc2_bias, qkv_bias, fc1_bias
    )
    at, pairs = 0, [(segs, seg.at[ctx]), (tables, table)]
    for vector in vectors:
        size = vec.shape[3]
        for start in range(0, vector.shape[1], size):
            pairs.append((vector.at[:, pl.ds(start, size)], vec.at[shard, at]))
            at += 1
    locals_in = [
        pltpu.make_async_copy(src, dst, local_sems.at[8 + index])
        for index, (src, dst) in enumerate(pairs)
    ]
    for copy in locals_in:
        copy.start()

    def small_start():
        for copy in locals_in:
            copy.wait()
        for bit in (1, 2, 3):
            send_small(vec.at[shard], vec.at[shard], vec.at[shard ^ bit], (ctx, shard ^ bit))
        for step in range(1, count):
            send_small(
                segs, seg.at[ctx], seg.at[lax.rem(ctx + count - step, count)],
                (lax.rem(ctx + step, count), shard),
            )

    def small_land():
        wait_small(small)

    def vector(row):
        return jnp.concatenate([vec[index, row] for index in range(shards)], axis=1)

    def rows_of(index):
        return pl.ds(pl.multiple_of(index * TILE, TILE), TILE)

    def loop(body, steps=tiles):
        lax.fori_loop(0, steps, lambda index, carry: (body(rows_of(index)), carry)[1], 0)

    def scaled_rows(rows):
        return centred(hid[rows])[0]

    def norm_two(rows):
        norm[rows] = (scaled_rows(rows) * vector(2) + vector(3)).astype(bf16)

    def norm_one(rows):
        norm[rows] = (scaled_rows(rows) * vector(0) + vector(1)).astype(bf16)

    def emit(steps, compute, dst, size, start=0):
        def write(index):
            return pltpu.make_async_copy(
                stage.at[lax.rem(index, 2), :, :size],
                dst.at[rows_of(index), pl.ds(start, size)],
                local_sems.at[lax.rem(index, 2)],
            )

        def body(index, carry):
            @pl.when(index >= 2)
            def _():
                write(index - 2).wait()

            stage[lax.rem(index, 2), :, :size] = compute(index).astype(bf16)
            write(index).start()
            return carry

        lax.fori_loop(0, steps, body, 0)
        write(steps - 2).wait()
        write(steps - 1).wait()

    def feed_forward():
        bias_start = ctx * columns
        bias_row = 9 + bias_start // row_size
        bias_column = pl.multiple_of(lax.rem(bias_start, row_size), columns)
        up_bias = jnp.concatenate(
            [vec[index, bias_row, :, pl.ds(bias_column, columns)] for index in range(shards)],
            axis=1,
        )

        def body(rows):
            value = dot(norm[rows], w_up[...]) + up_bias
            cdf = 0.5 * (1.0 + lax.erf(value * (0.5**0.5)))
            density = jnp.exp(-0.5 * value * value) * ((2.0 * math.pi) ** -0.5)
            act[rows] = (value * cdf).astype(bf16)
            wide_f[rows] = cdf + value * density

        loop(body)

    def down_grad(index):
        start, size = sum(cut[0] for cut in DOWN_CUTS[:index]), DOWN_CUTS[index][0]

        def body(step, carry):
            rows = rows_of(shard ^ (3 - step))
            cut = pl.ds(start, size)
            stage[0, :, :size] = dot_rows(act[:, rows], gra[:, cut]).astype(bf16)
            write = pltpu.make_async_copy(
                stage.at[0, :, :size], down_parts.at[rows, cut], local_sems.at[0]
            )
            write.start()
            write.wait()
            for number, slot in ((0, 1), (1, 2), (2, 0)):

                @pl.when(step == number)
                def _(slot=slot):
                    named[f"fd{index}"].send(slot)

            return carry

        lax.fori_loop(0, shards, body, 0)

    def feed_back():
        def body(rows):
            d_up[rows] = (dot_cols(gra[rows], w_down[...]) * wide_f[rows]).astype(bf16)

        loop(body)

    def up_grad(index):
        start, size = sum(cut[0] for cut in UP_CUTS[:index]), UP_CUTS[index][0]
        emit(
            width // TILE,
            lambda step: dot_rows(norm[:, rows_of(step)], d_up[:, pl.ds(start, size)]),
            up_parts,
            size,
            start,
        )

    rotary = table.shape[2]

    def turn(entries, rows, way):
        first = entries[:, :rotary]
        first = (
            first * table[0, rows]
            + way * (pltpu.roll(first, ROT // 2, 1) * table[1, rows])
            + way * (pltpu.roll(first, rotary - ROT // 2, 1) * table[2, rows])
        )
        return jnp.concatenate([first, entries[:, rotary:]], axis=1)

    def project():
        per = 3 * HEADS // shards
        bias_parts = []
        for index in range(3):
            place = index * HEADS + ctx
            rest = lax.rem(place, per) * head_dim
            bias_parts.append(
                vec[
                    place // per,
                    6 + rest // row_size,
                    :,
                    pl.ds(pl.multiple_of(lax.rem(rest, row_size), head_dim), head_dim),
                ]
            )

        def body(rows):
            joined = dot(norm[rows], w_qkv[...])
            parts = [
                joined[:, index * head_dim : (index + 1) * head_dim] + bias_parts[index]
                for index in range(3)
            ]
            queries[rows] = turn(parts[0], rows, 1.0).astype(bf16)
            keys[rows] = turn(parts[1], rows, 1.0).astype(bf16)
            values[rows] = parts[2].astype(bf16)

        loop(body)
        side = segs.shape[1]
        for index in range(count):
            block = seg[index].astype(f32)
            seg_col[index * side : (index + 1) * side] = jnp.broadcast_to(block, (side, side)).T

    def attend(index):
        rows = pl.ds(index * TILE, TILE)
        size = (index + 1) * TILE
        seg_row = jnp.concatenate([seg[block] for block in range(count)], axis=1)
        scores = dot_cols(queries[rows], keys[:size]) * factor
        query_place = index * TILE + lax.broadcasted_iota(jnp.int32, (TILE, size), 0)
        key_place = lax.broadcasted_iota(jnp.int32, (TILE, size), 1)
        same = seg_col[rows][:, :1] == seg_row[:, :size].astype(f32)
        allowed = (key_place <= query_place) & same
        scores = jnp.where(allowed, scores, -1e30)
        terms = jnp.where(
            allowed, jnp.exp(scores - jnp.max(scores, axis=-1, keepdims=True)), 0.0
        )
        probs = terms / jnp.sum(terms, axis=-1, keepdims=True)
        wide_f[rows, :size] = probs
        result = dot(probs.astype(bf16), values[:size])
        att_f[rows] = result
        att[rows] = result.astype(bf16)

    def attend_all():
        for index in range(tiles):
            attend(index)

    def output():
        def body(index):
            rows = rows_of(index)
            return dot(att[rows], w_dense[...]) + dot(act[rows], w_down[...])

        emit(tiles, body, out_parts, width)

    dense_size = width // shards

    def dense_grad():
        def body(index):
            start = pl.multiple_of(index * dense_size, dense_size)
            return dot_rows(att[...], gra[:, pl.ds(start, dense_size)])

        emit(shards, body, dense_parts, dense_size)

    def attend_back(index):
        rows = pl.ds(index * TILE, TILE)
        size = (index + 1) * TILE
        d_att = dot_cols(gra[rows], w_dense[...]).astype(bf16)
        delta = jnp.sum(d_att.astype(f32) * att_f[rows], axis=-1, keepdims=True)
        probs = wide_f[rows, :size]
        d_scores = (probs * (dot_cols(d_att, values[:size]) - delta)).astype(bf16)
        d_queries = dot(d_scores, keys[:size]) * factor
        d_joined[rows, :head_dim] = turn(d_queries, rows, -1.0).astype(bf16)
        d_keys[:size] += dot_rows(d_scores, queries[rows])
        d_values[:size] += dot_rows(probs.astype(bf16), d_att)

    def attend_back_all():
        d_keys[...] = jnp.zeros_like(d_keys)
        d_values[...] = jnp.zeros_like(d_values)
        for index in range(tiles):
            attend_back(index)

        def join(rows):
            d_joined[rows, head_dim : 2 * head_dim] = turn(d_keys[rows] * factor, rows, -1.0).astype(bf16)
            d_joined[rows, 2 * head_dim :] = d_values[rows].astype(bf16)

        loop(join)

    def qkv_grad(index):
        start, size = sum(cut[0] for cut in QKV_CUTS[:index]), QKV_CUTS[index][0]
        emit(
            width // TILE,
            lambda step: dot_rows(norm[:, rows_of(step)], d_joined[:, pl.ds(start, size)]),
            qkv_parts,
            size,
            start,
        )

    def inputs():
        sums[...] = jnp.zeros_like(sums)

        def body(index):
            rows = rows_of(index)
            d_one = dot_cols(d_joined[rows], w_qkv[...])
            d_two = dot_cols(d_up[rows], w_up[...])
            scaled = scaled_rows(rows)

            def gather(row, entries):
                sums[row : row + 1, : entries.shape[1]] += jnp.sum(
                    entries.astype(f32), axis=0, keepdims=True
                )

            gather(0, d_two * scaled)
            gather(1, d_two)
            gather(2, gra[rows])
            gather(3, d_up[rows])
            gather(4, d_one * scaled)
            gather(5, d_one)
            gather(6, d_joined[rows])
            return d_one * vector(0) + d_two * vector(2)

        emit(tiles, body, in_parts, width)

    sums_items = []

    def sums_start():
        for bit in (1, 2, 3):
            send_small(sums, sums_got.at[shard], sums_got.at[shard ^ bit], (ctx, shard ^ bit))
            sums_items.append(small[-1])
        sums_got[shard] = sums[...]

    def sums_land():
        wait_small(sums_items)
        total = sums_got[0]
        for index in range(1, shards):
            total = total + sums_got[index]
        sums_tot[...] = total

    exchanged = []

    def dense_block(owner):
        return pl.ds(pl.multiple_of(owner * dense_size, dense_size), dense_size)

    def own_dense():
        return pltpu.make_async_copy(
            dense_lines.at[dense_block(shard)], dense_all.at[dense_block(shard)], local_sems.at[2]
        )

    def exchange():
        for bit in (1, 2, 3):
            peer = shard ^ bit
            send_small(
                dense_lines.at[dense_block(peer)], dense_all.at[dense_block(shard)],
                dense_all.at[dense_block(peer)], (ctx, peer),
            )
            exchanged.append(small[-1])
        own_dense().start()

    steps = {
        "small_start": small_start, "small_land": small_land, "norm_two": lambda: loop(norm_two),
        "norm_one": lambda: loop(norm_one), "feed_forward": feed_forward, "down_grad": down_grad,
        "feed_back": feed_back, "up_grad": up_grad, "project": project, "attend": attend_all, "output": output,
        "dense_grad": dense_grad, "attend_back": attend_back_all, "qkv_grad": qkv_grad, "inputs": inputs,
        "sums_start": sums_start, "sums_land": sums_land, "exchange": exchange,
        "output_done": lambda: out_sink.finish(output_out, local_sems.at[3]),
        "input_done": lambda: in_sink.finish(input_out, local_sems.at[3]),
    }
    for step in ORDER:
        name, *rest = step.split(".")
        if name in steps:
            steps[name](*[int(number) for number in rest])
        else:
            getattr(named[name], rest[0])(*[int(number) for number in rest[1:]])

    write_vec = pltpu.make_async_copy(vec, vec_out, local_sems.at[8])
    write_vec.start()
    for item in lines:
        if item is not named["le00"]:
            item.arrived()
    wait_small(exchanged)
    own_dense().wait()
    for item in [hid_line, gra_line] + lines + squares + [tree] + folds:
        item.sent()
    for copy, _, _ in small:
        copy.wait_send()
    write_vec.wait()


DOWN_CUTS = ((512, False), (512, False), (1024, True))
UP_CUTS = ((512, True), (512, True))
QKV_CUTS = ((768, True),)
DENSE_CUTS = ((512, False),)

ORDER = (
    "wu.start", "hid.start", "gra.start", "small_start", "hid.land.1", "wu.forward", "gra.land.1", "wd.start",
    "hid.land.2", "hid.land.3", "small_land", "wd.forward", "wu.arrived", "hid.arrived", "norm_two", "gra.land.2",
    "feed_forward", "gra.land.3", "gra.arrived", "down_grad.2", "fd2.send.3", "wd.arrived", "feed_back", "up_grad.0",
    "fu0.send.3", "fd2.middle.1", "fd2.middle.0", "fu0.send.2", "down_grad.1", "fd2.finish.1", "ld21.start",
    "fu0.middle.1", "fd2.finish.0", "fu0.send.1", "ld20.start", "fd1.middle.0", "fu0.finish.1", "lu01.start",
    "fu0.send.0", "ld21.land.1", "fd1.send.3", "down_grad.0", "ld20.land.1", "fd0.send.3", "fd1.middle.1",
    "fu0.middle.0", "wq.start", "lu01.land.1", "fu0.finish.0", "ld20.land.2", "lu00.start", "ld20.land.3",
    "wq.forward", "fd1.finish.0", "fd0.middle.1", "fd0.middle.0", "wt.start", "lu01.land.2", "lu00.land.1",
    "up_grad.1", "fu1.send.3", "lu00.land.2", "fd1.finish.1", "ld10.start", "fd0.finish.1", "fd0.finish.0",
    "ld00.start", "ld10.land.1", "norm_one", "wq.arrived", "wt.forward", "project", "ld00.land.1", "attend",
    "ld21.land.2", "fu1.send.1", "fu1.send.0", "ld10.land.2", "fu1.send.2", "dense_grad", "ld00.land.2",
    "wt.arrived", "attend_back", "fe0.send.1", "fu1.middle.1", "fu1.middle.0", "qkv_grad.0", "fq0.send.1",
    "fq0.send.3", "fu1.finish.0", "lu10.start", "fq0.send.0", "ld21.land.3", "fq0.send.2", "fu1.finish.1",
    "lu11.start", "output", "so.start", "lu10.land.1", "fq0.middle.0", "fq0.middle.1", "lu11.land.1", "lu01.land.3",
    "lu10.land.2", "so.swap", "so.step.1", "fq0.finish.0", "lq00.start", "fq0.finish.1", "lq01.start", "lu11.land.2",
    "fe0.send.3", "inputs", "sums_start", "ld00.land.3", "lq00.land.1", "so.step.2", "fe0.send.2", "si.start",
    "sums_land", "ls.start", "fe0.middle.1", "lu11.land.3", "lu00.land.3", "fe0.send.0", "fe0.middle.0",
    "lq01.land.1", "fe0.finish.1", "fe0.finish.0", "le00.start", "si.swap", "ls.land.1", "lu10.land.3", "si.step.1",
    "lq00.land.2", "le00.land.1", "si.step.2", "ls.land.2", "ls.land.3", "le00.land.2", "so.step.3", "ld10.land.3",
    "si.step.3", "lq00.land.3", "le00.land.3", "lq01.land.2", "le00.arrived", "exchange", "output_done",
    "input_done", "lq01.land.3",
)


def rotary_table(length, lanes):
    half = ROT // 2
    freqs = (10000.0 ** (-2.0 * np.arange(half, dtype=np.float32) / ROT)).astype(np.float32)
    angles = np.arange(length, dtype=np.float32)[:, None] * freqs[None]
    cosine, sine = np.cos(angles), np.sin(angles)
    table = np.zeros((3, length, lanes), np.float32)
    table[0] = 1.0
    table[0, :, :half], table[0, :, half:ROT] = cosine, cosine
    table[1, :, half:ROT] = sine
    table[2, :, :half] = -sine
    return table


def whole_block(hidden, grad, fc1, fc2, qkv, dense, segs, vectors):
    chips, shards = lax.axis_size("ctx") // CORES, lax.axis_size("fsdp")
    count = chips * CORES
    tokens, width = hidden.shape
    length = tokens * count
    units = fc1.shape[1] // count
    head_dim = width // HEADS
    part = units // shards
    rows = width // shards
    bf16, f32 = jnp.bfloat16, jnp.float32
    wide, joint = (length, width), 3 * head_dim
    vectors = [vector.reshape(1, -1) for vector in vectors]
    vec_shape = (shards, sum(vector.shape[1] for vector in vectors) // rows, 1, rows)
    seg_shape = (count,) + segs.shape
    line = (tokens, width)
    hops = (2 * (chips - 1) * tokens, width)
    outs = [
        (vec_shape, f32), (line, f32), (line, f32), ((count * part, width), bf16), ((count * rows, units), bf16),
        ((count * rows, joint), bf16), ((width, rows), bf16), ((count * 8, width), f32),
        ((units, width), bf16), ((width, units), bf16), ((width, joint), bf16), ((shards * head_dim, rows), bf16),
        ((3 * part, width), bf16), ((3 * rows, units), bf16), ((3 * rows, joint), bf16), ((3 * head_dim, rows), bf16),
        (wide, bf16), ((chips * tokens, width), bf16), (hops, bf16),
        (wide, bf16), ((chips * tokens, width), bf16), (hops, bf16), ((count * head_dim, rows), bf16),
    ]
    table = rotary_table(length, 128)
    cuts = DOWN_CUTS + UP_CUTS + QKV_CUTS + DENSE_CUTS
    halves = [(part // 2, width), (rows // 2, units), (rows // 2, joint), (head_dim // 2, rows)]
    scratch = [
        (wide, bf16), (wide, bf16), (wide, bf16), ((width, units), bf16), ((units, width), bf16),
        ((width, joint), bf16), ((head_dim, width), bf16), (vec_shape, f32), (seg_shape, segs.dtype),
        ((length, segs.shape[1]), f32), (table.shape, f32),
        ((length, units), bf16), ((length, max(units, length)), f32), ((length, units), bf16),
        ((length, head_dim), bf16), ((length, head_dim), bf16), ((length, head_dim), bf16),
        ((length, head_dim), f32), ((length, head_dim), bf16), ((length, head_dim), f32), ((length, head_dim), f32),
        ((length, joint), bf16), ((8, width), f32), ((shards, 8, width), f32), ((8, width), f32),
        ((2, TILE, width), bf16),
    ]
    scratch += [((3,) + half, bf16) for half in halves[:2]]
    scratch += [((2,) + half, bf16) for half in halves]
    scratch += [((2 * half[0], half[1]), bf16) for half in halves]
    scratch += [((2, tokens, width), bf16), ((2, tokens, width), bf16), (line, f32)]
    slots = (
        (3 + sum(1 + split for _, split in cuts)) * Line.slots(chips)
        + 3 * Square.SLOTS + Tree.SLOTS + len(cuts) * Fold.SLOTS + 2 * Sink.slots(chips) + 9 + count - 1
    )
    outputs = pl.pallas_call(
        functools.partial(block_kernel, (chips, shards, part)),
        out_shape=[jax.ShapeDtypeStruct(shape, kind) for shape, kind in outs],
        in_specs=[pl.BlockSpec(memory_space=pl.ANY)] * 16,
        out_specs=[pl.BlockSpec(memory_space=pl.ANY)] * len(outs),
        scratch_shapes=[pltpu.VMEM(shape, kind) for shape, kind in scratch]
        + [
            pltpu.SemaphoreType.DMA((slots,)),
            pltpu.SemaphoreType.DMA((slots,)),
            pltpu.SemaphoreType.DMA((24,)),
        ],
        compiler_params=pltpu.CompilerParams(
            collective_id=0, has_side_effects=True, vmem_limit_bytes=62 * 2**20
        ),
        name="whole_block",
    )(hidden, grad, fc1, fc2, qkv, dense, segs, jnp.asarray(table), *vectors)
    return outputs[:8]


FINISH_STEPS = 16


def finish_kernel(
    sizes,
    up_all, qkv_all, dense_all, down_all, vec, branch, back, hidden, grad, sums,
    output, input_grad, gain_one, shift_one, qkv, qkv_bias, dense, columns_one, gain_two, shift_two, up, up_bias,
    down, columns_two,
):
    count, shards = sizes
    f32 = jnp.float32

    def spread(src, dst, pieces):
        groups, size = src.shape[0], src.shape[2] // pieces
        for piece in range(pieces):
            for group in range(groups):
                start = (piece * groups + group) * size
                dst[:, start : start + size] = src[group, :, piece * size : (piece + 1) * size].astype(f32)

    spread(up_all, up, shards)
    spread(qkv_all, qkv, 3)
    spread(dense_all, dense, 1)
    down[...] = down_all[...].astype(f32)

    @pl.when(pl.program_id(0) == 0)
    def _():
        own = hidden[...].astype(f32)
        shift = jnp.concatenate([vec[index, 4] + vec[index, 5] for index in range(shards)], axis=1)
        output[...] = (own + branch[...] + shift).astype(output.dtype)
        scaled, spread_own = centred(own)
        e = back[...]
        part = spread_own * (
            e
            - jnp.mean(e, axis=-1, keepdims=True)
            - scaled * jnp.mean(e * scaled, axis=-1, keepdims=True)
        )
        input_grad[...] = (grad[...].astype(f32) + part).astype(input_grad.dtype)

        shard = lax.axis_index("fsdp")
        rows = gain_one.shape[1]
        mine = pl.ds(pl.multiple_of(shard * rows, rows), rows)
        for row, dst in ((0, gain_two), (1, shift_two), (4, gain_one), (5, shift_one)):
            total = sums[0, row : row + 1, mine]
            for index in range(1, count):
                total = total + sums[index, row : row + 1, mine]
            dst[...] = total
        columns_one[...] = sums[0, 2:3, mine]
        columns_two[...] = sums[0, 2:3, mine]
        part = up_bias.shape[1] // count
        here = pl.ds(pl.multiple_of(shard * part, part), part)
        for index in range(count):
            up_bias[:, index * part : (index + 1) * part] = sums[index, 3:4, here]
        size = 3 * hidden.shape[1] // (3 * count)
        chunks = qkv_bias.shape[1] // size
        for chunk in range(chunks):
            place = shard * chunks + chunk
            start = pl.multiple_of(place // count * size, size)
            qkv_bias[:, chunk * size : (chunk + 1) * size] = sums[
                lax.rem(place, count), 6:7, pl.ds(start, size)
            ]


def finish(up_all, qkv_all, dense_all, down_all, vec, branch, back, hidden, grad, sums):
    count, shards = lax.axis_size("ctx"), lax.axis_size("fsdp")
    tokens, width = hidden.shape
    rows = width // shards
    f32 = jnp.float32
    steps = FINISH_STEPS

    def sliced(shape):
        block = shape[:-2] + (shape[-2] // steps, shape[-1])
        return pl.BlockSpec(block, lambda index: (0,) * (len(shape) - 2) + (index, 0))

    def entire(shape):
        return pl.BlockSpec(shape, lambda index: (0,) * len(shape))

    grads = [
        up_all.reshape(count, rows, -1), qkv_all.reshape(count, rows, -1), dense_all.reshape(shards, rows, rows),
        down_all,
    ]
    units = up_all.shape[1] * count
    sums = sums.reshape(count, 8, width)
    others = [vec, branch, back, hidden, grad, sums]
    vector = (1, rows)
    outs = [
        ((tokens, width), hidden.dtype, entire), ((tokens, width), hidden.dtype, entire),
        (vector, f32, entire), (vector, f32, entire), ((rows, 3 * width), f32, sliced),
        ((1, 3 * rows), f32, entire), ((rows, width), f32, sliced), (vector, f32, entire),
        (vector, f32, entire), (vector, f32, entire), ((rows, units), f32, sliced),
        ((1, units // shards), f32, entire), (down_all.shape, f32, sliced), (vector, f32, entire),
    ]
    return pl.pallas_call(
        functools.partial(finish_kernel, (count, shards)),
        grid=(steps,),
        in_specs=[sliced(array.shape) for array in grads] + [entire(array.shape) for array in others],
        out_specs=[kind(shape) for shape, _, kind in outs],
        out_shape=[jax.ShapeDtypeStruct(shape, dtype) for shape, dtype, _ in outs],
        compiler_params=pltpu.CompilerParams(vmem_limit_bytes=62 * 2**20),
        name="finish",
    )(*grads, *others)


def one_kernel(
    hidden, qkv_weight, dense_weight, fc1_weight, fc2_weight, segments, out_grad, vectors
):
    vec, branch, back, down_all, up_all, qkv_all, dense_all, sums_all = whole_block(
        hidden[0], out_grad[0], fc1_weight, fc2_weight, qkv_weight, dense_weight, segments, vectors
    )
    outs = finish(
        up_all, qkv_all, dense_all, down_all, vec, branch, back, hidden[0], out_grad[0], sums_all
    )
    outs = [out.reshape(-1) if out.shape[0] == 1 else out for out in outs]
    return (outs[0][None], outs[1][None], *outs[2:])


def per_device(
    hidden,
    ln1_gain,
    ln1_bias,
    qkv_weight,
    qkv_bias,
    dense_weight,
    dense_bias,
    ln2_gain,
    ln2_bias,
    fc1_weight,
    fc1_bias,
    fc2_weight,
    fc2_bias,
    segments,
    out_grad,
):
    ctx_count = lax.axis_size("ctx")
    shards = lax.axis_size("fsdp")
    ctx = lax.axis_index("ctx")
    tokens, width = hidden.shape[1], hidden.shape[2]
    length = tokens * ctx_count
    head_dim = width // HEADS
    repeat = ctx_count // HEADS
    head = ctx // repeat
    factor = head_dim ** (-0.5)
    rows = width // shards
    ff = fc1_weight.shape[1]
    units = ff // shards // ctx_count
    bf16, f32 = jnp.bfloat16, jnp.float32

    vectors = [ln1_gain, ln1_bias, ln2_gain, ln2_bias, dense_bias, fc2_bias, qkv_bias, fc1_bias]
    if ctx_count == HEADS and shards == 4:
        return one_kernel(
            hidden, qkv_weight, dense_weight, fc1_weight, fc2_weight, segments, out_grad, vectors
        )
    vectors = jnp.concatenate(vectors).reshape(-1, rows)
    vec = lax.all_gather(vectors, "fsdp", axis=0)
    query_seg = lax.all_gather(segments[0], "ctx", axis=0, tiled=True)
    up_part = lax.dynamic_index_in_dim(
        fc1_weight.reshape(rows, shards, ctx_count, units), ctx, 2, keepdims=False
    ).reshape(rows, shards * units)
    down_part = lax.dynamic_slice_in_dim(fc2_weight, ctx * units, units, 0)
    qkv_part = lax.dynamic_index_in_dim(
        qkv_weight.reshape(rows, 3, HEADS, head_dim), head, 2, keepdims=False
    ).reshape(rows, 3 * head_dim)
    dense_cols = lax.all_to_all(
        dense_weight, "fsdp", split_axis=1, concat_axis=0, tiled=True
    )
    dense_part = lax.dynamic_slice_in_dim(dense_cols, head * head_dim, head_dim, 0)
    up_w = gather_fsdp(up_part)
    down_w = gather_fsdp(down_part)
    qkv_w = gather_fsdp(qkv_part)
    dense_w = gather_fsdp(dense_part, axis=1)
    hidden_all = line_gather(hidden[0]).reshape(length, width)
    grad_all = line_gather(out_grad[0]).reshape(length, width)
    normed_one = (centred(hidden_all)[0] * vec[:, 0].reshape(-1) + vec[:, 1].reshape(-1)).astype(bf16)
    scaled = centred(hidden_all)[0]
    gain_two = vec[:, 2].reshape(-1)
    normed_two = (scaled * gain_two + vec[:, 3].reshape(-1)).astype(bf16)
    up_shift = lax.dynamic_index_in_dim(
        vec[:, 9 : 9 + ff // width].reshape(shards, ctx_count, units), ctx, 1, keepdims=False
    ).reshape(-1)
    act_f, slope = gelu_and_slope(dot(normed_two, up_w) + up_shift)
    act = act_f.astype(bf16)
    d_up = (dot_cols(grad_all, down_w) * slope).astype(bf16)
    down_part_grad = dot_rows(act, grad_all).astype(bf16)
    up_part_grad = dot_rows(normed_two, d_up).astype(bf16)
    ff_part = dot(act, down_w).astype(bf16)
    d_two = dot_cols(d_up, up_w)
    e_two = (d_two * gain_two).astype(bf16)
    gain_two_sum, shift_two_sum = jnp.sum(d_two * scaled, axis=0), jnp.sum(d_two, axis=0)
    columns = jnp.sum(grad_all.astype(f32), axis=0)
    up_sum = jnp.sum(d_up.astype(f32), axis=0)
    gain_one = vec[:, 0].reshape(-1)
    dense_shift, down_shift = vec[:, 4].reshape(-1), vec[:, 5].reshape(-1)
    qkv_shift = vec[:, 6:9].reshape(-1)
    down_grad = scatter_fsdp(down_part_grad)
    up_grad = scatter_fsdp(up_part_grad)

    qkv_shift_part = lax.dynamic_index_in_dim(
        qkv_shift.reshape(3, HEADS, head_dim), head, 1, keepdims=False
    ).reshape(-1)
    joined = dot(normed_one, qkv_w) + qkv_shift_part
    places = jnp.arange(length, dtype=jnp.int32)
    cosine, sine = rotary_tables(places, ROT)
    queries = rotate(joined[:, :head_dim], cosine, sine).astype(bf16)
    keys = rotate(joined[:, head_dim : 2 * head_dim], cosine, sine).astype(bf16)
    values = joined[:, 2 * head_dim :].astype(bf16)
    allowed = (places[None, :] <= places[:, None]) & (query_seg[None, :] == query_seg[:, None])
    if repeat > 1:
        allowed = allowed & (places // (length // repeat) == ctx % repeat)[:, None]
    scores = jnp.where(allowed, dot_cols(queries, keys) * factor, -1e30)
    top = jnp.max(scores, axis=-1, keepdims=True)
    terms = jnp.where(allowed, jnp.exp(scores - top), 0.0)
    total = jnp.sum(terms, axis=-1, keepdims=True)
    probs = terms * jnp.where(total > 0.0, 1.0 / total, 0.0)
    probs_low = probs.astype(bf16)
    att_f = dot(probs_low, values)
    att = att_f.astype(bf16)
    partial = dot(att, dense_w) + ff_part.astype(f32)
    branch = lax.psum_scatter(partial.astype(bf16), "ctx", scatter_dimension=0, tiled=True)
    own = hidden[0].astype(f32)
    layer_output = (own + branch.astype(f32) + dense_shift + down_shift).astype(bf16)

    d_att = dot_cols(grad_all, dense_w).astype(bf16)
    delta = jnp.sum(d_att.astype(f32) * att_f, axis=-1, keepdims=True)
    dense_grad = dot_rows(att, grad_all).astype(bf16)
    d_scores = (probs * (dot_cols(d_att, values) - delta)).astype(bf16)
    d_queries = rotate(dot(d_scores, keys) * factor, cosine, -sine)
    d_keys = rotate(dot_rows(d_scores, queries) * factor, cosine, -sine)
    d_values = dot_rows(probs_low, d_att)
    d_joined = jnp.concatenate([d_queries, d_keys, d_values], axis=1).astype(bf16)
    qkv_grad = dot_rows(normed_one, d_joined).astype(bf16)

    d_one = dot_cols(d_joined, qkv_w)
    both = (d_one * gain_one + e_two.astype(f32)).astype(bf16)
    back = lax.psum_scatter(both, "ctx", scatter_dimension=0, tiled=True).astype(f32)
    own_scaled, own_spread = centred(own)
    input_part = own_spread * (
        back
        - jnp.mean(back, axis=-1, keepdims=True)
        - own_scaled * jnp.mean(back * own_scaled, axis=-1, keepdims=True)
    )
    input_grad = (out_grad[0].astype(f32) + input_part).astype(bf16)

    first = (ctx == 0).astype(f32)
    joined_sum = jnp.sum(d_joined.astype(f32), axis=0).reshape(3, 1, head_dim)
    joined_full = jnp.where((jnp.arange(HEADS) == head)[None, :, None], joined_sum, 0.0)
    up_sum = up_sum.reshape(shards, 1, units)
    up_full = jnp.where((jnp.arange(ctx_count) == ctx)[None, :, None], up_sum, 0.0)
    small = [
        jnp.sum(d_one * centred(hidden_all)[0], axis=0),
        jnp.sum(d_one, axis=0),
        columns * first,
        gain_two_sum,
        shift_two_sum,
        joined_full,
        up_full,
    ]
    small = jnp.concatenate([piece.reshape(shards, -1) for piece in small], axis=1).astype(bf16)
    small_size = small.shape[1]
    small_rows = -(-small_size // (3 * head_dim * 16)) * 16
    small = jnp.pad(small, ((0, 0), (0, small_rows * 3 * head_dim - small_size)))
    last_grad = scatter_fsdp(
        jnp.concatenate(
            [
                qkv_grad.reshape(shards, rows, 3 * head_dim),
                small.reshape(shards, small_rows, 3 * head_dim),
            ],
            axis=1,
        ).reshape(-1, 3 * head_dim)
    )
    dense_share = scatter_fsdp(
        dense_grad.reshape(head_dim, shards, rows).transpose(1, 0, 2).reshape(-1, rows)
    )

    down_all = line_gather(down_grad).astype(f32).reshape(ctx_count * units, width)
    up_all = (
        line_gather(up_grad)
        .astype(f32)
        .reshape(ctx_count, rows, shards, units)
        .transpose(1, 2, 0, 3)
        .reshape(rows, ff)
    )
    dense_cols_all = line_gather(dense_share)
    if repeat > 1:
        dense_cols_all = jnp.sum(
            dense_cols_all.astype(f32).reshape(HEADS, repeat, head_dim, rows), axis=1
        ).astype(bf16)
    dense_all = lax.all_to_all(
        dense_cols_all.reshape(width, rows), "fsdp", split_axis=0, concat_axis=1, tiled=True
    ).astype(f32)
    last_all = line_gather(last_grad)
    qkv_all = last_all[:, :rows].astype(f32)
    if repeat > 1:
        qkv_all = jnp.sum(qkv_all.reshape(HEADS, repeat, rows, 3 * head_dim), axis=1)
    qkv_all = (
        qkv_all.reshape(HEADS, rows, 3, head_dim).transpose(1, 2, 0, 3).reshape(rows, 3 * width)
    )
    small_all = jnp.sum(last_all[:, rows:].astype(f32), axis=0).reshape(-1)
    sizes = [rows] * 5 + [3 * rows, ff // shards]
    parts, at = [], 0
    for size in sizes:
        parts.append(small_all[at : at + size])
        at += size
    gain_one_grad, shift_one_grad, columns_grad, gain_two_grad, shift_two_grad, joined_grad, up_b_grad = parts
    return (
        layer_output[None],
        input_grad[None],
        gain_one_grad,
        shift_one_grad,
        qkv_all,
        joined_grad,
        dense_all,
        columns_grad,
        gain_two_grad,
        shift_two_grad,
        up_all,
        up_b_grad,
        down_all,
        columns_grad,
    )


def solution(mesh):
    vec, mat, act = P("fsdp"), P("fsdp", None), P("fsdp", "ctx", None)
    return jax.shard_map(
        per_device,
        mesh=mesh,
        in_specs=(
            act, vec, vec, mat, vec, mat, vec, vec, vec, mat, vec, mat, vec, P("fsdp", "ctx"), act
        ),
        out_specs=(act, act, vec, vec, mat, vec, mat, vec, vec, vec, mat, vec, mat, vec),
        check_vma=False,
    )
```

```python
import functools
import math

import jax
import jax.numpy as jnp
import numpy as np
from jax import lax
from jax.experimental import pallas as pl
from jax.experimental.pallas import tpu as pltpu
from jax.sharding import PartitionSpec as P

HEADS = 8
ROT = 64
CORES = 2


def dot(left, right):
    return jnp.dot(left, right, preferred_element_type=jnp.float32)


def dot_rows(left, right):
    return lax.dot_general(
        left, right, (((0,), (0,)), ((), ())), preferred_element_type=jnp.float32
    )


def dot_cols(left, right):
    return lax.dot_general(
        left, right, (((1,), (1,)), ((), ())), preferred_element_type=jnp.float32
    )


def gelu_and_slope(values):
    cdf = 0.5 * (1.0 + lax.erf(values * (0.5**0.5)))
    density = jnp.exp(-0.5 * values * values) * ((2.0 * jnp.pi) ** -0.5)
    return values * cdf, cdf + values * density


def centred(values):
    values = values.astype(jnp.float32)
    center = values - jnp.mean(values, axis=-1, keepdims=True)
    spread = lax.rsqrt(jnp.mean(center * center, axis=-1, keepdims=True) + 1e-05)
    return center * spread, spread


def rotary_tables(places, width):
    half_rot = width // 2
    freqs = 10000.0 ** (-2.0 * jnp.arange(half_rot, dtype=jnp.float32) / width)
    angles = places.astype(jnp.float32)[:, None] * freqs[None, :]
    return (jnp.cos(angles), jnp.sin(angles))


def rotate(values, cosine, sine):
    half = cosine.shape[-1]
    first, second, remain = values[:, :half], values[:, half : 2 * half], values[:, 2 * half :]
    return jnp.concatenate(
        [first * cosine - second * sine, second * cosine + first * sine, remain], axis=1
    )


def line_gather(block):
    count = lax.axis_size("ctx")
    chips = count // CORES
    ctx = lax.axis_index("ctx")
    place, core = ctx // CORES, ctx % CORES
    up = down = block
    ups, downs = [], []
    for hop in range(1, chips):
        up = lax.ppermute(
            up,
            "ctx",
            [
                (i * CORES + k, (i + 1) * CORES + k)
                for i in range(hop - 1, chips - 1)
                for k in range(CORES)
            ],
        )
        down = lax.ppermute(
            down,
            "ctx",
            [
                (i * CORES + k, (i - 1) * CORES + k)
                for i in range(1, chips - hop + 1)
                for k in range(CORES)
            ],
        )
        ups.append(up)
        downs.append(down)
    around = jnp.stack(ups[::-1] + [block] + downs)
    mine = lax.dynamic_slice_in_dim(around, chips - 1 - place, chips, 0)
    other = lax.ppermute(mine, "ctx", [(i, i ^ 1) for i in range(count)])
    is_mine = (jnp.arange(CORES) == core).reshape((1, CORES) + (1,) * block.ndim)
    return jnp.where(is_mine, mine[:, None], other[:, None]).reshape((count,) + block.shape)


def gather_fsdp(values, axis=0):
    return lax.all_gather(values, "fsdp", axis=axis, tiled=True)


def scatter_fsdp(values):
    return lax.psum_scatter(values, "fsdp", scatter_dimension=0, tiled=True)


def remote(src, dst, sems, slot, device):
    return pltpu.make_async_remote_copy(
        src_ref=src,
        dst_ref=dst,
        send_sem=sems[0].at[slot],
        recv_sem=sems[1].at[slot],
        device_id=device,
        device_id_type=pl.DeviceIdType.MESH,
    )


class Line:
    def __init__(self, source, blocks, sems, base, place, chips, stride=None, offset=0, columns=slice(None)):
        self.source, self.sems, self.base, self.chips = source, sems, base, chips
        self.ctx, self.shard = place
        self.chip = self.ctx // CORES
        rows = source.shape[0]
        stride = stride or rows
        self.block = lambda index: blocks.at[
            pl.ds(pl.multiple_of(index * stride + offset, rows), rows), columns
        ]
        self.swap_base = base + 2 * (chips - 1)
        self.own_slot = base + 4 * (chips - 1)

    @staticmethod
    def slots(chips):
        return 4 * (chips - 1) + 2

    def hop(self, out, number):
        up = (self.chip >= self.chips // 2) == out
        place = jnp.where(up, self.chip, self.chips - 1 - self.chip)
        step = jnp.where(up, CORES, -CORES)
        slot = jnp.where(up, 0, self.chips - 1) + number - 1
        sends = (place >= number - 1) & (place < self.chips - 1)
        return slot, step, self.ctx - step * (number - 1), sends, place >= number

    def send(self, out, number):
        slot, step, origin, sends, _ = self.hop(out, number)

        @pl.when(sends)
        def _():
            remote(
                self.source if number == 1 else self.block(origin),
                self.block(origin),
                self.sems,
                self.base + slot,
                (self.ctx + step, self.shard),
            ).start()

    def start(self):
        self.send(True, 1)
        self.send(False, 1)
        remote(
            self.source, self.block(self.ctx), self.sems, self.own_slot, (self.ctx ^ 1, self.shard)
        ).start()
        self.local = pltpu.make_async_copy(
            self.source, self.block(self.ctx), self.sems[0].at[self.own_slot + 1]
        )
        self.local.start()

    def land(self, out, number):
        slot, step, origin, _, gets = self.hop(out, number)
        block = self.block(origin - step)

        @pl.when(gets)
        def _():
            remote(
                block, block, self.sems, self.base + slot, (self.ctx ^ 1, self.shard)
            ).wait_recv()

        if number < self.chips - 1:
            self.send(out, number + 1)

        @pl.when(gets)
        def _():
            remote(
                block, block, self.sems, self.swap_base + slot, (self.ctx ^ 1, self.shard)
            ).start()

    def out(self, number):
        self.land(True, number)

    def inward(self, number):
        self.land(False, number)

    def arrived(self):
        other = self.block(self.ctx ^ 1)
        remote(other, other, self.sems, self.own_slot, (self.ctx ^ 1, self.shard)).wait_recv()
        self.local.wait()
        for out in (True, False):
            for number in range(1, self.chips):
                slot, step, origin, _, gets = self.hop(out, number)
                block = self.block((origin - step) ^ 1)

                @pl.when(gets)
                def _(block=block, slot=slot):
                    remote(
                        block, block, self.sems, self.swap_base + slot, (self.ctx ^ 1, self.shard)
                    ).wait_recv()

    def sent(self):
        source = self.source
        peer = (self.ctx ^ 1, self.shard)
        remote(source, source, self.sems, self.own_slot, peer).wait_send()
        for out in (True, False):
            for number in range(1, self.chips):
                slot, _, _, sends, gets = self.hop(out, number)

                @pl.when(sends)
                def _(slot=slot):
                    remote(source, source, self.sems, self.base + slot, peer).wait_send()

                @pl.when(gets)
                def _(slot=slot):
                    remote(source, source, self.sems, self.swap_base + slot, peer).wait_send()


class Square:
    SLOTS = 8

    def __init__(self, pieces, blocks, sems, base, place):
        self.pieces, self.sems, self.base = pieces, sems, base
        self.ctx, self.shard = place
        half = blocks.shape[0] // 8

        def part(owner, which, columns=slice(None)):
            start = pl.multiple_of((2 * owner + which) * half, half)
            return blocks.at[pl.ds(start, half), columns]

        self.part = part

    def to(self, bit):
        return (self.ctx, self.shard ^ bit)

    def own(self, bit, which):
        for source, columns in self.pieces(which):
            remote(
                source,
                self.part(self.shard, which, columns),
                self.sems,
                self.base + 2 * (bit - 1) + which,
                self.to(bit),
            ).start()

    def start(self, part):
        self.own(1, part)
        self.own(2, 1 - part)
        if part == 1:
            return
        for which in (0, 1):
            for source, columns in self.pieces(which):
                pltpu.make_async_copy(
                    source,
                    self.part(self.shard, which, columns),
                    self.sems[0].at[self.base + 6 + which],
                ).start()

    def wait(self, owner, which, slot, bit):
        part = self.part(owner, which)
        remote(part, part, self.sems, self.base + slot, self.to(bit)).wait_recv()

    def forward(self):
        for bit in (1, 2):
            which = bit - 1
            owner = self.shard ^ bit
            self.wait(owner, which, 2 * (bit - 1) + which, bit)
            part = self.part(owner, which)
            remote(part, part, self.sems, self.base + 4 + which, self.to(3 - bit)).start()

    def arrived(self):
        self.wait(self.shard ^ 1, 1, 1, 1)
        self.wait(self.shard ^ 2, 0, 2, 2)
        self.wait(self.shard ^ 3, 0, 4, 2)
        self.wait(self.shard ^ 3, 1, 5, 1)
        for which in (0, 1):
            part = self.part(self.shard, which)
            pltpu.make_async_copy(part, part, self.sems[0].at[self.base + 6 + which]).wait()

    def sent(self):
        for slot in range(6):
            part = self.part(self.shard, 0)
            remote(part, part, self.sems, self.base + slot, self.to(1)).wait_send()


class Tree:
    SLOTS = 7

    def __init__(self, source, block, sems, base, place, owner):
        self.source, self.block, self.sems, self.base = source, block, sems, base
        self.ctx, self.shard = place
        self.turn = self.shard ^ owner
        self.half = block.shape[0] // 2

    def rows(self, ref, which):
        return ref.at[pl.ds(which * self.half, self.half)]

    def copy(self, slot, ref=None):
        which = slot % 2
        bit = 1 if slot in (0, 3, 4) else 2
        return remote(
            self.rows(self.block if ref is None else ref, which),
            self.rows(self.block, which),
            self.sems,
            self.base + slot,
            (self.ctx, self.shard ^ bit),
        )

    def at(self, turn, body):
        pl.when(self.turn == turn)(body)

    def start(self):
        def body():
            self.copy(0, self.source).start()
            self.copy(1, self.source).start()
            pltpu.make_async_copy(self.source, self.block, self.sems[0].at[self.base + 6]).start()

        self.at(0, body)

    def forward(self):
        for turn, slot in ((1, 0), (2, 1)):

            def body(slot=slot):
                self.copy(slot).wait_recv()
                self.copy(slot + 2).start()

            self.at(turn, body)

    def back(self):
        def body():
            for slot in (2, 3):
                self.copy(slot).wait_recv()
                self.copy(slot + 2).start()

        self.at(3, body)

    def arrived(self):
        def body():
            pltpu.make_async_copy(self.source, self.block, self.sems[0].at[self.base + 6]).wait()

        self.at(0, body)
        self.at(1, lambda: self.copy(5).wait_recv())
        self.at(2, lambda: self.copy(4).wait_recv())

    def sent(self):
        for turn, slots in ((0, (0, 1)), (1, (2,)), (2, (3,)), (3, (4, 5))):

            def body(slots=slots):
                for slot in slots:
                    self.copy(slot).wait_send()

            self.at(turn, body)


def add_rows(dst, sources):
    step = 32

    def body(index, carry):
        rows = pl.ds(pl.multiple_of(index * step, step), step)
        total = sources[0][rows].astype(jnp.float32)
        for source in sources[1:]:
            total += source[rows].astype(jnp.float32)
        dst[rows] = total.astype(dst.dtype)
        return carry

    lax.fori_loop(0, dst.shape[0] // step, body, 0)


class Fold:
    SLOTS = 6

    def __init__(self, parts, landing, stage, carry, final, sems, local, base, place):
        self.parts, self.landing, self.stage, self.carry, self.final = parts, landing, stage, carry, final
        self.sems, self.local, self.base = sems, local, base
        self.ctx, self.shard = place
        self.half = final.shape[0] // 2

    def part(self, owner, which):
        start = pl.multiple_of((2 * owner + which) * self.half, self.half)
        return self.parts.at[pl.ds(start, self.half)]

    def landed(self, slot):
        return self.landing.at[pl.ds(slot * self.half, self.half)]

    def copy(self, src, slot, bit):
        return remote(
            src, self.landed(slot), self.sems, self.base + slot, (self.ctx, self.shard ^ bit)
        )

    def send(self, slot):
        bit, which = (1, 0) if slot < 2 else (2, 1)
        owner = self.shard ^ (3 if slot % 2 else bit)
        self.copy(self.part(owner, which), slot, bit).start()

    def add(self, dst, sources):
        copies = []
        for index, source in enumerate(sources):
            copies.append(
                pltpu.make_async_copy(source, self.stage.at[index], self.local.at[index])
            )
            copies[-1].start()
        for copy in copies:
            copy.wait()
        add_rows(dst, [self.stage.at[index] for index in range(len(sources))])

    def wait(self, slot, bit):
        self.copy(self.landed(slot), slot, bit).wait_recv()

    def middle(self, which):
        first, second = (1, 2) if which == 0 else (2, 1)
        slot = 1 + 2 * which
        self.wait(slot, first)
        carry = self.carry.at[which]
        self.add(carry, [self.part(self.shard ^ second, which), self.landed(slot)])
        self.copy(carry, 4 + which, second).start()

    def finish(self, which):
        first, second = (1, 2) if which == 0 else (2, 1)
        self.wait(2 * which, first)
        self.wait(4 + which, second)
        self.add(
            self.final.at[pl.ds(which * self.half, self.half)],
            [self.part(self.shard, which), self.landed(2 * which), self.landed(4 + which)],
        )

    def sent(self):
        for slot in range(6):
            self.copy(self.part(self.shard, 0), slot, 1).wait_send()


class Sink:
    def __init__(self, parts, swapped, landing, stage, carry, final, sems, local, base, place, chips):
        self.parts, self.swapped, self.landing, self.stage = parts, swapped, landing, stage
        self.carry, self.final, self.sems, self.local, self.base = carry, final, sems, local, base
        self.ctx, self.shard = place
        self.chip, self.core, self.chips = self.ctx // CORES, self.ctx % CORES, chips
        self.rows = final.shape[0]

    @staticmethod
    def slots(chips):
        return 2 * (chips - 1) + 1

    def block(self, ref, index):
        return ref.at[pl.ds(pl.multiple_of(index * self.rows, self.rows), self.rows)]

    def start(self):
        for chip in range(self.chips):
            remote(
                self.block(self.parts, CORES * chip + (self.core ^ 1)),
                self.block(self.swapped, chip),
                self.sems,
                self.base,
                (self.ctx ^ 1, self.shard),
            ).start()

    def swap(self):
        swapped = self.swapped
        remote(swapped, swapped, self.sems, self.base, (self.ctx ^ 1, self.shard)).wait_recv()

    def hop(self, out, step):
        up = (self.chip >= self.chips // 2) == out
        place = jnp.where(up, self.chip, self.chips - 1 - self.chip)
        target = place + self.chips - step
        target = jnp.where(up, target, self.chips - 1 - target)
        slot = jnp.where(up, 0, self.chips - 1) + step - 1
        sends = (place + 1 <= step) & (place < self.chips - 1)
        gets = (place <= step) & (place > 0)
        return slot, target, sends, gets, place > 0

    def landed(self, slot):
        return self.landing.at[pl.ds(pl.multiple_of(slot * self.rows, self.rows), self.rows)]

    def copy(self, out, slot):
        up = (self.chip >= self.chips // 2) == out
        return remote(
            self.carry.at[0 if out else 1],
            self.landed(slot),
            self.sems,
            self.base + 1 + slot,
            (self.ctx + jnp.where(up, CORES, -CORES), self.shard),
        )

    def load(self, index, source):
        return pltpu.make_async_copy(source, self.stage.at[index], self.local.at[index])

    def own(self, target):
        return [
            self.load(0, self.block(self.parts, CORES * target + self.core)),
            self.load(1, self.block(self.swapped, target)),
        ]

    def step(self, out, number):
        slot, target, sends, _, passes = self.hop(out, number)
        if number > 1:
            before, _, sent, gets, _ = self.hop(out, number - 1)

            @pl.when(gets)
            def _():
                remote(
                    self.landed(before), self.landed(before), self.sems, self.base + 1 + before,
                    (self.ctx ^ 1, self.shard),
                ).wait_recv()

            @pl.when(sent)
            def _():
                self.copy(out, before).wait_send()

        @pl.when(sends)
        def _():
            loads = self.own(target)
            for load in loads:
                load.start()
            carry = self.carry.at[0 if out else 1]
            stage = self.stage
            if number > 1:

                @pl.when(passes)
                def _():
                    more = self.load(2, self.landed(slot - 1))
                    more.start()
                    for load in loads + [more]:
                        load.wait()
                    add_rows(carry, [stage.at[0], stage.at[1], stage.at[2]])

                @pl.when(jnp.logical_not(passes))
                def _():
                    for load in loads:
                        load.wait()
                    add_rows(carry, [stage.at[0], stage.at[1]])
            else:
                for load in loads:
                    load.wait()
                add_rows(carry, [stage.at[0], stage.at[1]])
            self.copy(out, slot).start()

    def inward(self, number):
        self.step(False, number)

    def last(self, handed, first, own, sem):
        number = self.chips - 1
        for out in (True, False):
            slot, target, sends, _, passes = self.hop(out, number)
            before, _, sent, gets, _ = self.hop(out, number - 1)

            @pl.when(gets)
            def _(before=before):
                remote(
                    self.landed(before), self.landed(before), self.sems, self.base + 1 + before,
                    (self.ctx ^ 1, self.shard),
                ).wait_recv()

            @pl.when(sent)
            def _(out=out, before=before):
                self.copy(out, before).wait_send()

            @pl.when(sends)
            def _(out=out, slot=slot, target=target, passes=passes):
                loads = self.own(target)
                for load in loads:
                    load.start()
                for load in loads:
                    load.wait()
                carry = self.carry.at[0 if out else 1]
                add_rows(carry, [self.stage.at[0], self.stage.at[1]])

                @pl.when(passes)
                def _():
                    more = self.load(2, self.landed(slot - 1))
                    more.start()
                    more.wait()
                    add_rows(carry, [self.stage.at[0], self.stage.at[1], self.stage.at[2]])

                up = (self.chip >= self.chips // 2) == out
                for way, dst in ((True, handed[0]), (False, handed[1])):

                    @pl.when(up == way)
                    def _(dst=dst):
                        write = pltpu.make_async_copy(carry, dst.at[pl.ds(first, self.rows)], sem)
                        write.start()
                        write.wait()

        loads = self.own(self.chip)
        for load in loads:
            load.start()
        for load in loads:
            load.wait()
        add_rows(self.final, [self.stage.at[0], self.stage.at[1]])
        swapped = self.swapped
        remote(swapped, swapped, self.sems, self.base, (self.ctx ^ 1, self.shard)).wait_send()
        write = pltpu.make_async_copy(self.final, own, sem)
        write.start()
        write.wait()


TILE = 256


def block_kernel(
    sizes,
    hidden, grad, fc1, fc2, qkv, dense, segs, tables,
    ln1_gain, ln1_bias, ln2_gain, ln2_bias, dense_bias, fc2_bias, qkv_bias, fc1_bias,
    vec_out, output_out, input_out, up_out, down_out, down_all, up_all, qkv_all, dense_all, sums_all,
    down_parts, up_parts, qkv_parts, dense_parts, down_land, up_land, qkv_land, dense_land,
    out_parts, out_swap, out_land, in_parts, in_swap, in_land, dense_lines,
    hid, gra, norm, w_up, w_down, w_qkv, w_dense, vec, seg, seg_col, table,
    act, wide_f, d_up, queries, keys, values, att_f, att, d_keys, d_values, d_joined, sums, sums_got, sums_tot,
    stage, down_stage, up_stage,
    down_carry, up_carry, qkv_carry, dense_carry, down_final, up_final, qkv_final, dense_final,
    out_carry, in_carry, sink_final,
    send_sems, recv_sems, local_sems,
):
    chips, shards, columns = sizes
    place = ctx, shard = lax.axis_index("ctx"), lax.axis_index("fsdp")
    chip, core = ctx // CORES, ctx % CORES
    count = CORES * chips
    sems = (send_sems, recv_sems)
    width, length = hidden.shape[1], hid.shape[0]
    ff_units = w_down.shape[0]
    head_dim = w_dense.shape[0]
    row_size = vec.shape[3]
    tiles = length // TILE
    f32, bf16 = jnp.float32, jnp.bfloat16
    factor = head_dim ** (-0.5)

    barrier = pltpu.get_barrier_semaphore()
    peers = [(ctx, shard ^ bit) for bit in (1, 2, 3)]
    peers += [(lax.rem(ctx + step, count), shard) for step in range(1, count)]
    for peer in peers:
        pl.semaphore_signal(barrier, inc=1, device_id=peer, device_id_type=pl.DeviceIdType.MESH)
    pl.semaphore_wait(barrier, len(peers))

    base = 0

    def take(slots):
        nonlocal base
        base += slots
        return base - slots

    def line(source, blocks, stride=None, offset=0, cut=slice(None)):
        return Line(source, blocks, sems, take(Line.slots(chips)), place, chips, stride, offset, cut)

    def fold(parts, landing, stage, carry, final):
        return Fold(
            parts, landing, stage, carry, final, sems, local_sems.at[pl.ds(4, 4)], take(Fold.SLOTS), place
        )

    def sink(parts, swapped, landing, carry):
        return Sink(
            parts, swapped, landing, down_stage, carry, sink_final, sems, local_sems.at[pl.ds(4, 4)],
            take(Sink.slots(chips)), place, chips,
        )

    def halves(ref, which, start, size):
        half = ref.shape[0] // 2
        return ref.at[pl.ds(which * half, half), pl.ds(pl.multiple_of(start, size), size)]

    def up_pieces(which):
        stride = fc1.shape[1] // shards
        return [
            (
                halves(fc1, which, index * stride + ctx * columns, columns),
                pl.ds(index * columns, columns),
            )
            for index in range(shards)
        ]

    def down_pieces(which):
        half = columns // 2
        start = pl.multiple_of(ctx * columns + which * half, half)
        return [(fc2.at[pl.ds(start, half)], slice(None))]

    def qkv_pieces(which):
        return [
            (
                halves(qkv, which, index * width + ctx * head_dim, head_dim),
                pl.ds(index * head_dim, head_dim),
            )
            for index in range(3)
        ]

    hid_line, gra_line = line(hidden, hid), line(grad, gra)
    squares = [
        Square(pieces, blocks, sems, take(Square.SLOTS), place)
        for pieces, blocks in ((up_pieces, w_up), (down_pieces, w_down), (qkv_pieces, w_qkv))
    ]
    up_square, down_square, qkv_square = squares
    heads_here = dense.shape[0] // head_dim
    dense_rows = dense.at[
        pl.ds(pl.multiple_of(lax.rem(ctx, heads_here) * head_dim, head_dim), head_dim)
    ]
    tree = Tree(dense_rows, w_dense, sems, take(Tree.SLOTS), place, ctx // heads_here)
    named = {"hid": hid_line, "gra": gra_line, "wu": up_square, "wd": down_square, "wq": qkv_square, "wt": tree}
    folds, lines = [], []

    def gradient(letter, cuts, parts, landing, stage, carry, final, gathered):
        start, half = 0, final.shape[0] // 2
        for index, (size, split) in enumerate(cuts):
            cut = pl.ds(start, size)
            item = fold(
                parts.at[:, cut], landing.at[:, cut], stage.at[:, :, :size], carry.at[:, :, cut], final.at[:, cut]
            )
            folds.append(item)
            named[f"f{letter}{index}"] = item
            for which in range(2 if split else 1):
                rows = half if split else 2 * half
                item = line(
                    final.at[pl.ds(which * rows, rows), cut], gathered, final.shape[0], which * rows, cut
                )
                lines.append(item)
                named[f"l{letter}{index}{which}"] = item
            start += size

    gradient("d", DOWN_CUTS, down_parts, down_land, down_stage, down_carry, down_final, down_all)
    gradient("u", UP_CUTS, up_parts, up_land, up_stage, up_carry, up_final, up_all)
    gradient("q", QKV_CUTS, qkv_parts, qkv_land, up_stage, qkv_carry, qkv_final, qkv_all)
    gradient("e", DENSE_CUTS, dense_parts, dense_land, down_stage, dense_carry, dense_final, dense_lines)
    named["ls"] = line(sums_tot, sums_all)
    lines.append(named["ls"])
    out_sink = sink(out_parts, out_swap, out_land, out_carry)
    in_sink = sink(in_parts, in_swap, in_land, in_carry)
    named["so"], named["si"] = out_sink, in_sink

    small = []

    def send_small(src, dst, landing, device):
        slot = take(1)
        small.append((remote(src, dst, sems, slot, device), landing, slot))
        small[-1][0].start()

    def wait_small(items):
        for _, landing, slot in items:
            remote(landing, landing, sems, slot, (ctx ^ 1, shard)).wait_recv()

    vectors = (
        ln1_gain, ln1_bias, ln2_gain, ln2_bias, dense_bias, fc2_bias, qkv_bias, fc1_bias
    )
    at, pairs = 0, [(segs, seg.at[ctx]), (tables, table)]
    for vector in vectors:
        size = vec.shape[3]
        for start in range(0, vector.shape[1], size):
            pairs.append((vector.at[:, pl.ds(start, size)], vec.at[shard, at]))
            at += 1
    locals_in = [
        pltpu.make_async_copy(src, dst, local_sems.at[8 + index])
        for index, (src, dst) in enumerate(pairs)
    ]
    for copy in locals_in:
        copy.start()

    def small_start():
        for copy in locals_in:
            copy.wait()
        for bit in (1, 2, 3):
            send_small(vec.at[shard], vec.at[shard], vec.at[shard ^ bit], (ctx, shard ^ bit))
        for step in range(1, count):
            send_small(
                segs, seg.at[ctx], seg.at[lax.rem(ctx + count - step, count)],
                (lax.rem(ctx + step, count), shard),
            )

    def small_land():
        wait_small(small)

    def vector(row):
        return jnp.concatenate([vec[index, row] for index in range(shards)], axis=1)

    def rows_of(index):
        return pl.ds(pl.multiple_of(index * TILE, TILE), TILE)

    def loop(body, steps=tiles):
        lax.fori_loop(0, steps, lambda index, carry: (body(rows_of(index)), carry)[1], 0)

    def scaled_rows(rows):
        return centred(hid[rows])[0]

    def norm_two(rows):
        norm[rows] = (scaled_rows(rows) * vector(2) + vector(3)).astype(bf16)

    def norm_one(rows):
        norm[rows] = (scaled_rows(rows) * vector(0) + vector(1)).astype(bf16)

    def emit(steps, compute, dst, size, start=0):
        def write(index):
            return pltpu.make_async_copy(
                stage.at[lax.rem(index, 2), :, :size],
                dst.at[rows_of(index), pl.ds(start, size)],
                local_sems.at[lax.rem(index, 2)],
            )

        def body(index, carry):
            @pl.when(index >= 2)
            def _():
                write(index - 2).wait()

            stage[lax.rem(index, 2), :, :size] = compute(index).astype(bf16)
            write(index).start()
            return carry

        lax.fori_loop(0, steps, body, 0)
        write(steps - 2).wait()
        write(steps - 1).wait()

    def feed_forward():
        bias_start = ctx * columns
        bias_row = 9 + bias_start // row_size
        bias_column = pl.multiple_of(lax.rem(bias_start, row_size), columns)
        up_bias = jnp.concatenate(
            [vec[index, bias_row, :, pl.ds(bias_column, columns)] for index in range(shards)],
            axis=1,
        )

        def body(rows):
            value = dot(norm[rows], w_up[...]) + up_bias
            cdf = 0.5 * (1.0 + lax.erf(value * (0.5**0.5)))
            density = jnp.exp(-0.5 * value * value) * ((2.0 * math.pi) ** -0.5)
            act[rows] = (value * cdf).astype(bf16)
            wide_f[rows] = cdf + value * density

        loop(body)

    def down_grad(index):
        start, size = sum(cut[0] for cut in DOWN_CUTS[:index]), DOWN_CUTS[index][0]

        def body(step, carry):
            rows = rows_of(shard ^ (3 - step))
            cut = pl.ds(start, size)
            stage[0, :, :size] = dot_rows(act[:, rows], gra[:, cut]).astype(bf16)
            write = pltpu.make_async_copy(
                stage.at[0, :, :size], down_parts.at[rows, cut], local_sems.at[0]
            )
            write.start()
            write.wait()
            for number, slot in ((0, 1), (0, 3), (1, 2), (2, 0)):

                @pl.when(step == number)
                def _(slot=slot):
                    named[f"fd{index}"].send(slot)

            return carry

        lax.fori_loop(0, shards, body, 0)

    def feed_back():
        def body(rows):
            d_up[rows] = (dot_cols(gra[rows], w_down[...]) * wide_f[rows]).astype(bf16)

        loop(body)

    def up_grad(index):
        start, size = sum(cut[0] for cut in UP_CUTS[:index]), UP_CUTS[index][0]
        emit(
            width // TILE,
            lambda step: dot_rows(norm[:, rows_of(step)], d_up[:, pl.ds(start, size)]),
            up_parts,
            size,
            start,
        )

    rotary = table.shape[2]

    def turn(entries, rows, way):
        first = entries[:, :rotary]
        first = (
            first * table[0, rows]
            + way * (pltpu.roll(first, ROT // 2, 1) * table[1, rows])
            + way * (pltpu.roll(first, rotary - ROT // 2, 1) * table[2, rows])
        )
        return jnp.concatenate([first, entries[:, rotary:]], axis=1)

    def project():
        per = 3 * HEADS // shards
        bias_parts = []
        for index in range(3):
            place = index * HEADS + ctx
            rest = lax.rem(place, per) * head_dim
            bias_parts.append(
                vec[
                    place // per,
                    6 + rest // row_size,
                    :,
                    pl.ds(pl.multiple_of(lax.rem(rest, row_size), head_dim), head_dim),
                ]
            )

        def body(rows):
            joined = dot(norm[rows], w_qkv[...])
            parts = [
                joined[:, index * head_dim : (index + 1) * head_dim] + bias_parts[index]
                for index in range(3)
            ]
            queries[rows] = turn(parts[0], rows, 1.0).astype(bf16)
            keys[rows] = turn(parts[1], rows, 1.0).astype(bf16)
            values[rows] = parts[2].astype(bf16)

        loop(body)
        side = segs.shape[1]
        for index in range(count):
            block = seg[index].astype(f32)
            seg_col[index * side : (index + 1) * side] = jnp.broadcast_to(block, (side, side)).T

    def attend(index):
        rows = pl.ds(index * TILE, TILE)
        size = (index + 1) * TILE
        seg_row = jnp.concatenate([seg[block] for block in range(count)], axis=1)
        scores = dot_cols(queries[rows], keys[:size]) * factor
        query_place = index * TILE + lax.broadcasted_iota(jnp.int32, (TILE, size), 0)
        key_place = lax.broadcasted_iota(jnp.int32, (TILE, size), 1)
        same = seg_col[rows][:, :1] == seg_row[:, :size].astype(f32)
        allowed = (key_place <= query_place) & same
        scores = jnp.where(allowed, scores, -1e30)
        terms = jnp.where(
            allowed, jnp.exp(scores - jnp.max(scores, axis=-1, keepdims=True)), 0.0
        )
        probs = terms / jnp.sum(terms, axis=-1, keepdims=True)
        wide_f[rows, :size] = probs
        result = dot(probs.astype(bf16), values[:size])
        att_f[rows] = result
        att[rows] = result.astype(bf16)

    def attend_all():
        for index in range(tiles):
            attend(index)

    def output():
        def body(index):
            rows = rows_of(index)
            return dot(att[rows], w_dense[...]) + dot(act[rows], w_down[...])

        emit(tiles, body, out_parts, width)

    dense_size = width // shards

    def dense_grad():
        def body(index):
            start = pl.multiple_of(index * dense_size, dense_size)
            return dot_rows(att[...], gra[:, pl.ds(start, dense_size)])

        emit(shards, body, dense_parts, dense_size)

    def attend_back(index):
        rows = pl.ds(index * TILE, TILE)
        size = (index + 1) * TILE
        d_att = dot_cols(gra[rows], w_dense[...]).astype(bf16)
        delta = jnp.sum(d_att.astype(f32) * att_f[rows], axis=-1, keepdims=True)
        probs = wide_f[rows, :size]
        d_scores = (probs * (dot_cols(d_att, values[:size]) - delta)).astype(bf16)
        d_queries = dot(d_scores, keys[:size]) * factor
        d_joined[rows, :head_dim] = turn(d_queries, rows, -1.0).astype(bf16)
        d_keys[:size] += dot_rows(d_scores, queries[rows])
        d_values[:size] += dot_rows(probs.astype(bf16), d_att)

    def attend_back_all():
        d_keys[...] = jnp.zeros_like(d_keys)
        d_values[...] = jnp.zeros_like(d_values)
        for index in range(tiles):
            attend_back(index)

        def join(rows):
            d_joined[rows, head_dim : 2 * head_dim] = turn(d_keys[rows] * factor, rows, -1.0).astype(bf16)
            d_joined[rows, 2 * head_dim :] = d_values[rows].astype(bf16)

        loop(join)

    def qkv_grad(index):
        start, size = sum(cut[0] for cut in QKV_CUTS[:index]), QKV_CUTS[index][0]
        emit(
            width // TILE,
            lambda step: dot_rows(norm[:, rows_of(step)], d_joined[:, pl.ds(start, size)]),
            qkv_parts,
            size,
            start,
        )

    def inputs():
        sums[...] = jnp.zeros_like(sums)

        def body(index):
            rows = rows_of(index)
            d_one = dot_cols(d_joined[rows], w_qkv[...])
            d_two = dot_cols(d_up[rows], w_up[...])
            scaled = scaled_rows(rows)

            def gather(row, entries):
                sums[row : row + 1, : entries.shape[1]] += jnp.sum(
                    entries.astype(f32), axis=0, keepdims=True
                )

            gather(0, d_two * scaled)
            gather(1, d_two)
            gather(2, gra[rows])
            gather(3, d_up[rows])
            gather(4, d_one * scaled)
            gather(5, d_one)
            gather(6, d_joined[rows])
            return d_one * vector(0) + d_two * vector(2)

        emit(tiles, body, in_parts, width)

    sums_items = []

    def sums_start():
        for bit in (1, 2, 3):
            send_small(sums, sums_got.at[shard], sums_got.at[shard ^ bit], (ctx, shard ^ bit))
            sums_items.append(small[-1])
        sums_got[shard] = sums[...]

    def sums_land():
        wait_small(sums_items)
        total = sums_got[0]
        for index in range(1, shards):
            total = total + sums_got[index]
        sums_tot[...] = total

    exchanged = []

    def dense_block(owner):
        return pl.ds(pl.multiple_of(owner * dense_size, dense_size), dense_size)

    def own_dense():
        return pltpu.make_async_copy(
            dense_lines.at[dense_block(shard)], dense_all.at[dense_block(shard)], local_sems.at[2]
        )

    def dense_part(owner, side):
        size = dense_size // CORES
        return pl.ds(pl.multiple_of(owner * dense_size + side * size, size), size)

    def exchange():
        for bit in (1, 2, 3):
            peer = shard ^ bit
            send_small(
                dense_lines.at[dense_part(peer, core)], dense_all.at[dense_part(shard, core)],
                dense_all.at[dense_part(peer, core)], (ctx, peer),
            )
            exchanged.append(small[-1])
        own_dense().start()

    relayed = []

    def relay():
        wait_small(exchanged)
        for bit in (1, 2, 3):
            rows = dense_part(shard ^ bit, core)
            send_small(
                dense_all.at[rows], dense_all.at[rows], dense_all.at[dense_part(shard ^ bit, 1 - core)],
                (ctx ^ 1, shard),
            )
            relayed.append(small[-1])

    def relay_done():
        wait_small(relayed)
        own_dense().wait()

    steps = {
        "small_start": small_start, "small_land": small_land, "norm_two": lambda: loop(norm_two),
        "norm_one": lambda: loop(norm_one), "feed_forward": feed_forward, "down_grad": down_grad,
        "feed_back": feed_back, "up_grad": up_grad, "project": project, "attend": attend_all, "output": output,
        "dense_grad": dense_grad, "attend_back": attend_back_all, "qkv_grad": qkv_grad, "inputs": inputs,
        "sums_start": sums_start, "sums_land": sums_land, "exchange": exchange, "relay": relay,
        "relay_done": relay_done,
        "output_done": lambda: out_sink.last((up_out, down_out), 0, output_out, local_sems.at[3]),
        "input_done": lambda: in_sink.last(
            (up_out, down_out), hidden.shape[0], input_out, local_sems.at[3]
        ),
    }
    for step in ORDER:
        name, *rest = step.split(".")
        if name in steps:
            steps[name](*[int(number) for number in rest])
        else:
            method = {"in": "inward"}.get(rest[0], rest[0])
            getattr(named[name], method)(*[int(number) for number in rest[1:]])

    pltpu.make_async_copy(vec, vec_out, local_sems.at[8]).start()
    for name, item in named.items():
        if isinstance(item, Line) and name + ".arrived" not in ORDER:
            item.arrived()
    for name, item in named.items():
        if not isinstance(item, Sink) and name + ".sent" not in ORDER:
            item.sent()
    for copy, _, _ in small:
        copy.wait_send()
    pltpu.make_async_copy(vec, vec_out, local_sems.at[8]).wait()


DOWN_CUTS = ((512, False), (512, False), (1024, True))
UP_CUTS = ((512, True), (512, True))
QKV_CUTS = ((768, True),)
DENSE_CUTS = ((512, False),)

ORDER = (
    "wd.start.0", "hid.start", "wu.start.0", "gra.start", "wu.start.1", "hid.out.1", "small_start", "wu.forward",
    "gra.out.1", "wd.forward", "hid.in.1", "gra.in.1", "wd.start.1", "hid.out.2", "hid.out.3", "gra.out.2",
    "small_land", "hid.arrived", "norm_two", "wu.arrived", "feed_forward", "gra.out.3", "gra.arrived", "down_grad.2",
    "fd2.middle.1", "wd.arrived", "down_grad.1", "fd2.middle.0", "fd1.middle.1", "wq.start.0", "fd2.finish.1",
    "ld21.start", "fd1.middle.0", "fd2.finish.0", "ld20.start", "down_grad.0", "ld21.out.1", "fd1.finish.1",
    "ld21.in.1", "ld20.out.1", "fd1.finish.0", "ld10.start", "wq.start.1", "feed_back", "up_grad.0", "fu0.send.1",
    "fu0.send.3", "ld21.out.2", "ld10.out.1", "ld20.in.1", "wd.sent", "fd0.middle.0", "fd0.middle.1", "fu0.send.2",
    "ld21.out.3", "fu0.middle.1", "wq.forward", "ld20.out.2", "ld10.in.1", "fd0.finish.0", "fd2.sent",
    "fd0.finish.1", "ld00.start", "wt.start", "fu0.finish.1", "lu01.start", "fu0.send.0", "up_grad.1", "fu1.send.1",
    "fu1.send.3", "norm_one", "fu0.middle.0", "ld10.out.2", "lu01.out.1", "wq.arrived", "ld00.in.1", "ld00.out.1",
    "project", "attend", "wt.forward", "dense_grad", "fe0.send.3", "lu01.in.1", "fu1.send.2", "fe0.send.1",
    "fu1.middle.1", "ld00.out.2", "ld21.arrived", "fu0.finish.0", "lu00.start", "wt.back", "fe0.send.0",
    "fu1.middle.0", "ld00.out.3", "fe0.middle.1", "hid.sent", "fe0.middle.0", "lu00.out.1", "lu01.out.2",
    "fu1.send.0", "wq.sent", "fu1.finish.1", "lu11.start", "fe0.send.2", "wt.arrived", "attend_back", "qkv_grad.0",
    "fq0.send.3", "fq0.send.1", "lu11.out.1", "lu00.in.1", "fe0.finish.1", "fe0.finish.0", "le00.start",
    "fq0.send.0", "fq0.send.2", "fu1.finish.0", "lu10.start", "fq0.middle.0", "output", "so.start", "lu10.out.1",
    "fq0.middle.1", "le00.in.1", "fd0.sent", "ld10.out.3", "lu10.in.1", "le00.out.1", "so.swap", "so.in.1",
    "fq0.finish.0", "lu11.in.1", "lq00.start", "le00.out.2", "fq0.finish.1", "lu10.out.2", "lq01.start", "fu1.sent",
    "inputs", "sums_start", "sums_land", "ld00.arrived", "ls.start", "lu01.out.3", "si.start", "ld20.out.3",
    "so.in.2", "gra.sent", "fe0.sent", "le00.out.3", "wu.sent", "ld10.arrived", "ld10.sent", "lu00.out.2",
    "ld20.arrived", "lu11.out.2", "lq01.in.1", "le00.arrived", "ls.in.1", "le00.sent", "lu01.arrived", "si.swap",
    "fd1.sent", "lu10.out.3", "exchange", "lu10.arrived", "lu10.sent", "lq01.out.1", "lu00.out.3", "si.in.1",
    "lu11.out.3", "ld00.sent", "ls.out.1", "lq00.out.1", "lu00.arrived", "lq00.in.1", "lu00.sent", "fu0.sent",
    "output_done", "lu01.sent", "si.in.2", "ld21.sent", "ls.out.2", "lu11.arrived", "lq01.out.2", "ld20.sent",
    "lu11.sent", "ls.out.3", "relay", "ls.arrived", "wt.sent", "ls.sent", "lq00.out.2", "input_done", "relay_done",
    "lq01.out.3", "lq01.arrived", "lq00.out.3", "lq01.sent", "fq0.sent", "lq00.arrived", "lq00.sent",
)


def rotary_table(length, lanes):
    half = ROT // 2
    freqs = (10000.0 ** (-2.0 * np.arange(half, dtype=np.float32) / ROT)).astype(np.float32)
    angles = np.arange(length, dtype=np.float32)[:, None] * freqs[None]
    cosine, sine = np.cos(angles), np.sin(angles)
    table = np.zeros((3, length, lanes), np.float32)
    table[0] = 1.0
    table[0, :, :half], table[0, :, half:ROT] = cosine, cosine
    table[1, :, half:ROT] = sine
    table[2, :, :half] = -sine
    return table


def whole_block(hidden, grad, fc1, fc2, qkv, dense, segs, vectors):
    chips, shards = lax.axis_size("ctx") // CORES, lax.axis_size("fsdp")
    count = chips * CORES
    tokens, width = hidden.shape
    length = tokens * count
    units = fc1.shape[1] // count
    head_dim = width // HEADS
    part = units // shards
    rows = width // shards
    bf16, f32 = jnp.bfloat16, jnp.float32
    wide, joint = (length, width), 3 * head_dim
    vectors = [vector.reshape(1, -1) for vector in vectors]
    vec_shape = (shards, sum(vector.shape[1] for vector in vectors) // rows, 1, rows)
    seg_shape = (count,) + segs.shape
    line = (tokens, width)
    hops = (2 * (chips - 1) * tokens, width)
    outs = [
        (vec_shape, f32), (line, f32), (line, f32), ((2 * tokens, width), bf16), ((2 * tokens, width), bf16),
        ((count * part, width), bf16), ((count * rows, units), bf16),
        ((count * rows, joint), bf16), ((width, rows), bf16), ((count * 8, width), f32),
        ((units, width), bf16), ((width, units), bf16), ((width, joint), bf16), ((shards * head_dim, rows), bf16),
        ((3 * part, width), bf16), ((3 * rows, units), bf16), ((3 * rows, joint), bf16), ((3 * head_dim, rows), bf16),
        (wide, bf16), ((chips * tokens, width), bf16), (hops, bf16),
        (wide, bf16), ((chips * tokens, width), bf16), (hops, bf16), ((count * head_dim, rows), bf16),
    ]
    table = rotary_table(length, 128)
    cuts = DOWN_CUTS + UP_CUTS + QKV_CUTS + DENSE_CUTS
    halves = [(part // 2, width), (rows // 2, units), (rows // 2, joint), (head_dim // 2, rows)]
    scratch = [
        (wide, bf16), (wide, bf16), (wide, bf16), ((width, units), bf16), ((units, width), bf16),
        ((width, joint), bf16), ((head_dim, width), bf16), (vec_shape, f32), (seg_shape, segs.dtype),
        ((length, segs.shape[1]), f32), (table.shape, f32),
        ((length, units), bf16), ((length, max(units, length)), f32), ((length, units), bf16),
        ((length, head_dim), bf16), ((length, head_dim), bf16), ((length, head_dim), bf16),
        ((length, head_dim), f32), ((length, head_dim), bf16), ((length, head_dim), f32), ((length, head_dim), f32),
        ((length, joint), bf16), ((8, width), f32), ((shards, 8, width), f32), ((8, width), f32),
        ((2, TILE, width), bf16),
    ]
    scratch += [((3,) + half, bf16) for half in halves[:2]]
    scratch += [((2,) + half, bf16) for half in halves]
    scratch += [((2 * half[0], half[1]), bf16) for half in halves]
    scratch += [((2, tokens, width), bf16), ((2, tokens, width), bf16), (line, f32)]
    slots = (
        (3 + sum(1 + split for _, split in cuts)) * Line.slots(chips)
        + 3 * Square.SLOTS + Tree.SLOTS + len(cuts) * Fold.SLOTS + 2 * Sink.slots(chips) + 12 + count - 1
    )
    outputs = pl.pallas_call(
        functools.partial(block_kernel, (chips, shards, part)),
        out_shape=[jax.ShapeDtypeStruct(shape, kind) for shape, kind in outs],
        in_specs=[pl.BlockSpec(memory_space=pl.ANY)] * 16,
        out_specs=[pl.BlockSpec(memory_space=pl.ANY)] * len(outs),
        scratch_shapes=[pltpu.VMEM(shape, kind) for shape, kind in scratch]
        + [
            pltpu.SemaphoreType.DMA((slots,)),
            pltpu.SemaphoreType.DMA((slots,)),
            pltpu.SemaphoreType.DMA((24,)),
        ],
        compiler_params=pltpu.CompilerParams(
            collective_id=0, has_side_effects=True, vmem_limit_bytes=62 * 2**20
        ),
        name="whole_block",
    )(hidden, grad, fc1, fc2, qkv, dense, segs, jnp.asarray(table), *vectors)
    return outputs[:10]


FINISH_STEPS = 8


def widen_kernel(
    sizes,
    up_all, qkv_all, dense_all, down_all, sums,
    gain_one, shift_one, qkv, qkv_bias, dense, columns_one, gain_two, shift_two, up, up_bias, down, columns_two,
):
    count, shards, width = sizes
    f32 = jnp.float32

    def spread(src, dst, pieces):
        groups, size = src.shape[0], src.shape[2] // pieces
        for piece in range(pieces):
            for group in range(groups):
                start = (piece * groups + group) * size
                dst[:, start : start + size] = src[group, :, piece * size : (piece + 1) * size].astype(f32)

    spread(up_all, up, shards)
    spread(qkv_all, qkv, 3)
    spread(dense_all, dense, 1)
    down[...] = down_all[...].astype(f32)

    @pl.when(pl.program_id(0) == 0)
    def _():
        shard = lax.axis_index("fsdp")
        rows = gain_one.shape[1]
        mine = pl.ds(pl.multiple_of(shard * rows, rows), rows)
        for row, dst in ((0, gain_two), (1, shift_two), (4, gain_one), (5, shift_one)):
            total = sums[0, row : row + 1, mine]
            for index in range(1, count):
                total = total + sums[index, row : row + 1, mine]
            dst[...] = total
        columns_one[...] = sums[0, 2:3, mine]
        columns_two[...] = sums[0, 2:3, mine]
        part = up_bias.shape[1] // count
        here = pl.ds(pl.multiple_of(shard * part, part), part)
        for index in range(count):
            up_bias[:, index * part : (index + 1) * part] = sums[index, 3:4, here]
        size = width // count
        chunks = qkv_bias.shape[1] // size
        for chunk in range(chunks):
            place = shard * chunks + chunk
            start = pl.multiple_of(place // count * size, size)
            qkv_bias[:, chunk * size : (chunk + 1) * size] = sums[
                lax.rem(place, count), 6:7, pl.ds(start, size)
            ]


def sliced(shape, steps):
    block = shape[:-2] + (shape[-2] // steps, shape[-1])
    return pl.BlockSpec(block, lambda index: (0,) * (len(shape) - 2) + (index, 0))


def entire(shape, _=None):
    return pl.BlockSpec(shape, lambda index: (0,) * len(shape))


def widen(up_all, qkv_all, dense_all, down_all, sums, width):
    count, shards = lax.axis_size("ctx"), lax.axis_size("fsdp")
    rows = width // shards
    f32 = jnp.float32
    steps = FINISH_STEPS
    grads = [
        up_all.reshape(count, rows, -1), qkv_all.reshape(count, rows, -1), dense_all.reshape(shards, rows, rows),
        down_all,
    ]
    units = up_all.shape[1] * count
    sums = sums.reshape(count, 8, width)
    vector = (1, rows)
    outs = [
        (vector, entire), (vector, entire), ((rows, 3 * width), sliced), ((1, 3 * rows), entire),
        ((rows, width), sliced), (vector, entire), (vector, entire), (vector, entire), ((rows, units), sliced),
        ((1, units // shards), entire), (down_all.shape, sliced), (vector, entire),
    ]
    size = sum(math.prod(shape) for shape, _ in outs)
    return pl.pallas_call(
        functools.partial(widen_kernel, (count, shards, width)),
        grid=(steps,),
        in_specs=[sliced(array.shape, steps) for array in grads] + [entire(sums.shape)],
        out_specs=[kind(shape, steps) for shape, kind in outs],
        out_shape=[jax.ShapeDtypeStruct(shape, f32) for shape, _ in outs],
        compiler_params=pltpu.CompilerParams(vmem_limit_bytes=62 * 2**20),
        cost_estimate=pl.CostEstimate(flops=size, bytes_accessed=6 * size, transcendentals=0),
        name="widen",
    )(*grads, sums)


def close_kernel(shards, vec, branch, back, upward, downward, hidden, grad, output, input_grad):
    f32 = jnp.float32
    own = hidden[...].astype(f32)
    shift = jnp.concatenate([vec[index, 4] + vec[index, 5] for index in range(shards)], axis=1)

    def total(ref, index):
        return ref[...] + upward[index].astype(f32) + downward[index].astype(f32)

    output[...] = (own + total(branch, 0) + shift).astype(output.dtype)
    scaled, spread = centred(own)
    e = total(back, 1)
    part = spread * (
        e
        - jnp.mean(e, axis=-1, keepdims=True)
        - scaled * jnp.mean(e * scaled, axis=-1, keepdims=True)
    )
    input_grad[...] = (grad[...].astype(f32) + part).astype(input_grad.dtype)


def close(vec, branch, back, upward, downward, hidden, grad):
    steps = 4
    shape = hidden.shape
    both = (2,) + shape
    wide = sliced(shape, steps)
    return pl.pallas_call(
        functools.partial(close_kernel, lax.axis_size("fsdp")),
        grid=(steps,),
        in_specs=[entire(vec.shape), wide, wide, sliced(both, steps), sliced(both, steps), wide, wide],
        out_specs=[wide, wide],
        out_shape=[jax.ShapeDtypeStruct(shape, hidden.dtype)] * 2,
        compiler_params=pltpu.CompilerParams(vmem_limit_bytes=62 * 2**20),
        name="close",
    )(vec, branch, back, upward.reshape(both), downward.reshape(both), hidden, grad)


def one_kernel(
    hidden, qkv_weight, dense_weight, fc1_weight, fc2_weight, segments, out_grad, vectors
):
    vec, branch, back, up_out, down_out, down_all, up_all, qkv_all, dense_all, sums_all = whole_block(
        hidden[0], out_grad[0], fc1_weight, fc2_weight, qkv_weight, dense_weight, segments, vectors
    )
    count = lax.axis_size("ctx")
    upward = lax.ppermute(up_out, "ctx", [(index, index + CORES) for index in range(count - CORES)])
    downward = lax.ppermute(down_out, "ctx", [(index + CORES, index) for index in range(count - CORES)])
    outs = widen(up_all, qkv_all, dense_all, down_all, sums_all, hidden.shape[2])
    outs = [out.reshape(-1) if out.shape[0] == 1 else out for out in outs]
    output, input_grad = close(vec, branch, back, upward, downward, hidden[0], out_grad[0])
    return (output[None], input_grad[None], *outs)


def per_device(
    hidden,
    ln1_gain,
    ln1_bias,
    qkv_weight,
    qkv_bias,
    dense_weight,
    dense_bias,
    ln2_gain,
    ln2_bias,
    fc1_weight,
    fc1_bias,
    fc2_weight,
    fc2_bias,
    segments,
    out_grad,
):
    ctx_count = lax.axis_size("ctx")
    shards = lax.axis_size("fsdp")
    ctx = lax.axis_index("ctx")
    tokens, width = hidden.shape[1], hidden.shape[2]
    length = tokens * ctx_count
    head_dim = width // HEADS
    repeat = ctx_count // HEADS
    head = ctx // repeat
    factor = head_dim ** (-0.5)
    rows = width // shards
    ff = fc1_weight.shape[1]
    units = ff // shards // ctx_count
    bf16, f32 = jnp.bfloat16, jnp.float32

    vectors = [ln1_gain, ln1_bias, ln2_gain, ln2_bias, dense_bias, fc2_bias, qkv_bias, fc1_bias]
    if ctx_count == HEADS and shards == 4:
        return one_kernel(
            hidden, qkv_weight, dense_weight, fc1_weight, fc2_weight, segments, out_grad, vectors
        )
    vectors = jnp.concatenate(vectors).reshape(-1, rows)
    vec = lax.all_gather(vectors, "fsdp", axis=0)
    query_seg = lax.all_gather(segments[0], "ctx", axis=0, tiled=True)
    up_part = lax.dynamic_index_in_dim(
        fc1_weight.reshape(rows, shards, ctx_count, units), ctx, 2, keepdims=False
    ).reshape(rows, shards * units)
    down_part = lax.dynamic_slice_in_dim(fc2_weight, ctx * units, units, 0)
    qkv_part = lax.dynamic_index_in_dim(
        qkv_weight.reshape(rows, 3, HEADS, head_dim), head, 2, keepdims=False
    ).reshape(rows, 3 * head_dim)
    dense_cols = lax.all_to_all(
        dense_weight, "fsdp", split_axis=1, concat_axis=0, tiled=True
    )
    dense_part = lax.dynamic_slice_in_dim(dense_cols, head * head_dim, head_dim, 0)
    up_w = gather_fsdp(up_part)
    down_w = gather_fsdp(down_part)
    qkv_w = gather_fsdp(qkv_part)
    dense_w = gather_fsdp(dense_part, axis=1)
    hidden_all = line_gather(hidden[0]).reshape(length, width)
    grad_all = line_gather(out_grad[0]).reshape(length, width)
    normed_one = (centred(hidden_all)[0] * vec[:, 0].reshape(-1) + vec[:, 1].reshape(-1)).astype(bf16)
    scaled = centred(hidden_all)[0]
    gain_two = vec[:, 2].reshape(-1)
    normed_two = (scaled * gain_two + vec[:, 3].reshape(-1)).astype(bf16)
    up_shift = lax.dynamic_index_in_dim(
        vec[:, 9 : 9 + ff // width].reshape(shards, ctx_count, units), ctx, 1, keepdims=False
    ).reshape(-1)
    act_f, slope = gelu_and_slope(dot(normed_two, up_w) + up_shift)
    act = act_f.astype(bf16)
    d_up = (dot_cols(grad_all, down_w) * slope).astype(bf16)
    down_part_grad = dot_rows(act, grad_all).astype(bf16)
    up_part_grad = dot_rows(normed_two, d_up).astype(bf16)
    ff_part = dot(act, down_w).astype(bf16)
    d_two = dot_cols(d_up, up_w)
    e_two = (d_two * gain_two).astype(bf16)
    gain_two_sum, shift_two_sum = jnp.sum(d_two * scaled, axis=0), jnp.sum(d_two, axis=0)
    columns = jnp.sum(grad_all.astype(f32), axis=0)
    up_sum = jnp.sum(d_up.astype(f32), axis=0)
    gain_one = vec[:, 0].reshape(-1)
    dense_shift, down_shift = vec[:, 4].reshape(-1), vec[:, 5].reshape(-1)
    qkv_shift = vec[:, 6:9].reshape(-1)
    down_grad = scatter_fsdp(down_part_grad)
    up_grad = scatter_fsdp(up_part_grad)

    qkv_shift_part = lax.dynamic_index_in_dim(
        qkv_shift.reshape(3, HEADS, head_dim), head, 1, keepdims=False
    ).reshape(-1)
    joined = dot(normed_one, qkv_w) + qkv_shift_part
    places = jnp.arange(length, dtype=jnp.int32)
    cosine, sine = rotary_tables(places, ROT)
    queries = rotate(joined[:, :head_dim], cosine, sine).astype(bf16)
    keys = rotate(joined[:, head_dim : 2 * head_dim], cosine, sine).astype(bf16)
    values = joined[:, 2 * head_dim :].astype(bf16)
    allowed = (places[None, :] <= places[:, None]) & (query_seg[None, :] == query_seg[:, None])
    if repeat > 1:
        allowed = allowed & (places // (length // repeat) == ctx % repeat)[:, None]
    scores = jnp.where(allowed, dot_cols(queries, keys) * factor, -1e30)
    top = jnp.max(scores, axis=-1, keepdims=True)
    terms = jnp.where(allowed, jnp.exp(scores - top), 0.0)
    total = jnp.sum(terms, axis=-1, keepdims=True)
    probs = terms * jnp.where(total > 0.0, 1.0 / total, 0.0)
    probs_low = probs.astype(bf16)
    att_f = dot(probs_low, values)
    att = att_f.astype(bf16)
    partial = dot(att, dense_w) + ff_part.astype(f32)
    branch = lax.psum_scatter(partial.astype(bf16), "ctx", scatter_dimension=0, tiled=True)
    own = hidden[0].astype(f32)
    layer_output = (own + branch.astype(f32) + dense_shift + down_shift).astype(bf16)

    d_att = dot_cols(grad_all, dense_w).astype(bf16)
    delta = jnp.sum(d_att.astype(f32) * att_f, axis=-1, keepdims=True)
    dense_grad = dot_rows(att, grad_all).astype(bf16)
    d_scores = (probs * (dot_cols(d_att, values) - delta)).astype(bf16)
    d_queries = rotate(dot(d_scores, keys) * factor, cosine, -sine)
    d_keys = rotate(dot_rows(d_scores, queries) * factor, cosine, -sine)
    d_values = dot_rows(probs_low, d_att)
    d_joined = jnp.concatenate([d_queries, d_keys, d_values], axis=1).astype(bf16)
    qkv_grad = dot_rows(normed_one, d_joined).astype(bf16)

    d_one = dot_cols(d_joined, qkv_w)
    both = (d_one * gain_one + e_two.astype(f32)).astype(bf16)
    back = lax.psum_scatter(both, "ctx", scatter_dimension=0, tiled=True).astype(f32)
    own_scaled, own_spread = centred(own)
    input_part = own_spread * (
        back
        - jnp.mean(back, axis=-1, keepdims=True)
        - own_scaled * jnp.mean(back * own_scaled, axis=-1, keepdims=True)
    )
    input_grad = (out_grad[0].astype(f32) + input_part).astype(bf16)

    first = (ctx == 0).astype(f32)
    joined_sum = jnp.sum(d_joined.astype(f32), axis=0).reshape(3, 1, head_dim)
    joined_full = jnp.where((jnp.arange(HEADS) == head)[None, :, None], joined_sum, 0.0)
    up_sum = up_sum.reshape(shards, 1, units)
    up_full = jnp.where((jnp.arange(ctx_count) == ctx)[None, :, None], up_sum, 0.0)
    small = [
        jnp.sum(d_one * centred(hidden_all)[0], axis=0),
        jnp.sum(d_one, axis=0),
        columns * first,
        gain_two_sum,
        shift_two_sum,
        joined_full,
        up_full,
    ]
    small = jnp.concatenate([piece.reshape(shards, -1) for piece in small], axis=1).astype(bf16)
    small_size = small.shape[1]
    small_rows = -(-small_size // (3 * head_dim * 16)) * 16
    small = jnp.pad(small, ((0, 0), (0, small_rows * 3 * head_dim - small_size)))
    last_grad = scatter_fsdp(
        jnp.concatenate(
            [
                qkv_grad.reshape(shards, rows, 3 * head_dim),
                small.reshape(shards, small_rows, 3 * head_dim),
            ],
            axis=1,
        ).reshape(-1, 3 * head_dim)
    )
    dense_share = scatter_fsdp(
        dense_grad.reshape(head_dim, shards, rows).transpose(1, 0, 2).reshape(-1, rows)
    )

    down_all = line_gather(down_grad).astype(f32).reshape(ctx_count * units, width)
    up_all = (
        line_gather(up_grad)
        .astype(f32)
        .reshape(ctx_count, rows, shards, units)
        .transpose(1, 2, 0, 3)
        .reshape(rows, ff)
    )
    dense_cols_all = line_gather(dense_share)
    if repeat > 1:
        dense_cols_all = jnp.sum(
            dense_cols_all.astype(f32).reshape(HEADS, repeat, head_dim, rows), axis=1
        ).astype(bf16)
    dense_all = lax.all_to_all(
        dense_cols_all.reshape(width, rows), "fsdp", split_axis=0, concat_axis=1, tiled=True
    ).astype(f32)
    last_all = line_gather(last_grad)
    qkv_all = last_all[:, :rows].astype(f32)
    if repeat > 1:
        qkv_all = jnp.sum(qkv_all.reshape(HEADS, repeat, rows, 3 * head_dim), axis=1)
    qkv_all = (
        qkv_all.reshape(HEADS, rows, 3, head_dim).transpose(1, 2, 0, 3).reshape(rows, 3 * width)
    )
    small_all = jnp.sum(last_all[:, rows:].astype(f32), axis=0).reshape(-1)
    sizes = [rows] * 5 + [3 * rows, ff // shards]
    parts, at = [], 0
    for size in sizes:
        parts.append(small_all[at : at + size])
        at += size
    gain_one_grad, shift_one_grad, columns_grad, gain_two_grad, shift_two_grad, joined_grad, up_b_grad = parts
    return (
        layer_output[None],
        input_grad[None],
        gain_one_grad,
        shift_one_grad,
        qkv_all,
        joined_grad,
        dense_all,
        columns_grad,
        gain_two_grad,
        shift_two_grad,
        up_all,
        up_b_grad,
        down_all,
        columns_grad,
    )


def solution(mesh):
    vec, mat, act = P("fsdp"), P("fsdp", None), P("fsdp", "ctx", None)
    return jax.shard_map(
        per_device,
        mesh=mesh,
        in_specs=(
            act, vec, vec, mat, vec, mat, vec, vec, vec, mat, vec, mat, vec, P("fsdp", "ctx"), act
        ),
        out_specs=(act, act, vec, vec, mat, vec, mat, vec, vec, vec, mat, vec, mat, vec),
        check_vma=False,
    )
```

```python
import functools
import math

import jax
import jax.numpy as jnp
import numpy as np
from jax import lax
from jax.experimental import pallas as pl
from jax.experimental.pallas import tpu as pltpu
from jax.sharding import PartitionSpec as P

HEADS = 8
ROT = 64
CORES = 2


def dot(left, right):
    return jnp.dot(left, right, preferred_element_type=jnp.float32)


def dot_rows(left, right):
    return lax.dot_general(
        left, right, (((0,), (0,)), ((), ())), preferred_element_type=jnp.float32
    )


def dot_cols(left, right):
    return lax.dot_general(
        left, right, (((1,), (1,)), ((), ())), preferred_element_type=jnp.float32
    )


def gelu_and_slope(values):
    cdf = 0.5 * (1.0 + lax.erf(values * (0.5**0.5)))
    density = jnp.exp(-0.5 * values * values) * ((2.0 * jnp.pi) ** -0.5)
    return values * cdf, cdf + values * density


def centred(values):
    values = values.astype(jnp.float32)
    center = values - jnp.mean(values, axis=-1, keepdims=True)
    spread = lax.rsqrt(jnp.mean(center * center, axis=-1, keepdims=True) + 1e-05)
    return center * spread, spread


def rotary_tables(places, width):
    half_rot = width // 2
    freqs = 10000.0 ** (-2.0 * jnp.arange(half_rot, dtype=jnp.float32) / width)
    angles = places.astype(jnp.float32)[:, None] * freqs[None, :]
    return (jnp.cos(angles), jnp.sin(angles))


def rotate(values, cosine, sine):
    half = cosine.shape[-1]
    first, second, remain = values[:, :half], values[:, half : 2 * half], values[:, 2 * half :]
    return jnp.concatenate(
        [first * cosine - second * sine, second * cosine + first * sine, remain], axis=1
    )


def line_gather(block):
    count = lax.axis_size("ctx")
    chips = count // CORES
    ctx = lax.axis_index("ctx")
    place, core = ctx // CORES, ctx % CORES
    up = down = block
    ups, downs = [], []
    for hop in range(1, chips):
        up = lax.ppermute(
            up,
            "ctx",
            [
                (i * CORES + k, (i + 1) * CORES + k)
                for i in range(hop - 1, chips - 1)
                for k in range(CORES)
            ],
        )
        down = lax.ppermute(
            down,
            "ctx",
            [
                (i * CORES + k, (i - 1) * CORES + k)
                for i in range(1, chips - hop + 1)
                for k in range(CORES)
            ],
        )
        ups.append(up)
        downs.append(down)
    around = jnp.stack(ups[::-1] + [block] + downs)
    mine = lax.dynamic_slice_in_dim(around, chips - 1 - place, chips, 0)
    other = lax.ppermute(mine, "ctx", [(i, i ^ 1) for i in range(count)])
    is_mine = (jnp.arange(CORES) == core).reshape((1, CORES) + (1,) * block.ndim)
    return jnp.where(is_mine, mine[:, None], other[:, None]).reshape((count,) + block.shape)


def gather_fsdp(values, axis=0):
    return lax.all_gather(values, "fsdp", axis=axis, tiled=True)


def scatter_fsdp(values):
    return lax.psum_scatter(values, "fsdp", scatter_dimension=0, tiled=True)


def remote(src, dst, sems, slot, device):
    return pltpu.make_async_remote_copy(
        src_ref=src,
        dst_ref=dst,
        send_sem=sems[0].at[slot],
        recv_sem=sems[1].at[slot],
        device_id=device,
        device_id_type=pl.DeviceIdType.MESH,
    )


class Line:
    def __init__(self, source, blocks, sems, base, place, chips, stride=None, offset=0):
        self.source, self.sems, self.base, self.chips = source, sems, base, chips
        self.ctx, self.shard = place
        self.chip = self.ctx // CORES
        rows = source.shape[0]
        stride = stride or rows
        self.block = lambda index: blocks.at[pl.ds(pl.multiple_of(index * stride + offset, rows), rows)]
        self.swap_base = base + 2 * (chips - 1)
        self.own_slot = base + 4 * (chips - 1)

    @staticmethod
    def slots(chips):
        return 4 * (chips - 1) + 2

    def hop(self, up, number):
        step = 1 if up else -1
        slot = (0 if up else self.chips - 1) + number - 1
        origin = self.ctx - step * (number - 1) * CORES
        if up:
            sends = (self.chip >= number - 1) & (self.chip < self.chips - 1)
            gets = self.chip >= number
        else:
            sends = (self.chip <= self.chips - number) & (self.chip > 0)
            gets = self.chip <= self.chips - 1 - number
        return slot, step, origin, sends, gets

    def send(self, up, number):
        slot, step, origin, sends, _ = self.hop(up, number)

        @pl.when(sends)
        def _():
            remote(
                self.source if number == 1 else self.block(origin),
                self.block(origin),
                self.sems,
                self.base + slot,
                (self.ctx + step * CORES, self.shard),
            ).start()

    def start(self):
        self.send(True, 1)
        self.send(False, 1)
        remote(
            self.source, self.block(self.ctx), self.sems, self.own_slot, (self.ctx ^ 1, self.shard)
        ).start()
        self.local = pltpu.make_async_copy(
            self.source, self.block(self.ctx), self.sems[0].at[self.own_slot + 1]
        )
        self.local.start()

    def land(self, number):
        for up in (True, False):
            slot, step, origin, _, gets = self.hop(up, number)
            block = self.block(origin - step * CORES)

            @pl.when(gets)
            def _(block=block, slot=slot):
                remote(
                    block, block, self.sems, self.base + slot, (self.ctx ^ 1, self.shard)
                ).wait_recv()

            if number < self.chips - 1:
                self.send(up, number + 1)

            @pl.when(gets)
            def _(block=block, slot=slot):
                remote(
                    block, block, self.sems, self.swap_base + slot, (self.ctx ^ 1, self.shard)
                ).start()

    def arrived(self):
        other = self.block(self.ctx ^ 1)
        remote(other, other, self.sems, self.own_slot, (self.ctx ^ 1, self.shard)).wait_recv()
        self.local.wait()
        for up in (True, False):
            for number in range(1, self.chips):
                slot, step, origin, _, gets = self.hop(up, number)
                block = self.block((origin - step * CORES) ^ 1)

                @pl.when(gets)
                def _(block=block, slot=slot):
                    remote(
                        block, block, self.sems, self.swap_base + slot, (self.ctx ^ 1, self.shard)
                    ).wait_recv()

    def sent(self):
        source = self.source
        peer = (self.ctx ^ 1, self.shard)
        remote(source, source, self.sems, self.own_slot, peer).wait_send()
        for up in (True, False):
            for number in range(1, self.chips):
                slot, _, _, sends, gets = self.hop(up, number)

                @pl.when(sends)
                def _(slot=slot):
                    remote(source, source, self.sems, self.base + slot, peer).wait_send()

                @pl.when(gets)
                def _(slot=slot):
                    remote(source, source, self.sems, self.swap_base + slot, peer).wait_send()


class Square:
    SLOTS = 8

    def __init__(self, pieces, blocks, sems, base, place):
        self.pieces, self.sems, self.base = pieces, sems, base
        self.ctx, self.shard = place
        half = blocks.shape[0] // 8

        def part(owner, which, columns=slice(None)):
            start = pl.multiple_of((2 * owner + which) * half, half)
            return blocks.at[pl.ds(start, half), columns]

        self.part = part

    def to(self, bit):
        return (self.ctx, self.shard ^ bit)

    def own(self, bit, which):
        for source, columns in self.pieces(which):
            remote(
                source,
                self.part(self.shard, which, columns),
                self.sems,
                self.base + 2 * (bit - 1) + which,
                self.to(bit),
            ).start()

    def start(self):
        self.own(1, 0)
        self.own(2, 1)
        self.own(1, 1)
        self.own(2, 0)
        for which in (0, 1):
            for source, columns in self.pieces(which):
                pltpu.make_async_copy(
                    source,
                    self.part(self.shard, which, columns),
                    self.sems[0].at[self.base + 6 + which],
                ).start()

    def wait(self, owner, which, slot, bit):
        part = self.part(owner, which)
        remote(part, part, self.sems, self.base + slot, self.to(bit)).wait_recv()

    def forward(self):
        for bit in (1, 2):
            which = bit - 1
            owner = self.shard ^ bit
            self.wait(owner, which, 2 * (bit - 1) + which, bit)
            part = self.part(owner, which)
            remote(part, part, self.sems, self.base + 4 + which, self.to(3 - bit)).start()

    def arrived(self):
        self.wait(self.shard ^ 1, 1, 1, 1)
        self.wait(self.shard ^ 2, 0, 2, 2)
        self.wait(self.shard ^ 3, 0, 4, 2)
        self.wait(self.shard ^ 3, 1, 5, 1)
        for which in (0, 1):
            part = self.part(self.shard, which)
            pltpu.make_async_copy(part, part, self.sems[0].at[self.base + 6 + which]).wait()

    def sent(self):
        for slot in range(6):
            part = self.part(self.shard, 0)
            remote(part, part, self.sems, self.base + slot, self.to(1)).wait_send()


class Tree:
    SLOTS = 8

    def __init__(self, source, block, sems, base, place, owner):
        self.source, self.block, self.sems, self.base = source, block, sems, base
        self.ctx, self.shard = place
        self.turn = self.shard ^ owner
        self.half = block.shape[0] // 2

    def rows(self, ref, which):
        return ref.at[pl.ds(which * self.half, self.half)]

    def copy(self, ref, which, slot, bit):
        return remote(
            self.rows(ref, which),
            self.rows(self.block, which),
            self.sems,
            self.base + slot,
            (self.ctx, self.shard ^ bit),
        )

    def start(self):
        @pl.when(self.turn == 0)
        def _():
            self.copy(self.source, 0, 0, 1).start()
            self.copy(self.source, 1, 3, 2).start()
            self.copy(self.source, 1, 1, 1).start()
            self.copy(self.source, 0, 2, 2).start()
            pltpu.make_async_copy(self.source, self.block, self.sems[0].at[self.base + 6]).start()

    def forward(self):
        for bit in (1, 2):
            which = bit - 1

            @pl.when(self.turn == bit)
            def _(bit=bit, which=which):
                self.copy(self.block, which, 2 * (bit - 1) + which, bit).wait_recv()
                self.copy(self.block, which, 4 + which, 3 - bit).start()

    def arrived(self):
        @pl.when(self.turn == 0)
        def _():
            pltpu.make_async_copy(self.source, self.block, self.sems[0].at[self.base + 6]).wait()

        for bit in (1, 2):

            @pl.when(self.turn == bit)
            def _(bit=bit):
                which = 2 - bit
                self.copy(self.block, which, 2 * (bit - 1) + which, bit).wait_recv()

        @pl.when(self.turn == 3)
        def _():
            self.copy(self.block, 0, 4, 2).wait_recv()
            self.copy(self.block, 1, 5, 1).wait_recv()

    def sent(self):
        @pl.when(self.turn == 0)
        def _():
            for slot in range(4):
                self.copy(self.block, 0, slot, 1).wait_send()

        for bit in (1, 2):

            @pl.when(self.turn == bit)
            def _(bit=bit):
                self.copy(self.block, bit - 1, 3 + bit, 3 - bit).wait_send()


def add_rows(dst, sources):
    step = 32

    def body(index, carry):
        rows = pl.ds(pl.multiple_of(index * step, step), step)
        total = sources[0][rows].astype(jnp.float32)
        for source in sources[1:]:
            total += source[rows].astype(jnp.float32)
        dst[rows] = total.astype(dst.dtype)
        return carry

    lax.fori_loop(0, dst.shape[0] // step, body, 0)


class Fold:
    SLOTS = 6

    def __init__(self, parts, landing, stage, carry, final, sems, local, base, place):
        self.parts, self.landing, self.stage, self.carry, self.final = parts, landing, stage, carry, final
        self.sems, self.local, self.base = sems, local, base
        self.ctx, self.shard = place
        self.half = final.shape[0] // 2

    def part(self, owner, which):
        start = pl.multiple_of((2 * owner + which) * self.half, self.half)
        return self.parts.at[pl.ds(start, self.half)]

    def landed(self, slot):
        return self.landing.at[pl.ds(slot * self.half, self.half)]

    def copy(self, src, slot, bit):
        return remote(
            src, self.landed(slot), self.sems, self.base + slot, (self.ctx, self.shard ^ bit)
        )

    def send(self, slot):
        bit, which = (1, 0) if slot < 2 else (2, 1)
        owner = self.shard ^ (3 if slot % 2 else bit)
        self.copy(self.part(owner, which), slot, bit).start()

    def add(self, dst, sources):
        copies = []
        for index, source in enumerate(sources):
            copies.append(
                pltpu.make_async_copy(source, self.stage.at[index], self.local.at[index])
            )
            copies[-1].start()
        for copy in copies:
            copy.wait()
        add_rows(dst, [self.stage.at[index] for index in range(len(sources))])

    def wait(self, slot, bit):
        self.copy(self.landed(slot), slot, bit).wait_recv()

    def middle(self, which):
        first, second = (1, 2) if which == 0 else (2, 1)
        slot = 1 + 2 * which
        self.wait(slot, first)
        carry = self.carry.at[which]
        self.add(carry, [self.part(self.shard ^ second, which), self.landed(slot)])
        self.copy(carry, 4 + which, second).start()

    def finish(self, which):
        first, second = (1, 2) if which == 0 else (2, 1)
        self.wait(2 * which, first)
        self.wait(4 + which, second)
        self.add(
            self.final.at[pl.ds(which * self.half, self.half)],
            [self.part(self.shard, which), self.landed(2 * which), self.landed(4 + which)],
        )

    def sent(self):
        for slot in range(6):
            self.copy(self.part(self.shard, 0), slot, 1).wait_send()


class Sink:
    def __init__(self, parts, swapped, landing, stage, carry, final, sems, local, base, place, chips):
        self.parts, self.swapped, self.landing, self.stage = parts, swapped, landing, stage
        self.carry, self.final, self.sems, self.local, self.base = carry, final, sems, local, base
        self.ctx, self.shard = place
        self.chip, self.core, self.chips = self.ctx // CORES, self.ctx % CORES, chips
        self.rows = final.shape[0]

    @staticmethod
    def slots(chips):
        return 2 * (chips - 1) + 1

    def block(self, ref, index):
        return ref.at[pl.ds(pl.multiple_of(index * self.rows, self.rows), self.rows)]

    def start(self):
        for chip in range(self.chips):
            remote(
                self.block(self.parts, CORES * chip + (self.core ^ 1)),
                self.block(self.swapped, chip),
                self.sems,
                self.base,
                (self.ctx ^ 1, self.shard),
            ).start()

    def swap(self):
        swapped = self.swapped
        remote(swapped, swapped, self.sems, self.base, (self.ctx ^ 1, self.shard)).wait_recv()

    def hop(self, up, step):
        place = self.chip if up else self.chips - 1 - self.chip
        target = place + self.chips - step
        target = target if up else self.chips - 1 - target
        slot = (0 if up else self.chips - 1) + step - 1
        sends = (place + 1 <= step) & (place < self.chips - 1)
        gets = (place <= step) & (place > 0)
        return slot, target, sends, gets, place > 0

    def landed(self, slot):
        return self.landing.at[pl.ds(slot * self.rows, self.rows)]

    def copy(self, up, slot):
        way = CORES if up else -CORES
        return remote(
            self.carry.at[0 if up else 1],
            self.landed(slot),
            self.sems,
            self.base + 1 + slot,
            (self.ctx + way, self.shard),
        )

    def load(self, index, source):
        return pltpu.make_async_copy(source, self.stage.at[index], self.local.at[index])

    def own(self, target):
        return [
            self.load(0, self.block(self.parts, CORES * target + self.core)),
            self.load(1, self.block(self.swapped, target)),
        ]

    def step(self, number):
        for up in (True, False):
            slot, target, sends, _, passes = self.hop(up, number)
            if number > 1:
                before, _, sent, gets, _ = self.hop(up, number - 1)

                @pl.when(gets)
                def _(before=before, up=up):
                    remote(
                        self.landed(before), self.landed(before), self.sems, self.base + 1 + before,
                        (self.ctx ^ 1, self.shard),
                    ).wait_recv()

                @pl.when(sent)
                def _(before=before, up=up):
                    self.copy(up, before).wait_send()

            @pl.when(sends)
            def _(up=up, slot=slot, target=target, passes=passes):
                loads = self.own(target)
                for load in loads:
                    load.start()
                carry = self.carry.at[0 if up else 1]
                stage = self.stage
                if number > 1:

                    @pl.when(passes)
                    def _():
                        more = self.load(2, self.landed(slot - 1))
                        more.start()
                        for load in loads + [more]:
                            load.wait()
                        add_rows(carry, [stage.at[0], stage.at[1], stage.at[2]])

                    @pl.when(jnp.logical_not(passes))
                    def _():
                        for load in loads:
                            load.wait()
                        add_rows(carry, [stage.at[0], stage.at[1]])
                else:
                    for load in loads:
                        load.wait()
                    add_rows(carry, [stage.at[0], stage.at[1]])
                self.copy(up, slot).start()

    def finish(self, dst, sem):
        loads = self.own(self.chip)
        for load in loads:
            load.start()
        for load in loads:
            load.wait()
        add_rows(self.final, [self.stage.at[0], self.stage.at[1]])
        for up in (True, False):
            slot, _, sends, gets, _ = self.hop(up, self.chips - 1)

            @pl.when(gets)
            def _(slot=slot):
                landed = self.landed(slot)
                remote(
                    landed, landed, self.sems, self.base + 1 + slot, (self.ctx ^ 1, self.shard)
                ).wait_recv()
                load = self.load(2, landed)
                load.start()
                load.wait()
                add_rows(self.final, [self.final, self.stage.at[2]])

            @pl.when(sends)
            def _(up=up, slot=slot):
                self.copy(up, slot).wait_send()

        swapped = self.swapped
        remote(swapped, swapped, self.sems, self.base, (self.ctx ^ 1, self.shard)).wait_send()
        copy = pltpu.make_async_copy(self.final, dst, sem)
        copy.start()
        copy.wait()


TILE = 256


def block_kernel(
    sizes,
    hidden, grad, fc1, fc2, qkv, dense, segs, tables,
    ln1_gain, ln1_bias, ln2_gain, ln2_bias, dense_bias, fc2_bias, qkv_bias, fc1_bias,
    vec_out, output_out, input_out, down_all, up_all, qkv_all, dense_all, sums_all,
    down_parts, up_parts, qkv_parts, dense_parts, down_land, up_land, qkv_land, dense_land,
    out_parts, out_swap, out_land, in_parts, in_swap, in_land, dense_lines,
    hid, gra, norm, w_up, w_down, w_qkv, w_dense, vec, seg, seg_col, table,
    act, wide_f, d_up, queries, keys, values, att_f, att, d_keys, d_values, d_joined, sums, sums_got, sums_tot,
    stage, down_stage, up_stage,
    down_carry, up_carry, qkv_carry, dense_carry, down_final, up_final, qkv_final, dense_final,
    out_carry, in_carry, sink_final,
    send_sems, recv_sems, local_sems,
):
    chips, shards, columns = sizes
    place = ctx, shard = lax.axis_index("ctx"), lax.axis_index("fsdp")
    chip, core = ctx // CORES, ctx % CORES
    count = CORES * chips
    sems = (send_sems, recv_sems)
    width, length = hidden.shape[1], hid.shape[0]
    ff_units = w_down.shape[0]
    head_dim = w_dense.shape[0]
    row_size = vec.shape[3]
    tiles = length // TILE
    f32, bf16 = jnp.float32, jnp.bfloat16
    factor = head_dim ** (-0.5)

    barrier = pltpu.get_barrier_semaphore()
    peers = [(ctx, shard ^ bit) for bit in (1, 2, 3)]
    peers += [(lax.rem(ctx + step, count), shard) for step in range(1, count)]
    for peer in peers:
        pl.semaphore_signal(barrier, inc=1, device_id=peer, device_id_type=pl.DeviceIdType.MESH)
    pl.semaphore_wait(barrier, len(peers))

    base = 0

    def take(slots):
        nonlocal base
        base += slots
        return base - slots

    def line(source, blocks, stride=None, offset=0):
        return Line(source, blocks, sems, take(Line.slots(chips)), place, chips, stride, offset)

    def line_pair(final, blocks):
        half = final.shape[0] // 2
        return [
            line(final.at[pl.ds(which * half, half)], blocks, final.shape[0], which * half)
            for which in (0, 1)
        ]

    def fold(parts, landing, stage, carry, final):
        return Fold(
            parts, landing, stage, carry, final, sems, local_sems.at[pl.ds(4, 4)], take(Fold.SLOTS), place
        )

    def sink(parts, swapped, landing, carry):
        return Sink(
            parts, swapped, landing, down_stage, carry, sink_final, sems, local_sems.at[pl.ds(4, 4)],
            take(Sink.slots(chips)), place, chips,
        )

    def halves(ref, which, start, size):
        half = ref.shape[0] // 2
        return ref.at[pl.ds(which * half, half), pl.ds(pl.multiple_of(start, size), size)]

    def up_pieces(which):
        stride = fc1.shape[1] // shards
        return [
            (
                halves(fc1, which, index * stride + ctx * columns, columns),
                pl.ds(index * columns, columns),
            )
            for index in range(shards)
        ]

    def down_pieces(which):
        half = columns // 2
        start = pl.multiple_of(ctx * columns + which * half, half)
        return [(fc2.at[pl.ds(start, half)], slice(None))]

    def qkv_pieces(which):
        return [
            (
                halves(qkv, which, index * width + ctx * head_dim, head_dim),
                pl.ds(index * head_dim, head_dim),
            )
            for index in range(3)
        ]

    hid_line, gra_line = line(hidden, hid), line(grad, gra)
    squares = [
        Square(pieces, blocks, sems, take(Square.SLOTS), place)
        for pieces, blocks in ((up_pieces, w_up), (down_pieces, w_down), (qkv_pieces, w_qkv))
    ]
    up_square, down_square, qkv_square = squares
    heads_here = dense.shape[0] // head_dim
    dense_rows = dense.at[
        pl.ds(pl.multiple_of(lax.rem(ctx, heads_here) * head_dim, head_dim), head_dim)
    ]
    tree = Tree(dense_rows, w_dense, sems, take(Tree.SLOTS), place, ctx // heads_here)
    down_fold = fold(down_parts, down_land, down_stage, down_carry, down_final)
    up_fold = fold(up_parts, up_land, up_stage, up_carry, up_final)
    qkv_fold = fold(
        qkv_parts, qkv_land, up_stage.at[:, :, : 3 * head_dim], qkv_carry, qkv_final
    )
    dense_fold = fold(
        dense_parts, dense_land, down_stage.at[:, :, : width // shards], dense_carry, dense_final
    )
    down_lines = line_pair(down_final, down_all)
    up_lines = line_pair(up_final, up_all)
    qkv_lines = line_pair(qkv_final, qkv_all)
    dense_line = line(dense_final, dense_lines)
    sums_line = line(sums_tot, sums_all)
    out_sink = sink(out_parts, out_swap, out_land, out_carry)
    in_sink = sink(in_parts, in_swap, in_land, in_carry)

    small = []

    def send_small(src, dst, landing, device):
        slot = take(1)
        small.append((remote(src, dst, sems, slot, device), landing, slot))

    vectors = (
        ln1_gain, ln1_bias, ln2_gain, ln2_bias, dense_bias, fc2_bias, qkv_bias, fc1_bias
    )
    at, pairs = 0, [(segs, seg.at[ctx]), (tables, table)]
    for vector in vectors:
        pairs.append((vector, vec.at[shard, pl.ds(at, vector.shape[0])]))
        at += vector.shape[0]
    locals_in = [
        pltpu.make_async_copy(src, dst, local_sems.at[8 + index])
        for index, (src, dst) in enumerate(pairs)
    ]
    for copy in locals_in:
        copy.start()

    hid_line.start()
    up_square.start()
    for copy in locals_in:
        copy.wait()
    for bit in (1, 2, 3):
        send_small(vec.at[shard], vec.at[shard], vec.at[shard ^ bit], (ctx, shard ^ bit))
    for step in range(1, count):
        send_small(
            segs, seg.at[ctx], seg.at[lax.rem(ctx + count - step, count)],
            (lax.rem(ctx + step, count), shard),
        )
    for copy, _, _ in small:
        copy.start()
    hid_line.land(1)
    up_square.forward()
    down_square.start()
    hid_line.land(2)
    gra_line.start()
    hid_line.land(3)
    for _, landing, slot in small:
        remote(landing, landing, sems, slot, (ctx ^ 1, shard)).wait_recv()
    hid_line.arrived()

    def vector(row):
        return jnp.concatenate([vec[index, row] for index in range(shards)], axis=1)

    def rows_of(index):
        return pl.ds(pl.multiple_of(index * TILE, TILE), TILE)

    def loop(body, steps=tiles):
        lax.fori_loop(0, steps, lambda index, carry: (body(rows_of(index)), carry)[1], 0)

    def scaled_rows(rows):
        return centred(hid[rows])[0]

    def norm_two(rows):
        norm[rows] = (scaled_rows(rows) * vector(2) + vector(3)).astype(bf16)

    def norm_one(rows):
        norm[rows] = (scaled_rows(rows) * vector(0) + vector(1)).astype(bf16)

    def emit(steps, compute, dst, size):
        def write(index):
            slot = lax.rem(index, 2)
            return pltpu.make_async_copy(
                stage.at[slot, :, :size], dst.at[rows_of(index)], local_sems.at[slot]
            )

        def body(index, carry):
            @pl.when(index >= 2)
            def _():
                write(index - 2).wait()

            stage[lax.rem(index, 2), :, :size] = compute(index).astype(bf16)
            write(index).start()
            return carry

        lax.fori_loop(0, steps, body, 0)
        write(steps - 2).wait()
        write(steps - 1).wait()

    loop(norm_two)
    up_square.arrived()
    down_square.forward()
    gra_line.land(1)

    bias_start = ctx * columns
    bias_row = 9 + bias_start // row_size
    bias_column = pl.multiple_of(lax.rem(bias_start, row_size), columns)
    up_bias = jnp.concatenate(
        [vec[index, bias_row, :, pl.ds(bias_column, columns)] for index in range(shards)],
        axis=1,
    )

    def feed_forward(rows):
        value = dot(norm[rows], w_up[...]) + up_bias
        cdf = 0.5 * (1.0 + lax.erf(value * (0.5**0.5)))
        density = jnp.exp(-0.5 * value * value) * ((2.0 * math.pi) ** -0.5)
        act[rows] = (value * cdf).astype(bf16)
        wide_f[rows] = cdf + value * density

    loop(feed_forward)
    gra_line.land(2)
    down_square.arrived()
    gra_line.land(3)
    gra_line.arrived()

    def fc2_grad(index, carry):
        owner = shard ^ (3 - index)
        rows = rows_of(owner)
        stage[0] = dot_rows(act[:, rows], gra[...]).astype(bf16)
        write = pltpu.make_async_copy(stage.at[0], down_parts.at[rows], local_sems.at[0])
        write.start()
        write.wait()
        for step, slot in ((0, 1), (1, 2), (2, 0)):

            @pl.when(index == step)
            def _(slot=slot):
                down_fold.send(slot)

        return carry

    lax.fori_loop(0, shards, fc2_grad, 0)

    def feed_back(rows):
        d_up[rows] = (dot_cols(gra[rows], w_down[...]) * wide_f[rows]).astype(bf16)

    loop(feed_back)
    down_fold.middle(0)
    down_fold.send(3)
    emit(
        width // TILE,
        lambda index: dot_rows(norm[:, rows_of(index)], d_up[...]),
        up_parts,
        ff_units,
    )
    down_fold.finish(0)
    down_lines[0].start()
    qkv_square.start()
    loop(norm_one)
    down_fold.middle(1)
    down_lines[0].land(1)
    qkv_square.forward()
    for slot in (1, 2, 0):
        up_fold.send(slot)
    tree.start()
    down_lines[0].land(2)
    down_fold.finish(1)
    down_lines[1].start()

    per = 3 * HEADS // shards
    bias_parts = []
    for index in range(3):
        at = index * HEADS + ctx
        rest = lax.rem(at, per) * head_dim
        bias_parts.append(
            vec[
                at // per,
                6 + rest // row_size,
                :,
                pl.ds(pl.multiple_of(lax.rem(rest, row_size), head_dim), head_dim),
            ]
        )
    rotary = table.shape[2]

    def turn(entries, rows, way):
        first = entries[:, :rotary]
        first = (
            first * table[0, rows]
            + way * (pltpu.roll(first, ROT // 2, 1) * table[1, rows])
            + way * (pltpu.roll(first, rotary - ROT // 2, 1) * table[2, rows])
        )
        return jnp.concatenate([first, entries[:, rotary:]], axis=1)

    def project(rows):
        joined = dot(norm[rows], w_qkv[...])
        parts = [
            joined[:, index * head_dim : (index + 1) * head_dim] + bias_parts[index]
            for index in range(3)
        ]
        queries[rows] = turn(parts[0], rows, 1.0).astype(bf16)
        keys[rows] = turn(parts[1], rows, 1.0).astype(bf16)
        values[rows] = parts[2].astype(bf16)

    seg_row = jnp.concatenate([seg[index] for index in range(count)], axis=1)
    side = segs.shape[1]
    for index in range(count):
        block = seg[index].astype(f32)
        seg_col[index * side : (index + 1) * side] = jnp.broadcast_to(block, (side, side)).T

    qkv_square.arrived()
    loop(project)
    down_lines[0].land(3)
    down_lines[1].land(1)
    up_fold.middle(0)
    up_fold.send(3)
    tree.forward()

    def attend(index):
        rows = pl.ds(index * TILE, TILE)
        size = (index + 1) * TILE
        scores = dot_cols(queries[rows], keys[:size]) * factor
        query_place = index * TILE + lax.broadcasted_iota(jnp.int32, (TILE, size), 0)
        key_place = lax.broadcasted_iota(jnp.int32, (TILE, size), 1)
        same = seg_col[rows][:, :1] == seg_row[:, :size].astype(f32)
        allowed = (key_place <= query_place) & same
        scores = jnp.where(allowed, scores, -1e30)
        terms = jnp.where(
            allowed, jnp.exp(scores - jnp.max(scores, axis=-1, keepdims=True)), 0.0
        )
        probs = terms / jnp.sum(terms, axis=-1, keepdims=True)
        wide_f[rows, :size] = probs
        result = dot(probs.astype(bf16), values[:size])
        att_f[rows] = result
        att[rows] = result.astype(bf16)

    attend(0)
    attend(1)
    down_lines[1].land(2)
    up_fold.finish(0)
    up_lines[0].start()
    attend(2)
    attend(3)
    up_fold.middle(1)
    tree.arrived()

    def output(index):
        rows = rows_of(index)
        return dot(att[rows], w_dense[...]) + dot(act[rows], w_down[...])

    emit(tiles, output, out_parts, width)
    out_sink.start()
    down_lines[1].land(3)
    up_lines[0].land(1)
    up_fold.finish(1)
    up_lines[1].start()

    dense_size = width // shards

    def dense_grad(index):
        start = pl.multiple_of(index * dense_size, dense_size)
        return dot_rows(att[...], gra[:, pl.ds(start, dense_size)])

    emit(shards, dense_grad, dense_parts, dense_size)
    for slot in (1, 2, 0, 3):
        dense_fold.send(slot)
    out_sink.swap()
    out_sink.step(1)

    d_keys[...] = jnp.zeros_like(d_keys)
    d_values[...] = jnp.zeros_like(d_values)

    def attend_back(index):
        rows = pl.ds(index * TILE, TILE)
        size = (index + 1) * TILE
        d_att = dot_cols(gra[rows], w_dense[...]).astype(bf16)
        delta = jnp.sum(d_att.astype(f32) * att_f[rows], axis=-1, keepdims=True)
        probs = wide_f[rows, :size]
        d_scores = (probs * (dot_cols(d_att, values[:size]) - delta)).astype(bf16)
        d_queries = dot(d_scores, keys[:size]) * factor
        d_joined[rows, :head_dim] = turn(d_queries, rows, -1.0).astype(bf16)
        d_keys[:size] += dot_rows(d_scores, queries[rows])
        d_values[:size] += dot_rows(probs.astype(bf16), d_att)

    attend_back(0)
    attend_back(1)
    up_lines[0].land(2)
    dense_fold.middle(0)
    dense_fold.middle(1)
    attend_back(2)
    attend_back(3)
    up_lines[1].land(1)

    def join(rows):
        d_joined[rows, head_dim : 2 * head_dim] = turn(d_keys[rows] * factor, rows, -1.0).astype(bf16)
        d_joined[rows, 2 * head_dim :] = d_values[rows].astype(bf16)

    loop(join)
    emit(
        width // TILE,
        lambda index: dot_rows(norm[:, rows_of(index)], d_joined[...]),
        qkv_parts,
        3 * head_dim,
    )
    for slot in (1, 2, 0, 3):
        qkv_fold.send(slot)
    out_sink.step(2)
    dense_fold.finish(0)
    dense_fold.finish(1)
    dense_line.start()
    up_lines[0].land(3)
    up_lines[1].land(2)
    qkv_fold.middle(0)
    qkv_fold.middle(1)

    sums[...] = jnp.zeros_like(sums)

    def inputs(index):
        rows = rows_of(index)
        d_one = dot_cols(d_joined[rows], w_qkv[...])
        d_two = dot_cols(d_up[rows], w_up[...])
        scaled = scaled_rows(rows)

        def gather(row, entries):
            sums[row : row + 1, : entries.shape[1]] += jnp.sum(
                entries.astype(f32), axis=0, keepdims=True
            )

        gather(0, d_two * scaled)
        gather(1, d_two)
        gather(2, gra[rows])
        gather(3, d_up[rows])
        gather(4, d_one * scaled)
        gather(5, d_one)
        gather(6, d_joined[rows])
        return d_one * vector(0) + d_two * vector(2)

    emit(tiles, inputs, in_parts, width)
    in_sink.start()
    sums_sent = []
    for bit in (1, 2, 3):
        slot = take(1)
        copy = remote(sums, sums_got.at[shard], sems, slot, (ctx, shard ^ bit))
        copy.start()
        sums_sent.append((copy, sums_got.at[shard ^ bit], slot))
    sums_got[shard] = sums[...]
    dense_line.land(1)
    out_sink.step(3)
    up_lines[1].land(3)
    qkv_fold.finish(0)
    qkv_lines[0].start()
    qkv_fold.finish(1)
    qkv_lines[1].start()
    in_sink.swap()
    in_sink.step(1)
    dense_line.land(2)
    for copy, landing, slot in sums_sent:
        remote(landing, landing, sems, slot, (ctx ^ 1, shard)).wait_recv()
    total = sums_got[0]
    for index in range(1, shards):
        total = total + sums_got[index]
    sums_tot[...] = total
    sums_line.start()
    dense_line.land(3)
    qkv_lines[0].land(1)
    in_sink.step(2)
    sums_line.land(1)
    qkv_lines[1].land(1)
    dense_line.arrived()
    dense_block = dense_size
    exchanged = []
    for bit in (1, 2, 3):
        slot = take(1)
        peer = shard ^ bit
        rows = pl.ds(pl.multiple_of(peer * dense_block, dense_block), dense_block)
        own_rows = pl.ds(pl.multiple_of(shard * dense_block, dense_block), dense_block)
        copy = remote(dense_lines.at[rows], dense_all.at[own_rows], sems, slot, (ctx, peer))
        copy.start()
        exchanged.append((copy, dense_all.at[rows], slot))
    own_dense = pltpu.make_async_copy(
        dense_lines.at[own_rows], dense_all.at[own_rows], local_sems.at[2]
    )
    own_dense.start()
    out_sink.finish(output_out, local_sems.at[3])
    qkv_lines[0].land(2)
    in_sink.step(3)
    sums_line.land(2)
    qkv_lines[1].land(2)
    qkv_lines[0].land(3)
    sums_line.land(3)
    qkv_lines[1].land(3)
    in_sink.finish(input_out, local_sems.at[3])

    write_vec = pltpu.make_async_copy(vec, vec_out, local_sems.at[8])
    write_vec.start()
    lines = down_lines + up_lines + qkv_lines + [sums_line]
    for item in lines:
        item.arrived()
    for copy, landing, slot in exchanged:
        remote(landing, landing, sems, slot, (ctx ^ 1, shard)).wait_recv()
    own_dense.wait()
    for item in [hid_line, gra_line, dense_line] + lines + squares + [tree]:
        item.sent()
    for item in (down_fold, up_fold, qkv_fold, dense_fold):
        item.sent()
    for copy, _, _ in small + sums_sent + exchanged:
        copy.wait_send()
    write_vec.wait()


def rotary_table(length, lanes):
    half = ROT // 2
    freqs = (10000.0 ** (-2.0 * np.arange(half, dtype=np.float32) / ROT)).astype(np.float32)
    angles = np.arange(length, dtype=np.float32)[:, None] * freqs[None]
    cosine, sine = np.cos(angles), np.sin(angles)
    table = np.zeros((3, length, lanes), np.float32)
    table[0] = 1.0
    table[0, :, :half], table[0, :, half:ROT] = cosine, cosine
    table[1, :, half:ROT] = sine
    table[2, :, :half] = -sine
    return table


def whole_block(hidden, grad, fc1, fc2, qkv, dense, segs, vectors):
    chips, shards = lax.axis_size("ctx") // CORES, lax.axis_size("fsdp")
    count = chips * CORES
    tokens, width = hidden.shape
    length = tokens * count
    units = fc1.shape[1] // count
    head_dim = width // HEADS
    part = units // shards
    rows = width // shards
    bf16, f32 = jnp.bfloat16, jnp.float32
    wide, joint = (length, width), 3 * head_dim
    vectors = [vector.reshape(-1, 1, rows) for vector in vectors]
    vec_shape = (shards, sum(vector.shape[0] for vector in vectors), 1, rows)
    seg_shape = (count,) + segs.shape
    line = (tokens, width)
    hops = (2 * (chips - 1) * tokens, width)
    outs = [
        (vec_shape, f32), (line, f32), (line, f32), ((count * part, width), bf16), ((count * rows, units), bf16),
        ((count * rows, joint), bf16), ((width, rows), bf16), ((count * 8, width), f32),
        ((units, width), bf16), ((width, units), bf16), ((width, joint), bf16), ((shards * head_dim, rows), bf16),
        ((3 * part, width), bf16), ((3 * rows, units), bf16), ((3 * rows, joint), bf16), ((3 * head_dim, rows), bf16),
        (wide, bf16), ((chips * tokens, width), bf16), (hops, bf16),
        (wide, bf16), ((chips * tokens, width), bf16), (hops, bf16), ((count * head_dim, rows), bf16),
    ]
    table = rotary_table(length, 128)
    halves = [(part // 2, width), (rows // 2, units), (rows // 2, joint), (head_dim // 2, rows)]
    scratch = [
        (wide, bf16), (wide, bf16), (wide, bf16), ((width, units), bf16), ((units, width), bf16),
        ((width, joint), bf16), ((head_dim, width), bf16), (vec_shape, f32), (seg_shape, segs.dtype),
        ((length, segs.shape[1]), f32), (table.shape, f32),
        ((length, units), bf16), ((length, max(units, length)), f32), ((length, units), bf16),
        ((length, head_dim), bf16), ((length, head_dim), bf16), ((length, head_dim), bf16),
        ((length, head_dim), f32), ((length, head_dim), bf16), ((length, head_dim), f32), ((length, head_dim), f32),
        ((length, joint), bf16), ((8, width), f32), ((shards, 8, width), f32), ((8, width), f32),
        ((2, TILE, width), bf16),
    ]
    scratch += [((3,) + half, bf16) for half in halves[:2]]
    scratch += [((2,) + half, bf16) for half in halves]
    scratch += [((2 * half[0], half[1]), bf16) for half in halves]
    scratch += [((2, tokens, width), bf16), ((2, tokens, width), bf16), (line, f32)]
    slots = (
        10 * Line.slots(chips) + 3 * Square.SLOTS + Tree.SLOTS + 4 * Fold.SLOTS + 2 * Sink.slots(chips)
        + 9 + count - 1
    )
    outputs = pl.pallas_call(
        functools.partial(block_kernel, (chips, shards, part)),
        out_shape=[jax.ShapeDtypeStruct(shape, kind) for shape, kind in outs],
        in_specs=[pl.BlockSpec(memory_space=pl.ANY)] * 16,
        out_specs=[pl.BlockSpec(memory_space=pl.ANY)] * len(outs),
        scratch_shapes=[pltpu.VMEM(shape, kind) for shape, kind in scratch]
        + [
            pltpu.SemaphoreType.DMA((slots,)),
            pltpu.SemaphoreType.DMA((slots,)),
            pltpu.SemaphoreType.DMA((18,)),
        ],
        compiler_params=pltpu.CompilerParams(
            collective_id=0, has_side_effects=True, vmem_limit_bytes=62 * 2**20
        ),
        name="whole_block",
    )(hidden, grad, fc1, fc2, qkv, dense, segs, jnp.asarray(table), *vectors)
    return outputs[:8]


FINISH_STEPS = 16


def finish_kernel(
    sizes,
    up_all, qkv_all, dense_all, down_all, vec, branch, back, hidden, grad, sums,
    output, input_grad, gain_one, shift_one, qkv, qkv_bias, dense, columns_one, gain_two, shift_two, up, up_bias,
    down, columns_two,
):
    count, shards = sizes
    f32 = jnp.float32

    def spread(src, dst, pieces):
        groups, size = src.shape[0], src.shape[2] // pieces
        for piece in range(pieces):
            for group in range(groups):
                start = (piece * groups + group) * size
                dst[:, start : start + size] = src[group, :, piece * size : (piece + 1) * size].astype(f32)

    spread(up_all, up, shards)
    spread(qkv_all, qkv, 3)
    spread(dense_all, dense, 1)
    down[...] = down_all[...].astype(f32)

    @pl.when(pl.program_id(0) == 0)
    def _():
        own = hidden[...].astype(f32)
        shift = jnp.concatenate([vec[index, 4] + vec[index, 5] for index in range(shards)], axis=1)
        output[...] = (own + branch[...] + shift).astype(output.dtype)
        scaled, spread_own = centred(own)
        e = back[...]
        part = spread_own * (
            e
            - jnp.mean(e, axis=-1, keepdims=True)
            - scaled * jnp.mean(e * scaled, axis=-1, keepdims=True)
        )
        input_grad[...] = (grad[...].astype(f32) + part).astype(input_grad.dtype)

        shard = lax.axis_index("fsdp")
        rows = gain_one.shape[1]
        mine = pl.ds(pl.multiple_of(shard * rows, rows), rows)
        for row, dst in ((0, gain_two), (1, shift_two), (4, gain_one), (5, shift_one)):
            total = sums[0, row : row + 1, mine]
            for index in range(1, count):
                total = total + sums[index, row : row + 1, mine]
            dst[...] = total
        columns_one[...] = sums[0, 2:3, mine]
        columns_two[...] = sums[0, 2:3, mine]
        part = up_bias.shape[1] // count
        here = pl.ds(pl.multiple_of(shard * part, part), part)
        for index in range(count):
            up_bias[:, index * part : (index + 1) * part] = sums[index, 3:4, here]
        size = 3 * hidden.shape[1] // (3 * count)
        chunks = qkv_bias.shape[1] // size
        for chunk in range(chunks):
            place = shard * chunks + chunk
            start = pl.multiple_of(place // count * size, size)
            qkv_bias[:, chunk * size : (chunk + 1) * size] = sums[
                lax.rem(place, count), 6:7, pl.ds(start, size)
            ]


def finish(up_all, qkv_all, dense_all, down_all, vec, branch, back, hidden, grad, sums):
    count, shards = lax.axis_size("ctx"), lax.axis_size("fsdp")
    tokens, width = hidden.shape
    rows = width // shards
    f32 = jnp.float32
    steps = FINISH_STEPS

    def sliced(shape):
        block = shape[:-2] + (shape[-2] // steps, shape[-1])
        return pl.BlockSpec(block, lambda index: (0,) * (len(shape) - 2) + (index, 0))

    def entire(shape):
        return pl.BlockSpec(shape, lambda index: (0,) * len(shape))

    grads = [
        up_all.reshape(count, rows, -1), qkv_all.reshape(count, rows, -1), dense_all.reshape(shards, rows, rows),
        down_all,
    ]
    units = up_all.shape[1] * count
    sums = sums.reshape(count, 8, width)
    others = [vec, branch, back, hidden, grad, sums]
    vector = (1, rows)
    outs = [
        ((tokens, width), hidden.dtype, entire), ((tokens, width), hidden.dtype, entire),
        (vector, f32, entire), (vector, f32, entire), ((rows, 3 * width), f32, sliced),
        ((1, 3 * rows), f32, entire), ((rows, width), f32, sliced), (vector, f32, entire),
        (vector, f32, entire), (vector, f32, entire), ((rows, units), f32, sliced),
        ((1, units // shards), f32, entire), (down_all.shape, f32, sliced), (vector, f32, entire),
    ]
    return pl.pallas_call(
        functools.partial(finish_kernel, (count, shards)),
        grid=(steps,),
        in_specs=[sliced(array.shape) for array in grads] + [entire(array.shape) for array in others],
        out_specs=[kind(shape) for shape, _, kind in outs],
        out_shape=[jax.ShapeDtypeStruct(shape, dtype) for shape, dtype, _ in outs],
        compiler_params=pltpu.CompilerParams(vmem_limit_bytes=48 * 2**20),
        name="finish",
    )(*grads, *others)


def one_kernel(
    hidden, qkv_weight, dense_weight, fc1_weight, fc2_weight, segments, out_grad, vectors
):
    vec, branch, back, down_all, up_all, qkv_all, dense_all, sums_all = whole_block(
        hidden[0], out_grad[0], fc1_weight, fc2_weight, qkv_weight, dense_weight, segments, vectors
    )
    outs = finish(
        up_all, qkv_all, dense_all, down_all, vec, branch, back, hidden[0], out_grad[0], sums_all
    )
    outs = [out.reshape(-1) if out.shape[0] == 1 else out for out in outs]
    return (outs[0][None], outs[1][None], *outs[2:])


def per_device(
    hidden,
    ln1_gain,
    ln1_bias,
    qkv_weight,
    qkv_bias,
    dense_weight,
    dense_bias,
    ln2_gain,
    ln2_bias,
    fc1_weight,
    fc1_bias,
    fc2_weight,
    fc2_bias,
    segments,
    out_grad,
):
    ctx_count = lax.axis_size("ctx")
    shards = lax.axis_size("fsdp")
    ctx = lax.axis_index("ctx")
    tokens, width = hidden.shape[1], hidden.shape[2]
    length = tokens * ctx_count
    head_dim = width // HEADS
    repeat = ctx_count // HEADS
    head = ctx // repeat
    factor = head_dim ** (-0.5)
    rows = width // shards
    ff = fc1_weight.shape[1]
    units = ff // shards // ctx_count
    bf16, f32 = jnp.bfloat16, jnp.float32

    vectors = [ln1_gain, ln1_bias, ln2_gain, ln2_bias, dense_bias, fc2_bias, qkv_bias, fc1_bias]
    if ctx_count == HEADS and shards == 4:
        return one_kernel(
            hidden, qkv_weight, dense_weight, fc1_weight, fc2_weight, segments, out_grad, vectors
        )
    vectors = jnp.concatenate(vectors).reshape(-1, rows)
    vec = lax.all_gather(vectors, "fsdp", axis=0)
    query_seg = lax.all_gather(segments[0], "ctx", axis=0, tiled=True)
    up_part = lax.dynamic_index_in_dim(
        fc1_weight.reshape(rows, shards, ctx_count, units), ctx, 2, keepdims=False
    ).reshape(rows, shards * units)
    down_part = lax.dynamic_slice_in_dim(fc2_weight, ctx * units, units, 0)
    qkv_part = lax.dynamic_index_in_dim(
        qkv_weight.reshape(rows, 3, HEADS, head_dim), head, 2, keepdims=False
    ).reshape(rows, 3 * head_dim)
    dense_cols = lax.all_to_all(
        dense_weight, "fsdp", split_axis=1, concat_axis=0, tiled=True
    )
    dense_part = lax.dynamic_slice_in_dim(dense_cols, head * head_dim, head_dim, 0)
    up_w = gather_fsdp(up_part)
    down_w = gather_fsdp(down_part)
    qkv_w = gather_fsdp(qkv_part)
    dense_w = gather_fsdp(dense_part, axis=1)
    hidden_all = line_gather(hidden[0]).reshape(length, width)
    grad_all = line_gather(out_grad[0]).reshape(length, width)
    normed_one = (centred(hidden_all)[0] * vec[:, 0].reshape(-1) + vec[:, 1].reshape(-1)).astype(bf16)
    scaled = centred(hidden_all)[0]
    gain_two = vec[:, 2].reshape(-1)
    normed_two = (scaled * gain_two + vec[:, 3].reshape(-1)).astype(bf16)
    up_shift = lax.dynamic_index_in_dim(
        vec[:, 9 : 9 + ff // width].reshape(shards, ctx_count, units), ctx, 1, keepdims=False
    ).reshape(-1)
    act_f, slope = gelu_and_slope(dot(normed_two, up_w) + up_shift)
    act = act_f.astype(bf16)
    d_up = (dot_cols(grad_all, down_w) * slope).astype(bf16)
    down_part_grad = dot_rows(act, grad_all).astype(bf16)
    up_part_grad = dot_rows(normed_two, d_up).astype(bf16)
    ff_part = dot(act, down_w).astype(bf16)
    d_two = dot_cols(d_up, up_w)
    e_two = (d_two * gain_two).astype(bf16)
    gain_two_sum, shift_two_sum = jnp.sum(d_two * scaled, axis=0), jnp.sum(d_two, axis=0)
    columns = jnp.sum(grad_all.astype(f32), axis=0)
    up_sum = jnp.sum(d_up.astype(f32), axis=0)
    gain_one = vec[:, 0].reshape(-1)
    dense_shift, down_shift = vec[:, 4].reshape(-1), vec[:, 5].reshape(-1)
    qkv_shift = vec[:, 6:9].reshape(-1)
    down_grad = scatter_fsdp(down_part_grad)
    up_grad = scatter_fsdp(up_part_grad)

    qkv_shift_part = lax.dynamic_index_in_dim(
        qkv_shift.reshape(3, HEADS, head_dim), head, 1, keepdims=False
    ).reshape(-1)
    joined = dot(normed_one, qkv_w) + qkv_shift_part
    places = jnp.arange(length, dtype=jnp.int32)
    cosine, sine = rotary_tables(places, ROT)
    queries = rotate(joined[:, :head_dim], cosine, sine).astype(bf16)
    keys = rotate(joined[:, head_dim : 2 * head_dim], cosine, sine).astype(bf16)
    values = joined[:, 2 * head_dim :].astype(bf16)
    allowed = (places[None, :] <= places[:, None]) & (query_seg[None, :] == query_seg[:, None])
    if repeat > 1:
        allowed = allowed & (places // (length // repeat) == ctx % repeat)[:, None]
    scores = jnp.where(allowed, dot_cols(queries, keys) * factor, -1e30)
    top = jnp.max(scores, axis=-1, keepdims=True)
    terms = jnp.where(allowed, jnp.exp(scores - top), 0.0)
    total = jnp.sum(terms, axis=-1, keepdims=True)
    probs = terms * jnp.where(total > 0.0, 1.0 / total, 0.0)
    probs_low = probs.astype(bf16)
    att_f = dot(probs_low, values)
    att = att_f.astype(bf16)
    partial = dot(att, dense_w) + ff_part.astype(f32)
    branch = lax.psum_scatter(partial.astype(bf16), "ctx", scatter_dimension=0, tiled=True)
    own = hidden[0].astype(f32)
    layer_output = (own + branch.astype(f32) + dense_shift + down_shift).astype(bf16)

    d_att = dot_cols(grad_all, dense_w).astype(bf16)
    delta = jnp.sum(d_att.astype(f32) * att_f, axis=-1, keepdims=True)
    dense_grad = dot_rows(att, grad_all).astype(bf16)
    d_scores = (probs * (dot_cols(d_att, values) - delta)).astype(bf16)
    d_queries = rotate(dot(d_scores, keys) * factor, cosine, -sine)
    d_keys = rotate(dot_rows(d_scores, queries) * factor, cosine, -sine)
    d_values = dot_rows(probs_low, d_att)
    d_joined = jnp.concatenate([d_queries, d_keys, d_values], axis=1).astype(bf16)
    qkv_grad = dot_rows(normed_one, d_joined).astype(bf16)

    d_one = dot_cols(d_joined, qkv_w)
    both = (d_one * gain_one + e_two.astype(f32)).astype(bf16)
    back = lax.psum_scatter(both, "ctx", scatter_dimension=0, tiled=True).astype(f32)
    own_scaled, own_spread = centred(own)
    input_part = own_spread * (
        back
        - jnp.mean(back, axis=-1, keepdims=True)
        - own_scaled * jnp.mean(back * own_scaled, axis=-1, keepdims=True)
    )
    input_grad = (out_grad[0].astype(f32) + input_part).astype(bf16)

    first = (ctx == 0).astype(f32)
    joined_sum = jnp.sum(d_joined.astype(f32), axis=0).reshape(3, 1, head_dim)
    joined_full = jnp.where((jnp.arange(HEADS) == head)[None, :, None], joined_sum, 0.0)
    up_sum = up_sum.reshape(shards, 1, units)
    up_full = jnp.where((jnp.arange(ctx_count) == ctx)[None, :, None], up_sum, 0.0)
    small = [
        jnp.sum(d_one * centred(hidden_all)[0], axis=0),
        jnp.sum(d_one, axis=0),
        columns * first,
        gain_two_sum,
        shift_two_sum,
        joined_full,
        up_full,
    ]
    small = jnp.concatenate([piece.reshape(shards, -1) for piece in small], axis=1).astype(bf16)
    small_size = small.shape[1]
    small_rows = -(-small_size // (3 * head_dim * 16)) * 16
    small = jnp.pad(small, ((0, 0), (0, small_rows * 3 * head_dim - small_size)))
    last_grad = scatter_fsdp(
        jnp.concatenate(
            [
                qkv_grad.reshape(shards, rows, 3 * head_dim),
                small.reshape(shards, small_rows, 3 * head_dim),
            ],
            axis=1,
        ).reshape(-1, 3 * head_dim)
    )
    dense_share = scatter_fsdp(
        dense_grad.reshape(head_dim, shards, rows).transpose(1, 0, 2).reshape(-1, rows)
    )

    down_all = line_gather(down_grad).astype(f32).reshape(ctx_count * units, width)
    up_all = (
        line_gather(up_grad)
        .astype(f32)
        .reshape(ctx_count, rows, shards, units)
        .transpose(1, 2, 0, 3)
        .reshape(rows, ff)
    )
    dense_cols_all = line_gather(dense_share)
    if repeat > 1:
        dense_cols_all = jnp.sum(
            dense_cols_all.astype(f32).reshape(HEADS, repeat, head_dim, rows), axis=1
        ).astype(bf16)
    dense_all = lax.all_to_all(
        dense_cols_all.reshape(width, rows), "fsdp", split_axis=0, concat_axis=1, tiled=True
    ).astype(f32)
    last_all = line_gather(last_grad)
    qkv_all = last_all[:, :rows].astype(f32)
    if repeat > 1:
        qkv_all = jnp.sum(qkv_all.reshape(HEADS, repeat, rows, 3 * head_dim), axis=1)
    qkv_all = (
        qkv_all.reshape(HEADS, rows, 3, head_dim).transpose(1, 2, 0, 3).reshape(rows, 3 * width)
    )
    small_all = jnp.sum(last_all[:, rows:].astype(f32), axis=0).reshape(-1)
    sizes = [rows] * 5 + [3 * rows, ff // shards]
    parts, at = [], 0
    for size in sizes:
        parts.append(small_all[at : at + size])
        at += size
    gain_one_grad, shift_one_grad, columns_grad, gain_two_grad, shift_two_grad, joined_grad, up_b_grad = parts
    return (
        layer_output[None],
        input_grad[None],
        gain_one_grad,
        shift_one_grad,
        qkv_all,
        joined_grad,
        dense_all,
        columns_grad,
        gain_two_grad,
        shift_two_grad,
        up_all,
        up_b_grad,
        down_all,
        columns_grad,
    )


def solution(mesh):
    vec, mat, act = P("fsdp"), P("fsdp", None), P("fsdp", "ctx", None)
    return jax.shard_map(
        per_device,
        mesh=mesh,
        in_specs=(
            act, vec, vec, mat, vec, mat, vec, vec, vec, mat, vec, mat, vec, P("fsdp", "ctx"), act
        ),
        out_specs=(act, act, vec, vec, mat, vec, mat, vec, vec, vec, mat, vec, mat, vec),
        check_vma=False,
    )
```

```python
import functools
import math

import jax
import jax.numpy as jnp
import numpy as np
from jax import lax
from jax.experimental import pallas as pl
from jax.experimental.pallas import tpu as pltpu
from jax.sharding import PartitionSpec as P

HEADS = 8
ROT = 64
CORES = 2


def dot(left, right):
    return jnp.dot(left, right, preferred_element_type=jnp.float32)


def dot_rows(left, right):
    return lax.dot_general(
        left, right, (((0,), (0,)), ((), ())), preferred_element_type=jnp.float32
    )


def dot_cols(left, right):
    return lax.dot_general(
        left, right, (((1,), (1,)), ((), ())), preferred_element_type=jnp.float32
    )


def gelu_and_slope(values):
    cdf = 0.5 * (1.0 + lax.erf(values * (0.5**0.5)))
    density = jnp.exp(-0.5 * values * values) * ((2.0 * jnp.pi) ** -0.5)
    return values * cdf, cdf + values * density


def centred(values):
    values = values.astype(jnp.float32)
    center = values - jnp.mean(values, axis=-1, keepdims=True)
    spread = lax.rsqrt(jnp.mean(center * center, axis=-1, keepdims=True) + 1e-05)
    return center * spread, spread


def rotary_tables(places, width):
    half_rot = width // 2
    freqs = 10000.0 ** (-2.0 * jnp.arange(half_rot, dtype=jnp.float32) / width)
    angles = places.astype(jnp.float32)[:, None] * freqs[None, :]
    return (jnp.cos(angles), jnp.sin(angles))


def rotate(values, cosine, sine):
    half = cosine.shape[-1]
    first, second, remain = values[:, :half], values[:, half : 2 * half], values[:, 2 * half :]
    return jnp.concatenate(
        [first * cosine - second * sine, second * cosine + first * sine, remain], axis=1
    )


def line_gather(block):
    count = lax.axis_size("ctx")
    chips = count // CORES
    ctx = lax.axis_index("ctx")
    place, core = ctx // CORES, ctx % CORES
    up = down = block
    ups, downs = [], []
    for hop in range(1, chips):
        up = lax.ppermute(
            up,
            "ctx",
            [
                (i * CORES + k, (i + 1) * CORES + k)
                for i in range(hop - 1, chips - 1)
                for k in range(CORES)
            ],
        )
        down = lax.ppermute(
            down,
            "ctx",
            [
                (i * CORES + k, (i - 1) * CORES + k)
                for i in range(1, chips - hop + 1)
                for k in range(CORES)
            ],
        )
        ups.append(up)
        downs.append(down)
    around = jnp.stack(ups[::-1] + [block] + downs)
    mine = lax.dynamic_slice_in_dim(around, chips - 1 - place, chips, 0)
    other = lax.ppermute(mine, "ctx", [(i, i ^ 1) for i in range(count)])
    is_mine = (jnp.arange(CORES) == core).reshape((1, CORES) + (1,) * block.ndim)
    return jnp.where(is_mine, mine[:, None], other[:, None]).reshape((count,) + block.shape)


def gather_fsdp(values, axis=0):
    return lax.all_gather(values, "fsdp", axis=axis, tiled=True)


def scatter_fsdp(values):
    return lax.psum_scatter(values, "fsdp", scatter_dimension=0, tiled=True)


def remote(src, dst, sems, slot, device):
    return pltpu.make_async_remote_copy(
        src_ref=src,
        dst_ref=dst,
        send_sem=sems[0].at[slot],
        recv_sem=sems[1].at[slot],
        device_id=device,
        device_id_type=pl.DeviceIdType.MESH,
    )


class Line:
    def __init__(self, source, blocks, sems, base, place, chips, stride=None, offset=0, columns=slice(None)):
        self.source, self.sems, self.base, self.chips = source, sems, base, chips
        self.ctx, self.shard = place
        self.chip = self.ctx // CORES
        rows = source.shape[0]
        stride = stride or rows
        self.block = lambda index: blocks.at[
            pl.ds(pl.multiple_of(index * stride + offset, rows), rows), columns
        ]
        self.swap_base = base + 2 * (chips - 1)
        self.own_slot = base + 4 * (chips - 1)

    @staticmethod
    def slots(chips):
        return 4 * (chips - 1) + 2

    def hop(self, out, number):
        up = (self.chip >= self.chips // 2) == out
        place = jnp.where(up, self.chip, self.chips - 1 - self.chip)
        step = jnp.where(up, CORES, -CORES)
        slot = jnp.where(up, 0, self.chips - 1) + number - 1
        sends = (place >= number - 1) & (place < self.chips - 1)
        return slot, step, self.ctx - step * (number - 1), sends, place >= number

    def send(self, out, number):
        slot, step, origin, sends, _ = self.hop(out, number)

        @pl.when(sends)
        def _():
            remote(
                self.source if number == 1 else self.block(origin),
                self.block(origin),
                self.sems,
                self.base + slot,
                (self.ctx + step, self.shard),
            ).start()

    def start(self):
        self.send(True, 1)
        self.send(False, 1)
        remote(
            self.source, self.block(self.ctx), self.sems, self.own_slot, (self.ctx ^ 1, self.shard)
        ).start()
        self.local = pltpu.make_async_copy(
            self.source, self.block(self.ctx), self.sems[0].at[self.own_slot + 1]
        )
        self.local.start()

    def land(self, out, number):
        slot, step, origin, _, gets = self.hop(out, number)
        block = self.block(origin - step)

        @pl.when(gets)
        def _():
            remote(
                block, block, self.sems, self.base + slot, (self.ctx ^ 1, self.shard)
            ).wait_recv()

        if number < self.chips - 1:
            self.send(out, number + 1)

        @pl.when(gets)
        def _():
            remote(
                block, block, self.sems, self.swap_base + slot, (self.ctx ^ 1, self.shard)
            ).start()

    def out(self, number):
        self.land(True, number)

    def inward(self, number):
        self.land(False, number)

    def arrived(self):
        other = self.block(self.ctx ^ 1)
        remote(other, other, self.sems, self.own_slot, (self.ctx ^ 1, self.shard)).wait_recv()
        self.local.wait()
        for out in (True, False):
            for number in range(1, self.chips):
                slot, step, origin, _, gets = self.hop(out, number)
                block = self.block((origin - step) ^ 1)

                @pl.when(gets)
                def _(block=block, slot=slot):
                    remote(
                        block, block, self.sems, self.swap_base + slot, (self.ctx ^ 1, self.shard)
                    ).wait_recv()

    def sent(self):
        source = self.source
        peer = (self.ctx ^ 1, self.shard)
        remote(source, source, self.sems, self.own_slot, peer).wait_send()
        for out in (True, False):
            for number in range(1, self.chips):
                slot, _, _, sends, gets = self.hop(out, number)

                @pl.when(sends)
                def _(slot=slot):
                    remote(source, source, self.sems, self.base + slot, peer).wait_send()

                @pl.when(gets)
                def _(slot=slot):
                    remote(source, source, self.sems, self.swap_base + slot, peer).wait_send()


class Square:
    SLOTS = 8

    def __init__(self, pieces, blocks, sems, base, place):
        self.pieces, self.sems, self.base = pieces, sems, base
        self.ctx, self.shard = place
        half = blocks.shape[0] // 8

        def part(owner, which, columns=slice(None)):
            start = pl.multiple_of((2 * owner + which) * half, half)
            return blocks.at[pl.ds(start, half), columns]

        self.part = part

    def to(self, bit):
        return (self.ctx, self.shard ^ bit)

    def own(self, bit, which):
        for source, columns in self.pieces(which):
            remote(
                source,
                self.part(self.shard, which, columns),
                self.sems,
                self.base + 2 * (bit - 1) + which,
                self.to(bit),
            ).start()

    def start(self, part):
        self.own(1, part)
        self.own(2, 1 - part)
        if part == 1:
            return
        for which in (0, 1):
            for source, columns in self.pieces(which):
                pltpu.make_async_copy(
                    source,
                    self.part(self.shard, which, columns),
                    self.sems[0].at[self.base + 6 + which],
                ).start()

    def wait(self, owner, which, slot, bit):
        part = self.part(owner, which)
        remote(part, part, self.sems, self.base + slot, self.to(bit)).wait_recv()

    def forward(self):
        for bit in (1, 2):
            which = bit - 1
            owner = self.shard ^ bit
            self.wait(owner, which, 2 * (bit - 1) + which, bit)
            part = self.part(owner, which)
            remote(part, part, self.sems, self.base + 4 + which, self.to(3 - bit)).start()

    def arrived(self):
        self.wait(self.shard ^ 1, 1, 1, 1)
        self.wait(self.shard ^ 2, 0, 2, 2)
        self.wait(self.shard ^ 3, 0, 4, 2)
        self.wait(self.shard ^ 3, 1, 5, 1)
        for which in (0, 1):
            part = self.part(self.shard, which)
            pltpu.make_async_copy(part, part, self.sems[0].at[self.base + 6 + which]).wait()

    def sent(self):
        for slot in range(6):
            part = self.part(self.shard, 0)
            remote(part, part, self.sems, self.base + slot, self.to(1)).wait_send()


class Tree:
    SLOTS = 7

    def __init__(self, source, block, sems, base, place, owner):
        self.source, self.block, self.sems, self.base = source, block, sems, base
        self.ctx, self.shard = place
        self.turn = self.shard ^ owner
        self.half = block.shape[0] // 2

    def rows(self, ref, which):
        return ref.at[pl.ds(which * self.half, self.half)]

    def copy(self, slot, ref=None):
        which = slot % 2
        bit = 1 if slot in (0, 3, 4) else 2
        return remote(
            self.rows(self.block if ref is None else ref, which),
            self.rows(self.block, which),
            self.sems,
            self.base + slot,
            (self.ctx, self.shard ^ bit),
        )

    def at(self, turn, body):
        pl.when(self.turn == turn)(body)

    def start(self):
        def body():
            self.copy(0, self.source).start()
            self.copy(1, self.source).start()
            pltpu.make_async_copy(self.source, self.block, self.sems[0].at[self.base + 6]).start()

        self.at(0, body)

    def forward(self):
        for turn, slot in ((1, 0), (2, 1)):

            def body(slot=slot):
                self.copy(slot).wait_recv()
                self.copy(slot + 2).start()

            self.at(turn, body)

    def back(self):
        def body():
            for slot in (2, 3):
                self.copy(slot).wait_recv()
                self.copy(slot + 2).start()

        self.at(3, body)

    def arrived(self):
        def body():
            pltpu.make_async_copy(self.source, self.block, self.sems[0].at[self.base + 6]).wait()

        self.at(0, body)
        self.at(1, lambda: self.copy(5).wait_recv())
        self.at(2, lambda: self.copy(4).wait_recv())

    def sent(self):
        for turn, slots in ((0, (0, 1)), (1, (2,)), (2, (3,)), (3, (4, 5))):

            def body(slots=slots):
                for slot in slots:
                    self.copy(slot).wait_send()

            self.at(turn, body)


def add_rows(dst, sources):
    step = 32

    def body(index, carry):
        rows = pl.ds(pl.multiple_of(index * step, step), step)
        total = sources[0][rows].astype(jnp.float32)
        for source in sources[1:]:
            total += source[rows].astype(jnp.float32)
        dst[rows] = total.astype(dst.dtype)
        return carry

    lax.fori_loop(0, dst.shape[0] // step, body, 0)


class Fold:
    SLOTS = 6

    def __init__(self, parts, landing, stage, carry, final, sems, local, base, place):
        self.parts, self.landing, self.stage, self.carry, self.final = parts, landing, stage, carry, final
        self.sems, self.local, self.base = sems, local, base
        self.ctx, self.shard = place
        self.half = final.shape[0] // 2

    def part(self, owner, which):
        start = pl.multiple_of((2 * owner + which) * self.half, self.half)
        return self.parts.at[pl.ds(start, self.half)]

    def landed(self, slot):
        return self.landing.at[pl.ds(slot * self.half, self.half)]

    def copy(self, src, slot, bit):
        return remote(
            src, self.landed(slot), self.sems, self.base + slot, (self.ctx, self.shard ^ bit)
        )

    def send(self, slot):
        bit, which = (1, 0) if slot < 2 else (2, 1)
        owner = self.shard ^ (3 if slot % 2 else bit)
        self.copy(self.part(owner, which), slot, bit).start()

    def add(self, dst, sources):
        copies = []
        for index, source in enumerate(sources):
            copies.append(
                pltpu.make_async_copy(source, self.stage.at[index], self.local.at[index])
            )
            copies[-1].start()
        for copy in copies:
            copy.wait()
        add_rows(dst, [self.stage.at[index] for index in range(len(sources))])

    def wait(self, slot, bit):
        self.copy(self.landed(slot), slot, bit).wait_recv()

    def middle(self, which):
        first, second = (1, 2) if which == 0 else (2, 1)
        slot = 1 + 2 * which
        self.wait(slot, first)
        carry = self.carry.at[which]
        self.add(carry, [self.part(self.shard ^ second, which), self.landed(slot)])
        self.copy(carry, 4 + which, second).start()

    def finish(self, which):
        first, second = (1, 2) if which == 0 else (2, 1)
        self.wait(2 * which, first)
        self.wait(4 + which, second)
        self.add(
            self.final.at[pl.ds(which * self.half, self.half)],
            [self.part(self.shard, which), self.landed(2 * which), self.landed(4 + which)],
        )

    def sent(self):
        for slot in range(6):
            self.copy(self.part(self.shard, 0), slot, 1).wait_send()


class Sink:
    def __init__(self, parts, swapped, landing, stage, carry, final, sems, local, base, place, chips):
        self.parts, self.swapped, self.landing, self.stage = parts, swapped, landing, stage
        self.carry, self.final, self.sems, self.local, self.base = carry, final, sems, local, base
        self.ctx, self.shard = place
        self.chip, self.core, self.chips = self.ctx // CORES, self.ctx % CORES, chips
        self.rows = final.shape[0]

    @staticmethod
    def slots(chips):
        return 2 * (chips - 1) + 1

    def block(self, ref, index):
        return ref.at[pl.ds(pl.multiple_of(index * self.rows, self.rows), self.rows)]

    def start(self):
        for chip in range(self.chips):
            remote(
                self.block(self.parts, CORES * chip + (self.core ^ 1)),
                self.block(self.swapped, chip),
                self.sems,
                self.base,
                (self.ctx ^ 1, self.shard),
            ).start()

    def swap(self):
        swapped = self.swapped
        remote(swapped, swapped, self.sems, self.base, (self.ctx ^ 1, self.shard)).wait_recv()

    def hop(self, out, step):
        up = (self.chip >= self.chips // 2) == out
        place = jnp.where(up, self.chip, self.chips - 1 - self.chip)
        target = place + self.chips - step
        target = jnp.where(up, target, self.chips - 1 - target)
        slot = jnp.where(up, 0, self.chips - 1) + step - 1
        sends = (place + 1 <= step) & (place < self.chips - 1)
        gets = (place <= step) & (place > 0)
        return slot, target, sends, gets, place > 0

    def landed(self, slot):
        return self.landing.at[pl.ds(pl.multiple_of(slot * self.rows, self.rows), self.rows)]

    def copy(self, out, slot):
        up = (self.chip >= self.chips // 2) == out
        return remote(
            self.carry.at[0 if out else 1],
            self.landed(slot),
            self.sems,
            self.base + 1 + slot,
            (self.ctx + jnp.where(up, CORES, -CORES), self.shard),
        )

    def load(self, index, source):
        return pltpu.make_async_copy(source, self.stage.at[index], self.local.at[index])

    def own(self, target):
        return [
            self.load(0, self.block(self.parts, CORES * target + self.core)),
            self.load(1, self.block(self.swapped, target)),
        ]

    def step(self, out, number):
        slot, target, sends, _, passes = self.hop(out, number)
        if number > 1:
            before, _, sent, gets, _ = self.hop(out, number - 1)

            @pl.when(gets)
            def _():
                remote(
                    self.landed(before), self.landed(before), self.sems, self.base + 1 + before,
                    (self.ctx ^ 1, self.shard),
                ).wait_recv()

            @pl.when(sent)
            def _():
                self.copy(out, before).wait_send()

        @pl.when(sends)
        def _():
            loads = self.own(target)
            for load in loads:
                load.start()
            carry = self.carry.at[0 if out else 1]
            stage = self.stage
            if number > 1:

                @pl.when(passes)
                def _():
                    more = self.load(2, self.landed(slot - 1))
                    more.start()
                    for load in loads + [more]:
                        load.wait()
                    add_rows(carry, [stage.at[0], stage.at[1], stage.at[2]])

                @pl.when(jnp.logical_not(passes))
                def _():
                    for load in loads:
                        load.wait()
                    add_rows(carry, [stage.at[0], stage.at[1]])
            else:
                for load in loads:
                    load.wait()
                add_rows(carry, [stage.at[0], stage.at[1]])
            self.copy(out, slot).start()

    def inward(self, number):
        self.step(False, number)

    def last(self, handed, first, own, sem):
        number = self.chips - 1
        for out in (True, False):
            slot, target, sends, _, passes = self.hop(out, number)
            before, _, sent, gets, _ = self.hop(out, number - 1)

            @pl.when(gets)
            def _(before=before):
                remote(
                    self.landed(before), self.landed(before), self.sems, self.base + 1 + before,
                    (self.ctx ^ 1, self.shard),
                ).wait_recv()

            @pl.when(sent)
            def _(out=out, before=before):
                self.copy(out, before).wait_send()

            @pl.when(sends)
            def _(out=out, slot=slot, target=target, passes=passes):
                loads = self.own(target)
                for load in loads:
                    load.start()
                for load in loads:
                    load.wait()
                carry = self.carry.at[0 if out else 1]
                add_rows(carry, [self.stage.at[0], self.stage.at[1]])

                @pl.when(passes)
                def _():
                    more = self.load(2, self.landed(slot - 1))
                    more.start()
                    more.wait()
                    add_rows(carry, [self.stage.at[0], self.stage.at[1], self.stage.at[2]])

                up = (self.chip >= self.chips // 2) == out
                for way, dst in ((True, handed[0]), (False, handed[1])):

                    @pl.when(up == way)
                    def _(dst=dst):
                        write = pltpu.make_async_copy(carry, dst.at[pl.ds(first, self.rows)], sem)
                        write.start()
                        write.wait()

        loads = self.own(self.chip)
        for load in loads:
            load.start()
        for load in loads:
            load.wait()
        add_rows(self.final, [self.stage.at[0], self.stage.at[1]])
        swapped = self.swapped
        remote(swapped, swapped, self.sems, self.base, (self.ctx ^ 1, self.shard)).wait_send()
        write = pltpu.make_async_copy(self.final, own, sem)
        write.start()
        write.wait()


TILE = 256


def block_kernel(
    sizes,
    hidden, grad, fc1, fc2, qkv, dense, segs, tables,
    ln1_gain, ln1_bias, ln2_gain, ln2_bias, dense_bias, fc2_bias, qkv_bias, fc1_bias,
    output_out, input_out, up_out, down_out, down_all, up_all, qkv_all, dense_all, sums_all,
    down_parts, up_parts, qkv_parts, dense_parts, down_land, up_land, qkv_land, dense_land,
    out_parts, out_swap, out_land, in_parts, in_swap, in_land, dense_lines,
    hid, gra, norm, w_up, w_down, w_qkv, w_dense, vec, seg, seg_col, table,
    act, wide_f, d_up, queries, keys, values, att_f, att, d_keys, d_values, d_joined, sums, sums_got, sums_tot,
    stage, down_stage, up_stage,
    down_carry, up_carry, qkv_carry, dense_carry, down_final, up_final, qkv_final, dense_final,
    out_carry, in_carry, sink_final,
    send_sems, recv_sems, local_sems,
):
    chips, shards, columns = sizes
    place = ctx, shard = lax.axis_index("ctx"), lax.axis_index("fsdp")
    chip, core = ctx // CORES, ctx % CORES
    count = CORES * chips
    sems = (send_sems, recv_sems)
    width, length = hidden.shape[1], hid.shape[0]
    ff_units = w_down.shape[0]
    head_dim = w_dense.shape[0]
    row_size = vec.shape[3]
    tiles = length // TILE
    f32, bf16 = jnp.float32, jnp.bfloat16
    factor = head_dim ** (-0.5)

    barrier = pltpu.get_barrier_semaphore()
    peers = [(ctx, shard ^ bit) for bit in (1, 2, 3)]
    peers += [(lax.rem(ctx + step, count), shard) for step in range(1, count)]
    for peer in peers:
        pl.semaphore_signal(barrier, inc=1, device_id=peer, device_id_type=pl.DeviceIdType.MESH)
    pl.semaphore_wait(barrier, len(peers))

    base = 0

    def take(slots):
        nonlocal base
        base += slots
        return base - slots

    def line(source, blocks, stride=None, offset=0, cut=slice(None)):
        return Line(source, blocks, sems, take(Line.slots(chips)), place, chips, stride, offset, cut)

    def fold(parts, landing, stage, carry, final):
        return Fold(
            parts, landing, stage, carry, final, sems, local_sems.at[pl.ds(4, 4)], take(Fold.SLOTS), place
        )

    def sink(parts, swapped, landing, carry):
        return Sink(
            parts, swapped, landing, down_stage, carry, sink_final, sems, local_sems.at[pl.ds(4, 4)],
            take(Sink.slots(chips)), place, chips,
        )

    def halves(ref, which, start, size):
        half = ref.shape[0] // 2
        return ref.at[pl.ds(which * half, half), pl.ds(pl.multiple_of(start, size), size)]

    def up_pieces(which):
        stride = fc1.shape[1] // shards
        return [
            (
                halves(fc1, which, index * stride + ctx * columns, columns),
                pl.ds(index * columns, columns),
            )
            for index in range(shards)
        ]

    def down_pieces(which):
        half = columns // 2
        start = pl.multiple_of(ctx * columns + which * half, half)
        return [(fc2.at[pl.ds(start, half)], slice(None))]

    def qkv_pieces(which):
        return [
            (
                halves(qkv, which, index * width + ctx * head_dim, head_dim),
                pl.ds(index * head_dim, head_dim),
            )
            for index in range(3)
        ]

    hid_line, gra_line = line(hidden, hid), line(grad, gra)
    squares = [
        Square(pieces, blocks, sems, take(Square.SLOTS), place)
        for pieces, blocks in ((up_pieces, w_up), (down_pieces, w_down), (qkv_pieces, w_qkv))
    ]
    up_square, down_square, qkv_square = squares
    heads_here = dense.shape[0] // head_dim
    dense_rows = dense.at[
        pl.ds(pl.multiple_of(lax.rem(ctx, heads_here) * head_dim, head_dim), head_dim)
    ]
    tree = Tree(dense_rows, w_dense, sems, take(Tree.SLOTS), place, ctx // heads_here)
    named = {"hid": hid_line, "gra": gra_line, "wu": up_square, "wd": down_square, "wq": qkv_square, "wt": tree}
    folds, lines = [], []

    def gradient(letter, cuts, parts, landing, stage, carry, final, gathered):
        start, half = 0, final.shape[0] // 2
        for index, (size, split) in enumerate(cuts):
            cut = pl.ds(start, size)
            item = fold(
                parts.at[:, cut], landing.at[:, cut], stage.at[:, :, :size], carry.at[:, :, cut], final.at[:, cut]
            )
            folds.append(item)
            named[f"f{letter}{index}"] = item
            for which in range(2 if split else 1):
                rows = half if split else 2 * half
                item = line(
                    final.at[pl.ds(which * rows, rows), cut], gathered, final.shape[0], which * rows, cut
                )
                lines.append(item)
                named[f"l{letter}{index}{which}"] = item
            start += size

    gradient("d", DOWN_CUTS, down_parts, down_land, down_stage, down_carry, down_final, down_all)
    gradient("u", UP_CUTS, up_parts, up_land, up_stage, up_carry, up_final, up_all)
    gradient("q", QKV_CUTS, qkv_parts, qkv_land, up_stage, qkv_carry, qkv_final, qkv_all)
    gradient("e", DENSE_CUTS, dense_parts, dense_land, down_stage, dense_carry, dense_final, dense_lines)
    named["ls"] = line(sums_tot, sums_all)
    lines.append(named["ls"])
    out_sink = sink(out_parts, out_swap, out_land, out_carry)
    in_sink = sink(in_parts, in_swap, in_land, in_carry)
    named["so"], named["si"] = out_sink, in_sink

    small = []

    def send_small(src, dst, landing, device):
        slot = take(1)
        small.append((remote(src, dst, sems, slot, device), landing, slot))
        small[-1][0].start()

    def wait_small(items):
        for _, landing, slot in items:
            remote(landing, landing, sems, slot, (ctx ^ 1, shard)).wait_recv()

    vectors = (
        ln1_gain, ln1_bias, ln2_gain, ln2_bias, dense_bias, fc2_bias, qkv_bias, fc1_bias
    )
    at, pairs = 0, [(segs, seg.at[ctx]), (tables, table)]
    for vector in vectors:
        size = vec.shape[3]
        for start in range(0, vector.shape[0], size):
            pairs.append((vector.at[pl.ds(start, size)], vec.at[shard, at, 0]))
            at += 1
    locals_in = [
        pltpu.make_async_copy(src, dst, local_sems.at[8 + index])
        for index, (src, dst) in enumerate(pairs)
    ]
    for copy in locals_in:
        copy.start()

    def small_start():
        for copy in locals_in:
            copy.wait()
        for bit in (1, 2, 3):
            send_small(vec.at[shard], vec.at[shard], vec.at[shard ^ bit], (ctx, shard ^ bit))
        for step in range(1, count):
            send_small(
                segs, seg.at[ctx], seg.at[lax.rem(ctx + count - step, count)],
                (lax.rem(ctx + step, count), shard),
            )

    def small_land():
        wait_small(small)

    def vector(row):
        return jnp.concatenate([vec[index, row] for index in range(shards)], axis=1)

    def rows_of(index):
        return pl.ds(pl.multiple_of(index * TILE, TILE), TILE)

    def loop(body, steps=tiles):
        lax.fori_loop(0, steps, lambda index, carry: (body(rows_of(index)), carry)[1], 0)

    def scaled_rows(rows):
        return centred(hid[rows])[0]

    def norm_two(rows):
        norm[rows] = (scaled_rows(rows) * vector(2) + vector(3)).astype(bf16)

    def norm_one(rows):
        norm[rows] = (scaled_rows(rows) * vector(0) + vector(1)).astype(bf16)

    def emit(steps, compute, dst, size, start=0):
        def write(index):
            return pltpu.make_async_copy(
                stage.at[lax.rem(index, 2), :, :size],
                dst.at[rows_of(index), pl.ds(start, size)],
                local_sems.at[lax.rem(index, 2)],
            )

        def body(index, carry):
            @pl.when(index >= 2)
            def _():
                write(index - 2).wait()

            stage[lax.rem(index, 2), :, :size] = compute(index).astype(bf16)
            write(index).start()
            return carry

        lax.fori_loop(0, steps, body, 0)
        write(steps - 2).wait()
        write(steps - 1).wait()

    def feed_forward():
        bias_start = ctx * columns
        bias_row = 9 + bias_start // row_size
        bias_column = pl.multiple_of(lax.rem(bias_start, row_size), columns)
        up_bias = jnp.concatenate(
            [vec[index, bias_row, :, pl.ds(bias_column, columns)] for index in range(shards)],
            axis=1,
        )

        def body(rows):
            value = dot(norm[rows], w_up[...]) + up_bias
            cdf = 0.5 * (1.0 + lax.erf(value * (0.5**0.5)))
            density = jnp.exp(-0.5 * value * value) * ((2.0 * math.pi) ** -0.5)
            act[rows] = (value * cdf).astype(bf16)
            wide_f[rows] = cdf + value * density

        loop(body)

    def down_grad(index):
        start, size = sum(cut[0] for cut in DOWN_CUTS[:index]), DOWN_CUTS[index][0]

        def body(step, carry):
            rows = rows_of(shard ^ (3 - step))
            cut = pl.ds(start, size)
            stage[0, :, :size] = dot_rows(act[:, rows], gra[:, cut]).astype(bf16)
            write = pltpu.make_async_copy(
                stage.at[0, :, :size], down_parts.at[rows, cut], local_sems.at[0]
            )
            write.start()
            write.wait()
            for number, slot in ((0, 1), (0, 3), (1, 2), (2, 0)):

                @pl.when(step == number)
                def _(slot=slot):
                    named[f"fd{index}"].send(slot)

            return carry

        lax.fori_loop(0, shards, body, 0)

    def feed_back():
        def body(rows):
            d_up[rows] = (dot_cols(gra[rows], w_down[...]) * wide_f[rows]).astype(bf16)

        loop(body)

    def up_grad(index):
        start, size = sum(cut[0] for cut in UP_CUTS[:index]), UP_CUTS[index][0]
        emit(
            width // TILE,
            lambda step: dot_rows(norm[:, rows_of(step)], d_up[:, pl.ds(start, size)]),
            up_parts,
            size,
            start,
        )

    rotary = table.shape[2]

    def turn(entries, rows, way):
        first = entries[:, :rotary]
        first = (
            first * table[0, rows]
            + way * (pltpu.roll(first, ROT // 2, 1) * table[1, rows])
            + way * (pltpu.roll(first, rotary - ROT // 2, 1) * table[2, rows])
        )
        return jnp.concatenate([first, entries[:, rotary:]], axis=1)

    def project():
        per = 3 * HEADS // shards
        bias_parts = []
        for index in range(3):
            place = index * HEADS + ctx
            rest = lax.rem(place, per) * head_dim
            bias_parts.append(
                vec[
                    place // per,
                    6 + rest // row_size,
                    :,
                    pl.ds(pl.multiple_of(lax.rem(rest, row_size), head_dim), head_dim),
                ]
            )

        def body(rows):
            joined = dot(norm[rows], w_qkv[...])
            parts = [
                joined[:, index * head_dim : (index + 1) * head_dim] + bias_parts[index]
                for index in range(3)
            ]
            queries[rows] = turn(parts[0], rows, 1.0).astype(bf16)
            keys[rows] = turn(parts[1], rows, 1.0).astype(bf16)
            values[rows] = parts[2].astype(bf16)

        loop(body)
        side = segs.shape[1]
        for index in range(count):
            block = seg[index].astype(f32)
            seg_col[index * side : (index + 1) * side] = jnp.broadcast_to(block, (side, side)).T

    def attend(index):
        rows = pl.ds(index * TILE, TILE)
        size = (index + 1) * TILE
        seg_row = jnp.concatenate([seg[block] for block in range(count)], axis=1)
        scores = dot_cols(queries[rows], keys[:size]) * factor
        query_place = index * TILE + lax.broadcasted_iota(jnp.int32, (TILE, size), 0)
        key_place = lax.broadcasted_iota(jnp.int32, (TILE, size), 1)
        same = seg_col[rows][:, :1] == seg_row[:, :size].astype(f32)
        allowed = (key_place <= query_place) & same
        scores = jnp.where(allowed, scores, -1e30)
        terms = jnp.where(
            allowed, jnp.exp(scores - jnp.max(scores, axis=-1, keepdims=True)), 0.0
        )
        probs = terms / jnp.sum(terms, axis=-1, keepdims=True)
        wide_f[rows, :size] = probs
        result = dot(probs.astype(bf16), values[:size])
        att_f[rows] = result
        att[rows] = result.astype(bf16)

    def attend_all():
        for index in range(tiles):
            attend(index)

    def output():
        def body(index):
            rows = rows_of(index)
            return dot(att[rows], w_dense[...]) + dot(act[rows], w_down[...])

        emit(tiles, body, out_parts, width)

    dense_size = width // shards

    def dense_grad():
        def body(index):
            start = pl.multiple_of(index * dense_size, dense_size)
            return dot_rows(att[...], gra[:, pl.ds(start, dense_size)])

        emit(shards, body, dense_parts, dense_size)

    def attend_back(index):
        rows = pl.ds(index * TILE, TILE)
        size = (index + 1) * TILE
        d_att = dot_cols(gra[rows], w_dense[...]).astype(bf16)
        delta = jnp.sum(d_att.astype(f32) * att_f[rows], axis=-1, keepdims=True)
        probs = wide_f[rows, :size]
        d_scores = (probs * (dot_cols(d_att, values[:size]) - delta)).astype(bf16)
        d_queries = dot(d_scores, keys[:size]) * factor
        d_joined[rows, :head_dim] = turn(d_queries, rows, -1.0).astype(bf16)
        d_keys[:size] += dot_rows(d_scores, queries[rows])
        d_values[:size] += dot_rows(probs.astype(bf16), d_att)

    def attend_back_all():
        d_keys[...] = jnp.zeros_like(d_keys)
        d_values[...] = jnp.zeros_like(d_values)
        for index in range(tiles):
            attend_back(index)

        def join(rows):
            d_joined[rows, head_dim : 2 * head_dim] = turn(d_keys[rows] * factor, rows, -1.0).astype(bf16)
            d_joined[rows, 2 * head_dim :] = d_values[rows].astype(bf16)

        loop(join)

    def qkv_grad(index):
        start, size = sum(cut[0] for cut in QKV_CUTS[:index]), QKV_CUTS[index][0]
        emit(
            width // TILE,
            lambda step: dot_rows(norm[:, rows_of(step)], d_joined[:, pl.ds(start, size)]),
            qkv_parts,
            size,
            start,
        )

    def inputs():
        sums[...] = jnp.zeros_like(sums)

        def body(index):
            rows = rows_of(index)
            d_one = dot_cols(d_joined[rows], w_qkv[...])
            d_two = dot_cols(d_up[rows], w_up[...])
            scaled = scaled_rows(rows)

            def gather(row, entries):
                sums[row : row + 1, : entries.shape[1]] += jnp.sum(
                    entries.astype(f32), axis=0, keepdims=True
                )

            gather(0, d_two * scaled)
            gather(1, d_two)
            gather(2, gra[rows])
            gather(3, d_up[rows])
            gather(4, d_one * scaled)
            gather(5, d_one)
            gather(6, d_joined[rows])
            return d_one * vector(0) + d_two * vector(2)

        emit(tiles, body, in_parts, width)

    sums_items = []

    def sums_start():
        for bit in (1, 2, 3):
            send_small(sums, sums_got.at[shard], sums_got.at[shard ^ bit], (ctx, shard ^ bit))
            sums_items.append(small[-1])
        sums_got[shard] = sums[...]

    def sums_land():
        wait_small(sums_items)
        total = sums_got[0]
        for index in range(1, shards):
            total = total + sums_got[index]
        sums_tot[...] = total
        sums_tot[7:8] = vector(4) + vector(5)

    exchanged = []

    def dense_block(owner):
        return pl.ds(pl.multiple_of(owner * dense_size, dense_size), dense_size)

    def own_dense():
        return pltpu.make_async_copy(
            dense_lines.at[dense_block(shard)], dense_all.at[dense_block(shard)], local_sems.at[2]
        )

    def dense_part(owner, side):
        size = dense_size // CORES
        return pl.ds(pl.multiple_of(owner * dense_size + side * size, size), size)

    def exchange():
        for bit in (1, 2, 3):
            peer = shard ^ bit
            send_small(
                dense_lines.at[dense_part(peer, core)], dense_all.at[dense_part(shard, core)],
                dense_all.at[dense_part(peer, core)], (ctx, peer),
            )
            exchanged.append(small[-1])
        own_dense().start()

    relayed = []

    def relay():
        wait_small(exchanged)
        for bit in (1, 2, 3):
            rows = dense_part(shard ^ bit, core)
            send_small(
                dense_all.at[rows], dense_all.at[rows], dense_all.at[dense_part(shard ^ bit, 1 - core)],
                (ctx ^ 1, shard),
            )
            relayed.append(small[-1])

    def relay_done():
        wait_small(relayed)
        own_dense().wait()

    steps = {
        "small_start": small_start, "small_land": small_land, "norm_two": lambda: loop(norm_two),
        "norm_one": lambda: loop(norm_one), "feed_forward": feed_forward, "down_grad": down_grad,
        "feed_back": feed_back, "up_grad": up_grad, "project": project, "attend": attend_all, "output": output,
        "dense_grad": dense_grad, "attend_back": attend_back_all, "qkv_grad": qkv_grad, "inputs": inputs,
        "sums_start": sums_start, "sums_land": sums_land, "exchange": exchange, "relay": relay,
        "relay_done": relay_done,
        "output_done": lambda: out_sink.last((up_out, down_out), 0, output_out, local_sems.at[3]),
        "input_done": lambda: in_sink.last(
            (up_out, down_out), hidden.shape[0], input_out, local_sems.at[3]
        ),
    }
    for step in ORDER:
        name, *rest = step.split(".")
        if name in steps:
            steps[name](*[int(number) for number in rest])
        else:
            method = getattr(named[name], {"in": "inward"}.get(rest[0], rest[0]))
            numbers = [int(number) for number in rest[1:] if number.isdigit()]
            if rest[-1] in WHERE:
                pl.when(((chip == 0) | (chip == chips - 1)) == WHERE[rest[-1]])(
                    functools.partial(method, *numbers)
                )
            else:
                method(*numbers)

    for name, item in named.items():
        if isinstance(item, Line) and name + ".arrived" not in ORDER:
            item.arrived()
    for name, item in named.items():
        if not isinstance(item, Sink) and name + ".sent" not in ORDER:
            item.sent()
    for copy, _, _ in small:
        copy.wait_send()


DOWN_CUTS = ((512, False), (512, False), (1024, True))
UP_CUTS = ((512, True), (512, True))
QKV_CUTS = ((768, True),)
DENSE_CUTS = ((512, False),)

WHERE = {"e": True, "m": False}

ORDER = (
    "wu.start.0", "wu.start.1", "hid.start", "small_start", "gra.start", "wd.start.0.m", "wu.forward", "hid.out.1",
    "hid.in.1", "wd.start.0.e", "wq.start.0.e", "gra.in.1", "wd.forward.e", "gra.out.1", "hid.out.2", "hid.out.3",
    "wq.start.1.e", "wd.forward.m", "hid.arrived", "small_land", "norm_two", "wu.arrived", "gra.out.2",
    "feed_forward", "gra.out.3", "gra.arrived", "down_grad.0", "fd0.middle.1", "fd0.middle.0", "wd.start.1.e",
    "wd.start.1.m", "fd0.finish.1", "fd0.finish.0", "ld00.start", "down_grad.2", "wd.arrived", "feed_back",
    "fd2.middle.1", "fd2.middle.0", "up_grad.1", "fu1.send.0", "fu1.send.3", "ld00.out.1", "fu1.send.1",
    "fu1.send.2", "fd2.finish.1", "ld21.start", "fd2.finish.0", "ld20.start", "down_grad.1", "ld21.out.1",
    "fu1.middle.1", "ld00.in.1", "fu1.middle.0", "fd1.middle.1", "ld20.out.1", "fd1.middle.0", "wt.start",
    "up_grad.0", "fu0.send.3", "fu0.send.1", "wq.forward.e", "ld00.out.2", "wq.start.0.m", "fd0.sent", "ld21.in.1",
    "fu1.finish.0", "lu10.start", "fu1.finish.1", "lu11.start", "fd1.finish.1", "fd1.finish.0", "wt.forward",
    "ld10.start", "lu10.out.1", "wq.start.1.m", "ld20.in.1", "wq.forward.m", "ld00.out.3", "norm_one", "lu11.out.1",
    "lu10.in.1", "ld21.out.2", "fu0.middle.1", "fu0.send.2", "lu11.in.1", "ld20.out.2", "fu0.middle.0", "fu0.send.0",
    "fd2.sent", "wu.sent", "ld10.in.1", "ld10.out.1", "hid.sent", "lu10.out.2", "lu11.out.2", "wt.back",
    "wq.arrived", "project", "attend", "fu0.finish.1", "lu01.start", "dense_grad", "fu0.finish.0", "lu00.start",
    "fe0.send.2", "fe0.send.1", "ld10.out.2", "wt.arrived", "attend_back", "fe0.send.0", "qkv_grad.0", "fq0.send.1",
    "fe0.send.3", "lu01.out.1", "fq0.send.0", "lu00.in.1", "lu01.in.1", "inputs", "sums_start", "lu00.out.1",
    "fe0.middle.0", "lu01.out.2", "fq0.middle.0", "fe0.middle.1", "sums_land", "ls.start", "fe0.finish.0",
    "fe0.finish.1", "le00.start", "fu0.sent", "fq0.send.3", "si.start", "fq0.finish.0", "lq00.start", "fq0.send.2",
    "lu01.out.3", "ld00.arrived", "si.swap", "si.in.1", "ls.out.1", "le00.out.1", "le00.in.1", "fq0.middle.1",
    "output", "ls.in.1", "so.start", "lq00.in.1", "le00.out.2", "fq0.finish.1", "lq01.start", "ld10.out.3",
    "ld10.arrived", "so.swap", "so.in.1", "le00.out.3", "le00.arrived", "exchange", "ls.out.2", "wt.sent",
    "fd1.sent", "lu00.out.2", "fe0.sent", "fq0.sent", "ld20.out.3", "wd.sent", "lq01.in.1", "ld21.out.3",
    "ld21.arrived", "ld21.sent", "lu10.out.3", "si.in.2", "lu11.out.3", "lu11.arrived", "lq01.out.1", "ls.out.3",
    "lu00.out.3", "fu1.sent", "ld10.sent", "lu10.arrived", "lu11.sent", "lu00.arrived", "lu01.arrived", "lu01.sent",
    "relay", "relay_done", "gra.sent", "lu00.sent", "ls.arrived", "ls.sent", "lq01.out.2", "le00.sent",
    "ld20.arrived", "lq00.out.1", "wq.sent", "lu10.sent", "ld20.sent", "ld00.sent", "so.in.2", "input_done",
    "lq01.out.3", "lq01.arrived", "lq00.out.2", "output_done", "lq00.out.3", "lq01.sent", "lq00.arrived",
    "lq00.sent",
)


def rotary_table(length, lanes):
    half = ROT // 2
    freqs = (10000.0 ** (-2.0 * np.arange(half, dtype=np.float32) / ROT)).astype(np.float32)
    angles = np.arange(length, dtype=np.float32)[:, None] * freqs[None]
    cosine, sine = np.cos(angles), np.sin(angles)
    table = np.zeros((3, length, lanes), np.float32)
    table[0] = 1.0
    table[0, :, :half], table[0, :, half:ROT] = cosine, cosine
    table[1, :, half:ROT] = sine
    table[2, :, :half] = -sine
    return table


def whole_block(hidden, grad, fc1, fc2, qkv, dense, segs, vectors):
    chips, shards = lax.axis_size("ctx") // CORES, lax.axis_size("fsdp")
    count = chips * CORES
    tokens, width = hidden.shape
    length = tokens * count
    units = fc1.shape[1] // count
    head_dim = width // HEADS
    part = units // shards
    rows = width // shards
    bf16, f32 = jnp.bfloat16, jnp.float32
    wide, joint = (length, width), 3 * head_dim
    vec_shape = (shards, sum(vector.shape[0] for vector in vectors) // rows, 1, rows)
    seg_shape = (count,) + segs.shape
    line = (tokens, width)
    hops = (2 * (chips - 1) * tokens, width)
    outs = [
        (line, f32), (line, f32), ((2 * tokens, width), bf16), ((2 * tokens, width), bf16),
        ((count * part, width), bf16), ((count * rows, units), bf16),
        ((count * rows, joint), bf16), ((width, rows), bf16), ((count * 8, width), f32),
        ((units, width), bf16), ((width, units), bf16), ((width, joint), bf16), ((shards * head_dim, rows), bf16),
        ((3 * part, width), bf16), ((3 * rows, units), bf16), ((3 * rows, joint), bf16), ((3 * head_dim, rows), bf16),
        (wide, bf16), ((chips * tokens, width), bf16), (hops, bf16),
        (wide, bf16), ((chips * tokens, width), bf16), (hops, bf16), ((count * head_dim, rows), bf16),
    ]
    table = rotary_table(length, 128)
    cuts = DOWN_CUTS + UP_CUTS + QKV_CUTS + DENSE_CUTS
    halves = [(part // 2, width), (rows // 2, units), (rows // 2, joint), (head_dim // 2, rows)]
    scratch = [
        (wide, bf16), (wide, bf16), (wide, bf16), ((width, units), bf16), ((units, width), bf16),
        ((width, joint), bf16), ((head_dim, width), bf16), (vec_shape, f32), (seg_shape, segs.dtype),
        ((length, segs.shape[1]), f32), (table.shape, f32),
        ((length, units), bf16), ((length, max(units, length)), f32), ((length, units), bf16),
        ((length, head_dim), bf16), ((length, head_dim), bf16), ((length, head_dim), bf16),
        ((length, head_dim), f32), ((length, head_dim), bf16), ((length, head_dim), f32), ((length, head_dim), f32),
        ((length, joint), bf16), ((8, width), f32), ((shards, 8, width), f32), ((8, width), f32),
        ((2, TILE, width), bf16),
    ]
    scratch += [((3,) + half, bf16) for half in halves[:2]]
    scratch += [((2,) + half, bf16) for half in halves]
    scratch += [((2 * half[0], half[1]), bf16) for half in halves]
    scratch += [((2, tokens, width), bf16), ((2, tokens, width), bf16), (line, f32)]
    slots = (
        (3 + sum(1 + split for _, split in cuts)) * Line.slots(chips)
        + 3 * Square.SLOTS + Tree.SLOTS + len(cuts) * Fold.SLOTS + 2 * Sink.slots(chips) + 12 + count - 1
    )
    outputs = pl.pallas_call(
        functools.partial(block_kernel, (chips, shards, part)),
        out_shape=[jax.ShapeDtypeStruct(shape, kind) for shape, kind in outs],
        in_specs=[pl.BlockSpec(memory_space=pl.ANY)] * 16,
        out_specs=[pl.BlockSpec(memory_space=pl.ANY)] * len(outs),
        scratch_shapes=[pltpu.VMEM(shape, kind) for shape, kind in scratch]
        + [
            pltpu.SemaphoreType.DMA((slots,)),
            pltpu.SemaphoreType.DMA((slots,)),
            pltpu.SemaphoreType.DMA((24,)),
        ],
        compiler_params=pltpu.CompilerParams(
            collective_id=0, has_side_effects=True, vmem_limit_bytes=62 * 2**20
        ),
        name="whole_block",
    )(hidden, grad, fc1, fc2, qkv, dense, segs, jnp.asarray(table), *vectors)
    return outputs[:9]


FINISH_STEPS = 8


def widen_kernel(
    sizes,
    up_all, qkv_all, dense_all, down_all, sums,
    gain_one, shift_one, qkv, qkv_bias, dense, columns_one, gain_two, shift_two, up, up_bias, down, columns_two,
):
    count, shards, width = sizes
    f32 = jnp.float32

    def spread(src, dst, pieces):
        groups, size = src.shape[0], src.shape[2] // pieces
        for piece in range(pieces):
            for group in range(groups):
                start = (piece * groups + group) * size
                dst[:, start : start + size] = src[group, :, piece * size : (piece + 1) * size].astype(f32)

    spread(up_all, up, shards)
    spread(qkv_all, qkv, 3)
    spread(dense_all, dense, 1)
    down[...] = down_all[...].astype(f32)

    @pl.when(pl.program_id(0) == 0)
    def _():
        shard = lax.axis_index("fsdp")
        rows = gain_one.shape[1]
        mine = pl.ds(pl.multiple_of(shard * rows, rows), rows)
        for row, dst in ((0, gain_two), (1, shift_two), (4, gain_one), (5, shift_one)):
            total = sums[0, row : row + 1, mine]
            for index in range(1, count):
                total = total + sums[index, row : row + 1, mine]
            dst[...] = total
        columns_one[...] = sums[0, 2:3, mine]
        columns_two[...] = sums[0, 2:3, mine]
        part = up_bias.shape[1] // count
        here = pl.ds(pl.multiple_of(shard * part, part), part)
        for index in range(count):
            up_bias[:, index * part : (index + 1) * part] = sums[index, 3:4, here]
        size = width // count
        chunks = qkv_bias.shape[0] // size
        for chunk in range(chunks):
            place = shard * chunks + chunk
            start = pl.multiple_of(place // count * size, size)
            qkv_bias[chunk * size : (chunk + 1) * size] = sums[
                lax.rem(place, count), 6, pl.ds(start, size)
            ]


def sliced(shape, steps):
    block = shape[:-2] + (shape[-2] // steps, shape[-1])
    return pl.BlockSpec(block, lambda index: (0,) * (len(shape) - 2) + (index, 0))


def entire(shape, _=None):
    return pl.BlockSpec(shape, lambda index: (0,) * len(shape))


def widen(up_all, qkv_all, dense_all, down_all, sums, width):
    count, shards = lax.axis_size("ctx"), lax.axis_size("fsdp")
    rows = width // shards
    f32 = jnp.float32
    steps = FINISH_STEPS
    grads = [
        up_all.reshape(count, rows, -1), qkv_all.reshape(count, rows, -1), dense_all.reshape(shards, rows, rows),
        down_all,
    ]
    units = up_all.shape[1] * count
    sums = sums.reshape(count, 8, width)
    vector = (1, rows)
    outs = [
        (vector, entire), (vector, entire), ((rows, 3 * width), sliced), ((3 * rows,), entire),
        ((rows, width), sliced), (vector, entire), (vector, entire), (vector, entire), ((rows, units), sliced),
        ((1, units // shards), entire), (down_all.shape, sliced), (vector, entire),
    ]
    size = sum(math.prod(shape) for shape, _ in outs)
    return pl.pallas_call(
        functools.partial(widen_kernel, (count, shards, width)),
        grid=(steps,),
        in_specs=[sliced(array.shape, steps) for array in grads] + [entire(sums.shape)],
        out_specs=[kind(shape, steps) for shape, kind in outs],
        out_shape=[jax.ShapeDtypeStruct(shape, f32) for shape, _ in outs],
        compiler_params=pltpu.CompilerParams(vmem_limit_bytes=62 * 2**20),
        cost_estimate=pl.CostEstimate(flops=size, bytes_accessed=6 * size, transcendentals=0),
        name="widen",
    )(*grads, sums)


def close_kernel(sums, branch, back, upward, downward, hidden, grad, output, input_grad):
    f32 = jnp.float32
    own = hidden[...].astype(f32)
    shift = sums[7:8]

    def total(ref, index):
        return ref[...] + upward[index].astype(f32) + downward[index].astype(f32)

    output[...] = (own + total(branch, 0) + shift).astype(output.dtype)
    scaled, spread = centred(own)
    e = total(back, 1)
    part = spread * (
        e
        - jnp.mean(e, axis=-1, keepdims=True)
        - scaled * jnp.mean(e * scaled, axis=-1, keepdims=True)
    )
    input_grad[...] = (grad[...].astype(f32) + part).astype(input_grad.dtype)


def close(sums, branch, back, upward, downward, hidden, grad):
    steps = 2
    shape = hidden.shape
    both = (2,) + shape
    wide = sliced(shape, steps)
    return pl.pallas_call(
        close_kernel,
        grid=(steps,),
        in_specs=[entire((8, shape[1])), wide, wide, sliced(both, steps), sliced(both, steps), wide, wide],
        out_specs=[wide, wide],
        out_shape=[jax.ShapeDtypeStruct(shape, hidden.dtype)] * 2,
        compiler_params=pltpu.CompilerParams(vmem_limit_bytes=62 * 2**20),
        name="close",
    )(sums, branch, back, upward.reshape(both), downward.reshape(both), hidden, grad)


def one_kernel(
    hidden, qkv_weight, dense_weight, fc1_weight, fc2_weight, segments, out_grad, vectors
):
    branch, back, up_out, down_out, down_all, up_all, qkv_all, dense_all, sums_all = whole_block(
        hidden[0], out_grad[0], fc1_weight, fc2_weight, qkv_weight, dense_weight, segments, vectors
    )
    count = lax.axis_size("ctx")
    upward = lax.ppermute(up_out, "ctx", [(index, index + CORES) for index in range(count - CORES)])
    downward = lax.ppermute(down_out, "ctx", [(index + CORES, index) for index in range(count - CORES)])
    outs = widen(up_all, qkv_all, dense_all, down_all, sums_all, hidden.shape[2])
    outs = [out.reshape(-1) if out.shape[0] == 1 else out for out in outs]
    output, input_grad = close(sums_all, branch, back, upward, downward, hidden[0], out_grad[0])
    return (output[None], input_grad[None], *outs)


def per_device(
    hidden,
    ln1_gain,
    ln1_bias,
    qkv_weight,
    qkv_bias,
    dense_weight,
    dense_bias,
    ln2_gain,
    ln2_bias,
    fc1_weight,
    fc1_bias,
    fc2_weight,
    fc2_bias,
    segments,
    out_grad,
):
    ctx_count = lax.axis_size("ctx")
    shards = lax.axis_size("fsdp")
    ctx = lax.axis_index("ctx")
    tokens, width = hidden.shape[1], hidden.shape[2]
    length = tokens * ctx_count
    head_dim = width // HEADS
    repeat = ctx_count // HEADS
    head = ctx // repeat
    factor = head_dim ** (-0.5)
    rows = width // shards
    ff = fc1_weight.shape[1]
    units = ff // shards // ctx_count
    bf16, f32 = jnp.bfloat16, jnp.float32

    vectors = [ln1_gain, ln1_bias, ln2_gain, ln2_bias, dense_bias, fc2_bias, qkv_bias, fc1_bias]
    if ctx_count == HEADS and shards == 4:
        return one_kernel(
            hidden, qkv_weight, dense_weight, fc1_weight, fc2_weight, segments, out_grad, vectors
        )
    vectors = jnp.concatenate(vectors).reshape(-1, rows)
    vec = lax.all_gather(vectors, "fsdp", axis=0)
    query_seg = lax.all_gather(segments[0], "ctx", axis=0, tiled=True)
    up_part = lax.dynamic_index_in_dim(
        fc1_weight.reshape(rows, shards, ctx_count, units), ctx, 2, keepdims=False
    ).reshape(rows, shards * units)
    down_part = lax.dynamic_slice_in_dim(fc2_weight, ctx * units, units, 0)
    qkv_part = lax.dynamic_index_in_dim(
        qkv_weight.reshape(rows, 3, HEADS, head_dim), head, 2, keepdims=False
    ).reshape(rows, 3 * head_dim)
    dense_cols = lax.all_to_all(
        dense_weight, "fsdp", split_axis=1, concat_axis=0, tiled=True
    )
    dense_part = lax.dynamic_slice_in_dim(dense_cols, head * head_dim, head_dim, 0)
    up_w = gather_fsdp(up_part)
    down_w = gather_fsdp(down_part)
    qkv_w = gather_fsdp(qkv_part)
    dense_w = gather_fsdp(dense_part, axis=1)
    hidden_all = line_gather(hidden[0]).reshape(length, width)
    grad_all = line_gather(out_grad[0]).reshape(length, width)
    normed_one = (centred(hidden_all)[0] * vec[:, 0].reshape(-1) + vec[:, 1].reshape(-1)).astype(bf16)
    scaled = centred(hidden_all)[0]
    gain_two = vec[:, 2].reshape(-1)
    normed_two = (scaled * gain_two + vec[:, 3].reshape(-1)).astype(bf16)
    up_shift = lax.dynamic_index_in_dim(
        vec[:, 9 : 9 + ff // width].reshape(shards, ctx_count, units), ctx, 1, keepdims=False
    ).reshape(-1)
    act_f, slope = gelu_and_slope(dot(normed_two, up_w) + up_shift)
    act = act_f.astype(bf16)
    d_up = (dot_cols(grad_all, down_w) * slope).astype(bf16)
    down_part_grad = dot_rows(act, grad_all).astype(bf16)
    up_part_grad = dot_rows(normed_two, d_up).astype(bf16)
    ff_part = dot(act, down_w).astype(bf16)
    d_two = dot_cols(d_up, up_w)
    e_two = (d_two * gain_two).astype(bf16)
    gain_two_sum, shift_two_sum = jnp.sum(d_two * scaled, axis=0), jnp.sum(d_two, axis=0)
    columns = jnp.sum(grad_all.astype(f32), axis=0)
    up_sum = jnp.sum(d_up.astype(f32), axis=0)
    gain_one = vec[:, 0].reshape(-1)
    dense_shift, down_shift = vec[:, 4].reshape(-1), vec[:, 5].reshape(-1)
    qkv_shift = vec[:, 6:9].reshape(-1)
    down_grad = scatter_fsdp(down_part_grad)
    up_grad = scatter_fsdp(up_part_grad)

    qkv_shift_part = lax.dynamic_index_in_dim(
        qkv_shift.reshape(3, HEADS, head_dim), head, 1, keepdims=False
    ).reshape(-1)
    joined = dot(normed_one, qkv_w) + qkv_shift_part
    places = jnp.arange(length, dtype=jnp.int32)
    cosine, sine = rotary_tables(places, ROT)
    queries = rotate(joined[:, :head_dim], cosine, sine).astype(bf16)
    keys = rotate(joined[:, head_dim : 2 * head_dim], cosine, sine).astype(bf16)
    values = joined[:, 2 * head_dim :].astype(bf16)
    allowed = (places[None, :] <= places[:, None]) & (query_seg[None, :] == query_seg[:, None])
    if repeat > 1:
        allowed = allowed & (places // (length // repeat) == ctx % repeat)[:, None]
    scores = jnp.where(allowed, dot_cols(queries, keys) * factor, -1e30)
    top = jnp.max(scores, axis=-1, keepdims=True)
    terms = jnp.where(allowed, jnp.exp(scores - top), 0.0)
    total = jnp.sum(terms, axis=-1, keepdims=True)
    probs = terms * jnp.where(total > 0.0, 1.0 / total, 0.0)
    probs_low = probs.astype(bf16)
    att_f = dot(probs_low, values)
    att = att_f.astype(bf16)
    partial = dot(att, dense_w) + ff_part.astype(f32)
    branch = lax.psum_scatter(partial.astype(bf16), "ctx", scatter_dimension=0, tiled=True)
    own = hidden[0].astype(f32)
    layer_output = (own + branch.astype(f32) + dense_shift + down_shift).astype(bf16)

    d_att = dot_cols(grad_all, dense_w).astype(bf16)
    delta = jnp.sum(d_att.astype(f32) * att_f, axis=-1, keepdims=True)
    dense_grad = dot_rows(att, grad_all).astype(bf16)
    d_scores = (probs * (dot_cols(d_att, values) - delta)).astype(bf16)
    d_queries = rotate(dot(d_scores, keys) * factor, cosine, -sine)
    d_keys = rotate(dot_rows(d_scores, queries) * factor, cosine, -sine)
    d_values = dot_rows(probs_low, d_att)
    d_joined = jnp.concatenate([d_queries, d_keys, d_values], axis=1).astype(bf16)
    qkv_grad = dot_rows(normed_one, d_joined).astype(bf16)

    d_one = dot_cols(d_joined, qkv_w)
    both = (d_one * gain_one + e_two.astype(f32)).astype(bf16)
    back = lax.psum_scatter(both, "ctx", scatter_dimension=0, tiled=True).astype(f32)
    own_scaled, own_spread = centred(own)
    input_part = own_spread * (
        back
        - jnp.mean(back, axis=-1, keepdims=True)
        - own_scaled * jnp.mean(back * own_scaled, axis=-1, keepdims=True)
    )
    input_grad = (out_grad[0].astype(f32) + input_part).astype(bf16)

    first = (ctx == 0).astype(f32)
    joined_sum = jnp.sum(d_joined.astype(f32), axis=0).reshape(3, 1, head_dim)
    joined_full = jnp.where((jnp.arange(HEADS) == head)[None, :, None], joined_sum, 0.0)
    up_sum = up_sum.reshape(shards, 1, units)
    up_full = jnp.where((jnp.arange(ctx_count) == ctx)[None, :, None], up_sum, 0.0)
    small = [
        jnp.sum(d_one * centred(hidden_all)[0], axis=0),
        jnp.sum(d_one, axis=0),
        columns * first,
        gain_two_sum,
        shift_two_sum,
        joined_full,
        up_full,
    ]
    small = jnp.concatenate([piece.reshape(shards, -1) for piece in small], axis=1).astype(bf16)
    small_size = small.shape[1]
    small_rows = -(-small_size // (3 * head_dim * 16)) * 16
    small = jnp.pad(small, ((0, 0), (0, small_rows * 3 * head_dim - small_size)))
    last_grad = scatter_fsdp(
        jnp.concatenate(
            [
                qkv_grad.reshape(shards, rows, 3 * head_dim),
                small.reshape(shards, small_rows, 3 * head_dim),
            ],
            axis=1,
        ).reshape(-1, 3 * head_dim)
    )
    dense_share = scatter_fsdp(
        dense_grad.reshape(head_dim, shards, rows).transpose(1, 0, 2).reshape(-1, rows)
    )

    down_all = line_gather(down_grad).astype(f32).reshape(ctx_count * units, width)
    up_all = (
        line_gather(up_grad)
        .astype(f32)
        .reshape(ctx_count, rows, shards, units)
        .transpose(1, 2, 0, 3)
        .reshape(rows, ff)
    )
    dense_cols_all = line_gather(dense_share)
    if repeat > 1:
        dense_cols_all = jnp.sum(
            dense_cols_all.astype(f32).reshape(HEADS, repeat, head_dim, rows), axis=1
        ).astype(bf16)
    dense_all = lax.all_to_all(
        dense_cols_all.reshape(width, rows), "fsdp", split_axis=0, concat_axis=1, tiled=True
    ).astype(f32)
    last_all = line_gather(last_grad)
    qkv_all = last_all[:, :rows].astype(f32)
    if repeat > 1:
        qkv_all = jnp.sum(qkv_all.reshape(HEADS, repeat, rows, 3 * head_dim), axis=1)
    qkv_all = (
        qkv_all.reshape(HEADS, rows, 3, head_dim).transpose(1, 2, 0, 3).reshape(rows, 3 * width)
    )
    small_all = jnp.sum(last_all[:, rows:].astype(f32), axis=0).reshape(-1)
    sizes = [rows] * 5 + [3 * rows, ff // shards]
    parts, at = [], 0
    for size in sizes:
        parts.append(small_all[at : at + size])
        at += size
    gain_one_grad, shift_one_grad, columns_grad, gain_two_grad, shift_two_grad, joined_grad, up_b_grad = parts
    return (
        layer_output[None],
        input_grad[None],
        gain_one_grad,
        shift_one_grad,
        qkv_all,
        joined_grad,
        dense_all,
        columns_grad,
        gain_two_grad,
        shift_two_grad,
        up_all,
        up_b_grad,
        down_all,
        columns_grad,
    )


def solution(mesh):
    vec, mat, act = P("fsdp"), P("fsdp", None), P("fsdp", "ctx", None)
    return jax.shard_map(
        per_device,
        mesh=mesh,
        in_specs=(
            act, vec, vec, mat, vec, mat, vec, vec, vec, mat, vec, mat, vec, P("fsdp", "ctx"), act
        ),
        out_specs=(act, act, vec, vec, mat, vec, mat, vec, vec, vec, mat, vec, mat, vec),
        check_vma=False,
    )
```

```python
import functools
import math

import jax
import jax.numpy as jnp
import numpy as np
from jax import lax
from jax.experimental import pallas as pl
from jax.experimental.pallas import tpu as pltpu
from jax.sharding import PartitionSpec as P

HEADS = 8
ROT = 64
CORES = 2


def dot(left, right):
    return jnp.dot(left, right, preferred_element_type=jnp.float32)


def dot_rows(left, right):
    return lax.dot_general(
        left, right, (((0,), (0,)), ((), ())), preferred_element_type=jnp.float32
    )


def dot_cols(left, right):
    return lax.dot_general(
        left, right, (((1,), (1,)), ((), ())), preferred_element_type=jnp.float32
    )


def gelu_and_slope(values):
    cdf = 0.5 * (1.0 + lax.erf(values * (0.5**0.5)))
    density = jnp.exp(-0.5 * values * values) * ((2.0 * jnp.pi) ** -0.5)
    return values * cdf, cdf + values * density


def centred(values):
    values = values.astype(jnp.float32)
    center = values - jnp.mean(values, axis=-1, keepdims=True)
    spread = lax.rsqrt(jnp.mean(center * center, axis=-1, keepdims=True) + 1e-05)
    return center * spread, spread


def rotary_tables(places, width):
    half_rot = width // 2
    freqs = 10000.0 ** (-2.0 * jnp.arange(half_rot, dtype=jnp.float32) / width)
    angles = places.astype(jnp.float32)[:, None] * freqs[None, :]
    return (jnp.cos(angles), jnp.sin(angles))


def rotate(values, cosine, sine):
    half = cosine.shape[-1]
    first, second, remain = values[:, :half], values[:, half : 2 * half], values[:, 2 * half :]
    return jnp.concatenate(
        [first * cosine - second * sine, second * cosine + first * sine, remain], axis=1
    )


def line_gather(block):
    count = lax.axis_size("ctx")
    chips = count // CORES
    ctx = lax.axis_index("ctx")
    place, core = ctx // CORES, ctx % CORES
    up = down = block
    ups, downs = [], []
    for hop in range(1, chips):
        up = lax.ppermute(
            up,
            "ctx",
            [
                (i * CORES + k, (i + 1) * CORES + k)
                for i in range(hop - 1, chips - 1)
                for k in range(CORES)
            ],
        )
        down = lax.ppermute(
            down,
            "ctx",
            [
                (i * CORES + k, (i - 1) * CORES + k)
                for i in range(1, chips - hop + 1)
                for k in range(CORES)
            ],
        )
        ups.append(up)
        downs.append(down)
    around = jnp.stack(ups[::-1] + [block] + downs)
    mine = lax.dynamic_slice_in_dim(around, chips - 1 - place, chips, 0)
    other = lax.ppermute(mine, "ctx", [(i, i ^ 1) for i in range(count)])
    is_mine = (jnp.arange(CORES) == core).reshape((1, CORES) + (1,) * block.ndim)
    return jnp.where(is_mine, mine[:, None], other[:, None]).reshape((count,) + block.shape)


def gather_fsdp(values, axis=0):
    return lax.all_gather(values, "fsdp", axis=axis, tiled=True)


def scatter_fsdp(values):
    return lax.psum_scatter(values, "fsdp", scatter_dimension=0, tiled=True)


def remote(src, dst, sems, slot, device):
    return pltpu.make_async_remote_copy(
        src_ref=src,
        dst_ref=dst,
        send_sem=sems[0].at[slot],
        recv_sem=sems[1].at[slot],
        device_id=device,
        device_id_type=pl.DeviceIdType.MESH,
    )


class Line:
    def __init__(self, source, blocks, sems, base, place, chips, stride=None, offset=0, columns=slice(None)):
        self.source, self.sems, self.base, self.chips = source, sems, base, chips
        self.ctx, self.shard = place
        self.chip = self.ctx // CORES
        rows = source.shape[0]
        stride = stride or rows
        self.block = lambda index: blocks.at[
            pl.ds(pl.multiple_of(index * stride + offset, rows), rows), columns
        ]
        self.swap_base = base + 2 * (chips - 1)
        self.own_slot = base + 4 * (chips - 1)

    @staticmethod
    def slots(chips):
        return 4 * (chips - 1) + 2

    def hop(self, out, number):
        up = (self.chip >= self.chips // 2) == out
        place = jnp.where(up, self.chip, self.chips - 1 - self.chip)
        step = jnp.where(up, CORES, -CORES)
        slot = jnp.where(up, 0, self.chips - 1) + number - 1
        sends = (place >= number - 1) & (place < self.chips - 1)
        return slot, step, self.ctx - step * (number - 1), sends, place >= number

    def send(self, out, number):
        slot, step, origin, sends, _ = self.hop(out, number)

        @pl.when(sends)
        def _():
            remote(
                self.source if number == 1 else self.block(origin),
                self.block(origin),
                self.sems,
                self.base + slot,
                (self.ctx + step, self.shard),
            ).start()

    def start(self):
        self.send(True, 1)
        self.send(False, 1)
        remote(
            self.source, self.block(self.ctx), self.sems, self.own_slot, (self.ctx ^ 1, self.shard)
        ).start()
        self.local = pltpu.make_async_copy(
            self.source, self.block(self.ctx), self.sems[0].at[self.own_slot + 1]
        )
        self.local.start()

    def land(self, out, number):
        slot, step, origin, _, gets = self.hop(out, number)
        block = self.block(origin - step)

        @pl.when(gets)
        def _():
            remote(
                block, block, self.sems, self.base + slot, (self.ctx ^ 1, self.shard)
            ).wait_recv()

        if number < self.chips - 1:
            self.send(out, number + 1)

        @pl.when(gets)
        def _():
            remote(
                block, block, self.sems, self.swap_base + slot, (self.ctx ^ 1, self.shard)
            ).start()

    def out(self, number):
        self.land(True, number)

    def inward(self, number):
        self.land(False, number)

    def arrived(self):
        other = self.block(self.ctx ^ 1)
        remote(other, other, self.sems, self.own_slot, (self.ctx ^ 1, self.shard)).wait_recv()
        self.local.wait()
        for out in (True, False):
            for number in range(1, self.chips):
                slot, step, origin, _, gets = self.hop(out, number)
                block = self.block((origin - step) ^ 1)

                @pl.when(gets)
                def _(block=block, slot=slot):
                    remote(
                        block, block, self.sems, self.swap_base + slot, (self.ctx ^ 1, self.shard)
                    ).wait_recv()

    def sent(self):
        source = self.source
        peer = (self.ctx ^ 1, self.shard)
        remote(source, source, self.sems, self.own_slot, peer).wait_send()
        for out in (True, False):
            for number in range(1, self.chips):
                slot, _, _, sends, gets = self.hop(out, number)

                @pl.when(sends)
                def _(slot=slot):
                    remote(source, source, self.sems, self.base + slot, peer).wait_send()

                @pl.when(gets)
                def _(slot=slot):
                    remote(source, source, self.sems, self.swap_base + slot, peer).wait_send()


class Square:
    SLOTS = 8

    def __init__(self, pieces, blocks, sems, base, place):
        self.pieces, self.sems, self.base = pieces, sems, base
        self.ctx, self.shard = place
        half = blocks.shape[0] // 8

        def part(owner, which, columns=slice(None)):
            start = pl.multiple_of((2 * owner + which) * half, half)
            return blocks.at[pl.ds(start, half), columns]

        self.part = part

    def to(self, bit):
        return (self.ctx, self.shard ^ bit)

    def own(self, bit, which):
        for source, columns in self.pieces(which):
            remote(
                source,
                self.part(self.shard, which, columns),
                self.sems,
                self.base + 2 * (bit - 1) + which,
                self.to(bit),
            ).start()

    def start(self, part):
        self.own(1, part)
        self.own(2, 1 - part)
        if part == 1:
            return
        for which in (0, 1):
            for source, columns in self.pieces(which):
                pltpu.make_async_copy(
                    source,
                    self.part(self.shard, which, columns),
                    self.sems[0].at[self.base + 6 + which],
                ).start()

    def wait(self, owner, which, slot, bit):
        part = self.part(owner, which)
        remote(part, part, self.sems, self.base + slot, self.to(bit)).wait_recv()

    def forward(self):
        for bit in (1, 2):
            which = bit - 1
            owner = self.shard ^ bit
            self.wait(owner, which, 2 * (bit - 1) + which, bit)
            part = self.part(owner, which)
            remote(part, part, self.sems, self.base + 4 + which, self.to(3 - bit)).start()

    def arrived(self):
        self.wait(self.shard ^ 1, 1, 1, 1)
        self.wait(self.shard ^ 2, 0, 2, 2)
        self.wait(self.shard ^ 3, 0, 4, 2)
        self.wait(self.shard ^ 3, 1, 5, 1)
        for which in (0, 1):
            part = self.part(self.shard, which)
            pltpu.make_async_copy(part, part, self.sems[0].at[self.base + 6 + which]).wait()

    def sent(self):
        for slot in range(6):
            part = self.part(self.shard, 0)
            remote(part, part, self.sems, self.base + slot, self.to(1)).wait_send()


class Tree:
    SLOTS = 7

    def __init__(self, source, block, sems, base, place, owner):
        self.source, self.block, self.sems, self.base = source, block, sems, base
        self.ctx, self.shard = place
        self.turn = self.shard ^ owner
        self.half = block.shape[0] // 2

    def rows(self, ref, which):
        return ref.at[pl.ds(which * self.half, self.half)]

    def copy(self, slot, ref=None):
        which = slot % 2
        bit = 1 if slot in (0, 3, 4) else 2
        return remote(
            self.rows(self.block if ref is None else ref, which),
            self.rows(self.block, which),
            self.sems,
            self.base + slot,
            (self.ctx, self.shard ^ bit),
        )

    def at(self, turn, body):
        pl.when(self.turn == turn)(body)

    def start(self):
        def body():
            self.copy(0, self.source).start()
            self.copy(1, self.source).start()
            pltpu.make_async_copy(self.source, self.block, self.sems[0].at[self.base + 6]).start()

        self.at(0, body)

    def forward(self):
        for turn, slot in ((1, 0), (2, 1)):

            def body(slot=slot):
                self.copy(slot).wait_recv()
                self.copy(slot + 2).start()

            self.at(turn, body)

    def back(self):
        def body():
            for slot in (2, 3):
                self.copy(slot).wait_recv()
                self.copy(slot + 2).start()

        self.at(3, body)

    def arrived(self):
        def body():
            pltpu.make_async_copy(self.source, self.block, self.sems[0].at[self.base + 6]).wait()

        self.at(0, body)
        self.at(1, lambda: self.copy(5).wait_recv())
        self.at(2, lambda: self.copy(4).wait_recv())

    def sent(self):
        for turn, slots in ((0, (0, 1)), (1, (2,)), (2, (3,)), (3, (4, 5))):

            def body(slots=slots):
                for slot in slots:
                    self.copy(slot).wait_send()

            self.at(turn, body)


def add_rows(dst, sources):
    step = 32

    def body(index, carry):
        rows = pl.ds(pl.multiple_of(index * step, step), step)
        total = sources[0][rows].astype(jnp.float32)
        for source in sources[1:]:
            total += source[rows].astype(jnp.float32)
        dst[rows] = total.astype(dst.dtype)
        return carry

    lax.fori_loop(0, dst.shape[0] // step, body, 0)


class Fold:
    SLOTS = 6

    def __init__(self, parts, landing, stage, carry, final, sems, local, base, place):
        self.parts, self.landing, self.stage, self.carry, self.final = parts, landing, stage, carry, final
        self.sems, self.local, self.base = sems, local, base
        self.ctx, self.shard = place
        self.half = final.shape[0] // 2

    def part(self, owner, which):
        start = pl.multiple_of((2 * owner + which) * self.half, self.half)
        return self.parts.at[pl.ds(start, self.half)]

    def landed(self, slot):
        return self.landing.at[pl.ds(slot * self.half, self.half)]

    def copy(self, src, slot, bit):
        return remote(
            src, self.landed(slot), self.sems, self.base + slot, (self.ctx, self.shard ^ bit)
        )

    def send(self, slot):
        bit, which = (1, 0) if slot < 2 else (2, 1)
        owner = self.shard ^ (3 if slot % 2 else bit)
        self.copy(self.part(owner, which), slot, bit).start()

    def add(self, dst, sources):
        copies = []
        for index, source in enumerate(sources):
            copies.append(
                pltpu.make_async_copy(source, self.stage.at[index], self.local.at[index])
            )
            copies[-1].start()
        for copy in copies:
            copy.wait()
        add_rows(dst, [self.stage.at[index] for index in range(len(sources))])

    def wait(self, slot, bit):
        self.copy(self.landed(slot), slot, bit).wait_recv()

    def middle(self, which):
        first, second = (1, 2) if which == 0 else (2, 1)
        slot = 1 + 2 * which
        self.wait(slot, first)
        carry = self.carry.at[which]
        self.add(carry, [self.part(self.shard ^ second, which), self.landed(slot)])
        self.copy(carry, 4 + which, second).start()

    def finish(self, which):
        first, second = (1, 2) if which == 0 else (2, 1)
        self.wait(2 * which, first)
        self.wait(4 + which, second)
        self.add(
            self.final.at[pl.ds(which * self.half, self.half)],
            [self.part(self.shard, which), self.landed(2 * which), self.landed(4 + which)],
        )

    def sent(self):
        for slot in range(6):
            self.copy(self.part(self.shard, 0), slot, 1).wait_send()


class Sink:
    def __init__(self, parts, swapped, landing, stage, carry, final, sems, local, base, place, chips):
        self.parts, self.swapped, self.landing, self.stage = parts, swapped, landing, stage
        self.carry, self.final, self.sems, self.local, self.base = carry, final, sems, local, base
        self.ctx, self.shard = place
        self.chip, self.core, self.chips = self.ctx // CORES, self.ctx % CORES, chips
        self.rows = final.shape[0]

    @staticmethod
    def slots(chips):
        return 2 * (chips - 1) + 1

    def block(self, ref, index):
        return ref.at[pl.ds(pl.multiple_of(index * self.rows, self.rows), self.rows)]

    def start(self):
        for chip in range(self.chips):
            remote(
                self.block(self.parts, CORES * chip + (self.core ^ 1)),
                self.block(self.swapped, chip),
                self.sems,
                self.base,
                (self.ctx ^ 1, self.shard),
            ).start()

    def swap(self):
        swapped = self.swapped
        remote(swapped, swapped, self.sems, self.base, (self.ctx ^ 1, self.shard)).wait_recv()

    def hop(self, out, step):
        up = (self.chip >= self.chips // 2) == out
        place = jnp.where(up, self.chip, self.chips - 1 - self.chip)
        target = place + self.chips - step
        target = jnp.where(up, target, self.chips - 1 - target)
        slot = jnp.where(up, 0, self.chips - 1) + step - 1
        sends = (place + 1 <= step) & (place < self.chips - 1)
        gets = (place <= step) & (place > 0)
        return slot, target, sends, gets, place > 0

    def landed(self, slot):
        return self.landing.at[pl.ds(pl.multiple_of(slot * self.rows, self.rows), self.rows)]

    def copy(self, out, slot):
        up = (self.chip >= self.chips // 2) == out
        return remote(
            self.carry.at[0 if out else 1],
            self.landed(slot),
            self.sems,
            self.base + 1 + slot,
            (self.ctx + jnp.where(up, CORES, -CORES), self.shard),
        )

    def load(self, index, source):
        return pltpu.make_async_copy(source, self.stage.at[index], self.local.at[index])

    def own(self, target):
        return [
            self.load(0, self.block(self.parts, CORES * target + self.core)),
            self.load(1, self.block(self.swapped, target)),
        ]

    def step(self, out, number):
        slot, target, sends, _, passes = self.hop(out, number)
        if number > 1:
            before, _, sent, gets, _ = self.hop(out, number - 1)

            @pl.when(gets)
            def _():
                remote(
                    self.landed(before), self.landed(before), self.sems, self.base + 1 + before,
                    (self.ctx ^ 1, self.shard),
                ).wait_recv()

            @pl.when(sent)
            def _():
                self.copy(out, before).wait_send()

        @pl.when(sends)
        def _():
            loads = self.own(target)
            for load in loads:
                load.start()
            carry = self.carry.at[0 if out else 1]
            stage = self.stage
            if number > 1:

                @pl.when(passes)
                def _():
                    more = self.load(2, self.landed(slot - 1))
                    more.start()
                    for load in loads + [more]:
                        load.wait()
                    add_rows(carry, [stage.at[0], stage.at[1], stage.at[2]])

                @pl.when(jnp.logical_not(passes))
                def _():
                    for load in loads:
                        load.wait()
                    add_rows(carry, [stage.at[0], stage.at[1]])
            else:
                for load in loads:
                    load.wait()
                add_rows(carry, [stage.at[0], stage.at[1]])
            self.copy(out, slot).start()

    def inward(self, number):
        self.step(False, number)

    def last(self, handed, first, own, sem):
        number = self.chips - 1
        for out in (True, False):
            slot, target, sends, _, passes = self.hop(out, number)
            before, _, sent, gets, _ = self.hop(out, number - 1)

            @pl.when(gets)
            def _(before=before):
                remote(
                    self.landed(before), self.landed(before), self.sems, self.base + 1 + before,
                    (self.ctx ^ 1, self.shard),
                ).wait_recv()

            @pl.when(sent)
            def _(out=out, before=before):
                self.copy(out, before).wait_send()

            @pl.when(sends)
            def _(out=out, slot=slot, target=target, passes=passes):
                loads = self.own(target)
                for load in loads:
                    load.start()
                for load in loads:
                    load.wait()
                carry = self.carry.at[0 if out else 1]
                add_rows(carry, [self.stage.at[0], self.stage.at[1]])

                @pl.when(passes)
                def _():
                    more = self.load(2, self.landed(slot - 1))
                    more.start()
                    more.wait()
                    add_rows(carry, [self.stage.at[0], self.stage.at[1], self.stage.at[2]])

                up = (self.chip >= self.chips // 2) == out
                for way, dst in ((True, handed[0]), (False, handed[1])):

                    @pl.when(up == way)
                    def _(dst=dst):
                        write = pltpu.make_async_copy(carry, dst.at[pl.ds(first, self.rows)], sem)
                        write.start()
                        write.wait()

        loads = self.own(self.chip)
        for load in loads:
            load.start()
        for load in loads:
            load.wait()
        add_rows(self.final, [self.stage.at[0], self.stage.at[1]])
        swapped = self.swapped
        remote(swapped, swapped, self.sems, self.base, (self.ctx ^ 1, self.shard)).wait_send()
        write = pltpu.make_async_copy(self.final, own, sem)
        write.start()
        write.wait()


TILE = 256


def block_kernel(
    sizes,
    hidden, grad, fc1, fc2, qkv, dense, segs, tables,
    ln1_gain, ln1_bias, ln2_gain, ln2_bias, dense_bias, fc2_bias, qkv_bias, fc1_bias,
    output_out, input_out, up_out, down_out, down_all, up_all, qkv_all, dense_all, sums_all,
    down_parts, up_parts, qkv_parts, dense_parts, down_land, up_land, qkv_land, dense_land,
    out_parts, out_swap, out_land, in_parts, in_swap, in_land, dense_lines,
    hid, gra, norm, w_up, w_down, w_qkv, w_dense, vec, seg, seg_col, table,
    act, wide_f, d_up, queries, keys, values, att_f, att, d_keys, d_values, d_joined, sums, sums_got, sums_tot,
    stage, down_stage, up_stage,
    down_carry, up_carry, qkv_carry, dense_carry, down_final, up_final, qkv_final, dense_final,
    out_carry, in_carry, sink_final,
    send_sems, recv_sems, local_sems,
):
    chips, shards, columns = sizes
    place = ctx, shard = lax.axis_index("ctx"), lax.axis_index("fsdp")
    chip, core = ctx // CORES, ctx % CORES
    count = CORES * chips
    sems = (send_sems, recv_sems)
    width, length = hidden.shape[1], hid.shape[0]
    ff_units = w_down.shape[0]
    head_dim = w_dense.shape[0]
    row_size = vec.shape[3]
    tiles = length // TILE
    f32, bf16 = jnp.float32, jnp.bfloat16
    factor = head_dim ** (-0.5)

    barrier = pltpu.get_barrier_semaphore()
    peers = [(ctx, shard ^ bit) for bit in (1, 2, 3)]
    peers += [(lax.rem(ctx + step, count), shard) for step in range(1, count)]
    for peer in peers:
        pl.semaphore_signal(barrier, inc=1, device_id=peer, device_id_type=pl.DeviceIdType.MESH)
    pl.semaphore_wait(barrier, len(peers))

    base = 0

    def take(slots):
        nonlocal base
        base += slots
        return base - slots

    def line(source, blocks, stride=None, offset=0, cut=slice(None)):
        return Line(source, blocks, sems, take(Line.slots(chips)), place, chips, stride, offset, cut)

    def fold(parts, landing, stage, carry, final):
        return Fold(
            parts, landing, stage, carry, final, sems, local_sems.at[pl.ds(4, 4)], take(Fold.SLOTS), place
        )

    def sink(parts, swapped, landing, carry):
        return Sink(
            parts, swapped, landing, down_stage, carry, sink_final, sems, local_sems.at[pl.ds(4, 4)],
            take(Sink.slots(chips)), place, chips,
        )

    def halves(ref, which, start, size):
        half = ref.shape[0] // 2
        return ref.at[pl.ds(which * half, half), pl.ds(pl.multiple_of(start, size), size)]

    def up_pieces(which):
        stride = fc1.shape[1] // shards
        return [
            (
                halves(fc1, which, index * stride + ctx * columns, columns),
                pl.ds(index * columns, columns),
            )
            for index in range(shards)
        ]

    def down_pieces(which):
        half = columns // 2
        start = pl.multiple_of(ctx * columns + which * half, half)
        return [(fc2.at[pl.ds(start, half)], slice(None))]

    def qkv_pieces(which):
        return [
            (
                halves(qkv, which, index * width + ctx * head_dim, head_dim),
                pl.ds(index * head_dim, head_dim),
            )
            for index in range(3)
        ]

    hid_line, gra_line = line(hidden, hid), line(grad, gra)
    squares = [
        Square(pieces, blocks, sems, take(Square.SLOTS), place)
        for pieces, blocks in ((up_pieces, w_up), (down_pieces, w_down), (qkv_pieces, w_qkv))
    ]
    up_square, down_square, qkv_square = squares
    heads_here = dense.shape[0] // head_dim
    dense_rows = dense.at[
        pl.ds(pl.multiple_of(lax.rem(ctx, heads_here) * head_dim, head_dim), head_dim)
    ]
    tree = Tree(dense_rows, w_dense, sems, take(Tree.SLOTS), place, ctx // heads_here)
    named = {"hid": hid_line, "gra": gra_line, "wu": up_square, "wd": down_square, "wq": qkv_square, "wt": tree}
    folds, lines = [], []

    def gradient(letter, cuts, parts, landing, stage, carry, final, gathered):
        start, half = 0, final.shape[0] // 2
        for index, (size, split) in enumerate(cuts):
            cut = pl.ds(start, size)
            item = fold(
                parts.at[:, cut], landing.at[:, cut], stage.at[:, :, :size], carry.at[:, :, cut], final.at[:, cut]
            )
            folds.append(item)
            named[f"f{letter}{index}"] = item
            for which in range(2 if split else 1):
                rows = half if split else 2 * half
                item = line(
                    final.at[pl.ds(which * rows, rows), cut], gathered, final.shape[0], which * rows, cut
                )
                lines.append(item)
                named[f"l{letter}{index}{which}"] = item
            start += size

    gradient("d", DOWN_CUTS, down_parts, down_land, down_stage, down_carry, down_final, down_all)
    gradient("u", UP_CUTS, up_parts, up_land, up_stage, up_carry, up_final, up_all)
    gradient("q", QKV_CUTS, qkv_parts, qkv_land, up_stage, qkv_carry, qkv_final, qkv_all)
    gradient("e", DENSE_CUTS, dense_parts, dense_land, down_stage, dense_carry, dense_final, dense_lines)
    named["ls"] = line(sums_tot, sums_all)
    lines.append(named["ls"])
    out_sink = sink(out_parts, out_swap, out_land, out_carry)
    in_sink = sink(in_parts, in_swap, in_land, in_carry)
    named["so"], named["si"] = out_sink, in_sink

    small = []

    def send_small(src, dst, landing, device):
        slot = take(1)
        small.append((remote(src, dst, sems, slot, device), landing, slot))
        small[-1][0].start()

    def wait_small(items):
        for _, landing, slot in items:
            remote(landing, landing, sems, slot, (ctx ^ 1, shard)).wait_recv()

    vectors = (
        ln1_gain, ln1_bias, ln2_gain, ln2_bias, dense_bias, fc2_bias, qkv_bias, fc1_bias
    )
    at, pairs = 0, [(segs, seg.at[ctx]), (tables, table)]
    for vector in vectors:
        size = vec.shape[3]
        for start in range(0, vector.shape[0], size):
            pairs.append((vector.at[pl.ds(start, size)], vec.at[shard, at, 0]))
            at += 1
    locals_in = [
        pltpu.make_async_copy(src, dst, local_sems.at[8 + index])
        for index, (src, dst) in enumerate(pairs)
    ]
    for copy in locals_in:
        copy.start()

    def small_start():
        for copy in locals_in:
            copy.wait()
        for bit in (1, 2, 3):
            send_small(vec.at[shard], vec.at[shard], vec.at[shard ^ bit], (ctx, shard ^ bit))
        for step in range(1, count):
            send_small(
                segs, seg.at[ctx], seg.at[lax.rem(ctx + count - step, count)],
                (lax.rem(ctx + step, count), shard),
            )

    def small_land():
        wait_small(small)

    def vector(row):
        return jnp.concatenate([vec[index, row] for index in range(shards)], axis=1)

    def rows_of(index):
        return pl.ds(pl.multiple_of(index * TILE, TILE), TILE)

    def loop(body, steps=tiles):
        lax.fori_loop(0, steps, lambda index, carry: (body(rows_of(index)), carry)[1], 0)

    def scaled_rows(rows):
        return centred(hid[rows])[0]

    def norm_two(rows):
        norm[rows] = (scaled_rows(rows) * vector(2) + vector(3)).astype(bf16)

    def norm_one(rows):
        norm[rows] = (scaled_rows(rows) * vector(0) + vector(1)).astype(bf16)

    def emit(steps, compute, dst, size, start=0):
        def write(index):
            return pltpu.make_async_copy(
                stage.at[lax.rem(index, 2), :, :size],
                dst.at[rows_of(index), pl.ds(start, size)],
                local_sems.at[lax.rem(index, 2)],
            )

        def body(index, carry):
            @pl.when(index >= 2)
            def _():
                write(index - 2).wait()

            stage[lax.rem(index, 2), :, :size] = compute(index).astype(bf16)
            write(index).start()
            return carry

        lax.fori_loop(0, steps, body, 0)
        write(steps - 2).wait()
        write(steps - 1).wait()

    def feed_forward():
        bias_start = ctx * columns
        bias_row = 9 + bias_start // row_size
        bias_column = pl.multiple_of(lax.rem(bias_start, row_size), columns)
        up_bias = jnp.concatenate(
            [vec[index, bias_row, :, pl.ds(bias_column, columns)] for index in range(shards)],
            axis=1,
        )

        def body(rows):
            value = dot(norm[rows], w_up[...]) + up_bias
            cdf = 0.5 * (1.0 + lax.erf(value * (0.5**0.5)))
            density = jnp.exp(-0.5 * value * value) * ((2.0 * math.pi) ** -0.5)
            act[rows] = (value * cdf).astype(bf16)
            wide_f[rows] = cdf + value * density

        loop(body)

    def down_grad(index):
        start, size = sum(cut[0] for cut in DOWN_CUTS[:index]), DOWN_CUTS[index][0]

        def body(step, carry):
            rows = rows_of(shard ^ (3 - step))
            cut = pl.ds(start, size)
            stage[0, :, :size] = dot_rows(act[:, rows], gra[:, cut]).astype(bf16)
            write = pltpu.make_async_copy(
                stage.at[0, :, :size], down_parts.at[rows, cut], local_sems.at[0]
            )
            write.start()
            write.wait()
            for number, slot in ((0, 1), (0, 3), (1, 2), (2, 0)):

                @pl.when(step == number)
                def _(slot=slot):
                    named[f"fd{index}"].send(slot)

            return carry

        lax.fori_loop(0, shards, body, 0)

    def feed_back():
        def body(rows):
            d_up[rows] = (dot_cols(gra[rows], w_down[...]) * wide_f[rows]).astype(bf16)

        loop(body)

    def up_grad(index):
        start, size = sum(cut[0] for cut in UP_CUTS[:index]), UP_CUTS[index][0]
        emit(
            width // TILE,
            lambda step: dot_rows(norm[:, rows_of(step)], d_up[:, pl.ds(start, size)]),
            up_parts,
            size,
            start,
        )

    rotary = table.shape[2]

    def turn(entries, rows, way):
        first = entries[:, :rotary]
        first = (
            first * table[0, rows]
            + way * (pltpu.roll(first, ROT // 2, 1) * table[1, rows])
            + way * (pltpu.roll(first, rotary - ROT // 2, 1) * table[2, rows])
        )
        return jnp.concatenate([first, entries[:, rotary:]], axis=1)

    def project():
        per = 3 * HEADS // shards
        bias_parts = []
        for index in range(3):
            place = index * HEADS + ctx
            rest = lax.rem(place, per) * head_dim
            bias_parts.append(
                vec[
                    place // per,
                    6 + rest // row_size,
                    :,
                    pl.ds(pl.multiple_of(lax.rem(rest, row_size), head_dim), head_dim),
                ]
            )

        def body(rows):
            joined = dot(norm[rows], w_qkv[...])
            parts = [
                joined[:, index * head_dim : (index + 1) * head_dim] + bias_parts[index]
                for index in range(3)
            ]
            queries[rows] = turn(parts[0], rows, 1.0).astype(bf16)
            keys[rows] = turn(parts[1], rows, 1.0).astype(bf16)
            values[rows] = parts[2].astype(bf16)

        loop(body)
        side = segs.shape[1]
        for index in range(count):
            block = seg[index].astype(f32)
            seg_col[index * side : (index + 1) * side] = jnp.broadcast_to(block, (side, side)).T

    def attend(index):
        rows = pl.ds(index * TILE, TILE)
        size = (index + 1) * TILE
        seg_row = jnp.concatenate([seg[block] for block in range(count)], axis=1)
        scores = dot_cols(queries[rows], keys[:size]) * factor
        query_place = index * TILE + lax.broadcasted_iota(jnp.int32, (TILE, size), 0)
        key_place = lax.broadcasted_iota(jnp.int32, (TILE, size), 1)
        same = seg_col[rows][:, :1] == seg_row[:, :size].astype(f32)
        allowed = (key_place <= query_place) & same
        scores = jnp.where(allowed, scores, -1e30)
        terms = jnp.where(
            allowed, jnp.exp(scores - jnp.max(scores, axis=-1, keepdims=True)), 0.0
        )
        probs = terms / jnp.sum(terms, axis=-1, keepdims=True)
        wide_f[rows, :size] = probs
        result = dot(probs.astype(bf16), values[:size])
        att_f[rows] = result
        att[rows] = result.astype(bf16)

    def attend_all():
        for index in range(tiles):
            attend(index)

    def output():
        def body(index):
            rows = rows_of(index)
            return dot(att[rows], w_dense[...]) + dot(act[rows], w_down[...])

        emit(tiles, body, out_parts, width)

    dense_size = width // shards

    def dense_grad():
        def body(index):
            start = pl.multiple_of(index * dense_size, dense_size)
            return dot_rows(att[...], gra[:, pl.ds(start, dense_size)])

        emit(shards, body, dense_parts, dense_size)

    def attend_back(index):
        rows = pl.ds(index * TILE, TILE)
        size = (index + 1) * TILE
        d_att = dot_cols(gra[rows], w_dense[...]).astype(bf16)
        delta = jnp.sum(d_att.astype(f32) * att_f[rows], axis=-1, keepdims=True)
        probs = wide_f[rows, :size]
        d_scores = (probs * (dot_cols(d_att, values[:size]) - delta)).astype(bf16)
        d_queries = dot(d_scores, keys[:size]) * factor
        d_joined[rows, :head_dim] = turn(d_queries, rows, -1.0).astype(bf16)
        d_keys[:size] += dot_rows(d_scores, queries[rows])
        d_values[:size] += dot_rows(probs.astype(bf16), d_att)

    def attend_back_all():
        d_keys[...] = jnp.zeros_like(d_keys)
        d_values[...] = jnp.zeros_like(d_values)
        for index in range(tiles):
            attend_back(index)

        def join(rows):
            d_joined[rows, head_dim : 2 * head_dim] = turn(d_keys[rows] * factor, rows, -1.0).astype(bf16)
            d_joined[rows, 2 * head_dim :] = d_values[rows].astype(bf16)

        loop(join)

    def qkv_grad(index):
        start, size = sum(cut[0] for cut in QKV_CUTS[:index]), QKV_CUTS[index][0]
        emit(
            width // TILE,
            lambda step: dot_rows(norm[:, rows_of(step)], d_joined[:, pl.ds(start, size)]),
            qkv_parts,
            size,
            start,
        )

    def inputs():
        sums[...] = jnp.zeros_like(sums)

        def body(index):
            rows = rows_of(index)
            d_one = dot_cols(d_joined[rows], w_qkv[...])
            d_two = dot_cols(d_up[rows], w_up[...])
            scaled = scaled_rows(rows)

            def gather(row, entries):
                sums[row : row + 1, : entries.shape[1]] += jnp.sum(
                    entries.astype(f32), axis=0, keepdims=True
                )

            gather(0, d_two * scaled)
            gather(1, d_two)
            gather(2, gra[rows])
            gather(3, d_up[rows])
            gather(4, d_one * scaled)
            gather(5, d_one)
            gather(6, d_joined[rows])
            return d_one * vector(0) + d_two * vector(2)

        emit(tiles, body, in_parts, width)

    sums_items = []

    def sums_start():
        for bit in (1, 2, 3):
            send_small(sums, sums_got.at[shard], sums_got.at[shard ^ bit], (ctx, shard ^ bit))
            sums_items.append(small[-1])
        sums_got[shard] = sums[...]

    def sums_land():
        wait_small(sums_items)
        total = sums_got[0]
        for index in range(1, shards):
            total = total + sums_got[index]
        sums_tot[...] = total
        sums_tot[7:8] = vector(4) + vector(5)

    exchanged = []

    def dense_block(owner):
        return pl.ds(pl.multiple_of(owner * dense_size, dense_size), dense_size)

    def own_dense():
        return pltpu.make_async_copy(
            dense_lines.at[dense_block(shard)], dense_all.at[dense_block(shard)], local_sems.at[2]
        )

    def dense_part(owner, side):
        size = dense_size // CORES
        return pl.ds(pl.multiple_of(owner * dense_size + side * size, size), size)

    def exchange():
        for bit in (1, 2, 3):
            peer = shard ^ bit
            send_small(
                dense_lines.at[dense_part(peer, core)], dense_all.at[dense_part(shard, core)],
                dense_all.at[dense_part(peer, core)], (ctx, peer),
            )
            exchanged.append(small[-1])
        own_dense().start()

    relayed = []

    def relay():
        wait_small(exchanged)
        for bit in (1, 2, 3):
            rows = dense_part(shard ^ bit, core)
            send_small(
                dense_all.at[rows], dense_all.at[rows], dense_all.at[dense_part(shard ^ bit, 1 - core)],
                (ctx ^ 1, shard),
            )
            relayed.append(small[-1])

    def relay_done():
        wait_small(relayed)
        own_dense().wait()

    steps = {
        "small_start": small_start, "small_land": small_land, "norm_two": lambda: loop(norm_two),
        "norm_one": lambda: loop(norm_one), "feed_forward": feed_forward, "down_grad": down_grad,
        "feed_back": feed_back, "up_grad": up_grad, "project": project, "attend": attend_all, "output": output,
        "dense_grad": dense_grad, "attend_back": attend_back_all, "qkv_grad": qkv_grad, "inputs": inputs,
        "sums_start": sums_start, "sums_land": sums_land, "exchange": exchange, "relay": relay,
        "relay_done": relay_done,
        "output_done": lambda: out_sink.last((up_out, down_out), 0, output_out, local_sems.at[3]),
        "input_done": lambda: in_sink.last(
            (up_out, down_out), hidden.shape[0], input_out, local_sems.at[3]
        ),
    }
    for step in ORDER:
        name, *rest = step.split(".")
        if name in steps:
            steps[name](*[int(number) for number in rest])
        else:
            method = getattr(named[name], {"in": "inward"}.get(rest[0], rest[0]))
            numbers = [int(number) for number in rest[1:] if number.isdigit()]
            if rest[-1] in WHERE:
                pl.when(((chip == 0) | (chip == chips - 1)) == WHERE[rest[-1]])(
                    functools.partial(method, *numbers)
                )
            else:
                method(*numbers)

    for name, item in named.items():
        if isinstance(item, Line) and name + ".arrived" not in ORDER:
            item.arrived()
    for name, item in named.items():
        if not isinstance(item, Sink) and name + ".sent" not in ORDER:
            item.sent()
    for copy, _, _ in small:
        copy.wait_send()


DOWN_CUTS = ((512, False), (512, False), (1024, True))
UP_CUTS = ((512, True), (512, True))
QKV_CUTS = ((768, True),)
DENSE_CUTS = ((512, False),)

WHERE = {"e": True, "m": False}

ORDER = (
    "wu.start.0", "hid.start", "wu.start.1", "gra.start", "wd.start.0.e", "wu.forward", "wd.forward.e",
    "small_start", "wq.start.0.e", "hid.out.1", "hid.in.1", "wd.start.0.m", "wd.start.1.m", "wq.start.1.e",
    "gra.out.1", "gra.in.1", "hid.out.2", "hid.out.3", "small_land", "hid.arrived", "norm_two", "gra.out.2",
    "wu.arrived", "feed_forward", "gra.out.3", "gra.arrived", "down_grad.0", "fd0.middle.1", "fd0.middle.0",
    "wd.forward.m", "wd.start.1.e", "fd0.finish.1", "fd0.finish.0", "ld00.start", "down_grad.2", "wd.arrived",
    "feed_back", "fd2.middle.1", "fd2.middle.0", "ld00.out.1", "up_grad.1", "fu1.send.3", "fu1.send.0", "fu1.send.2",
    "fd2.finish.1", "ld21.start", "fu1.send.1", "ld00.in.1", "fd2.finish.0", "ld20.start", "fu1.middle.1",
    "ld21.out.1", "down_grad.1", "fu1.middle.0", "wq.start.0.m", "ld00.out.2", "fu1.finish.1", "lu11.start",
    "fd1.middle.0", "wt.start", "fd1.middle.1", "up_grad.0", "fu0.send.1", "ld21.in.1", "fu0.send.3", "ld20.out.1",
    "wq.forward.e", "fu1.finish.0", "lu10.start", "fu1.sent", "wq.forward.m", "lu11.out.1", "ld20.in.1", "fd2.sent",
    "wq.start.1.m", "fd1.finish.0", "fd1.finish.1", "ld10.start", "lu10.out.1", "lu11.in.1", "wt.forward",
    "ld00.out.3", "ld10.out.1", "ld21.out.2", "fu0.send.2", "fu0.middle.1", "lu10.in.1", "norm_one", "ld20.out.2",
    "fu0.send.0", "fu0.middle.0", "ld10.in.1", "lu10.out.2", "lu11.out.2", "wq.arrived", "project", "attend",
    "wt.back", "dense_grad", "fe0.send.2", "fe0.send.3", "fe0.send.0", "fe0.send.1", "fu0.finish.1", "lu01.start",
    "fu0.finish.0", "lu00.start", "wt.arrived", "attend_back", "qkv_grad.0", "fq0.send.1", "fq0.send.3",
    "ld10.out.2", "fe0.middle.0", "lu00.out.1", "lu01.out.1", "lu00.in.1", "fe0.middle.1", "output", "fq0.middle.0",
    "fq0.send.0", "fq0.send.2", "lu00.out.2", "lu01.in.1", "fe0.finish.1", "fe0.finish.0", "le00.start",
    "fq0.middle.1", "so.start", "fq0.finish.0", "lq00.start", "lu00.out.3", "ld10.out.3", "so.swap", "le00.in.1",
    "wu.sent", "so.in.1", "fd1.sent", "fq0.finish.1", "lq01.start", "le00.out.1", "inputs", "si.start", "sums_start",
    "le00.out.2", "lq00.in.1", "sums_land", "ls.start", "si.swap", "si.in.1", "ld20.out.3", "lu01.out.2",
    "le00.out.3", "ls.in.1", "ld21.out.3", "ld21.arrived", "lq01.in.1", "ld10.arrived", "ls.out.1", "fq0.sent",
    "le00.arrived", "exchange", "fu0.sent", "le00.sent", "lq01.out.1", "ld21.sent", "lu10.out.3", "lu11.out.3",
    "wq.sent", "lu00.arrived", "lu11.arrived", "lu11.sent", "lu01.out.3", "lu00.sent", "si.in.2", "ls.out.2",
    "lu10.arrived", "lu10.sent", "fd0.sent", "ld20.arrived", "ld00.arrived", "lq01.out.2", "gra.sent", "ls.out.3",
    "relay", "ld00.sent", "ls.arrived", "lu01.arrived", "so.in.2", "fe0.sent", "lu01.sent", "hid.sent", "relay_done",
    "ld10.sent", "ld20.sent", "wd.sent", "ls.sent", "wt.sent", "lq00.out.1", "lq01.out.3", "input_done",
    "lq01.arrived", "lq00.out.2", "output_done", "lq00.out.3", "lq01.sent", "lq00.arrived", "lq00.sent",
)


def rotary_table(length, lanes):
    half = ROT // 2
    freqs = (10000.0 ** (-2.0 * np.arange(half, dtype=np.float32) / ROT)).astype(np.float32)
    angles = np.arange(length, dtype=np.float32)[:, None] * freqs[None]
    cosine, sine = np.cos(angles), np.sin(angles)
    table = np.zeros((3, length, lanes), np.float32)
    table[0] = 1.0
    table[0, :, :half], table[0, :, half:ROT] = cosine, cosine
    table[1, :, half:ROT] = sine
    table[2, :, :half] = -sine
    return table


def whole_block(hidden, grad, fc1, fc2, qkv, dense, segs, vectors):
    chips, shards = lax.axis_size("ctx") // CORES, lax.axis_size("fsdp")
    count = chips * CORES
    tokens, width = hidden.shape
    length = tokens * count
    units = fc1.shape[1] // count
    head_dim = width // HEADS
    part = units // shards
    rows = width // shards
    bf16, f32 = jnp.bfloat16, jnp.float32
    wide, joint = (length, width), 3 * head_dim
    vec_shape = (shards, sum(vector.shape[0] for vector in vectors) // rows, 1, rows)
    seg_shape = (count,) + segs.shape
    line = (tokens, width)
    hops = (2 * (chips - 1) * tokens, width)
    outs = [
        (line, f32), (line, f32), ((2 * tokens, width), bf16), ((2 * tokens, width), bf16),
        ((count * part, width), bf16), ((count * rows, units), bf16),
        ((count * rows, joint), bf16), ((width, rows), bf16), ((count * 8, width), f32),
        ((units, width), bf16), ((width, units), bf16), ((width, joint), bf16), ((shards * head_dim, rows), bf16),
        ((3 * part, width), bf16), ((3 * rows, units), bf16), ((3 * rows, joint), bf16), ((3 * head_dim, rows), bf16),
        (wide, bf16), ((chips * tokens, width), bf16), (hops, bf16),
        (wide, bf16), ((chips * tokens, width), bf16), (hops, bf16), ((count * head_dim, rows), bf16),
    ]
    table = rotary_table(length, 128)
    cuts = DOWN_CUTS + UP_CUTS + QKV_CUTS + DENSE_CUTS
    halves = [(part // 2, width), (rows // 2, units), (rows // 2, joint), (head_dim // 2, rows)]
    scratch = [
        (wide, bf16), (wide, bf16), (wide, bf16), ((width, units), bf16), ((units, width), bf16),
        ((width, joint), bf16), ((head_dim, width), bf16), (vec_shape, f32), (seg_shape, segs.dtype),
        ((length, segs.shape[1]), f32), (table.shape, f32),
        ((length, units), bf16), ((length, max(units, length)), f32), ((length, units), bf16),
        ((length, head_dim), bf16), ((length, head_dim), bf16), ((length, head_dim), bf16),
        ((length, head_dim), f32), ((length, head_dim), bf16), ((length, head_dim), f32), ((length, head_dim), f32),
        ((length, joint), bf16), ((8, width), f32), ((shards, 8, width), f32), ((8, width), f32),
        ((2, TILE, width), bf16),
    ]
    scratch += [((3,) + half, bf16) for half in halves[:2]]
    scratch += [((2,) + half, bf16) for half in halves]
    scratch += [((2 * half[0], half[1]), bf16) for half in halves]
    scratch += [((2, tokens, width), bf16), ((2, tokens, width), bf16), (line, f32)]
    slots = (
        (3 + sum(1 + split for _, split in cuts)) * Line.slots(chips)
        + 3 * Square.SLOTS + Tree.SLOTS + len(cuts) * Fold.SLOTS + 2 * Sink.slots(chips) + 12 + count - 1
    )
    outputs = pl.pallas_call(
        functools.partial(block_kernel, (chips, shards, part)),
        out_shape=[jax.ShapeDtypeStruct(shape, kind) for shape, kind in outs],
        in_specs=[pl.BlockSpec(memory_space=pl.ANY)] * 16,
        out_specs=[pl.BlockSpec(memory_space=pl.ANY)] * len(outs),
        scratch_shapes=[pltpu.VMEM(shape, kind) for shape, kind in scratch]
        + [
            pltpu.SemaphoreType.DMA((slots,)),
            pltpu.SemaphoreType.DMA((slots,)),
            pltpu.SemaphoreType.DMA((24,)),
        ],
        compiler_params=pltpu.CompilerParams(
            collective_id=0, has_side_effects=True, vmem_limit_bytes=62 * 2**20
        ),
        name="whole_block",
    )(hidden, grad, fc1, fc2, qkv, dense, segs, jnp.asarray(table), *vectors)
    return outputs[:9]


FINISH_STEPS = 4


def widen_kernel(
    sizes,
    up_all, qkv_all, dense_all, down_all, sums,
    gain_one, shift_one, qkv, qkv_bias, dense, columns_one, gain_two, shift_two, up, up_bias, down, columns_two,
):
    count, shards, width = sizes
    f32 = jnp.float32

    def spread(src, dst, pieces):
        groups, size = src.shape[0], src.shape[2] // pieces
        for piece in range(pieces):
            for group in range(groups):
                start = (piece * groups + group) * size
                dst[:, start : start + size] = src[group, :, piece * size : (piece + 1) * size].astype(f32)

    spread(up_all, up, shards)
    spread(qkv_all, qkv, 3)
    spread(dense_all, dense, 1)
    down[...] = down_all[...].astype(f32)

    @pl.when(pl.program_id(0) == 0)
    def _():
        shard = lax.axis_index("fsdp")
        rows = gain_one.shape[1]
        mine = pl.ds(pl.multiple_of(shard * rows, rows), rows)
        for row, dst in ((0, gain_two), (1, shift_two), (4, gain_one), (5, shift_one)):
            total = sums[0, row : row + 1, mine]
            for index in range(1, count):
                total = total + sums[index, row : row + 1, mine]
            dst[...] = total
        columns_one[...] = sums[0, 2:3, mine]
        columns_two[...] = sums[0, 2:3, mine]
        part = up_bias.shape[1] // count
        here = pl.ds(pl.multiple_of(shard * part, part), part)
        for index in range(count):
            up_bias[:, index * part : (index + 1) * part] = sums[index, 3:4, here]
        size = width // count
        chunks = qkv_bias.shape[0] // size
        for chunk in range(chunks):
            place = shard * chunks + chunk
            start = pl.multiple_of(place // count * size, size)
            qkv_bias[chunk * size : (chunk + 1) * size] = sums[
                lax.rem(place, count), 6, pl.ds(start, size)
            ]


def sliced(shape, steps):
    block = shape[:-2] + (shape[-2] // steps, shape[-1])
    return pl.BlockSpec(block, lambda index: (0,) * (len(shape) - 2) + (index, 0))


def entire(shape, _=None):
    return pl.BlockSpec(shape, lambda index: (0,) * len(shape))


def widen(up_all, qkv_all, dense_all, down_all, sums, width):
    count, shards = lax.axis_size("ctx"), lax.axis_size("fsdp")
    rows = width // shards
    f32 = jnp.float32
    steps = FINISH_STEPS
    grads = [
        up_all.reshape(count, rows, -1), qkv_all.reshape(count, rows, -1), dense_all.reshape(shards, rows, rows),
        down_all,
    ]
    units = up_all.shape[1] * count
    sums = sums.reshape(count, 8, width)
    vector = (1, rows)
    outs = [
        (vector, entire), (vector, entire), ((rows, 3 * width), sliced), ((3 * rows,), entire),
        ((rows, width), sliced), (vector, entire), (vector, entire), (vector, entire), ((rows, units), sliced),
        ((1, units // shards), entire), (down_all.shape, sliced), (vector, entire),
    ]
    size = sum(math.prod(shape) for shape, _ in outs)
    return pl.pallas_call(
        functools.partial(widen_kernel, (count, shards, width)),
        grid=(steps,),
        in_specs=[sliced(array.shape, steps) for array in grads] + [entire(sums.shape)],
        out_specs=[kind(shape, steps) for shape, kind in outs],
        out_shape=[jax.ShapeDtypeStruct(shape, f32) for shape, _ in outs],
        compiler_params=pltpu.CompilerParams(vmem_limit_bytes=62 * 2**20),
        cost_estimate=pl.CostEstimate(flops=size, bytes_accessed=6 * size, transcendentals=0),
        name="widen",
    )(*grads, sums)


def close_kernel(sums, branch, back, upward, downward, hidden, grad, output, input_grad):
    f32 = jnp.float32
    own = hidden[...].astype(f32)
    shift = sums[7:8]

    def total(ref, index):
        return ref[...] + upward[index].astype(f32) + downward[index].astype(f32)

    output[...] = (own + total(branch, 0) + shift).astype(output.dtype)
    scaled, spread = centred(own)
    e = total(back, 1)
    part = spread * (
        e
        - jnp.mean(e, axis=-1, keepdims=True)
        - scaled * jnp.mean(e * scaled, axis=-1, keepdims=True)
    )
    input_grad[...] = (grad[...].astype(f32) + part).astype(input_grad.dtype)


def close(sums, branch, back, upward, downward, hidden, grad):
    steps = 2
    shape = hidden.shape
    both = (2,) + shape
    wide = sliced(shape, steps)
    return pl.pallas_call(
        close_kernel,
        grid=(steps,),
        in_specs=[entire((8, shape[1])), wide, wide, sliced(both, steps), sliced(both, steps), wide, wide],
        out_specs=[wide, wide],
        out_shape=[jax.ShapeDtypeStruct(shape, hidden.dtype)] * 2,
        compiler_params=pltpu.CompilerParams(vmem_limit_bytes=62 * 2**20),
        name="close",
    )(sums, branch, back, upward.reshape(both), downward.reshape(both), hidden, grad)


def one_kernel(
    hidden, qkv_weight, dense_weight, fc1_weight, fc2_weight, segments, out_grad, vectors
):
    branch, back, up_out, down_out, down_all, up_all, qkv_all, dense_all, sums_all = whole_block(
        hidden[0], out_grad[0], fc1_weight, fc2_weight, qkv_weight, dense_weight, segments, vectors
    )
    count = lax.axis_size("ctx")
    upward = lax.ppermute(up_out, "ctx", [(index, index + CORES) for index in range(count - CORES)])
    downward = lax.ppermute(down_out, "ctx", [(index + CORES, index) for index in range(count - CORES)])
    outs = widen(up_all, qkv_all, dense_all, down_all, sums_all, hidden.shape[2])
    outs = [out.reshape(-1) if out.shape[0] == 1 else out for out in outs]
    output, input_grad = close(sums_all, branch, back, upward, downward, hidden[0], out_grad[0])
    return (output[None], input_grad[None], *outs)


def per_device(
    hidden,
    ln1_gain,
    ln1_bias,
    qkv_weight,
    qkv_bias,
    dense_weight,
    dense_bias,
    ln2_gain,
    ln2_bias,
    fc1_weight,
    fc1_bias,
    fc2_weight,
    fc2_bias,
    segments,
    out_grad,
):
    ctx_count = lax.axis_size("ctx")
    shards = lax.axis_size("fsdp")
    ctx = lax.axis_index("ctx")
    tokens, width = hidden.shape[1], hidden.shape[2]
    length = tokens * ctx_count
    head_dim = width // HEADS
    repeat = ctx_count // HEADS
    head = ctx // repeat
    factor = head_dim ** (-0.5)
    rows = width // shards
    ff = fc1_weight.shape[1]
    units = ff // shards // ctx_count
    bf16, f32 = jnp.bfloat16, jnp.float32

    vectors = [ln1_gain, ln1_bias, ln2_gain, ln2_bias, dense_bias, fc2_bias, qkv_bias, fc1_bias]
    if ctx_count == HEADS and shards == 4 and width == sum(size for size, _ in DOWN_CUTS):
        return one_kernel(
            hidden, qkv_weight, dense_weight, fc1_weight, fc2_weight, segments, out_grad, vectors
        )
    vectors = jnp.concatenate(vectors).reshape(-1, rows)
    vec = lax.all_gather(vectors, "fsdp", axis=0)
    query_seg = lax.all_gather(segments[0], "ctx", axis=0, tiled=True)
    up_part = lax.dynamic_index_in_dim(
        fc1_weight.reshape(rows, shards, ctx_count, units), ctx, 2, keepdims=False
    ).reshape(rows, shards * units)
    down_part = lax.dynamic_slice_in_dim(fc2_weight, ctx * units, units, 0)
    qkv_part = lax.dynamic_index_in_dim(
        qkv_weight.reshape(rows, 3, HEADS, head_dim), head, 2, keepdims=False
    ).reshape(rows, 3 * head_dim)
    dense_cols = lax.all_to_all(
        dense_weight, "fsdp", split_axis=1, concat_axis=0, tiled=True
    )
    dense_part = lax.dynamic_slice_in_dim(dense_cols, head * head_dim, head_dim, 0)
    up_w = gather_fsdp(up_part)
    down_w = gather_fsdp(down_part)
    qkv_w = gather_fsdp(qkv_part)
    dense_w = gather_fsdp(dense_part, axis=1)
    hidden_all = line_gather(hidden[0]).reshape(length, width)
    grad_all = line_gather(out_grad[0]).reshape(length, width)
    normed_one = (centred(hidden_all)[0] * vec[:, 0].reshape(-1) + vec[:, 1].reshape(-1)).astype(bf16)
    scaled = centred(hidden_all)[0]
    gain_two = vec[:, 2].reshape(-1)
    normed_two = (scaled * gain_two + vec[:, 3].reshape(-1)).astype(bf16)
    up_shift = lax.dynamic_index_in_dim(
        vec[:, 9 : 9 + ff // width].reshape(shards, ctx_count, units), ctx, 1, keepdims=False
    ).reshape(-1)
    act_f, slope = gelu_and_slope(dot(normed_two, up_w) + up_shift)
    act = act_f.astype(bf16)
    d_up = (dot_cols(grad_all, down_w) * slope).astype(bf16)
    down_part_grad = dot_rows(act, grad_all).astype(bf16)
    up_part_grad = dot_rows(normed_two, d_up).astype(bf16)
    ff_part = dot(act, down_w).astype(bf16)
    d_two = dot_cols(d_up, up_w)
    e_two = (d_two * gain_two).astype(bf16)
    gain_two_sum, shift_two_sum = jnp.sum(d_two * scaled, axis=0), jnp.sum(d_two, axis=0)
    columns = jnp.sum(grad_all.astype(f32), axis=0)
    up_sum = jnp.sum(d_up.astype(f32), axis=0)
    gain_one = vec[:, 0].reshape(-1)
    dense_shift, down_shift = vec[:, 4].reshape(-1), vec[:, 5].reshape(-1)
    qkv_shift = vec[:, 6:9].reshape(-1)
    down_grad = scatter_fsdp(down_part_grad)
    up_grad = scatter_fsdp(up_part_grad)

    qkv_shift_part = lax.dynamic_index_in_dim(
        qkv_shift.reshape(3, HEADS, head_dim), head, 1, keepdims=False
    ).reshape(-1)
    joined = dot(normed_one, qkv_w) + qkv_shift_part
    places = jnp.arange(length, dtype=jnp.int32)
    cosine, sine = rotary_tables(places, ROT)
    queries = rotate(joined[:, :head_dim], cosine, sine).astype(bf16)
    keys = rotate(joined[:, head_dim : 2 * head_dim], cosine, sine).astype(bf16)
    values = joined[:, 2 * head_dim :].astype(bf16)
    allowed = (places[None, :] <= places[:, None]) & (query_seg[None, :] == query_seg[:, None])
    if repeat > 1:
        allowed = allowed & (places // (length // repeat) == ctx % repeat)[:, None]
    scores = jnp.where(allowed, dot_cols(queries, keys) * factor, -1e30)
    top = jnp.max(scores, axis=-1, keepdims=True)
    terms = jnp.where(allowed, jnp.exp(scores - top), 0.0)
    total = jnp.sum(terms, axis=-1, keepdims=True)
    probs = terms * jnp.where(total > 0.0, 1.0 / total, 0.0)
    probs_low = probs.astype(bf16)
    att_f = dot(probs_low, values)
    att = att_f.astype(bf16)
    partial = dot(att, dense_w) + ff_part.astype(f32)
    branch = lax.psum_scatter(partial.astype(bf16), "ctx", scatter_dimension=0, tiled=True)
    own = hidden[0].astype(f32)
    layer_output = (own + branch.astype(f32) + dense_shift + down_shift).astype(bf16)

    d_att = dot_cols(grad_all, dense_w).astype(bf16)
    delta = jnp.sum(d_att.astype(f32) * att_f, axis=-1, keepdims=True)
    dense_grad = dot_rows(att, grad_all).astype(bf16)
    d_scores = (probs * (dot_cols(d_att, values) - delta)).astype(bf16)
    d_queries = rotate(dot(d_scores, keys) * factor, cosine, -sine)
    d_keys = rotate(dot_rows(d_scores, queries) * factor, cosine, -sine)
    d_values = dot_rows(probs_low, d_att)
    d_joined = jnp.concatenate([d_queries, d_keys, d_values], axis=1).astype(bf16)
    qkv_grad = dot_rows(normed_one, d_joined).astype(bf16)

    d_one = dot_cols(d_joined, qkv_w)
    both = (d_one * gain_one + e_two.astype(f32)).astype(bf16)
    back = lax.psum_scatter(both, "ctx", scatter_dimension=0, tiled=True).astype(f32)
    own_scaled, own_spread = centred(own)
    input_part = own_spread * (
        back
        - jnp.mean(back, axis=-1, keepdims=True)
        - own_scaled * jnp.mean(back * own_scaled, axis=-1, keepdims=True)
    )
    input_grad = (out_grad[0].astype(f32) + input_part).astype(bf16)

    first = (ctx == 0).astype(f32)
    joined_sum = jnp.sum(d_joined.astype(f32), axis=0).reshape(3, 1, head_dim)
    joined_full = jnp.where((jnp.arange(HEADS) == head)[None, :, None], joined_sum, 0.0)
    up_sum = up_sum.reshape(shards, 1, units)
    up_full = jnp.where((jnp.arange(ctx_count) == ctx)[None, :, None], up_sum, 0.0)
    small = [
        jnp.sum(d_one * centred(hidden_all)[0], axis=0),
        jnp.sum(d_one, axis=0),
        columns * first,
        gain_two_sum,
        shift_two_sum,
        joined_full,
        up_full,
    ]
    small = jnp.concatenate([piece.reshape(shards, -1) for piece in small], axis=1).astype(bf16)
    small_size = small.shape[1]
    small_rows = -(-small_size // (3 * head_dim * 16)) * 16
    small = jnp.pad(small, ((0, 0), (0, small_rows * 3 * head_dim - small_size)))
    last_grad = scatter_fsdp(
        jnp.concatenate(
            [
                qkv_grad.reshape(shards, rows, 3 * head_dim),
                small.reshape(shards, small_rows, 3 * head_dim),
            ],
            axis=1,
        ).reshape(-1, 3 * head_dim)
    )
    dense_share = scatter_fsdp(
        dense_grad.reshape(head_dim, shards, rows).transpose(1, 0, 2).reshape(-1, rows)
    )

    down_all = line_gather(down_grad).astype(f32).reshape(ctx_count * units, width)
    up_all = (
        line_gather(up_grad)
        .astype(f32)
        .reshape(ctx_count, rows, shards, units)
        .transpose(1, 2, 0, 3)
        .reshape(rows, ff)
    )
    dense_cols_all = line_gather(dense_share)
    if repeat > 1:
        dense_cols_all = jnp.sum(
            dense_cols_all.astype(f32).reshape(HEADS, repeat, head_dim, rows), axis=1
        ).astype(bf16)
    dense_all = lax.all_to_all(
        dense_cols_all.reshape(width, rows), "fsdp", split_axis=0, concat_axis=1, tiled=True
    ).astype(f32)
    last_all = line_gather(last_grad)
    qkv_all = last_all[:, :rows].astype(f32)
    if repeat > 1:
        qkv_all = jnp.sum(qkv_all.reshape(HEADS, repeat, rows, 3 * head_dim), axis=1)
    qkv_all = (
        qkv_all.reshape(HEADS, rows, 3, head_dim).transpose(1, 2, 0, 3).reshape(rows, 3 * width)
    )
    small_all = jnp.sum(last_all[:, rows:].astype(f32), axis=0).reshape(-1)
    sizes = [rows] * 5 + [3 * rows, ff // shards]
    parts, at = [], 0
    for size in sizes:
        parts.append(small_all[at : at + size])
        at += size
    gain_one_grad, shift_one_grad, columns_grad, gain_two_grad, shift_two_grad, joined_grad, up_b_grad = parts
    return (
        layer_output[None],
        input_grad[None],
        gain_one_grad,
        shift_one_grad,
        qkv_all,
        joined_grad,
        dense_all,
        columns_grad,
        gain_two_grad,
        shift_two_grad,
        up_all,
        up_b_grad,
        down_all,
        columns_grad,
    )


def solution(mesh):
    vec, mat, act = P("fsdp"), P("fsdp", None), P("fsdp", "ctx", None)
    return jax.shard_map(
        per_device,
        mesh=mesh,
        in_specs=(
            act, vec, vec, mat, vec, mat, vec, vec, vec, mat, vec, mat, vec, P("fsdp", "ctx"), act
        ),
        out_specs=(act, act, vec, vec, mat, vec, mat, vec, vec, vec, mat, vec, mat, vec),
        check_vma=False,
    )
```

```python
import functools
import math

import jax
import jax.numpy as jnp
import numpy as np
from jax import lax
from jax.experimental import pallas as pl
from jax.experimental.pallas import tpu as pltpu
from jax.sharding import PartitionSpec as P

HEADS = 8
ROT = 64
CORES = 2


def dot(left, right):
    return jnp.dot(left, right, preferred_element_type=jnp.float32)


def dot_rows(left, right):
    return lax.dot_general(
        left, right, (((0,), (0,)), ((), ())), preferred_element_type=jnp.float32
    )


def dot_cols(left, right):
    return lax.dot_general(
        left, right, (((1,), (1,)), ((), ())), preferred_element_type=jnp.float32
    )


def gelu_and_slope(values):
    cdf = 0.5 * (1.0 + lax.erf(values * (0.5**0.5)))
    density = jnp.exp(-0.5 * values * values) * ((2.0 * jnp.pi) ** -0.5)
    return values * cdf, cdf + values * density


def centred(values):
    values = values.astype(jnp.float32)
    center = values - jnp.mean(values, axis=-1, keepdims=True)
    spread = lax.rsqrt(jnp.mean(center * center, axis=-1, keepdims=True) + 1e-05)
    return center * spread, spread


def rotary_tables(places, width):
    half_rot = width // 2
    freqs = 10000.0 ** (-2.0 * jnp.arange(half_rot, dtype=jnp.float32) / width)
    angles = places.astype(jnp.float32)[:, None] * freqs[None, :]
    return (jnp.cos(angles), jnp.sin(angles))


def rotate(values, cosine, sine):
    half = cosine.shape[-1]
    first, second, remain = values[:, :half], values[:, half : 2 * half], values[:, 2 * half :]
    return jnp.concatenate(
        [first * cosine - second * sine, second * cosine + first * sine, remain], axis=1
    )


def line_gather(block):
    count = lax.axis_size("ctx")
    chips = count // CORES
    ctx = lax.axis_index("ctx")
    place, core = ctx // CORES, ctx % CORES
    up = down = block
    ups, downs = [], []
    for hop in range(1, chips):
        up = lax.ppermute(
            up,
            "ctx",
            [
                (i * CORES + k, (i + 1) * CORES + k)
                for i in range(hop - 1, chips - 1)
                for k in range(CORES)
            ],
        )
        down = lax.ppermute(
            down,
            "ctx",
            [
                (i * CORES + k, (i - 1) * CORES + k)
                for i in range(1, chips - hop + 1)
                for k in range(CORES)
            ],
        )
        ups.append(up)
        downs.append(down)
    around = jnp.stack(ups[::-1] + [block] + downs)
    mine = lax.dynamic_slice_in_dim(around, chips - 1 - place, chips, 0)
    other = lax.ppermute(mine, "ctx", [(i, i ^ 1) for i in range(count)])
    is_mine = (jnp.arange(CORES) == core).reshape((1, CORES) + (1,) * block.ndim)
    return jnp.where(is_mine, mine[:, None], other[:, None]).reshape((count,) + block.shape)


def gather_fsdp(values, axis=0):
    return lax.all_gather(values, "fsdp", axis=axis, tiled=True)


def scatter_fsdp(values):
    return lax.psum_scatter(values, "fsdp", scatter_dimension=0, tiled=True)


def remote(src, dst, sems, slot, device):
    return pltpu.make_async_remote_copy(
        src_ref=src,
        dst_ref=dst,
        send_sem=sems[0].at[slot],
        recv_sem=sems[1].at[slot],
        device_id=device,
        device_id_type=pl.DeviceIdType.MESH,
    )


class Line:
    def __init__(self, source, blocks, sems, base, place, chips, stride=None, offset=0, columns=slice(None)):
        self.source, self.sems, self.base, self.chips = source, sems, base, chips
        self.ctx, self.shard = place
        self.chip = self.ctx // CORES
        rows = source.shape[0]
        stride = stride or rows
        self.block = lambda index: blocks.at[
            pl.ds(pl.multiple_of(index * stride + offset, rows), rows), columns
        ]
        self.swap_base = base + 2 * (chips - 1)
        self.own_slot = base + 4 * (chips - 1)

    @staticmethod
    def slots(chips):
        return 4 * (chips - 1) + 2

    def hop(self, out, number):
        up = (self.chip >= self.chips // 2) == out
        place = jnp.where(up, self.chip, self.chips - 1 - self.chip)
        step = jnp.where(up, CORES, -CORES)
        slot = jnp.where(up, 0, self.chips - 1) + number - 1
        sends = (place >= number - 1) & (place < self.chips - 1)
        return slot, step, self.ctx - step * (number - 1), sends, place >= number

    def send(self, out, number):
        slot, step, origin, sends, _ = self.hop(out, number)

        @pl.when(sends)
        def _():
            remote(
                self.source if number == 1 else self.block(origin),
                self.block(origin),
                self.sems,
                self.base + slot,
                (self.ctx + step, self.shard),
            ).start()

    def start(self):
        self.send(True, 1)
        self.send(False, 1)
        remote(
            self.source, self.block(self.ctx), self.sems, self.own_slot, (self.ctx ^ 1, self.shard)
        ).start()
        self.local = pltpu.make_async_copy(
            self.source, self.block(self.ctx), self.sems[0].at[self.own_slot + 1]
        )
        self.local.start()

    def land(self, out, number):
        slot, step, origin, _, gets = self.hop(out, number)
        block = self.block(origin - step)

        @pl.when(gets)
        def _():
            remote(
                block, block, self.sems, self.base + slot, (self.ctx ^ 1, self.shard)
            ).wait_recv()

        if number < self.chips - 1:
            self.send(out, number + 1)

        @pl.when(gets)
        def _():
            remote(
                block, block, self.sems, self.swap_base + slot, (self.ctx ^ 1, self.shard)
            ).start()

    def out(self, number):
        self.land(True, number)

    def inward(self, number):
        self.land(False, number)

    def arrived(self):
        other = self.block(self.ctx ^ 1)
        remote(other, other, self.sems, self.own_slot, (self.ctx ^ 1, self.shard)).wait_recv()
        self.local.wait()
        for out in (True, False):
            for number in range(1, self.chips):
                slot, step, origin, _, gets = self.hop(out, number)
                block = self.block((origin - step) ^ 1)

                @pl.when(gets)
                def _(block=block, slot=slot):
                    remote(
                        block, block, self.sems, self.swap_base + slot, (self.ctx ^ 1, self.shard)
                    ).wait_recv()

    def sent(self):
        source = self.source
        peer = (self.ctx ^ 1, self.shard)
        remote(source, source, self.sems, self.own_slot, peer).wait_send()
        for out in (True, False):
            for number in range(1, self.chips):
                slot, _, _, sends, gets = self.hop(out, number)

                @pl.when(sends)
                def _(slot=slot):
                    remote(source, source, self.sems, self.base + slot, peer).wait_send()

                @pl.when(gets)
                def _(slot=slot):
                    remote(source, source, self.sems, self.swap_base + slot, peer).wait_send()


class Square:
    SLOTS = 8

    def __init__(self, pieces, blocks, sems, base, place):
        self.pieces, self.sems, self.base = pieces, sems, base
        self.ctx, self.shard = place
        half = blocks.shape[0] // 8

        def part(owner, which, columns=slice(None)):
            start = pl.multiple_of((2 * owner + which) * half, half)
            return blocks.at[pl.ds(start, half), columns]

        self.part = part

    def to(self, bit):
        return (self.ctx, self.shard ^ bit)

    def own(self, bit, which):
        for source, columns in self.pieces(which):
            remote(
                source,
                self.part(self.shard, which, columns),
                self.sems,
                self.base + 2 * (bit - 1) + which,
                self.to(bit),
            ).start()

    def start(self, part):
        self.own(1, part)
        self.own(2, 1 - part)
        if part == 1:
            return
        for which in (0, 1):
            for source, columns in self.pieces(which):
                pltpu.make_async_copy(
                    source,
                    self.part(self.shard, which, columns),
                    self.sems[0].at[self.base + 6 + which],
                ).start()

    def wait(self, owner, which, slot, bit):
        part = self.part(owner, which)
        remote(part, part, self.sems, self.base + slot, self.to(bit)).wait_recv()

    def forward(self):
        for bit in (1, 2):
            which = bit - 1
            owner = self.shard ^ bit
            self.wait(owner, which, 2 * (bit - 1) + which, bit)
            part = self.part(owner, which)
            remote(part, part, self.sems, self.base + 4 + which, self.to(3 - bit)).start()

    def arrived(self):
        self.wait(self.shard ^ 1, 1, 1, 1)
        self.wait(self.shard ^ 2, 0, 2, 2)
        self.wait(self.shard ^ 3, 0, 4, 2)
        self.wait(self.shard ^ 3, 1, 5, 1)
        for which in (0, 1):
            part = self.part(self.shard, which)
            pltpu.make_async_copy(part, part, self.sems[0].at[self.base + 6 + which]).wait()

    def sent(self):
        for slot in range(6):
            part = self.part(self.shard, 0)
            remote(part, part, self.sems, self.base + slot, self.to(1)).wait_send()


class Tree:
    SLOTS = 7

    def __init__(self, source, block, sems, base, place, owner):
        self.source, self.block, self.sems, self.base = source, block, sems, base
        self.ctx, self.shard = place
        self.turn = self.shard ^ owner
        self.half = block.shape[0] // 2

    def rows(self, ref, which):
        return ref.at[pl.ds(which * self.half, self.half)]

    def copy(self, slot, ref=None):
        which = slot % 2
        bit = 1 if slot in (0, 3, 4) else 2
        return remote(
            self.rows(self.block if ref is None else ref, which),
            self.rows(self.block, which),
            self.sems,
            self.base + slot,
            (self.ctx, self.shard ^ bit),
        )

    def at(self, turn, body):
        pl.when(self.turn == turn)(body)

    def start(self):
        def body():
            self.copy(0, self.source).start()
            self.copy(1, self.source).start()
            pltpu.make_async_copy(self.source, self.block, self.sems[0].at[self.base + 6]).start()

        self.at(0, body)

    def forward(self):
        for turn, slot in ((1, 0), (2, 1)):

            def body(slot=slot):
                self.copy(slot).wait_recv()
                self.copy(slot + 2).start()

            self.at(turn, body)

    def back(self):
        def body():
            for slot in (2, 3):
                self.copy(slot).wait_recv()
                self.copy(slot + 2).start()

        self.at(3, body)

    def arrived(self):
        def body():
            pltpu.make_async_copy(self.source, self.block, self.sems[0].at[self.base + 6]).wait()

        self.at(0, body)
        self.at(1, lambda: self.copy(5).wait_recv())
        self.at(2, lambda: self.copy(4).wait_recv())

    def sent(self):
        for turn, slots in ((0, (0, 1)), (1, (2,)), (2, (3,)), (3, (4, 5))):

            def body(slots=slots):
                for slot in slots:
                    self.copy(slot).wait_send()

            self.at(turn, body)


def add_rows(dst, sources):
    step = 32

    def body(index, carry):
        rows = pl.ds(pl.multiple_of(index * step, step), step)
        total = sources[0][rows].astype(jnp.float32)
        for source in sources[1:]:
            total += source[rows].astype(jnp.float32)
        dst[rows] = total.astype(dst.dtype)
        return carry

    lax.fori_loop(0, dst.shape[0] // step, body, 0)


class Fold:
    SLOTS = 6

    def __init__(self, parts, landing, stage, carry, final, sems, local, base, place):
        self.parts, self.landing, self.stage, self.carry, self.final = parts, landing, stage, carry, final
        self.sems, self.local, self.base = sems, local, base
        self.ctx, self.shard = place
        self.half = final.shape[0] // 2

    def part(self, owner, which):
        start = pl.multiple_of((2 * owner + which) * self.half, self.half)
        return self.parts.at[pl.ds(start, self.half)]

    def landed(self, slot):
        return self.landing.at[pl.ds(slot * self.half, self.half)]

    def copy(self, src, slot, bit):
        return remote(
            src, self.landed(slot), self.sems, self.base + slot, (self.ctx, self.shard ^ bit)
        )

    def send(self, slot):
        bit, which = (1, 0) if slot < 2 else (2, 1)
        owner = self.shard ^ (3 if slot % 2 else bit)
        self.copy(self.part(owner, which), slot, bit).start()

    def load(self, index, source):
        copy = pltpu.make_async_copy(source, self.stage.at[index], self.local.at[index])
        copy.start()
        return copy

    def add(self, dst, copies):
        for copy in copies:
            copy.wait()
        add_rows(dst, [self.stage.at[index] for index in range(len(copies))])

    def wait(self, slot, bit):
        self.copy(self.landed(slot), slot, bit).wait_recv()

    def middle(self, which):
        first, second = (1, 2) if which == 0 else (2, 1)
        slot = 1 + 2 * which
        own = self.load(0, self.part(self.shard ^ second, which))
        self.wait(slot, first)
        carry = self.carry.at[which]
        self.add(carry, [own, self.load(1, self.landed(slot))])
        self.copy(carry, 4 + which, second).start()

    def finish(self, which):
        first, second = (1, 2) if which == 0 else (2, 1)
        copies = [self.load(0, self.part(self.shard, which))]
        self.wait(2 * which, first)
        copies.append(self.load(1, self.landed(2 * which)))
        self.wait(4 + which, second)
        copies.append(self.load(2, self.landed(4 + which)))
        self.add(self.final.at[pl.ds(which * self.half, self.half)], copies)

    def sent(self):
        for slot in range(6):
            self.copy(self.part(self.shard, 0), slot, 1).wait_send()


class Sink:
    def __init__(self, parts, swapped, landing, stage, carry, final, sems, local, base, place, chips):
        self.parts, self.swapped, self.landing, self.stage = parts, swapped, landing, stage
        self.carry, self.final, self.sems, self.local, self.base = carry, final, sems, local, base
        self.ctx, self.shard = place
        self.chip, self.core, self.chips = self.ctx // CORES, self.ctx % CORES, chips
        self.rows = final.shape[0]

    @staticmethod
    def slots(chips):
        return 2 * (chips - 1) + 1

    def block(self, ref, index):
        return ref.at[pl.ds(pl.multiple_of(index * self.rows, self.rows), self.rows)]

    def start(self):
        for chip in range(self.chips):
            remote(
                self.block(self.parts, CORES * chip + (self.core ^ 1)),
                self.block(self.swapped, chip),
                self.sems,
                self.base,
                (self.ctx ^ 1, self.shard),
            ).start()

    def swap(self):
        swapped = self.swapped
        remote(swapped, swapped, self.sems, self.base, (self.ctx ^ 1, self.shard)).wait_recv()

    def hop(self, out, step):
        up = (self.chip >= self.chips // 2) == out
        place = jnp.where(up, self.chip, self.chips - 1 - self.chip)
        target = place + self.chips - step
        target = jnp.where(up, target, self.chips - 1 - target)
        slot = jnp.where(up, 0, self.chips - 1) + step - 1
        sends = (place + 1 <= step) & (place < self.chips - 1)
        gets = (place <= step) & (place > 0)
        return slot, target, sends, gets, place > 0

    def landed(self, slot):
        return self.landing.at[pl.ds(pl.multiple_of(slot * self.rows, self.rows), self.rows)]

    def copy(self, out, slot):
        up = (self.chip >= self.chips // 2) == out
        return remote(
            self.carry.at[0 if out else 1],
            self.landed(slot),
            self.sems,
            self.base + 1 + slot,
            (self.ctx + jnp.where(up, CORES, -CORES), self.shard),
        )

    def load(self, index, source):
        return pltpu.make_async_copy(source, self.stage.at[index], self.local.at[index])

    def own(self, target):
        return [
            self.load(0, self.block(self.parts, CORES * target + self.core)),
            self.load(1, self.block(self.swapped, target)),
        ]

    def step(self, out, number):
        slot, target, sends, _, passes = self.hop(out, number)
        if number > 1:
            before, _, sent, gets, _ = self.hop(out, number - 1)

            @pl.when(gets)
            def _():
                remote(
                    self.landed(before), self.landed(before), self.sems, self.base + 1 + before,
                    (self.ctx ^ 1, self.shard),
                ).wait_recv()

            @pl.when(sent)
            def _():
                self.copy(out, before).wait_send()

        @pl.when(sends)
        def _():
            loads = self.own(target)
            for load in loads:
                load.start()
            carry = self.carry.at[0 if out else 1]
            stage = self.stage
            if number > 1:

                @pl.when(passes)
                def _():
                    more = self.load(2, self.landed(slot - 1))
                    more.start()
                    for load in loads + [more]:
                        load.wait()
                    add_rows(carry, [stage.at[0], stage.at[1], stage.at[2]])

                @pl.when(jnp.logical_not(passes))
                def _():
                    for load in loads:
                        load.wait()
                    add_rows(carry, [stage.at[0], stage.at[1]])
            else:
                for load in loads:
                    load.wait()
                add_rows(carry, [stage.at[0], stage.at[1]])
            self.copy(out, slot).start()

    def inward(self, number):
        self.step(False, number)

    def last(self, handed, first, own, sem):
        number = self.chips - 1
        for out in (True, False):
            slot, target, sends, _, passes = self.hop(out, number)
            before, _, sent, gets, _ = self.hop(out, number - 1)

            @pl.when(gets)
            def _(before=before):
                remote(
                    self.landed(before), self.landed(before), self.sems, self.base + 1 + before,
                    (self.ctx ^ 1, self.shard),
                ).wait_recv()

            @pl.when(sent)
            def _(out=out, before=before):
                self.copy(out, before).wait_send()

            @pl.when(sends)
            def _(out=out, slot=slot, target=target, passes=passes):
                loads = self.own(target)
                for load in loads:
                    load.start()
                for load in loads:
                    load.wait()
                carry = self.carry.at[0 if out else 1]
                add_rows(carry, [self.stage.at[0], self.stage.at[1]])

                @pl.when(passes)
                def _():
                    more = self.load(2, self.landed(slot - 1))
                    more.start()
                    more.wait()
                    add_rows(carry, [self.stage.at[0], self.stage.at[1], self.stage.at[2]])

                up = (self.chip >= self.chips // 2) == out
                for way, dst in ((True, handed[0]), (False, handed[1])):

                    @pl.when(up == way)
                    def _(dst=dst):
                        write = pltpu.make_async_copy(carry, dst.at[pl.ds(first, self.rows)], sem)
                        write.start()
                        write.wait()

        loads = self.own(self.chip)
        for load in loads:
            load.start()
        for load in loads:
            load.wait()
        add_rows(self.final, [self.stage.at[0], self.stage.at[1]])
        swapped = self.swapped
        remote(swapped, swapped, self.sems, self.base, (self.ctx ^ 1, self.shard)).wait_send()
        write = pltpu.make_async_copy(self.final, own, sem)
        write.start()
        write.wait()


TILE = 256


def block_kernel(
    sizes,
    hidden, grad, fc1, fc2, qkv, dense, segs, tables,
    ln1_gain, ln1_bias, ln2_gain, ln2_bias, dense_bias, fc2_bias, qkv_bias, fc1_bias,
    output_out, input_out, up_out, down_out, down_all, up_all, qkv_all, dense_all, sums_all,
    down_parts, up_parts, qkv_parts, dense_parts, down_land, up_land, qkv_land, dense_land,
    out_parts, out_swap, out_land, in_parts, in_swap, in_land, dense_lines,
    hid, gra, norm, w_up, w_down, w_qkv, w_dense, vec, seg, seg_col, table,
    act, wide_f, d_up, queries, keys, values, att_f, att, d_keys, d_values, d_joined, sums, sums_got, sums_tot,
    stage, down_stage, up_stage,
    down_carry, up_carry, qkv_carry, dense_carry, down_final, up_final, qkv_final, dense_final,
    out_carry, in_carry, sink_final,
    send_sems, recv_sems, local_sems,
):
    chips, shards, columns = sizes
    place = ctx, shard = lax.axis_index("ctx"), lax.axis_index("fsdp")
    chip, core = ctx // CORES, ctx % CORES
    count = CORES * chips
    sems = (send_sems, recv_sems)
    width, length = hidden.shape[1], hid.shape[0]
    ff_units = w_down.shape[0]
    head_dim = w_dense.shape[0]
    row_size = vec.shape[3]
    tiles = length // TILE
    f32, bf16 = jnp.float32, jnp.bfloat16
    factor = head_dim ** (-0.5)

    barrier = pltpu.get_barrier_semaphore()
    peers = [(ctx, shard ^ bit) for bit in (1, 2, 3)]
    peers += [(lax.rem(ctx + step, count), shard) for step in range(1, count)]
    for peer in peers:
        pl.semaphore_signal(barrier, inc=1, device_id=peer, device_id_type=pl.DeviceIdType.MESH)
    pl.semaphore_wait(barrier, len(peers))

    base = 0

    def take(slots):
        nonlocal base
        base += slots
        return base - slots

    def line(source, blocks, stride=None, offset=0, cut=slice(None)):
        return Line(source, blocks, sems, take(Line.slots(chips)), place, chips, stride, offset, cut)

    def fold(parts, landing, stage, carry, final):
        return Fold(
            parts, landing, stage, carry, final, sems, local_sems.at[pl.ds(4, 4)], take(Fold.SLOTS), place
        )

    def sink(parts, swapped, landing, carry):
        return Sink(
            parts, swapped, landing, down_stage, carry, sink_final, sems, local_sems.at[pl.ds(4, 4)],
            take(Sink.slots(chips)), place, chips,
        )

    def halves(ref, which, start, size):
        half = ref.shape[0] // 2
        return ref.at[pl.ds(which * half, half), pl.ds(pl.multiple_of(start, size), size)]

    def up_pieces(which):
        stride = fc1.shape[1] // shards
        return [
            (
                halves(fc1, which, index * stride + ctx * columns, columns),
                pl.ds(index * columns, columns),
            )
            for index in range(shards)
        ]

    def down_pieces(which):
        half = columns // 2
        start = pl.multiple_of(ctx * columns + which * half, half)
        return [(fc2.at[pl.ds(start, half)], slice(None))]

    def qkv_pieces(which):
        return [
            (
                halves(qkv, which, index * width + ctx * head_dim, head_dim),
                pl.ds(index * head_dim, head_dim),
            )
            for index in range(3)
        ]

    hid_line, gra_line = line(hidden, hid), line(grad, gra)
    squares = [
        Square(pieces, blocks, sems, take(Square.SLOTS), place)
        for pieces, blocks in ((up_pieces, w_up), (down_pieces, w_down), (qkv_pieces, w_qkv))
    ]
    up_square, down_square, qkv_square = squares
    heads_here = dense.shape[0] // head_dim
    dense_rows = dense.at[
        pl.ds(pl.multiple_of(lax.rem(ctx, heads_here) * head_dim, head_dim), head_dim)
    ]
    tree = Tree(dense_rows, w_dense, sems, take(Tree.SLOTS), place, ctx // heads_here)
    named = {"hid": hid_line, "gra": gra_line, "wu": up_square, "wd": down_square, "wq": qkv_square, "wt": tree}
    folds, lines = [], []

    def gradient(letter, cuts, parts, landing, stage, carry, final, gathered):
        start, half = 0, final.shape[0] // 2
        for index, (size, split) in enumerate(cuts):
            cut = pl.ds(start, size)
            item = fold(
                parts.at[:, cut], landing.at[:, cut], stage.at[:, :, :size], carry.at[:, :, cut], final.at[:, cut]
            )
            folds.append(item)
            named[f"f{letter}{index}"] = item
            for which in range(2 if split else 1):
                rows = half if split else 2 * half
                item = line(
                    final.at[pl.ds(which * rows, rows), cut], gathered, final.shape[0], which * rows, cut
                )
                lines.append(item)
                named[f"l{letter}{index}{which}"] = item
            start += size

    gradient("d", DOWN_CUTS, down_parts, down_land, down_stage, down_carry, down_final, down_all)
    gradient("u", UP_CUTS, up_parts, up_land, up_stage, up_carry, up_final, up_all)
    gradient("q", QKV_CUTS, qkv_parts, qkv_land, up_stage, qkv_carry, qkv_final, qkv_all)
    gradient("e", DENSE_CUTS, dense_parts, dense_land, down_stage, dense_carry, dense_final, dense_lines)
    named["ls"] = line(sums_tot, sums_all)
    lines.append(named["ls"])
    out_sink = sink(out_parts, out_swap, out_land, out_carry)
    in_sink = sink(in_parts, in_swap, in_land, in_carry)
    named["so"], named["si"] = out_sink, in_sink

    small = []

    def send_small(src, dst, landing, device):
        slot = take(1)
        small.append((remote(src, dst, sems, slot, device), landing, slot))
        small[-1][0].start()

    def wait_small(items):
        for _, landing, slot in items:
            remote(landing, landing, sems, slot, (ctx ^ 1, shard)).wait_recv()

    vectors = (
        ln1_gain, ln1_bias, ln2_gain, ln2_bias, dense_bias, fc2_bias, qkv_bias, fc1_bias
    )
    at, pairs = 0, [(segs, seg.at[ctx]), (tables, table)]
    for vector in vectors:
        size = vec.shape[3]
        for start in range(0, vector.shape[0], size):
            pairs.append((vector.at[pl.ds(start, size)], vec.at[shard, at, 0]))
            at += 1
    locals_in = [
        pltpu.make_async_copy(src, dst, local_sems.at[8 + index])
        for index, (src, dst) in enumerate(pairs)
    ]
    for copy in locals_in:
        copy.start()

    def small_start():
        for copy in locals_in:
            copy.wait()
        for bit in (1, 2, 3):
            send_small(vec.at[shard], vec.at[shard], vec.at[shard ^ bit], (ctx, shard ^ bit))
        for step in range(1, count):
            send_small(
                segs, seg.at[ctx], seg.at[lax.rem(ctx + count - step, count)],
                (lax.rem(ctx + step, count), shard),
            )

    def small_land():
        wait_small(small)

    def vector(row):
        return jnp.concatenate([vec[index, row] for index in range(shards)], axis=1)

    def rows_of(index):
        return pl.ds(pl.multiple_of(index * TILE, TILE), TILE)

    def loop(body, steps=tiles):
        lax.fori_loop(0, steps, lambda index, carry: (body(rows_of(index)), carry)[1], 0)

    def scaled_rows(rows):
        return centred(hid[rows])[0]

    def norm_two(rows):
        norm[rows] = (scaled_rows(rows) * vector(2) + vector(3)).astype(bf16)

    def norm_one(rows):
        norm[rows] = (scaled_rows(rows) * vector(0) + vector(1)).astype(bf16)

    def emit(steps, compute, dst, size, start=0):
        def write(index):
            return pltpu.make_async_copy(
                stage.at[lax.rem(index, 2), :, :size],
                dst.at[rows_of(index), pl.ds(start, size)],
                local_sems.at[lax.rem(index, 2)],
            )

        def body(index, carry):
            @pl.when(index >= 2)
            def _():
                write(index - 2).wait()

            stage[lax.rem(index, 2), :, :size] = compute(index).astype(bf16)
            write(index).start()
            return carry

        lax.fori_loop(0, steps, body, 0)
        write(steps - 2).wait()
        write(steps - 1).wait()

    def feed_forward():
        bias_start = ctx * columns
        bias_row = 9 + bias_start // row_size
        bias_column = pl.multiple_of(lax.rem(bias_start, row_size), columns)
        up_bias = jnp.concatenate(
            [vec[index, bias_row, :, pl.ds(bias_column, columns)] for index in range(shards)],
            axis=1,
        )

        def body(rows):
            value = dot(norm[rows], w_up[...]) + up_bias
            cdf = 0.5 * (1.0 + lax.erf(value * (0.5**0.5)))
            density = jnp.exp(-0.5 * value * value) * ((2.0 * math.pi) ** -0.5)
            act[rows] = (value * cdf).astype(bf16)
            wide_f[rows] = cdf + value * density

        loop(body)

    def down_grad(index):
        start, size = sum(cut[0] for cut in DOWN_CUTS[:index]), DOWN_CUTS[index][0]

        def body(step, carry):
            rows = rows_of(shard ^ (3 - step))
            cut = pl.ds(start, size)
            stage[0, :, :size] = dot_rows(act[:, rows], gra[:, cut]).astype(bf16)
            write = pltpu.make_async_copy(
                stage.at[0, :, :size], down_parts.at[rows, cut], local_sems.at[0]
            )
            write.start()
            write.wait()
            for number, slot in ((0, 1), (0, 3), (1, 2), (2, 0)):

                @pl.when(step == number)
                def _(slot=slot):
                    named[f"fd{index}"].send(slot)

            return carry

        lax.fori_loop(0, shards, body, 0)

    def feed_back():
        def body(rows):
            d_up[rows] = (dot_cols(gra[rows], w_down[...]) * wide_f[rows]).astype(bf16)

        loop(body)

    def up_grad(index):
        start, size = sum(cut[0] for cut in UP_CUTS[:index]), UP_CUTS[index][0]
        emit(
            width // TILE,
            lambda step: dot_rows(norm[:, rows_of(step)], d_up[:, pl.ds(start, size)]),
            up_parts,
            size,
            start,
        )

    rotary = table.shape[2]

    def turn(entries, rows, way):
        first = entries[:, :rotary]
        first = (
            first * table[0, rows]
            + way * (pltpu.roll(first, ROT // 2, 1) * table[1, rows])
            + way * (pltpu.roll(first, rotary - ROT // 2, 1) * table[2, rows])
        )
        return jnp.concatenate([first, entries[:, rotary:]], axis=1)

    def project():
        per = 3 * HEADS // shards
        bias_parts = []
        for index in range(3):
            place = index * HEADS + ctx
            rest = lax.rem(place, per) * head_dim
            bias_parts.append(
                vec[
                    place // per,
                    6 + rest // row_size,
                    :,
                    pl.ds(pl.multiple_of(lax.rem(rest, row_size), head_dim), head_dim),
                ]
            )

        def body(rows):
            joined = dot(norm[rows], w_qkv[...])
            parts = [
                joined[:, index * head_dim : (index + 1) * head_dim] + bias_parts[index]
                for index in range(3)
            ]
            queries[rows] = turn(parts[0], rows, 1.0).astype(bf16)
            keys[rows] = turn(parts[1], rows, 1.0).astype(bf16)
            values[rows] = parts[2].astype(bf16)

        loop(body)
        side = segs.shape[1]
        for index in range(count):
            block = seg[index].astype(f32)
            seg_col[index * side : (index + 1) * side] = jnp.broadcast_to(block, (side, side)).T

    def attend(index):
        rows = pl.ds(index * TILE, TILE)
        size = (index + 1) * TILE
        seg_row = jnp.concatenate([seg[block] for block in range(count)], axis=1)
        scores = dot_cols(queries[rows], keys[:size]) * factor
        query_place = index * TILE + lax.broadcasted_iota(jnp.int32, (TILE, size), 0)
        key_place = lax.broadcasted_iota(jnp.int32, (TILE, size), 1)
        same = seg_col[rows][:, :1] == seg_row[:, :size].astype(f32)
        allowed = (key_place <= query_place) & same
        scores = jnp.where(allowed, scores, -1e30)
        terms = jnp.where(
            allowed, jnp.exp(scores - jnp.max(scores, axis=-1, keepdims=True)), 0.0
        )
        probs = terms / jnp.sum(terms, axis=-1, keepdims=True)
        wide_f[rows, :size] = probs
        result = dot(probs.astype(bf16), values[:size])
        att_f[rows] = result
        att[rows] = result.astype(bf16)

    def attend_all():
        for index in range(tiles):
            attend(index)

    def output():
        def body(index):
            rows = rows_of(index)
            return dot(att[rows], w_dense[...]) + dot(act[rows], w_down[...])

        emit(tiles, body, out_parts, width)

    dense_size = width // shards

    def dense_grad():
        def body(index):
            start = pl.multiple_of(index * dense_size, dense_size)
            return dot_rows(att[...], gra[:, pl.ds(start, dense_size)])

        emit(shards, body, dense_parts, dense_size)

    def attend_back(index):
        rows = pl.ds(index * TILE, TILE)
        size = (index + 1) * TILE
        d_att = dot_cols(gra[rows], w_dense[...]).astype(bf16)
        delta = jnp.sum(d_att.astype(f32) * att_f[rows], axis=-1, keepdims=True)
        probs = wide_f[rows, :size]
        d_scores = (probs * (dot_cols(d_att, values[:size]) - delta)).astype(bf16)
        d_queries = dot(d_scores, keys[:size]) * factor
        d_joined[rows, :head_dim] = turn(d_queries, rows, -1.0).astype(bf16)
        d_keys[:size] += dot_rows(d_scores, queries[rows])
        d_values[:size] += dot_rows(probs.astype(bf16), d_att)

    def attend_back_all():
        d_keys[...] = jnp.zeros_like(d_keys)
        d_values[...] = jnp.zeros_like(d_values)
        for index in range(tiles):
            attend_back(index)

        def join(rows):
            d_joined[rows, head_dim : 2 * head_dim] = turn(d_keys[rows] * factor, rows, -1.0).astype(bf16)
            d_joined[rows, 2 * head_dim :] = d_values[rows].astype(bf16)

        loop(join)

    def qkv_grad(index):
        start, size = sum(cut[0] for cut in QKV_CUTS[:index]), QKV_CUTS[index][0]
        emit(
            width // TILE,
            lambda step: dot_rows(norm[:, rows_of(step)], d_joined[:, pl.ds(start, size)]),
            qkv_parts,
            size,
            start,
        )

    def inputs():
        sums[...] = jnp.zeros_like(sums)

        def body(index):
            rows = rows_of(index)
            d_one = dot_cols(d_joined[rows], w_qkv[...])
            d_two = dot_cols(d_up[rows], w_up[...])
            scaled = scaled_rows(rows)

            def gather(row, entries):
                sums[row : row + 1, : entries.shape[1]] += jnp.sum(
                    entries.astype(f32), axis=0, keepdims=True
                )

            gather(0, d_two * scaled)
            gather(1, d_two)
            gather(2, gra[rows])
            gather(3, d_up[rows])
            gather(4, d_one * scaled)
            gather(5, d_one)
            gather(6, d_joined[rows])
            return d_one * vector(0) + d_two * vector(2)

        emit(tiles, body, in_parts, width)

    sums_items = []

    def sums_start():
        for bit in (1, 2, 3):
            send_small(sums, sums_got.at[shard], sums_got.at[shard ^ bit], (ctx, shard ^ bit))
            sums_items.append(small[-1])
        sums_got[shard] = sums[...]

    def sums_land():
        wait_small(sums_items)
        total = sums_got[0]
        for index in range(1, shards):
            total = total + sums_got[index]
        sums_tot[...] = total
        sums_tot[7:8] = vector(4) + vector(5)

    exchanged = []

    def dense_block(owner):
        return pl.ds(pl.multiple_of(owner * dense_size, dense_size), dense_size)

    def own_dense():
        return pltpu.make_async_copy(
            dense_lines.at[dense_block(shard)], dense_all.at[dense_block(shard)], local_sems.at[2]
        )

    def dense_part(owner, side):
        size = dense_size // CORES
        return pl.ds(pl.multiple_of(owner * dense_size + side * size, size), size)

    def exchange():
        for bit in (1, 2, 3):
            peer = shard ^ bit
            send_small(
                dense_lines.at[dense_part(peer, core)], dense_all.at[dense_part(shard, core)],
                dense_all.at[dense_part(peer, core)], (ctx, peer),
            )
            exchanged.append(small[-1])
        own_dense().start()

    relayed = []

    def relay():
        wait_small(exchanged)
        for bit in (1, 2, 3):
            rows = dense_part(shard ^ bit, core)
            send_small(
                dense_all.at[rows], dense_all.at[rows], dense_all.at[dense_part(shard ^ bit, 1 - core)],
                (ctx ^ 1, shard),
            )
            relayed.append(small[-1])

    def relay_done():
        wait_small(relayed)
        own_dense().wait()

    steps = {
        "small_start": small_start, "small_land": small_land, "norm_two": lambda: loop(norm_two),
        "norm_one": lambda: loop(norm_one), "feed_forward": feed_forward, "down_grad": down_grad,
        "feed_back": feed_back, "up_grad": up_grad, "project": project, "attend": attend_all, "output": output,
        "dense_grad": dense_grad, "attend_back": attend_back_all, "qkv_grad": qkv_grad, "inputs": inputs,
        "sums_start": sums_start, "sums_land": sums_land, "exchange": exchange, "relay": relay,
        "relay_done": relay_done,
        "output_done": lambda: out_sink.last((up_out, down_out), 0, output_out, local_sems.at[3]),
        "input_done": lambda: in_sink.last(
            (up_out, down_out), hidden.shape[0], input_out, local_sems.at[3]
        ),
    }
    for step in ORDER:
        name, *rest = step.split(".")
        if name in steps:
            steps[name](*[int(number) for number in rest])
        else:
            method = getattr(named[name], {"in": "inward"}.get(rest[0], rest[0]))
            numbers = [int(number) for number in rest[1:] if number.isdigit()]
            if rest[-1] in WHERE:
                pl.when(((chip == 0) | (chip == chips - 1)) == WHERE[rest[-1]])(
                    functools.partial(method, *numbers)
                )
            else:
                method(*numbers)

    for name, item in named.items():
        if isinstance(item, Line) and name + ".arrived" not in ORDER:
            item.arrived()
    for name, item in named.items():
        if not isinstance(item, Sink) and name + ".sent" not in ORDER:
            item.sent()
    for copy, _, _ in small:
        copy.wait_send()


DOWN_CUTS = ((512, False), (512, False), (1024, True))
UP_CUTS = ((512, True), (512, True))
QKV_CUTS = ((768, True),)
DENSE_CUTS = ((512, False),)

WHERE = {"e": True, "m": False}

ORDER = (
    "wu.start.0", "hid.start", "wu.start.1", "gra.start", "wd.start.0.e", "wu.forward", "wd.forward.e",
    "small_start", "wq.start.0.e", "hid.out.1", "hid.in.1", "wd.start.0.m", "wd.start.1.m", "wq.start.1.e",
    "gra.out.1", "gra.in.1", "hid.out.2", "hid.out.3", "small_land", "hid.arrived", "norm_two", "gra.out.2",
    "wu.arrived", "feed_forward", "gra.out.3", "gra.arrived", "down_grad.0", "fd0.middle.1", "fd0.middle.0",
    "wd.forward.m", "wd.start.1.e", "fd0.finish.1", "fd0.finish.0", "ld00.start", "down_grad.2", "wd.arrived",
    "feed_back", "fd2.middle.1", "fd2.middle.0", "ld00.out.1", "up_grad.1", "fu1.send.3", "fu1.send.0", "fu1.send.2",
    "fd2.finish.1", "ld21.start", "fu1.send.1", "ld00.in.1", "fd2.finish.0", "ld20.start", "fu1.middle.1",
    "ld21.out.1", "down_grad.1", "fu1.middle.0", "wq.start.0.m", "ld00.out.2", "fu1.finish.1", "lu11.start",
    "fd1.middle.0", "wt.start", "fd1.middle.1", "up_grad.0", "fu0.send.1", "ld21.in.1", "fu0.send.3", "ld20.out.1",
    "wq.forward.e", "fu1.finish.0", "lu10.start", "fu1.sent", "wq.forward.m", "lu11.out.1", "ld20.in.1", "fd2.sent",
    "wq.start.1.m", "fd1.finish.0", "fd1.finish.1", "ld10.start", "lu10.out.1", "lu11.in.1", "wt.forward",
    "ld00.out.3", "ld10.out.1", "ld21.out.2", "fu0.send.2", "fu0.middle.1", "lu10.in.1", "norm_one", "ld20.out.2",
    "fu0.send.0", "fu0.middle.0", "ld10.in.1", "lu10.out.2", "lu11.out.2", "wq.arrived", "project", "attend",
    "wt.back", "dense_grad", "fe0.send.2", "fe0.send.3", "fe0.send.0", "fe0.send.1", "fu0.finish.1", "lu01.start",
    "fu0.finish.0", "lu00.start", "wt.arrived", "attend_back", "qkv_grad.0", "fq0.send.1", "fq0.send.3",
    "ld10.out.2", "fe0.middle.0", "lu00.out.1", "lu01.out.1", "lu00.in.1", "fe0.middle.1", "output", "fq0.middle.0",
    "fq0.send.0", "fq0.send.2", "lu00.out.2", "lu01.in.1", "fe0.finish.1", "fe0.finish.0", "le00.start",
    "fq0.middle.1", "so.start", "fq0.finish.0", "lq00.start", "lu00.out.3", "ld10.out.3", "so.swap", "le00.in.1",
    "wu.sent", "so.in.1", "fd1.sent", "fq0.finish.1", "lq01.start", "le00.out.1", "inputs", "si.start", "sums_start",
    "le00.out.2", "lq00.in.1", "sums_land", "ls.start", "si.swap", "si.in.1", "ld20.out.3", "lu01.out.2",
    "le00.out.3", "ls.in.1", "ld21.out.3", "ld21.arrived", "lq01.in.1", "ld10.arrived", "ls.out.1", "fq0.sent",
    "le00.arrived", "exchange", "fu0.sent", "le00.sent", "lq01.out.1", "ld21.sent", "lu10.out.3", "lu11.out.3",
    "wq.sent", "lu00.arrived", "lu11.arrived", "lu11.sent", "lu01.out.3", "lu00.sent", "si.in.2", "ls.out.2",
    "lu10.arrived", "lu10.sent", "fd0.sent", "ld20.arrived", "ld00.arrived", "lq01.out.2", "gra.sent", "ls.out.3",
    "relay", "ld00.sent", "ls.arrived", "lu01.arrived", "so.in.2", "fe0.sent", "lu01.sent", "hid.sent", "relay_done",
    "ld10.sent", "ld20.sent", "wd.sent", "ls.sent", "wt.sent", "lq00.out.1", "lq01.out.3", "input_done",
    "lq01.arrived", "lq00.out.2", "output_done", "lq00.out.3", "lq01.sent", "lq00.arrived", "lq00.sent",
)


def rotary_table(length, lanes):
    half = ROT // 2
    freqs = (10000.0 ** (-2.0 * np.arange(half, dtype=np.float32) / ROT)).astype(np.float32)
    angles = np.arange(length, dtype=np.float32)[:, None] * freqs[None]
    cosine, sine = np.cos(angles), np.sin(angles)
    table = np.zeros((3, length, lanes), np.float32)
    table[0] = 1.0
    table[0, :, :half], table[0, :, half:ROT] = cosine, cosine
    table[1, :, half:ROT] = sine
    table[2, :, :half] = -sine
    return table


def whole_block(hidden, grad, fc1, fc2, qkv, dense, segs, vectors):
    chips, shards = lax.axis_size("ctx") // CORES, lax.axis_size("fsdp")
    count = chips * CORES
    tokens, width = hidden.shape
    length = tokens * count
    units = fc1.shape[1] // count
    head_dim = width // HEADS
    part = units // shards
    rows = width // shards
    bf16, f32 = jnp.bfloat16, jnp.float32
    wide, joint = (length, width), 3 * head_dim
    vec_shape = (shards, sum(vector.shape[0] for vector in vectors) // rows, 1, rows)
    seg_shape = (count,) + segs.shape
    line = (tokens, width)
    hops = (2 * (chips - 1) * tokens, width)
    outs = [
        (line, f32), (line, f32), ((2 * tokens, width), bf16), ((2 * tokens, width), bf16),
        ((count * part, width), bf16), ((count * rows, units), bf16),
        ((count * rows, joint), bf16), ((width, rows), bf16), ((count * 8, width), f32),
        ((units, width), bf16), ((width, units), bf16), ((width, joint), bf16), ((shards * head_dim, rows), bf16),
        ((3 * part, width), bf16), ((3 * rows, units), bf16), ((3 * rows, joint), bf16), ((3 * head_dim, rows), bf16),
        (wide, bf16), ((chips * tokens, width), bf16), (hops, bf16),
        (wide, bf16), ((chips * tokens, width), bf16), (hops, bf16), ((count * head_dim, rows), bf16),
    ]
    table = rotary_table(length, 128)
    cuts = DOWN_CUTS + UP_CUTS + QKV_CUTS + DENSE_CUTS
    halves = [(part // 2, width), (rows // 2, units), (rows // 2, joint), (head_dim // 2, rows)]
    scratch = [
        (wide, bf16), (wide, bf16), (wide, bf16), ((width, units), bf16), ((units, width), bf16),
        ((width, joint), bf16), ((head_dim, width), bf16), (vec_shape, f32), (seg_shape, segs.dtype),
        ((length, segs.shape[1]), f32), (table.shape, f32),
        ((length, units), bf16), ((length, max(units, length)), f32), ((length, units), bf16),
        ((length, head_dim), bf16), ((length, head_dim), bf16), ((length, head_dim), bf16),
        ((length, head_dim), f32), ((length, head_dim), bf16), ((length, head_dim), f32), ((length, head_dim), f32),
        ((length, joint), bf16), ((8, width), f32), ((shards, 8, width), f32), ((8, width), f32),
        ((2, TILE, width), bf16),
    ]
    scratch += [((3,) + half, bf16) for half in halves[:2]]
    scratch += [((2,) + half, bf16) for half in halves]
    scratch += [((2 * half[0], half[1]), bf16) for half in halves]
    scratch += [((2, tokens, width), bf16), ((2, tokens, width), bf16), (line, f32)]
    slots = (
        (3 + sum(1 + split for _, split in cuts)) * Line.slots(chips)
        + 3 * Square.SLOTS + Tree.SLOTS + len(cuts) * Fold.SLOTS + 2 * Sink.slots(chips) + 12 + count - 1
    )
    outputs = pl.pallas_call(
        functools.partial(block_kernel, (chips, shards, part)),
        out_shape=[jax.ShapeDtypeStruct(shape, kind) for shape, kind in outs],
        in_specs=[pl.BlockSpec(memory_space=pl.ANY)] * 16,
        out_specs=[pl.BlockSpec(memory_space=pl.ANY)] * len(outs),
        scratch_shapes=[pltpu.VMEM(shape, kind) for shape, kind in scratch]
        + [
            pltpu.SemaphoreType.DMA((slots,)),
            pltpu.SemaphoreType.DMA((slots,)),
            pltpu.SemaphoreType.DMA((24,)),
        ],
        compiler_params=pltpu.CompilerParams(
            collective_id=0, has_side_effects=True, vmem_limit_bytes=62 * 2**20
        ),
        name="whole_block",
    )(hidden, grad, fc1, fc2, qkv, dense, segs, jnp.asarray(table), *vectors)
    return outputs[:9]


FINISH_STEPS = 4


def widen_kernel(
    sizes,
    up_all, qkv_all, dense_all, down_all, sums,
    gain_one, shift_one, qkv, qkv_bias, dense, columns_one, gain_two, shift_two, up, up_bias, down, columns_two,
):
    count, shards, width = sizes
    f32 = jnp.float32

    def spread(src, dst, pieces):
        groups, size = src.shape[0], src.shape[2] // pieces
        for piece in range(pieces):
            for group in range(groups):
                start = (piece * groups + group) * size
                dst[:, start : start + size] = src[group, :, piece * size : (piece + 1) * size].astype(f32)

    spread(up_all, up, shards)
    spread(qkv_all, qkv, 3)
    spread(dense_all, dense, 1)
    down[...] = down_all[...].astype(f32)

    @pl.when(pl.program_id(0) == 0)
    def _():
        shard = lax.axis_index("fsdp")
        rows = gain_one.shape[1]
        mine = pl.ds(pl.multiple_of(shard * rows, rows), rows)
        for row, dst in ((0, gain_two), (1, shift_two), (4, gain_one), (5, shift_one)):
            total = sums[0, row : row + 1, mine]
            for index in range(1, count):
                total = total + sums[index, row : row + 1, mine]
            dst[...] = total
        columns_one[...] = sums[0, 2:3, mine]
        columns_two[...] = sums[0, 2:3, mine]
        part = up_bias.shape[1] // count
        here = pl.ds(pl.multiple_of(shard * part, part), part)
        for index in range(count):
            up_bias[:, index * part : (index + 1) * part] = sums[index, 3:4, here]
        size = width // count
        chunks = qkv_bias.shape[0] // size
        for chunk in range(chunks):
            place = shard * chunks + chunk
            start = pl.multiple_of(place // count * size, size)
            qkv_bias[chunk * size : (chunk + 1) * size] = sums[
                lax.rem(place, count), 6, pl.ds(start, size)
            ]


def sliced(shape, steps):
    block = shape[:-2] + (shape[-2] // steps, shape[-1])
    return pl.BlockSpec(block, lambda index: (0,) * (len(shape) - 2) + (index, 0))


def entire(shape, _=None):
    return pl.BlockSpec(shape, lambda index: (0,) * len(shape))


def widen(up_all, qkv_all, dense_all, down_all, sums, width):
    count, shards = lax.axis_size("ctx"), lax.axis_size("fsdp")
    rows = width // shards
    f32 = jnp.float32
    steps = FINISH_STEPS
    grads = [
        up_all.reshape(count, rows, -1), qkv_all.reshape(count, rows, -1), dense_all.reshape(shards, rows, rows),
        down_all,
    ]
    units = up_all.shape[1] * count
    sums = sums.reshape(count, 8, width)
    vector = (1, rows)
    outs = [
        (vector, entire), (vector, entire), ((rows, 3 * width), sliced), ((3 * rows,), entire),
        ((rows, width), sliced), (vector, entire), (vector, entire), (vector, entire), ((rows, units), sliced),
        ((1, units // shards), entire), (down_all.shape, sliced), (vector, entire),
    ]
    size = sum(math.prod(shape) for shape, _ in outs)
    return pl.pallas_call(
        functools.partial(widen_kernel, (count, shards, width)),
        grid=(steps,),
        in_specs=[sliced(array.shape, steps) for array in grads] + [entire(sums.shape)],
        out_specs=[kind(shape, steps) for shape, kind in outs],
        out_shape=[jax.ShapeDtypeStruct(shape, f32) for shape, _ in outs],
        compiler_params=pltpu.CompilerParams(vmem_limit_bytes=62 * 2**20),
        cost_estimate=pl.CostEstimate(flops=size, bytes_accessed=6 * size, transcendentals=0),
        name="widen",
    )(*grads, sums)


def close_kernel(sums, branch, back, upward, downward, hidden, grad, output, input_grad):
    f32 = jnp.float32
    own = hidden[...].astype(f32)
    shift = sums[7:8]

    def total(ref, index):
        return ref[...] + upward[index].astype(f32) + downward[index].astype(f32)

    output[...] = (own + total(branch, 0) + shift).astype(output.dtype)
    scaled, spread = centred(own)
    e = total(back, 1)
    part = spread * (
        e
        - jnp.mean(e, axis=-1, keepdims=True)
        - scaled * jnp.mean(e * scaled, axis=-1, keepdims=True)
    )
    input_grad[...] = (grad[...].astype(f32) + part).astype(input_grad.dtype)


def close(sums, branch, back, upward, downward, hidden, grad):
    steps = 2
    shape = hidden.shape
    both = (2,) + shape
    wide = sliced(shape, steps)
    return pl.pallas_call(
        close_kernel,
        grid=(steps,),
        in_specs=[entire((8, shape[1])), wide, wide, sliced(both, steps), sliced(both, steps), wide, wide],
        out_specs=[wide, wide],
        out_shape=[jax.ShapeDtypeStruct(shape, hidden.dtype)] * 2,
        compiler_params=pltpu.CompilerParams(vmem_limit_bytes=62 * 2**20),
        name="close",
    )(sums, branch, back, upward.reshape(both), downward.reshape(both), hidden, grad)


def one_kernel(
    hidden, qkv_weight, dense_weight, fc1_weight, fc2_weight, segments, out_grad, vectors
):
    branch, back, up_out, down_out, down_all, up_all, qkv_all, dense_all, sums_all = whole_block(
        hidden[0], out_grad[0], fc1_weight, fc2_weight, qkv_weight, dense_weight, segments, vectors
    )
    count = lax.axis_size("ctx")
    upward = lax.ppermute(up_out, "ctx", [(index, index + CORES) for index in range(count - CORES)])
    downward = lax.ppermute(down_out, "ctx", [(index + CORES, index) for index in range(count - CORES)])
    outs = widen(up_all, qkv_all, dense_all, down_all, sums_all, hidden.shape[2])
    outs = [out.reshape(-1) if out.shape[0] == 1 else out for out in outs]
    output, input_grad = close(sums_all, branch, back, upward, downward, hidden[0], out_grad[0])
    return (output[None], input_grad[None], *outs)


def per_device(
    hidden,
    ln1_gain,
    ln1_bias,
    qkv_weight,
    qkv_bias,
    dense_weight,
    dense_bias,
    ln2_gain,
    ln2_bias,
    fc1_weight,
    fc1_bias,
    fc2_weight,
    fc2_bias,
    segments,
    out_grad,
):
    ctx_count = lax.axis_size("ctx")
    shards = lax.axis_size("fsdp")
    ctx = lax.axis_index("ctx")
    tokens, width = hidden.shape[1], hidden.shape[2]
    length = tokens * ctx_count
    head_dim = width // HEADS
    repeat = ctx_count // HEADS
    head = ctx // repeat
    factor = head_dim ** (-0.5)
    rows = width // shards
    ff = fc1_weight.shape[1]
    units = ff // shards // ctx_count
    bf16, f32 = jnp.bfloat16, jnp.float32

    vectors = [ln1_gain, ln1_bias, ln2_gain, ln2_bias, dense_bias, fc2_bias, qkv_bias, fc1_bias]
    if ctx_count == HEADS and shards == 4 and width == sum(size for size, _ in DOWN_CUTS):
        return one_kernel(
            hidden, qkv_weight, dense_weight, fc1_weight, fc2_weight, segments, out_grad, vectors
        )
    vectors = jnp.concatenate(vectors).reshape(-1, rows)
    vec = lax.all_gather(vectors, "fsdp", axis=0)
    query_seg = lax.all_gather(segments[0], "ctx", axis=0, tiled=True)
    up_part = lax.dynamic_index_in_dim(
        fc1_weight.reshape(rows, shards, ctx_count, units), ctx, 2, keepdims=False
    ).reshape(rows, shards * units)
    down_part = lax.dynamic_slice_in_dim(fc2_weight, ctx * units, units, 0)
    qkv_part = lax.dynamic_index_in_dim(
        qkv_weight.reshape(rows, 3, HEADS, head_dim), head, 2, keepdims=False
    ).reshape(rows, 3 * head_dim)
    dense_cols = lax.all_to_all(
        dense_weight, "fsdp", split_axis=1, concat_axis=0, tiled=True
    )
    dense_part = lax.dynamic_slice_in_dim(dense_cols, head * head_dim, head_dim, 0)
    up_w = gather_fsdp(up_part)
    down_w = gather_fsdp(down_part)
    qkv_w = gather_fsdp(qkv_part)
    dense_w = gather_fsdp(dense_part, axis=1)
    hidden_all = line_gather(hidden[0]).reshape(length, width)
    grad_all = line_gather(out_grad[0]).reshape(length, width)
    normed_one = (centred(hidden_all)[0] * vec[:, 0].reshape(-1) + vec[:, 1].reshape(-1)).astype(bf16)
    scaled = centred(hidden_all)[0]
    gain_two = vec[:, 2].reshape(-1)
    normed_two = (scaled * gain_two + vec[:, 3].reshape(-1)).astype(bf16)
    up_shift = lax.dynamic_index_in_dim(
        vec[:, 9 : 9 + ff // width].reshape(shards, ctx_count, units), ctx, 1, keepdims=False
    ).reshape(-1)
    act_f, slope = gelu_and_slope(dot(normed_two, up_w) + up_shift)
    act = act_f.astype(bf16)
    d_up = (dot_cols(grad_all, down_w) * slope).astype(bf16)
    down_part_grad = dot_rows(act, grad_all).astype(bf16)
    up_part_grad = dot_rows(normed_two, d_up).astype(bf16)
    ff_part = dot(act, down_w).astype(bf16)
    d_two = dot_cols(d_up, up_w)
    e_two = (d_two * gain_two).astype(bf16)
    gain_two_sum, shift_two_sum = jnp.sum(d_two * scaled, axis=0), jnp.sum(d_two, axis=0)
    columns = jnp.sum(grad_all.astype(f32), axis=0)
    up_sum = jnp.sum(d_up.astype(f32), axis=0)
    gain_one = vec[:, 0].reshape(-1)
    dense_shift, down_shift = vec[:, 4].reshape(-1), vec[:, 5].reshape(-1)
    qkv_shift = vec[:, 6:9].reshape(-1)
    down_grad = scatter_fsdp(down_part_grad)
    up_grad = scatter_fsdp(up_part_grad)

    qkv_shift_part = lax.dynamic_index_in_dim(
        qkv_shift.reshape(3, HEADS, head_dim), head, 1, keepdims=False
    ).reshape(-1)
    joined = dot(normed_one, qkv_w) + qkv_shift_part
    places = jnp.arange(length, dtype=jnp.int32)
    cosine, sine = rotary_tables(places, ROT)
    queries = rotate(joined[:, :head_dim], cosine, sine).astype(bf16)
    keys = rotate(joined[:, head_dim : 2 * head_dim], cosine, sine).astype(bf16)
    values = joined[:, 2 * head_dim :].astype(bf16)
    allowed = (places[None, :] <= places[:, None]) & (query_seg[None, :] == query_seg[:, None])
    if repeat > 1:
        allowed = allowed & (places // (length // repeat) == ctx % repeat)[:, None]
    scores = jnp.where(allowed, dot_cols(queries, keys) * factor, -1e30)
    top = jnp.max(scores, axis=-1, keepdims=True)
    terms = jnp.where(allowed, jnp.exp(scores - top), 0.0)
    total = jnp.sum(terms, axis=-1, keepdims=True)
    probs = terms * jnp.where(total > 0.0, 1.0 / total, 0.0)
    probs_low = probs.astype(bf16)
    att_f = dot(probs_low, values)
    att = att_f.astype(bf16)
    partial = dot(att, dense_w) + ff_part.astype(f32)
    branch = lax.psum_scatter(partial.astype(bf16), "ctx", scatter_dimension=0, tiled=True)
    own = hidden[0].astype(f32)
    layer_output = (own + branch.astype(f32) + dense_shift + down_shift).astype(bf16)

    d_att = dot_cols(grad_all, dense_w).astype(bf16)
    delta = jnp.sum(d_att.astype(f32) * att_f, axis=-1, keepdims=True)
    dense_grad = dot_rows(att, grad_all).astype(bf16)
    d_scores = (probs * (dot_cols(d_att, values) - delta)).astype(bf16)
    d_queries = rotate(dot(d_scores, keys) * factor, cosine, -sine)
    d_keys = rotate(dot_rows(d_scores, queries) * factor, cosine, -sine)
    d_values = dot_rows(probs_low, d_att)
    d_joined = jnp.concatenate([d_queries, d_keys, d_values], axis=1).astype(bf16)
    qkv_grad = dot_rows(normed_one, d_joined).astype(bf16)

    d_one = dot_cols(d_joined, qkv_w)
    both = (d_one * gain_one + e_two.astype(f32)).astype(bf16)
    back = lax.psum_scatter(both, "ctx", scatter_dimension=0, tiled=True).astype(f32)
    own_scaled, own_spread = centred(own)
    input_part = own_spread * (
        back
        - jnp.mean(back, axis=-1, keepdims=True)
        - own_scaled * jnp.mean(back * own_scaled, axis=-1, keepdims=True)
    )
    input_grad = (out_grad[0].astype(f32) + input_part).astype(bf16)

    first = (ctx == 0).astype(f32)
    joined_sum = jnp.sum(d_joined.astype(f32), axis=0).reshape(3, 1, head_dim)
    joined_full = jnp.where((jnp.arange(HEADS) == head)[None, :, None], joined_sum, 0.0)
    up_sum = up_sum.reshape(shards, 1, units)
    up_full = jnp.where((jnp.arange(ctx_count) == ctx)[None, :, None], up_sum, 0.0)
    small = [
        jnp.sum(d_one * centred(hidden_all)[0], axis=0),
        jnp.sum(d_one, axis=0),
        columns * first,
        gain_two_sum,
        shift_two_sum,
        joined_full,
        up_full,
    ]
    small = jnp.concatenate([piece.reshape(shards, -1) for piece in small], axis=1).astype(bf16)
    small_size = small.shape[1]
    small_rows = -(-small_size // (3 * head_dim * 16)) * 16
    small = jnp.pad(small, ((0, 0), (0, small_rows * 3 * head_dim - small_size)))
    last_grad = scatter_fsdp(
        jnp.concatenate(
            [
                qkv_grad.reshape(shards, rows, 3 * head_dim),
                small.reshape(shards, small_rows, 3 * head_dim),
            ],
            axis=1,
        ).reshape(-1, 3 * head_dim)
    )
    dense_share = scatter_fsdp(
        dense_grad.reshape(head_dim, shards, rows).transpose(1, 0, 2).reshape(-1, rows)
    )

    down_all = line_gather(down_grad).astype(f32).reshape(ctx_count * units, width)
    up_all = (
        line_gather(up_grad)
        .astype(f32)
        .reshape(ctx_count, rows, shards, units)
        .transpose(1, 2, 0, 3)
        .reshape(rows, ff)
    )
    dense_cols_all = line_gather(dense_share)
    if repeat > 1:
        dense_cols_all = jnp.sum(
            dense_cols_all.astype(f32).reshape(HEADS, repeat, head_dim, rows), axis=1
        ).astype(bf16)
    dense_all = lax.all_to_all(
        dense_cols_all.reshape(width, rows), "fsdp", split_axis=0, concat_axis=1, tiled=True
    ).astype(f32)
    last_all = line_gather(last_grad)
    qkv_all = last_all[:, :rows].astype(f32)
    if repeat > 1:
        qkv_all = jnp.sum(qkv_all.reshape(HEADS, repeat, rows, 3 * head_dim), axis=1)
    qkv_all = (
        qkv_all.reshape(HEADS, rows, 3, head_dim).transpose(1, 2, 0, 3).reshape(rows, 3 * width)
    )
    small_all = jnp.sum(last_all[:, rows:].astype(f32), axis=0).reshape(-1)
    sizes = [rows] * 5 + [3 * rows, ff // shards]
    parts, at = [], 0
    for size in sizes:
        parts.append(small_all[at : at + size])
        at += size
    gain_one_grad, shift_one_grad, columns_grad, gain_two_grad, shift_two_grad, joined_grad, up_b_grad = parts
    return (
        layer_output[None],
        input_grad[None],
        gain_one_grad,
        shift_one_grad,
        qkv_all,
        joined_grad,
        dense_all,
        columns_grad,
        gain_two_grad,
        shift_two_grad,
        up_all,
        up_b_grad,
        down_all,
        columns_grad,
    )


def solution(mesh):
    vec, mat, act = P("fsdp"), P("fsdp", None), P("fsdp", "ctx", None)
    return jax.shard_map(
        per_device,
        mesh=mesh,
        in_specs=(
            act, vec, vec, mat, vec, mat, vec, vec, vec, mat, vec, mat, vec, P("fsdp", "ctx"), act
        ),
        out_specs=(act, act, vec, vec, mat, vec, mat, vec, vec, vec, mat, vec, mat, vec),
        check_vma=False,
    )
```
